32 devices in a mesh: section: 2 (over x), dp: 16 (over z, y, core).
Axes of the slice: x: 2, y: 2, z: 4, core: 2. Of those that a mesh axis runs over, the one named last changes fastest.
Arguments:
- tokens: bfloat16 [48, 261, 768], P('dp'), may hold values from -6 to 6
- cotangent: bfloat16 [48, 261, 768], P('dp'), may hold values from -6 to 6
- patch_mask: int32 [48, 78], P('dp'), may hold values from 1 to 196, as said below
- text_mask: int32 [48, 32], P('dp'), may hold values from -1 to 260, as said below
- qkv_weight: bfloat16 [2, 768, 2304], P('section'), may hold values from -0.21875 to 0.21875
- qv_bias: float32 [2, 2, 768], P('section'), may hold values from -1.8 to 1.8
- out_weight: bfloat16 [2, 768, 768], P('section'), may hold values from -1.75 to 1.75
- out_bias: float32 [2, 768], P('section'), may hold values from -1.8 to 1.8
- norm_gain: float32 [2, 2, 768], P('section'), may hold values from 0.25 to 1.75
- norm_bias: float32 [2, 2, 768], P('section'), may hold values from -1.8 to 1.8
- up_table: bfloat16 [3, 768, 3072], replicated, may hold values from -0.21875 to 0.21875
- up_bias: float32 [3, 3072], replicated, may hold values from -1.8 to 1.8
- down_table: bfloat16 [3, 3072, 768], replicated, may hold values from -0.109375 to 0.109375
- down_bias: float32 [3, 768], replicated, may hold values from -1.8 to 1.8
Outputs:
- input_grad: float32 [48, 261, 768], P('dp', None, 'section')
- qkv_grad: float32 [2, 768, 2304], P('section', None, 'dp')
- qv_bias_grad: float32 [2, 2, 768], P('section', None, 'dp')
- out_grad: float32 [2, 768, 768], P('section', None, 'dp')
- out_bias_grad: float32 [2, 768], P('section', 'dp')
- gain_grad: float32 [2, 2, 768], P('section', None, 'dp')
- norm_bias_grad: float32 [2, 2, 768], P('section', None, 'dp')
- up_grad: float32 [3, 768, 3072], P(None, None, 'dp')
- up_bias_grad: float32 [3, 3072], P(None, 'dp')
- down_grad: float32 [3, 3072, 768], P(None, 'dp')
- down_bias_grad: float32 [3, 768], P(None, 'dp')
The draws below stay inside these ranges and needn't reach their ends.
Inputs may be any that keep to these rules, and one draw needn't show every extreme that they name: `patch_mask`: each row holds the positions of a block of 6 patch rows by 13 patch columns of the 14 x 14 grid, position 1 + row * 14 + column, all distinct. `text_mask`: each row holds 10 to 32 distinct text positions (from 197 on), then -1 in the remaining slots.
All inputs are finite; a program needn't handle non-finite values.
Results may differ from the reference program's by a relative error of at most 0.014.
Values may be sent and summed in bfloat16 or wider, within the bound.
A program may use at most 640 MiB of HBM per device.

```python
import jax
import jax.numpy as jnp
from jax import lax

D = 768
HEADS = 12
HEAD_DIM = 64
FF = 3072
GRID = 14
TEXT = 64
BLOCK_ROWS = 6
BLOCK_COLS = 13
PATCHES = 197
SEQ = 261
PMASK = 78
TMASK = 32
TMIN = 10
ITEMS = 48


def draw_patch_mask(key, part):
    key = jax.random.fold_in(key, 11)
    row_key, col_key = jax.random.split(key)
    top_row = jax.random.randint(row_key, (ITEMS,), 0, GRID - BLOCK_ROWS + 1)
    left_col = jax.random.randint(col_key, (ITEMS,), 0, GRID - BLOCK_COLS + 1)
    item_ids = jnp.arange(ITEMS)
    top_row = jnp.where(item_ids == 0, GRID - BLOCK_ROWS, jnp.where(item_ids == 1, 0, top_row))
    left_col = jnp.where(item_ids == 0, GRID - BLOCK_COLS, jnp.where(item_ids == 1, 0, left_col))
    grid_rows = top_row[:, None] + (jnp.arange(PMASK) // BLOCK_COLS)[None, :]
    grid_cols = left_col[:, None] + (jnp.arange(PMASK) % BLOCK_COLS)[None, :]
    return (1 + grid_rows * GRID + grid_cols).astype(jnp.int32)


def draw_text_mask(key, part):
    key = jax.random.fold_in(key, 23)
    count_key, order_key = jax.random.split(key)
    numbers = jnp.arange(ITEMS)
    counts = jax.random.randint(count_key, (ITEMS,), TMIN, TMASK + 1)
    counts = jnp.where(numbers == 0, TMASK, jnp.where(numbers == 1, TMIN, counts))
    orders = jax.vmap(lambda single: jax.random.permutation(single, TEXT))(jax.random.split(order_key, ITEMS))
    turned = (orders + (TEXT - 1 - orders[:, :1])) % TEXT
    orders = jnp.where((numbers == 0)[:, None], turned, orders)
    slot_ids = jnp.arange(TMASK)
    chosen = PATCHES + orders[:, :TMASK]
    return jnp.where(slot_ids[None, :] < counts[:, None], chosen, -1).astype(jnp.int32)


def levels(stream_key, shape, cuts, least, high):
    def one(axis_at, parts):
        steps = jax.random.uniform(jax.random.fold_in(jax.random.fold_in(stream_key, 6), axis_at), (parts,), jnp.float32, least / len(cuts), high / len(cuts))
        return jnp.repeat(jnp.exp(steps), shape[axis_at] // parts).reshape((-1,) + (1,) * (len(shape) - axis_at - 1))

    loudness = one(*cuts[0])
    for cut in cuts[1:]:
        loudness = loudness * one(*cut)
    return loudness


def gaussian(key, shape, scale, limit, cuts=(), kind=jnp.bfloat16):
    gain = levels(key, shape, cuts, -0.22, 0.18) if cuts else 1.0
    drawn = jax.random.normal(key, shape, jnp.float32) * scale * gain
    return jnp.minimum(jnp.maximum(drawn, -limit), limit).astype(kind)


def setup_inputs(seed: int = 0) -> dict:
    splits = jax.random.split(jax.random.key(seed), 15)
    tokens = gaussian(splits[0], (ITEMS, SEQ, D), 1.0, 6.0, ((0, 16),))
    cotangent = gaussian(splits[1], (ITEMS, SEQ, D), 1.0, 6.0, ((0, 16),))
    patch_mask = draw_patch_mask(jax.random.fold_in(splits[14], 71), 0)
    text_mask = draw_text_mask(jax.random.fold_in(splits[14], 71), 0)
    qkv_weight = gaussian(splits[4], (2, D, 3 * D), D ** -0.5, 0.21875, ((0, 2),))
    qv_bias = gaussian(splits[5], (2, 2, D), 0.3, 1.8, ((0, 2),), jnp.float32)
    out_weight = gaussian(splits[6], (2, D, D), (max(D // 64, 8)) ** -0.5, 1.75, ((0, 2),))
    out_bias = gaussian(splits[7], (2, D), 0.3, 1.8, ((0, 2),), jnp.float32)
    norm_gain = jnp.clip(1.0 + 0.15 * jax.random.normal(splits[8], (2, 2, D), jnp.float32), 0.25, 1.75)
    norm_bias = gaussian(splits[9], (2, 2, D), 0.3, 1.8, ((0, 2),), jnp.float32)
    up_table = gaussian(splits[10], (3, D, FF), D ** -0.5, 0.21875)
    up_bias = gaussian(splits[11], (3, FF), 0.3, 1.8, (), jnp.float32)
    down_table = gaussian(splits[12], (3, FF, D), FF ** -0.5, 0.109375)
    down_bias = gaussian(splits[13], (3, D), 0.3, 1.8, (), jnp.float32)
    return dict(tokens=tokens, cotangent=cotangent, patch_mask=patch_mask, text_mask=text_mask, qkv_weight=qkv_weight, qv_bias=qv_bias, out_weight=out_weight, out_bias=out_bias, norm_gain=norm_gain, norm_bias=norm_bias, up_table=up_table, up_bias=up_bias, down_table=down_table, down_bias=down_bias)


EPSILON = 1e-05

@jax.custom_vjp
def low(v):
    return lax.optimization_barrier(v.astype(jnp.bfloat16)).astype(jnp.float32)

@jax.custom_vjp
def low_back(v):
    return v

def low_keep(v):
    return (low(v), None)

def low_pass(kept, grad):
    return (grad,)

def back_keep(v):
    return (v, None)

def back_low(kept, grad):
    return (low(grad),)
low.defvjp(low_keep, low_pass)
low_back.defvjp(back_keep, back_low)

def layer_norm(values, gain_row, bias_row):
    centre = values - lax.optimization_barrier(jnp.mean(values, -1, keepdims=True))
    spread = lax.optimization_barrier(jnp.mean(centre * centre, -1, keepdims=True))
    return centre * lax.rsqrt(spread + EPSILON) * gain_row + bias_row

def feed_forward(inputs, expert):
    w_inner, b_inner, w_outer, b_outer = expert
    hidden = low_back(jnp.einsum('gsd,df->gsf', inputs, w_inner, precision=lax.Precision.HIGHEST) + b_inner)
    active = low(jax.nn.gelu(hidden, approximate=False))
    return low_back(jnp.einsum('gsf,fd->gsd', active, w_outer, precision=lax.Precision.HIGHEST) + b_outer)

def block(values, layer_params):
    attn_in, attn_bias, attn_out, proj_bias, norm_gains, norm_shifts, vision_ffn, text_ffn = layer_params
    groups = values.shape[0]
    normed = low(layer_norm(values, norm_gains[0], norm_shifts[0]))
    mixed_proj = jnp.einsum('gsd,de->gse', normed, attn_in, precision=lax.Precision.HIGHEST)
    query_heads = low_back(low(mixed_proj[..., :D] + attn_bias[0])).reshape(groups, SEQ, HEADS, HEAD_DIM)
    key_heads = low_back(low(mixed_proj[..., D:2 * D])).reshape(groups, SEQ, HEADS, HEAD_DIM)
    value_heads = low_back(low(mixed_proj[..., 2 * D:] + attn_bias[1])).reshape(groups, SEQ, HEADS, HEAD_DIM)
    scores = low_back(jnp.einsum('gqhc,gkhc->ghqk', query_heads, key_heads, precision=lax.Precision.HIGHEST) * HEAD_DIM ** (-0.5))
    attn_probs = low(jax.nn.softmax(scores, axis=-1))
    attended = jnp.einsum('ghqk,gkhc->gqhc', attn_probs, value_heads, precision=lax.Precision.HIGHEST).reshape(groups, SEQ, D)
    attended = low_back(low(attended))
    branch = low_back(jnp.einsum('gsd,de->gse', attended, attn_out, precision=lax.Precision.HIGHEST) + proj_bias)
    middle = values + branch
    normed_two = low(layer_norm(middle, norm_gains[1], norm_shifts[1]))
    expert_out = jnp.concatenate([feed_forward(normed_two[:, :PATCHES], vision_ffn), feed_forward(normed_two[:, PATCHES:], text_ffn)], axis=1)
    return middle + expert_out

def model(layer_input, qkv_weight, qv_bias, out_weight, out_bias, norm_gain, norm_bias, up_table, up_bias, down_table, down_bias):

    def expert(row_index):
        return (up_table[row_index], up_bias[row_index], down_table[row_index], down_bias[row_index])
    first_layer = (qkv_weight[0], qv_bias[0], out_weight[0], out_bias[0], norm_gain[0], norm_bias[0], expert(0), expert(1))
    second_layer = (qkv_weight[1], qv_bias[1], out_weight[1], out_bias[1], norm_gain[1], norm_bias[1], expert(2), expert(2))
    passed = low_back(low(block(layer_input, first_layer)))
    return block(passed, second_layer)

def reference(tokens, cotangent, patch_mask, text_mask, qkv_weight, qv_bias, out_weight, out_bias, norm_gain, norm_bias, up_table, up_bias, down_table, down_bias):
    params = tuple((argument.astype(jnp.float32) for argument in (qkv_weight, qv_bias, out_weight, out_bias, norm_gain, norm_bias, up_table, up_bias, down_table, down_bias)))
    positions = jnp.arange(SEQ, dtype=jnp.int32)

    def accumulate(totals, inputs):
        item_tokens, item_cot, item_patch, item_text = inputs
        hit_rows = jnp.any(positions[:, None] == item_patch[None, :], axis=1) | jnp.any(positions[:, None] == item_text[None, :], axis=1)
        target = item_cot.astype(jnp.float32) * hit_rows.astype(jnp.float32)[:, None]
        result, pullback = jax.vjp(model, item_tokens.astype(jnp.float32)[None], *params)
        pulled = pullback(target[None])
        return (tuple((summed + piece for summed, piece in zip(totals, pulled[1:]))), pulled[0][0])
    initial = tuple((jnp.zeros(argument.shape, jnp.float32) for argument in params))
    totals, input_grad = lax.scan(accumulate, initial, (tokens, cotangent, patch_mask, text_mask))
    return (input_grad, totals[0], totals[1], totals[2], totals[3], totals[4], totals[5], totals[6], totals[7], totals[8], totals[9])
```

```python
import jax
import jax.numpy as jnp
from jax import lax
from jax.experimental import pallas as pl
from jax.experimental.pallas import tpu as pltpu
from jax.sharding import PartitionSpec as P

HEAD_DIM = 64
PATCHES = 197
EPSILON = 1e-05
BLOCK = 384
RING = 3
TEXT = 64
ROWS = 272
MESH = pl.DeviceIdType.MESH


def sum_kernel(
    lt_ref, hd_ref, act_ref, mix_ref, proj_ref, res_ref,
    rt, part, xs, xr, yr, zr, zl,
    rt_sem, core_send, core_recv, y_send, y_recv, right_send, right_recv, left_send, left_recv,
    own_sem, peer_send, peer_recv, cross_send, cross_recv, hand_send, hand_recv, credit,
):
    section = lax.axis_index("section")
    me = lax.axis_index("dp")
    z, y, core = me // 4, (me // 2) % 2, me % 2
    peer = (section, me + 1 - 2 * core)
    beside = (section, me + 2 - 4 * y)
    right = (section, me + 4)
    left = (section, me - 4)
    across = (1 - section, me)
    units = jnp.where(section == 0, 20, 12)
    other_kinds = jnp.where(section == 0, 2, 4)

    def kind_of(u):
        q = u // 4
        return jnp.where((section == 1) & (q == 2), 4, q)

    def plane_of(u):
        o = u % 4
        return jnp.where(o == 0, 0, jnp.where(o == 1, 3, o - 1))

    def remote(src, dst, send, recv, device):
        return pltpu.make_async_remote_copy(
            src_ref=src, dst_ref=dst, send_sem=send, recv_sem=recv, device_id=device, device_id_type=MESH
        )

    def core_copy(u, b):
        slot = u % RING
        return remote(xs.at[slot, b], xr.at[slot, b], core_send.at[u, b], core_recv.at[u, b], peer)

    def y_copy(u):
        return remote(part.at[u, 0], yr.at[u], y_send.at[u], y_recv.at[u], beside)

    def right_copy(u):
        return remote(part.at[u, 1], zr.at[u], right_send.at[u], right_recv.at[u], right)

    def left_copy(u):
        return remote(part.at[u, 1], zl.at[u], left_send.at[u], left_recv.at[u], left)

    def own_copy(u):
        k = kind_of(u)
        return pltpu.make_async_copy(part.at[u, 1], res_ref.at[0, core, k], own_sem.at[k])

    def peer_copy(u):
        k = kind_of(u)
        return remote(part.at[u, 1], res_ref.at[0, core, k], peer_send.at[k], peer_recv.at[k], peer)

    def cross_copy(u):
        k = kind_of(u)
        return remote(part.at[u, 1], res_ref.at[1, core, k], cross_send.at[k], cross_recv.at[k], across)

    def cross_arrival(k):
        return remote(part.at[0, 1], res_ref.at[1, core, k], cross_send.at[k], cross_recv.at[k], across)

    def hand_copy(k):
        return remote(res_ref.at[1, core, k], res_ref.at[1, core, k], hand_send.at[k], hand_recv.at[k], peer)

    def tile_copies(s):
        u, b, slot = s // 2, s % 2, s % 2
        k = kind_of(u)
        t = plane_of(u) * 2 + jnp.where(b == 0, 1 - y, y)
        columns = pl.ds(pl.multiple_of(t * BLOCK, 128), BLOCK)
        cases = []
        for ref, which, here in (
            (hd_ref, 0, (k == 0) | (k == 2)),
            (act_ref, 0, (k == 1) | (k == 3)),
            (mix_ref, 0, k == 4),
            (proj_ref, 1, k == 4),
        ):
            cases.append((here, pltpu.make_async_copy(ref.at[:, columns], rt.at[slot, which], rt_sem.at[slot, which])))
        return cases

    def start_tile(s):
        for here, copy in tile_copies(s):
            pl.when(here)(copy.start)

    def wait_tile(s):
        for here, copy in tile_copies(s):
            pl.when(here)(copy.wait)

    def add_into(target, source):
        target[...] = (target[...].astype(jnp.float32) + source[...].astype(jnp.float32)).astype(jnp.bfloat16)

    def rows(half):
        return pl.ds(pl.multiple_of(half * BLOCK, BLOCK), BLOCK)

    def dot(index, half, tile):
        return jnp.dot(lt_ref[index, rows(half), :], tile[...], preferred_element_type=jnp.float32)

    def compute(u):
        k = kind_of(u)
        ring = u % RING

        @pl.when(u >= RING)
        def _():
            core_copy(u - RING, 0).wait_send()
            core_copy(u - RING, 1).wait_send()
            pl.semaphore_wait(credit, 1)

        def block(b, carry):
            s = 2 * u + b
            slot = s % 2

            @pl.when(s + 1 < 2 * units)
            def _():
                start_tile(s + 1)

            wait_tile(s)

            @pl.when(k < 4)
            def _():
                xs[ring, b] = dot(k, 1 - core, rt.at[slot, 0]).astype(jnp.bfloat16)

            @pl.when(k == 4)
            def _():
                value = dot(4, 1 - core, rt.at[slot, 0]) + dot(5, 1 - core, rt.at[slot, 1])
                xs[ring, b] = value.astype(jnp.bfloat16)

            core_copy(u, b).start()

            @pl.when(k < 4)
            def _():
                part[u, b] = dot(k, core, rt.at[slot, 0]).astype(jnp.bfloat16)

            @pl.when(k == 4)
            def _():
                value = dot(4, core, rt.at[slot, 0]) + dot(5, core, rt.at[slot, 1])
                part[u, b] = value.astype(jnp.bfloat16)

            return carry

        lax.fori_loop(0, 2, block, 0)

    def join_core(u):
        ring = u % RING
        core_copy(u, 0).wait_recv()
        add_into(part.at[u, 0], xr.at[ring, 0])
        y_copy(u).start()
        core_copy(u, 1).wait_recv()
        add_into(part.at[u, 1], xr.at[ring, 1])

        @pl.when(u + RING < units)
        def _():
            pl.semaphore_signal(credit, inc=1, device_id=peer, device_id_type=MESH)

    def join_y(u):
        y_copy(u).wait_recv()
        add_into(part.at[u, 1], yr.at[u])

    def take_right(u):
        right_copy(u).wait_recv()
        add_into(part.at[u, 1], zr.at[u])

    def take_left(u):
        left_copy(u).wait_recv()
        add_into(part.at[u, 1], zl.at[u])

    def pass_right(u):
        pl.when(z > 0)(lambda: take_right(u))
        right_copy(u).start()

    def pass_left(u):
        pl.when(z < 3)(lambda: take_left(u))
        left_copy(u).start()

    def finish(u):
        pl.when(z > 0)(lambda: take_right(u))
        pl.when(z < 3)(lambda: take_left(u))
        own_copy(u).start()
        peer_copy(u).start()

        @pl.when(kind_of(u) < 4)
        def _():
            cross_copy(u).start()

    def within(u):
        return (u >= 0) & (u < units)

    def when_in(u, condition, action):
        @pl.when(within(u) & condition)
        def _():
            action(u)

    barrier = pltpu.get_barrier_semaphore()
    for device in (peer, beside, across):
        pl.semaphore_signal(barrier, inc=1, device_id=device, device_id_type=MESH)

    @pl.when(z < 3)
    def _():
        pl.semaphore_signal(barrier, inc=1, device_id=right, device_id_type=MESH)

    @pl.when(z > 0)
    def _():
        pl.semaphore_signal(barrier, inc=1, device_id=left, device_id_type=MESH)

    start_tile(0)
    pl.semaphore_wait(barrier, 3 + jnp.where(z < 3, 1, 0) + jnp.where(z > 0, 1, 0))

    def step(i, carry):
        pl.when(i < units)(lambda: compute(i))
        when_in(i - 1, True, join_core)
        when_in(i - 4, True, join_y)
        u = i - 4 - 2 * z
        when_in(u, plane_of(jnp.maximum(u, 0)) > z, pass_right)
        u = i - 10 + 2 * z
        when_in(u, plane_of(jnp.maximum(u, 0)) < z, pass_left)
        u = i - 12
        when_in(u, plane_of(jnp.maximum(u, 0)) == z, finish)
        return carry

    lax.fori_loop(0, units + 12, step, 0)

    def settle(u, carry):
        @pl.when(u >= units - RING)
        def _():
            core_copy(u, 0).wait_send()
            core_copy(u, 1).wait_send()

        y_copy(u).wait_send()
        plane = plane_of(u)

        @pl.when(plane > z)
        def _():
            right_copy(u).wait_send()

        @pl.when(plane < z)
        def _():
            left_copy(u).wait_send()

        @pl.when(plane == z)
        def _():
            own_copy(u).wait()
            peer_copy(u).wait()

            @pl.when(kind_of(u) < 4)
            def _():
                cross_copy(u).wait_send()

        return carry

    def hand(k, carry):
        cross_arrival(k).wait_recv()
        hand_copy(k).start()
        return carry

    lax.fori_loop(0, other_kinds, hand, 0)
    lax.fori_loop(0, units, settle, 0)

    def handed(k, carry):
        hand_copy(k).wait()
        return carry

    lax.fori_loop(0, other_kinds, handed, 0)


def summed_blocks(left, hidden_delta, active, mixed, proj):
    dma = pltpu.SemaphoreType.DMA
    depth = left.shape[2]
    tile = (BLOCK, BLOCK)
    return pl.pallas_call(
        sum_kernel,
        out_shape=jax.ShapeDtypeStruct((2, 2, 5) + tile, jnp.bfloat16),
        in_specs=[pl.BlockSpec(memory_space=pltpu.VMEM)] + [pl.BlockSpec(memory_space=pl.ANY)] * 4,
        out_specs=pl.BlockSpec(memory_space=pl.ANY),
        scratch_shapes=[
            pltpu.VMEM((2, 2, depth, BLOCK), jnp.bfloat16),
            pltpu.VMEM((20, 2) + tile, jnp.bfloat16),
            pltpu.VMEM((RING, 2) + tile, jnp.bfloat16),
            pltpu.VMEM((RING, 2) + tile, jnp.bfloat16),
            pltpu.VMEM((20,) + tile, jnp.bfloat16),
            pltpu.VMEM((20,) + tile, jnp.bfloat16),
            pltpu.VMEM((20,) + tile, jnp.bfloat16),
            dma((2, 2)),
            dma((20, 2)),
            dma((20, 2)),
            dma((20,)),
            dma((20,)),
            dma((20,)),
            dma((20,)),
            dma((20,)),
            dma((20,)),
            dma((5,)),
            dma((5,)),
            dma((5,)),
            dma((5,)),
            dma((5,)),
            dma((5,)),
            dma((5,)),
            pltpu.SemaphoreType.REGULAR,
        ],
        compiler_params=pltpu.CompilerParams(
            collective_id=0, has_side_effects=True, vmem_limit_bytes=56 * 1024 * 1024
        ),
        cost_estimate=pl.CostEstimate(flops=48 * 2 * 768 * 384 * depth, bytes_accessed=40_000_000, transcendentals=0),
    )(left, hidden_delta, active, mixed, proj)


def passed_along(block, axis, distance):
    devices = range(lax.axis_size(axis))
    route = [(i - distance, i) for i in devices if i - distance in devices]
    return lax.ppermute(block, axis, route)


def exact_gelu(values):
    return jax.nn.gelu(values, approximate=False)


def layer_norm(values, gain_row, bias_row):
    centre = values - jnp.mean(values, -1, keepdims=True)
    spread = jnp.mean(centre * centre, -1, keepdims=True)
    inverse = lax.rsqrt(spread + EPSILON)
    standard = centre * inverse
    return (standard * gain_row + bias_row, standard, inverse)


def norm_back(out_delta, standard, inverse, gain_row):
    scaled_delta = out_delta * gain_row
    result = inverse * (
        scaled_delta
        - jnp.mean(scaled_delta, -1, keepdims=True)
        - standard * jnp.mean(scaled_delta * standard, -1, keepdims=True)
    )
    return (result, jnp.sum(out_delta * standard, axis=(0, 1)), jnp.sum(out_delta, axis=(0, 1)))


def project(left_side, right_side):
    return jnp.einsum("bsk,kn->bsn", left_side, right_side, preferred_element_type=jnp.float32)


def project_back(left_side, right_side):
    return jnp.einsum("bsn,kn->bsk", left_side, right_side, preferred_element_type=jnp.float32)


def forward_pass(inputs, layer_params, length):
    (attn_in, attn_bias, attn_out, proj_bias, norm_gains, norm_shifts, w_inner, b_inner, w_outer, b_outer) = layer_params
    batch_size, rows, model_width = inputs.shape
    head_count = model_width // HEAD_DIM
    normed, standard_one, inverse_one = layer_norm(inputs, norm_gains[0], norm_shifts[0])
    normed_low = normed.astype(jnp.bfloat16)
    mixed_proj = project(normed_low, attn_in)

    def heads(values):
        return values.astype(jnp.bfloat16).reshape(batch_size, rows, head_count, HEAD_DIM)

    query_heads = heads(mixed_proj[..., :model_width] + attn_bias[0])
    key_heads = heads(mixed_proj[..., model_width : 2 * model_width])
    value_heads = heads(mixed_proj[..., 2 * model_width :] + attn_bias[1])
    scores = jnp.einsum(
        "bqhc,bkhc->bhqk", query_heads, key_heads, preferred_element_type=jnp.float32
    ) * HEAD_DIM ** (-0.5)
    scores = jnp.where(jnp.arange(rows) < length, scores, -1e30)
    shifted = jnp.exp(scores - jnp.max(scores, -1, keepdims=True))
    attn_probs = shifted / jnp.sum(shifted, -1, keepdims=True)
    probs_low = attn_probs.astype(jnp.bfloat16)
    attended = (
        jnp.einsum("bhqk,bkhc->bqhc", probs_low, value_heads, preferred_element_type=jnp.float32)
        .reshape(batch_size, rows, model_width)
        .astype(jnp.bfloat16)
    )
    middle = inputs + project(attended, attn_out) + proj_bias
    normed_two, standard_two, inverse_two = layer_norm(middle, norm_gains[1], norm_shifts[1])
    normed_two_low = normed_two.astype(jnp.bfloat16)
    bounds = ((TEXT, rows), (0, TEXT))
    hiddens = []
    actives = []
    outputs = []
    for slot_id in range(2):
        begin_row, end_row = bounds[slot_id]
        hidden = project(normed_two_low[:, begin_row:end_row], w_inner[slot_id]) + b_inner[slot_id]
        active = exact_gelu(hidden).astype(jnp.bfloat16)
        hiddens.append(hidden)
        actives.append(active)
        outputs.append(project(active, w_outer[slot_id]) + b_outer[slot_id])
    result = middle + jnp.concatenate(outputs[::-1], axis=1)
    saved_parts = (
        normed_low, standard_one, inverse_one, query_heads, key_heads, value_heads, attn_probs, probs_low,
        attended, standard_two, inverse_two, normed_two_low, hiddens, actives,
    )
    return (result, saved_parts)


def backward_pass(out_delta, saved_parts, layer_params):
    (attn_in, attn_bias, attn_out, proj_bias, norm_gains, norm_shifts, w_inner, b_inner, w_outer, b_outer) = layer_params
    (
        normed_low, standard_one, inverse_one, query_heads, key_heads, value_heads, attn_probs, probs_low,
        attended, standard_two, inverse_two, normed_two_low, hiddens, actives,
    ) = saved_parts
    batch_size, rows, model_width = out_delta.shape
    scaling = HEAD_DIM ** (-0.5)
    bounds = ((TEXT, rows), (0, TEXT))
    branch_delta = out_delta.astype(jnp.bfloat16)
    inner_bias_grads = []
    outer_bias_grads = []
    hidden_deltas = []
    pieces = []
    for slot_id in range(2):
        begin_row, end_row = bounds[slot_id]
        branch = branch_delta[:, begin_row:end_row]
        outer_bias_grads.append(jnp.sum(branch.astype(jnp.float32), axis=(0, 1)))
        active_delta = project_back(branch, w_outer[slot_id])
        unused, gelu_pull = jax.vjp(exact_gelu, hiddens[slot_id])
        hidden_delta = gelu_pull(active_delta)[0].astype(jnp.bfloat16)
        inner_bias_grads.append(jnp.sum(hidden_delta.astype(jnp.float32), axis=(0, 1)))
        hidden_deltas.append(hidden_delta)
        pieces.append(project_back(hidden_delta, w_inner[slot_id]))
    middle_part, gain_two, shift_two = norm_back(
        jnp.concatenate(pieces[::-1], axis=1), standard_two, inverse_two, norm_gains[1]
    )
    middle_delta = out_delta + middle_part
    proj_delta = middle_delta.astype(jnp.bfloat16)
    proj_bias_grad = jnp.sum(proj_delta.astype(jnp.float32), axis=(0, 1))
    attended_delta = (
        project_back(proj_delta, attn_out).astype(jnp.bfloat16).reshape(batch_size, rows, -1, HEAD_DIM)
    )
    probs_delta = jnp.einsum(
        "bqhc,bkhc->bhqk", attended_delta, value_heads, preferred_element_type=jnp.float32
    )
    value_delta = jnp.einsum(
        "bhqk,bqhc->bkhc", probs_low, attended_delta, preferred_element_type=jnp.float32
    ).astype(jnp.bfloat16)
    score_delta = (
        attn_probs * (probs_delta - jnp.sum(probs_delta * attn_probs, -1, keepdims=True))
    ).astype(jnp.bfloat16)
    query_delta = (
        jnp.einsum("bhqk,bkhc->bqhc", score_delta, key_heads, preferred_element_type=jnp.float32) * scaling
    ).astype(jnp.bfloat16)
    key_delta = (
        jnp.einsum("bhqk,bqhc->bkhc", score_delta, query_heads, preferred_element_type=jnp.float32) * scaling
    ).astype(jnp.bfloat16)
    flat = (batch_size, rows, model_width)
    query_flat = query_delta.reshape(flat)
    value_flat = value_delta.reshape(flat)
    mixed_delta = jnp.concatenate([query_flat, key_delta.reshape(flat), value_flat], axis=2)
    attn_bias_grad = jnp.stack(
        [jnp.sum(query_flat.astype(jnp.float32), axis=(0, 1)), jnp.sum(value_flat.astype(jnp.float32), axis=(0, 1))]
    )
    input_part, gain_one, shift_one = norm_back(
        project_back(mixed_delta, attn_in), standard_one, inverse_one, norm_gains[0]
    )
    input_delta = middle_delta + input_part
    small = (
        attn_bias_grad,
        proj_bias_grad[None],
        jnp.stack([gain_one, gain_two]),
        jnp.stack([shift_one, shift_two]),
        jnp.stack(inner_bias_grads),
        jnp.stack(outer_bias_grads),
    )
    large = (
        normed_low, attended, normed_two_low, branch_delta, mixed_delta, proj_delta,
        jnp.concatenate(hidden_deltas[::-1], axis=1), jnp.concatenate(actives[::-1], axis=1),
    )
    return (input_delta, small, large)


def text_first(values):
    pad = jnp.zeros((values.shape[0], ROWS - values.shape[1]) + values.shape[2:], values.dtype)
    return jnp.concatenate([values[:, PATCHES:], values[:, :PATCHES], pad], axis=1)


def patches_first(values, length):
    return jnp.concatenate([values[:, TEXT:length], values[:, :TEXT]], axis=1)


def pick(table_rows, row_index):
    return lax.dynamic_index_in_dim(table_rows, row_index, 0, keepdims=False)


def large_grads(large, is_first):
    normed_one, attended, normed_two, branch_delta, mixed_delta, proj_delta, hidden_delta, active = (
        piece.reshape((-1, piece.shape[-1])) for piece in large
    )
    count = lax.axis_size("dp")
    total, width = normed_one.shape
    text = (jnp.arange(total) % ROWS < TEXT)[:, None]
    vision = jnp.logical_not(text & is_first).astype(jnp.bfloat16)
    text = text.astype(jnp.bfloat16)
    lefts = [
        (piece).T
        for piece in (
            normed_two * vision, branch_delta * vision, normed_two * text, branch_delta * text, normed_one, attended,
        )
    ]
    if count == 16:
        chips = count // 2
        core = lax.axis_index("dp") % 2
        mixed = jnp.pad(mixed_delta.reshape(total, chips, -1), ((0, 0), (0, 0), (0, 96))).reshape(total, -1)
        proj = jnp.pad(proj_delta.reshape(total, chips, -1), ((0, 0), (0, 0), (288, 0))).reshape(total, -1)
        blocks = summed_blocks(jnp.stack(lefts), hidden_delta, active, mixed, proj)
        own, other = blocks[0], blocks[1]

        def whole(block, begin, wide):
            both = block.reshape(width, BLOCK)
            return lax.dynamic_slice_in_dim(both, begin + core * wide, wide, 1).astype(jnp.float32)

        first = [jnp.where(is_first, own[:, k], other[:, k]) for k in range(4)]
        second = [jnp.where(is_first, other[:, k], own[:, k]) for k in range(2)]
        up = jnp.stack([whole(block, 0, 192) for block in (first[0], first[2], second[0])])
        down = jnp.stack([whole(block, 0, 192).T for block in (first[1], first[3], second[1])])
        return (whole(own[:, 4], 0, 144), whole(own[:, 4], 288, 48), up, down)

    def total_of(left, right):
        product = jnp.dot(left, right, preferred_element_type=jnp.float32).astype(jnp.bfloat16)
        return lax.psum_scatter(product, "dp", scatter_dimension=1, tiled=True)

    def table(vision_part, text_part):
        def swapped(part):
            return lax.psum(part, "section").astype(jnp.float32)

        return jnp.stack(
            [
                swapped(jnp.where(is_first, vision_part, 0)),
                swapped(jnp.where(is_first, text_part, 0)),
                swapped(jnp.where(is_first, 0, vision_part)),
            ]
        )

    up = table(total_of(lefts[0], hidden_delta), total_of(lefts[2], hidden_delta))
    down = table(total_of(lefts[1], active), total_of(lefts[3], active))
    return (
        total_of(lefts[4], mixed_delta).astype(jnp.float32),
        total_of(lefts[5], proj_delta).astype(jnp.float32),
        up,
        down.transpose(0, 2, 1),
    )


def small_grads(small, is_first):
    count = lax.axis_size("dp")
    inner, outer = small[4], small[5]

    def slots(parts):
        return jnp.stack([jnp.where(is_first, parts[0], parts[0] + parts[1]), parts[1]])

    pieces = list(small[:4]) + [slots(inner), slots(outer)]
    split = [piece.reshape(piece.shape[0], count, -1).transpose(1, 0, 2) for piece in pieces]
    shapes = [piece.shape[1:] for piece in split]
    joined = jnp.concatenate([piece.reshape(count, -1) for piece in split], axis=1)
    mine = lax.psum_scatter(joined, "dp", scatter_dimension=0, tiled=True)[0]
    outs = []
    at = 0
    for shape in shapes:
        size = shape[0] * shape[1]
        outs.append(mine[at : at + size].reshape(shape))
        at += size
    moved = jnp.concatenate([outs[4], outs[5]], axis=1)
    other = lax.ppermute(moved, "section", [(0, 1), (1, 0)])
    first = jnp.where(is_first, moved, other)
    second = jnp.where(is_first, other, moved)
    table = jnp.concatenate([first, second[:1]])
    wide = outs[4].shape[1]
    return outs[0], outs[1], outs[2], outs[3], table[:, :wide], table[:, wide:]


def shards(
    tokens, cotangent, patch_mask, text_mask, qkv_weight, qv_bias, out_weight, out_bias, norm_gain, norm_bias,
    up_table, up_bias, down_table, down_bias,
):
    section_index = lax.axis_index("section")
    is_first = section_index == 0
    vision_slot = jnp.where(is_first, 0, 2)
    text_slot = jnp.where(is_first, 1, 2)
    layer_params = (
        qkv_weight[0], qv_bias[0], out_weight[0], out_bias[0], norm_gain[0], norm_bias[0],
        [pick(up_table, vision_slot), pick(up_table, text_slot)],
        [pick(up_bias, vision_slot), pick(up_bias, text_slot)],
        [pick(down_table, vision_slot), pick(down_table, text_slot)],
        [pick(down_bias, vision_slot), pick(down_bias, text_slot)],
    )
    items_dev, length, model_width = tokens.shape
    positions = jnp.arange(length, dtype=jnp.int32)
    chosen = jnp.any(positions[None, :, None] == patch_mask[:, None, :], axis=2) | jnp.any(
        positions[None, :, None] == text_mask[:, None, :], axis=2
    )
    targets = text_first(cotangent * chosen.astype(jnp.bfloat16)[..., None])
    own = text_first(tokens)
    out, unused = forward_pass(own.astype(jnp.float32), layer_params, length)
    arrived = passed_along(out.astype(jnp.bfloat16), "section", 1)
    inside = (jnp.arange(ROWS) < length)[:, None]
    layer_in = jnp.where(is_first, own, jnp.where(inside, arrived, 0))
    unused, saved = forward_pass(layer_in.astype(jnp.float32), layer_params, length)
    input_delta, unused, unused = backward_pass(targets.astype(jnp.float32), saved, layer_params)
    returned = passed_along(input_delta.astype(jnp.bfloat16), "section", -1)
    out_delta = jnp.where(is_first, returned, targets)
    input_delta, small, large = backward_pass(out_delta.astype(jnp.float32), saved, layer_params)
    half_width = model_width // 2
    input_delta = patches_first(input_delta, length)
    moved_half = passed_along(input_delta[..., half_width:].astype(jnp.bfloat16), "section", 1)
    qkv, out, up, down = large_grads(large, is_first)
    qv_part, proj_part, gain_part, shift_part, up_part, down_part = small_grads(small, is_first)
    input_grad = jnp.where(is_first, input_delta[..., :half_width], moved_half.astype(jnp.float32))
    return (
        input_grad, qkv[None], qv_part[None], out[None], proj_part, gain_part[None], shift_part[None],
        up, up_part, down, down_part,
    )


def solution(mesh):
    return jax.shard_map(
        shards,
        mesh=mesh,
        in_specs=(
            P("dp", None, None), P("dp", None, None), P("dp", None), P("dp", None),
            P("section", None, None), P("section", None, None), P("section", None, None), P("section", None),
            P("section", None, None), P("section", None, None), P(), P(), P(), P(),
        ),
        out_specs=(
            P("dp", None, "section"), P("section", None, "dp"), P("section", None, "dp"), P("section", None, "dp"),
            P("section", "dp"), P("section", None, "dp"), P("section", None, "dp"),
            P(None, None, "dp"), P(None, "dp"), P(None, "dp", None), P(None, "dp"),
        ),
        check_vma=False,
    )
```

```python
import functools

import jax
import jax.numpy as jnp
from jax import lax
from jax.experimental import pallas as pl
from jax.experimental.pallas import tpu as pltpu
from jax.sharding import PartitionSpec as P

HEAD_DIM = 64
PATCHES = 197
EPSILON = 1e-05
BLOCK = 384
RING = 3
TEXT = 64
ROWS = 272
MESH = pl.DeviceIdType.MESH


def sum_kernel(
    lt_ref, small_ref, hd_refs, act_refs, mix_refs, proj_refs, res_ref, small_out,
    rt, part, xs, xr, yr, zr, zl, small_sum, small_in, small_send, small_recv,
    rt_sem, core_send, core_recv, y_send, y_recv, right_send, right_recv, left_send, left_recv,
    own_sem, peer_send, peer_recv, cross_send, cross_recv, hand_send, hand_recv, credit,
):
    section = lax.axis_index("section")
    me = lax.axis_index("dp")
    z, y, core = me // 4, (me // 2) % 2, me % 2
    peer = (section, me + 1 - 2 * core)
    beside = (section, me + 2 - 4 * y)
    right = (section, me + 4)
    left = (section, me - 4)
    across = (1 - section, me)
    units = jnp.where(section == 0, 20, 12)
    other_kinds = jnp.where(section == 0, 2, 4)

    def kind_of(u):
        q = u // 4
        return jnp.where((section == 1) & (q == 2), 4, q)

    def plane_of(u):
        o = u % 4
        return jnp.where(o == 0, 0, jnp.where(o == 1, 3, o - 1))

    def remote(src, dst, send, recv, device):
        return pltpu.make_async_remote_copy(
            src_ref=src, dst_ref=dst, send_sem=send, recv_sem=recv, device_id=device, device_id_type=MESH
        )

    def core_copy(u, b):
        slot = u % RING
        return remote(xs.at[slot, b], xr.at[slot, b], core_send.at[u, b], core_recv.at[u, b], peer)

    def y_copy(u):
        return remote(part.at[u, 0], yr.at[u], y_send.at[u], y_recv.at[u], beside)

    def right_copy(u):
        return remote(part.at[u, 1], zr.at[u], right_send.at[u], right_recv.at[u], right)

    def left_copy(u):
        return remote(part.at[u, 1], zl.at[u], left_send.at[u], left_recv.at[u], left)

    def own_copy(u):
        k = kind_of(u)
        return pltpu.make_async_copy(part.at[u, 1], res_ref.at[0, core, k], own_sem.at[k])

    def peer_copy(u):
        k = kind_of(u)
        return remote(part.at[u, 1], res_ref.at[0, core, k], peer_send.at[k], peer_recv.at[k], peer)

    def cross_copy(u):
        k = kind_of(u)
        return remote(part.at[u, 1], res_ref.at[1, core, k], cross_send.at[k], cross_recv.at[k], across)

    def cross_arrival(k):
        return remote(part.at[0, 1], res_ref.at[1, core, k], cross_send.at[k], cross_recv.at[k], across)

    def hand_copy(k):
        return remote(res_ref.at[1, core, k], res_ref.at[1, core, k], hand_send.at[k], hand_recv.at[k], peer)

    def tile_copies(s):
        u, b, slot = s // 2, s % 2, s % 2
        k = kind_of(u)
        t = plane_of(u) * 2 + jnp.where(b == 0, 1 - y, y)
        columns = pl.ds(pl.multiple_of(t * BLOCK, 128), BLOCK)
        cases = []
        for refs, which, here in (
            (hd_refs, 0, (k == 0) | (k == 2)),
            (act_refs, 0, (k == 1) | (k == 3)),
            (mix_refs, 0, k == 4),
            (proj_refs, 1, k == 4),
        ):
            for item, ref in enumerate(refs):
                target = rt.at[slot, which, item * ROWS : (item + 1) * ROWS]
                cases.append((here, pltpu.make_async_copy(ref.at[:, columns], target, rt_sem.at[slot, which, item])))
        return cases

    def start_tile(s):
        for here, copy in tile_copies(s):
            pl.when(here)(copy.start)

    def wait_tile(s):
        for here, copy in tile_copies(s):
            pl.when(here)(copy.wait)

    def add_into(target, source):
        target[...] = (target[...].astype(jnp.float32) + source[...].astype(jnp.float32)).astype(jnp.bfloat16)

    def rows(half):
        return pl.ds(pl.multiple_of(half * BLOCK, BLOCK), BLOCK)

    def dot(index, half, tile):
        return jnp.dot(lt_ref[index, rows(half), :], tile[...], preferred_element_type=jnp.float32)

    def compute(u):
        k = kind_of(u)
        ring = u % RING

        @pl.when(u >= RING)
        def _():
            core_copy(u - RING, 0).wait_send()
            core_copy(u - RING, 1).wait_send()
            pl.semaphore_wait(credit, 1)

        def block(b, carry):
            s = 2 * u + b
            slot = s % 2

            @pl.when(s + 1 < 2 * units)
            def _():
                start_tile(s + 1)

            wait_tile(s)

            @pl.when(k < 4)
            def _():
                xs[ring, b] = dot(k, 1 - core, rt.at[slot, 0]).astype(jnp.bfloat16)

            @pl.when(k == 4)
            def _():
                value = dot(4, 1 - core, rt.at[slot, 0]) + dot(5, 1 - core, rt.at[slot, 1])
                xs[ring, b] = value.astype(jnp.bfloat16)

            core_copy(u, b).start()

            @pl.when(k < 4)
            def _():
                part[u, b] = dot(k, core, rt.at[slot, 0]).astype(jnp.bfloat16)

            @pl.when(k == 4)
            def _():
                value = dot(4, core, rt.at[slot, 0]) + dot(5, core, rt.at[slot, 1])
                part[u, b] = value.astype(jnp.bfloat16)

            return carry

        lax.fori_loop(0, 2, block, 0)

    def join_core(u):
        ring = u % RING
        core_copy(u, 0).wait_recv()
        add_into(part.at[u, 0], xr.at[ring, 0])
        y_copy(u).start()
        core_copy(u, 1).wait_recv()
        add_into(part.at[u, 1], xr.at[ring, 1])

        @pl.when(u + RING < units)
        def _():
            pl.semaphore_signal(credit, inc=1, device_id=peer, device_id_type=MESH)

    def join_y(u):
        y_copy(u).wait_recv()
        add_into(part.at[u, 1], yr.at[u])

    def take_right(u):
        right_copy(u).wait_recv()
        add_into(part.at[u, 1], zr.at[u])

    def take_left(u):
        left_copy(u).wait_recv()
        add_into(part.at[u, 1], zl.at[u])

    def pass_right(u):
        pl.when(z > 0)(lambda: take_right(u))
        right_copy(u).start()

    def pass_left(u):
        pl.when(z < 3)(lambda: take_left(u))
        left_copy(u).start()

    def finish(u):
        pl.when(z > 0)(lambda: take_right(u))
        pl.when(z < 3)(lambda: take_left(u))
        own_copy(u).start()
        peer_copy(u).start()

        @pl.when(kind_of(u) < 4)
        def _():
            cross_copy(u).start()

    flips = (peer, beside, (section, me + 4 - 8 * (z % 2)), (section, me + 8 - 16 * (z // 2)), across)

    def small_copy(j):
        return remote(small_sum.at[j], small_in.at[j], small_send.at[j], small_recv.at[j], flips[j])

    def small_step(j):
        if j == 0:
            small_sum[0] = small_ref[...]
        else:
            small_copy(j - 1).wait_recv()
            if j == 5:
                small_out[0] = small_sum[4]
                small_out[1] = small_in[4]
            else:
                small_sum[j] = small_sum[j - 1] + small_in[j - 1]
        if j < 5:
            small_copy(j).start()

    def within(u):
        return (u >= 0) & (u < units)

    def when_in(u, condition, action):
        @pl.when(within(u) & condition)
        def _():
            action(u)

    barrier = pltpu.get_barrier_semaphore()
    for device in (peer, beside, across, flips[3]):
        pl.semaphore_signal(barrier, inc=1, device_id=device, device_id_type=MESH)

    @pl.when(z < 3)
    def _():
        pl.semaphore_signal(barrier, inc=1, device_id=right, device_id_type=MESH)

    @pl.when(z > 0)
    def _():
        pl.semaphore_signal(barrier, inc=1, device_id=left, device_id_type=MESH)

    start_tile(0)
    pl.semaphore_wait(barrier, 4 + jnp.where(z < 3, 1, 0) + jnp.where(z > 0, 1, 0))

    def step(i, carry):
        pl.when(i < units)(lambda: compute(i))
        when_in(i - 1, True, join_core)
        when_in(i - 4, True, join_y)
        u = i - 4 - 2 * z
        when_in(u, plane_of(jnp.maximum(u, 0)) > z, pass_right)
        u = i - 10 + 2 * z
        when_in(u, plane_of(jnp.maximum(u, 0)) < z, pass_left)
        u = i - 12
        when_in(u, plane_of(jnp.maximum(u, 0)) == z, finish)
        for j in range(6):
            pl.when(i == 2 + j)(functools.partial(small_step, j))
        return carry

    lax.fori_loop(0, units + 12, step, 0)

    def settle(u, carry):
        @pl.when(u >= units - RING)
        def _():
            core_copy(u, 0).wait_send()
            core_copy(u, 1).wait_send()

        y_copy(u).wait_send()
        plane = plane_of(u)

        @pl.when(plane > z)
        def _():
            right_copy(u).wait_send()

        @pl.when(plane < z)
        def _():
            left_copy(u).wait_send()

        @pl.when(plane == z)
        def _():
            own_copy(u).wait()
            peer_copy(u).wait()

            @pl.when(kind_of(u) < 4)
            def _():
                cross_copy(u).wait_send()

        return carry

    def hand(k, carry):
        cross_arrival(k).wait_recv()
        hand_copy(k).start()
        return carry

    lax.fori_loop(0, other_kinds, hand, 0)
    lax.fori_loop(0, units, settle, 0)

    def handed(k, carry):
        hand_copy(k).wait()
        return carry

    lax.fori_loop(0, other_kinds, handed, 0)
    for j in range(5):
        small_copy(j).wait_send()


def gather_refs(items, *refs):
    lists = [refs[2 + items * n : 2 + items * (n + 1)] for n in range(4)]
    sum_kernel(*refs[:2], *lists, *refs[2 + 4 * items :])


def summed_blocks(left, small, hidden_delta, active, mixed, proj):
    dma = pltpu.SemaphoreType.DMA
    depth = left.shape[2]
    items = len(hidden_delta)
    tile = (BLOCK, BLOCK)
    vmem, anywhere = pl.BlockSpec(memory_space=pltpu.VMEM), pl.BlockSpec(memory_space=pl.ANY)
    return pl.pallas_call(
        functools.partial(gather_refs, items),
        out_shape=[
            jax.ShapeDtypeStruct((2, 2, 5) + tile, jnp.bfloat16),
            jax.ShapeDtypeStruct((2,) + small.shape, jnp.float32),
        ],
        in_specs=[vmem] * 2 + [anywhere] * (4 * items),
        out_specs=[anywhere, vmem],
        scratch_shapes=[
            pltpu.VMEM((2, 2, depth, BLOCK), jnp.bfloat16),
            pltpu.VMEM((20, 2) + tile, jnp.bfloat16),
            pltpu.VMEM((RING, 2) + tile, jnp.bfloat16),
            pltpu.VMEM((RING, 2) + tile, jnp.bfloat16),
            pltpu.VMEM((20,) + tile, jnp.bfloat16),
            pltpu.VMEM((20,) + tile, jnp.bfloat16),
            pltpu.VMEM((20,) + tile, jnp.bfloat16),
            pltpu.VMEM((5,) + small.shape, jnp.float32),
            pltpu.VMEM((5,) + small.shape, jnp.float32),
            dma((5,)),
            dma((5,)),
            dma((2, 2, items)),
            dma((20, 2)),
            dma((20, 2)),
        ]
        + [dma((20,))] * 6
        + [dma((5,))] * 7
        + [pltpu.SemaphoreType.REGULAR],
        compiler_params=pltpu.CompilerParams(
            collective_id=0, has_side_effects=True, vmem_limit_bytes=56 * 1024 * 1024
        ),
        cost_estimate=pl.CostEstimate(flops=48 * 2 * 768 * 384 * depth, bytes_accessed=40_000_000, transcendentals=0),
    )(left, small, *hidden_delta, *active, *mixed, *proj)


CHUNK = 768
KEY_SPLIT = 256
TAIL = (0.319381530, -0.356563782, 1.781477937, -1.821255978, 1.330274429)
PEAK = 0.3989422804014327


def normal_parts(z):
    size = jnp.abs(z)
    scale = 1.0 + 0.2316419 * size
    t = pl.reciprocal(scale, approx=True)
    t = t * (2.0 - scale * t)
    bell = jnp.exp(-0.5 * z * z) * PEAK
    series = TAIL[4]
    for factor in TAIL[3::-1]:
        series = series * t + factor
    upper = bell * (series * t)
    return jnp.where(z >= 0, 1.0 - upper, upper), bell


def matmul(left, right):
    return jnp.dot(left, right, preferred_element_type=jnp.float32)


def matmul_turned(left, right):
    return lax.dot_general(left, right, (((1,), (1,)), ((), ())), preferred_element_type=jnp.float32)


def standardized(values):
    centre = values - jnp.mean(values, -1, keepdims=True)
    inverse = lax.rsqrt(jnp.mean(centre * centre, -1, keepdims=True) + EPSILON)
    return centre * inverse, inverse


def norm_step_back(delta, values, gain_row):
    standard, inverse = standardized(values)
    scaled = delta * gain_row
    moved = inverse * (
        scaled - jnp.mean(scaled, -1, keepdims=True) - standard * jnp.mean(scaled * standard, -1, keepdims=True)
    )
    return moved, jnp.sum(delta * standard, 0, keepdims=True), jnp.sum(delta, 0, keepdims=True)


def half_mask(half):
    lanes = lax.broadcasted_iota(jnp.int32, (1, 128), 1)
    return (lanes < 64) if half == 0 else (lanes >= 64)


def attention_forward(m, length):
    rows = m["qkv"].shape[0]
    width = m["att"].shape[1]

    def pair(p, carry):
        at = pl.multiple_of(p * 128, 128)
        q2 = m["qkv"][:, pl.ds(at, 128)]
        k2 = m["qkv"][:, pl.ds(pl.multiple_of(width + at, 128), 128)]
        v2 = m["qkv"][:, pl.ds(pl.multiple_of(2 * width + at, 128), 128)]
        v_turned = v2.T
        parts = []
        for half in range(2):
            kh = jnp.where(half_mask(half), k2, jnp.zeros_like(k2))
            top = matmul_turned(kh[:KEY_SPLIT], q2)
            low = matmul_turned(kh[KEY_SPLIT:], q2)
            key_row = KEY_SPLIT + lax.broadcasted_iota(jnp.int32, low.shape, 0)
            low = jnp.where(key_row < length, low, -1e30)
            peak = jnp.maximum(jnp.max(top, 0, keepdims=True), jnp.max(low, 0, keepdims=True))
            top = jnp.exp(top - peak)
            low = jnp.exp(low - peak)
            over = 1.0 / (jnp.sum(top, 0, keepdims=True) + jnp.sum(low, 0, keepdims=True))
            probs = jnp.concatenate([(top * over).astype(jnp.bfloat16), (low * over).astype(jnp.bfloat16)], axis=0)
            m["probs"][2 * p + half] = probs
            parts.append(matmul(v_turned[64 * half : 64 * half + 64], probs))
        turned = jnp.concatenate(parts, axis=0)
        m["att_turned"][pl.ds(at, 128), :] = turned.astype(jnp.bfloat16)
        m["att"][:, pl.ds(at, 128)] = turned.T.astype(jnp.bfloat16)
        return carry

    lax.fori_loop(0, width // 128, pair, 0)


def attention_back(m):
    width = m["att"].shape[1]

    def pair(p, carry):
        at = pl.multiple_of(p * 128, 128)
        k_at = pl.ds(pl.multiple_of(width + at, 128), 128)
        v_at = pl.ds(pl.multiple_of(2 * width + at, 128), 128)
        q2 = m["qkv"][:, pl.ds(at, 128)]
        k2 = m["qkv"][:, k_at]
        v2 = m["qkv"][:, v_at]
        d2 = m["att_delta"][:, pl.ds(at, 128)]
        d_turned = d2.T
        k_turned = k2.T
        product = d_turned.astype(jnp.float32) * m["att_turned"][pl.ds(at, 128), :].astype(jnp.float32)
        values, keys, queries = [], [], []
        for half in range(2):
            vh = jnp.where(half_mask(half), v2, jnp.zeros_like(v2))
            probs = m["probs"][2 * p + half]
            inner = jnp.sum(product[64 * half : 64 * half + 64], 0, keepdims=True)
            score = (probs.astype(jnp.float32) * (matmul(vh, d_turned) - inner)).astype(jnp.bfloat16)
            values.append(matmul(probs, d2))
            keys.append(matmul(score, q2))
            queries.append(matmul(k_turned[64 * half : 64 * half + 64], score))
        dq = (jnp.concatenate(queries, axis=0).T * HEAD_DIM ** (-0.5)).astype(jnp.bfloat16)
        dk = jnp.where(half_mask(0), keys[0], keys[1]).astype(jnp.bfloat16)
        dv = jnp.where(half_mask(0), values[0], values[1]).astype(jnp.bfloat16)
        m["mixed"][:, pl.ds(at, 128)] = dq
        m["mixed"][:, k_at] = dk
        m["mixed"][:, v_at] = dv
        m["sums"][2:3, pl.ds(at, 128)] = jnp.sum(dq.astype(jnp.float32), 0, keepdims=True)
        m["sums"][3:4, pl.ds(at, 128)] = jnp.sum(dv.astype(jnp.float32), 0, keepdims=True)
        return carry

    lax.fori_loop(0, width // 128, pair, 0)


def forward_front(m, x_ref, length):
    x = x_ref[...].astype(jnp.float32)
    standard, unused = standardized(x)
    m["n1"][...] = (standard * m["gain"][0:1] + m["shift"][0:1]).astype(jnp.bfloat16)
    width = x.shape[1]
    m["wait"]("qkv_w")
    n1 = m["n1"][...]
    for part in range(3):
        value = matmul(n1, m["qkv_w"][:, part * width : (part + 1) * width])
        if part == 0:
            value = (value + m["qv"][0:1]).astype(jnp.bfloat16) * jnp.bfloat16(HEAD_DIM ** (-0.5))
        elif part == 2:
            value = value + m["qv"][1:2]
        m["qkv"][:, part * width : (part + 1) * width] = value.astype(jnp.bfloat16)
    attention_forward(m, length)
    m["wait"]("out_w")
    middle = x_ref[...].astype(jnp.float32) + matmul(m["att"][...], m["out_w"][...]) + m["proj"][0:1]
    m["middle"][...] = middle
    standard, unused = standardized(middle)
    m["n2"][...] = (standard * m["gain"][1:2] + m["shift"][1:2]).astype(jnp.bfloat16)


def back_tail(m, x_ref, g_ref, n2_delta, keep):
    middle_part, gain, shift = norm_step_back(n2_delta, m["middle"][...], m["gain"][1:2])
    m["sums"][6:7] = gain
    m["sums"][8:9] = shift
    middle_delta = g_ref[...].astype(jnp.float32) + middle_part
    proj_delta = middle_delta.astype(jnp.bfloat16)
    m["sums"][4:5] = jnp.sum(proj_delta.astype(jnp.float32), 0, keepdims=True)
    m["proj_delta"][...] = proj_delta
    m["middle_delta"][...] = middle_delta
    m["att_delta"][...] = matmul_turned(proj_delta, m["out_w"][...]).astype(jnp.bfloat16)
    attention_back(m)
    width = m["att"].shape[1]
    total = None
    for part in range(3):
        columns = slice(part * width, (part + 1) * width)
        piece = matmul_turned(m["mixed"][:, columns], m["qkv_w"][:, columns])
        total = piece if total is None else total + piece
    input_part, gain, shift = norm_step_back(total, x_ref[...].astype(jnp.float32), m["gain"][0:1])
    m["sums"][5:6] = gain
    m["sums"][7:8] = shift
    keep(m["middle_delta"][...] + input_part)


def forward_expert(m, slot, begin, end):
    steps = m["up_w"].shape[2] // CHUNK

    def step(j, carry):
        columns = pl.ds(pl.multiple_of(j * CHUNK, CHUNK), CHUNK)
        hidden = matmul(m["n2"][begin:end], m["up_w"][slot, :, columns]) + m["up_b"][slot : slot + 1, columns]
        below, bell = normal_parts(hidden)
        active = (hidden * below).astype(jnp.bfloat16)
        m["active"][begin:end, columns] = active
        m["slope"][begin:end, columns] = (below + hidden * bell).astype(jnp.bfloat16)
        m["total"][begin:end] += matmul(active, m["down_w"][slot, columns, :])
        return carry

    m["total"][begin:end] = m["middle"][begin:end] + m["down_b"][slot : slot + 1]
    lax.fori_loop(0, steps, step, 0)


def back_expert(m, g_ref, slot, begin, end):
    steps = m["up_w"].shape[2] // CHUNK
    m["total"][begin:end] = jnp.zeros((end - begin, m["total"].shape[1]), jnp.float32)
    m["sums"][slot : slot + 1] = jnp.sum(g_ref[begin:end].astype(jnp.float32), 0, keepdims=True)

    def step(j, carry):
        columns = pl.ds(pl.multiple_of(j * CHUNK, CHUNK), CHUNK)
        active_delta = matmul_turned(g_ref[begin:end], m["down_w"][slot, columns, :])
        hidden_delta = (active_delta * m["slope"][begin:end, columns].astype(jnp.float32)).astype(jnp.bfloat16)
        m["hidden_delta"][begin:end, columns] = hidden_delta
        m["up_sums"][slot : slot + 1, columns] = jnp.sum(hidden_delta.astype(jnp.float32), 0, keepdims=True)
        m["total"][begin:end] += matmul_turned(hidden_delta, m["up_w"][slot, :, columns])
        return carry

    lax.fori_loop(0, steps, step, 0)


def both_expert(m, g_ref):
    steps = m["up_w"].shape[2] // CHUNK
    m["total"][...] = jnp.zeros(m["total"].shape, jnp.float32)
    m["sums"][0:1] = jnp.sum(g_ref[...].astype(jnp.float32), 0, keepdims=True)
    m["sums"][1:2] = jnp.zeros((1, m["sums"].shape[1]), jnp.float32)
    m["up_sums"][1:2] = jnp.zeros((1, m["up_sums"].shape[1]), jnp.float32)

    def step(j, carry):
        columns = pl.ds(pl.multiple_of(j * CHUNK, CHUNK), CHUNK)
        active_delta = matmul_turned(g_ref[...], m["down_w"][0, columns, :])
        hidden = matmul(m["n2"][...], m["up_w"][0, :, columns]) + m["up_b"][2:3, columns]
        below, bell = normal_parts(hidden)
        m["active"][:, columns] = (hidden * below).astype(jnp.bfloat16)
        hidden_delta = (active_delta * (below + hidden * bell)).astype(jnp.bfloat16)
        m["hidden_delta"][:, columns] = hidden_delta
        m["up_sums"][0:1, columns] = jnp.sum(hidden_delta.astype(jnp.float32), 0, keepdims=True)
        m["total"][...] += matmul_turned(hidden_delta, m["up_w"][0, :, columns])
        return carry

    lax.fori_loop(0, steps, step, 0)


FRONT = ("n1", "att", "n2", "active")
BACK = ("mixed", "proj_delta", "hidden_delta")
KEPT = ("qkv", "probs", "att_turned", "middle", "slope")
WEIGHTS = ("qkv_w", "out_w", "up_w", "down_w")


def tick_kernel(plan, *refs):
    names = plan["ins"] + plan["outs"] + plan["scratch"]
    m = dict(zip(names, refs))
    section = lax.axis_index("section")
    sources = {"qkv_w": ("in_qkv",), "out_w": ("in_out",), "up_w": ("in_up",), "down_w": ("in_down",)}

    def run(first_layer, front, back):
        started = {}

        def copy_in(name):
            copies = []
            if name in ("qkv_w", "out_w"):
                copies.append(pltpu.make_async_copy(m[sources[name][0]].at[0], m[name], m["load_sem"].at[WEIGHTS.index(name), 0]))
            else:
                for slot in range(2 if first_layer else 1):
                    expert = slot if first_layer else 2
                    copies.append(
                        pltpu.make_async_copy(
                            m[sources[name][0]].at[expert], m[name].at[slot], m["load_sem"].at[WEIGHTS.index(name), slot]
                        )
                    )
            return copies

        def wait(name):
            for copy in started.pop(name, ()):
                copy.wait()

        order = WEIGHTS if front else ("down_w", "up_w", "out_w", "qkv_w")
        kept_loads = []
        if not front:
            for number, name in enumerate(KEPT):
                copy = pltpu.make_async_copy(m["kept_" + name], m[name], m["kept_sem"].at[number])
                copy.start()
                kept_loads.append(copy)
        for name in order:
            started[name] = copy_in(name)
            for copy in started[name]:
                copy.start()
        m["wait"] = wait
        pending = []

        def put(name, target, number):
            copy = pltpu.make_async_copy(m[name], m[target], m["store_sem"].at[number])
            copy.start()
            pending.append(copy)

        if front:
            x_ref = m["x_first"] if first_layer else m["x_second"]
            forward_front(m, x_ref, plan["length"])
            for number, name in enumerate(("n1", "att", "n2")):
                put(name, ("front_first_" if first_layer else "front_second_") + name, number)
            if first_layer:
                for number, name in enumerate(("qkv", "probs", "att_turned", "middle")):
                    put(name, "kept_" + name, 8 + number)
        wait("up_w")
        wait("down_w")
        if front and first_layer:
            forward_expert(m, 0, TEXT, ROWS)
            forward_expert(m, 1, 0, TEXT)
            m["passed"][...] = m["total"][...].astype(jnp.bfloat16)
            put("active", "front_first_active", 3)
            put("slope", "kept_slope", 12)
        if back:
            g_ref = m["g_first"] if first_layer else m["g_second"]
            back_name = "back_first_" if first_layer else "back_second_"
            for copy in kept_loads:
                copy.wait()
            if first_layer:
                back_expert(m, g_ref, 0, TEXT, ROWS)
                back_expert(m, g_ref, 1, 0, TEXT)
            else:
                both_expert(m, g_ref)
                put("active", "front_second_active", 3)
            put("hidden_delta", back_name + "hidden_delta", 4)
            wait("out_w")
            wait("qkv_w")

            def keep(value):
                if first_layer:
                    m["input_delta"][...] = value
                else:
                    m["sent_back"][...] = value.astype(jnp.bfloat16)

            back_x = m["x_back"] if first_layer else m["x_second"]
            back_tail(m, back_x, g_ref, m["total"][...], keep)
            put("mixed", back_name + "mixed", 5)
            put("proj_delta", back_name + "proj_delta", 6)
        for copy in pending:
            copy.wait()

    if plan["first"] == "front":
        pl.when(section == 0)(lambda: run(True, True, False))
    if plan["first"] == "back":
        pl.when(section == 0)(lambda: run(True, False, True))
    if plan["second"]:
        pl.when(section == 1)(lambda: run(False, True, True))


def tick(params, length, first=None, second=False, x_first=None, x_second=None, g_second=None, front_second=None,
         back_first=None, kept=None, x_back=None, g_first=None):
    rows, width = ROWS, params["in_out"].shape[-1]
    ff = params["in_up"].shape[-1]
    heads = width // HEAD_DIM
    bf16, f32 = jnp.bfloat16, jnp.float32
    kinds = dict(
        n1=((rows, width), bf16), att=((rows, width), bf16), n2=((rows, width), bf16), active=((rows, ff), bf16),
        mixed=((rows, 3 * width), bf16), proj_delta=((rows, width), bf16), hidden_delta=((rows, ff), bf16),
        qkv=((rows, 3 * width), bf16), probs=((heads, rows, rows), bf16), att_turned=((width, rows), bf16),
        middle=((rows, width), f32), slope=((rows, ff), bf16), total=((rows, width), f32),
        att_delta=((rows, width), bf16), middle_delta=((rows, width), f32),
        qkv_w=((width, 3 * width), bf16), out_w=((width, width), bf16),
        up_w=((2, width, ff), bf16), down_w=((2, ff, width), bf16),
    )
    vmem, anywhere = pl.BlockSpec(memory_space=pltpu.VMEM), pl.BlockSpec(memory_space=pl.ANY)
    ins, outs, aliases = [], [], {}

    def add_in(name, value, spec):
        ins.append((name, value, spec))

    def add_out(name, shape, dtype, spec, source=None):
        if source is not None:
            aliases[len(ins)] = len(outs)
            ins.append(("old_" + name, source, anywhere))
        outs.append((name, jax.ShapeDtypeStruct(shape, dtype), spec))

    for name in ("in_qkv", "in_out", "in_up", "in_down"):
        add_in(name, params[name], anywhere)
    for name in ("qv", "proj", "gain", "shift", "up_b", "down_b"):
        add_in(name, params[name], vmem)
    if first == "front":
        add_in("x_first", x_first, vmem)
        for name in FRONT:
            add_out("front_first_" + name, *kinds[name], anywhere)
        for name in KEPT:
            add_out("kept_" + name, *kinds[name], anywhere)
        add_out("passed", (rows, width), bf16, vmem)
    if first == "back":
        add_in("x_back", x_back, vmem)
        add_in("g_first", g_first, vmem)
        for name in KEPT:
            add_in("kept_" + name, kept[name], anywhere)
        for name in BACK:
            add_out("back_first_" + name, *kinds[name], anywhere, back_first[name])
        add_out("input_delta", (rows, width), f32, vmem)
    if second:
        add_in("x_second", x_second, vmem)
        add_in("g_second", g_second, vmem)
        for name in FRONT:
            add_out("front_second_" + name, *kinds[name], anywhere, front_second[name])
        for name in BACK:
            add_out("back_second_" + name, *kinds[name], anywhere)
        add_out("sent_back", (rows, width), bf16, vmem)
    if second or first == "back":
        add_out("sums", (9, width), f32, vmem)
        add_out("up_sums", (2, ff), f32, vmem)
    scratch = [
        "qkv_w", "out_w", "up_w", "down_w", "n1", "att", "n2", "active", "qkv", "probs", "att_turned", "middle", "slope", "total",
    ]
    if second or first == "back":
        scratch += ["mixed", "proj_delta", "hidden_delta", "att_delta", "middle_delta"]
    dma = pltpu.SemaphoreType.DMA
    plan = dict(
        ins=[name for name, *unused in ins], outs=[name for name, *unused in outs],
        scratch=scratch + ["load_sem", "kept_sem", "store_sem"], first=first, second=second, length=length,
    )
    results = pl.pallas_call(
        functools.partial(tick_kernel, plan),
        out_shape=[shape for unused, shape, spec in outs],
        in_specs=[spec for unused, value, spec in ins],
        out_specs=[spec for unused, shape, spec in outs],
        scratch_shapes=[pltpu.VMEM(*kinds[name]) for name in scratch] + [dma((4, 2)), dma((5,)), dma((13,))],
        input_output_aliases=aliases,
        compiler_params=pltpu.CompilerParams(vmem_limit_bytes=58 * 1024 * 1024),
        cost_estimate=pl.CostEstimate(flops=8_000_000_000, bytes_accessed=30_000_000, transcendentals=0),
    )(*[value for unused, value, spec in ins])
    return dict(zip(plan["outs"], results))


def passed_along(block, axis, distance):
    devices = range(lax.axis_size(axis))
    route = [(i - distance, i) for i in devices if i - distance in devices]
    return lax.ppermute(block, axis, route)


def text_first(values):
    pad = jnp.zeros((values.shape[0], ROWS - values.shape[1]) + values.shape[2:], values.dtype)
    return jnp.concatenate([values[:, PATCHES:], values[:, :PATCHES], pad], axis=1)


def patches_first(values, length):
    return jnp.concatenate([values[:, TEXT:length], values[:, :TEXT]], axis=1)


def small_rows(sums, up_sums):
    count = lax.axis_size("dp")
    pieces = [piece.reshape(piece.shape[0], count, -1).transpose(1, 0, 2) for piece in (sums, up_sums)]
    return jnp.concatenate([piece.reshape(count, -1) for piece in pieces], axis=1)


def small_outs(own, other, is_first, wide, ff):
    first = jnp.where(is_first, own, other)
    second = jnp.where(is_first, other, own)
    own, first, second = own[: 9 * wide].reshape(9, wide), first, second

    def table(begin, size):
        return jnp.stack(
            [first[begin : begin + size], first[begin + size : begin + 2 * size], second[begin : begin + size]]
        )

    return own[2:4], own[4:5], own[5:7], own[7:9], table(9 * wide, ff), table(0, wide)


def left_parts(front, branch_delta, is_first):
    n1, att, n2 = (jnp.concatenate([part[name] for part in front]) for name in ("n1", "att", "n2"))
    text = (jnp.arange(n1.shape[0]) % ROWS < TEXT)[:, None]
    vision = jnp.logical_not(text & is_first).astype(jnp.bfloat16)
    text = text.astype(jnp.bfloat16)
    return [
        piece.T for piece in (n2 * vision, branch_delta * vision, n2 * text, branch_delta * text, n1, att)
    ]


def large_grads(lefts, front, back, small, is_first):
    width = lefts[0].shape[0]
    chips = 8
    me = lax.axis_index("dp")
    core = me % 2

    def spread(value, before, after):
        value = value.reshape(ROWS, chips, -1)
        return jnp.pad(value, ((0, 0), (0, 0), (before, after))).reshape(ROWS, -1)

    mixed = [spread(part["mixed"], 0, 96) for part in back]
    proj = [spread(part["proj_delta"], 288, 0) for part in back]
    blocks, smalls = summed_blocks(
        jnp.stack(lefts), small, [part["hidden_delta"] for part in back], [part["active"] for part in front], mixed, proj
    )
    own, other = blocks[0], blocks[1]

    def whole(block, begin, wide):
        both = block.reshape(width, BLOCK)
        return lax.dynamic_slice_in_dim(both, begin + core * wide, wide, 1).astype(jnp.float32)

    first = [jnp.where(is_first, own[:, k], other[:, k]) for k in range(4)]
    second = [jnp.where(is_first, other[:, k], own[:, k]) for k in range(2)]
    up = jnp.stack([whole(block, 0, 192) for block in (first[0], first[2], second[0])])
    down = jnp.stack([whole(block, 0, 192).T for block in (first[1], first[3], second[1])])
    mine = lax.dynamic_slice_in_dim(smalls, me, 1, 1)[:, 0]
    return whole(own[:, 4], 0, 144), whole(own[:, 4], 288, 48), up, down, mine[0], mine[1]


def large_grads_plain(lefts, front, back, small, is_first):
    joined = {name: jnp.concatenate([part[name] for part in back]) for name in BACK}
    active = jnp.concatenate([part["active"] for part in front])

    def total_of(left, right):
        product = jnp.dot(left, right, preferred_element_type=jnp.float32).astype(jnp.bfloat16)
        return lax.psum_scatter(product, "dp", scatter_dimension=1, tiled=True)

    def table(vision_part, text_part):
        def swapped(part):
            return lax.psum(part, "section").astype(jnp.float32)

        return jnp.stack(
            [
                swapped(jnp.where(is_first, vision_part, 0)),
                swapped(jnp.where(is_first, text_part, 0)),
                swapped(jnp.where(is_first, 0, vision_part)),
            ]
        )

    hidden_delta = joined["hidden_delta"]
    up = table(total_of(lefts[0], hidden_delta), total_of(lefts[2], hidden_delta))
    down = table(total_of(lefts[1], active), total_of(lefts[3], active))
    mine = lax.psum_scatter(small, "dp", scatter_dimension=0, tiled=True)[0]
    return (
        total_of(lefts[4], joined["mixed"]).astype(jnp.float32),
        total_of(lefts[5], joined["proj_delta"]).astype(jnp.float32),
        up,
        down.transpose(0, 2, 1),
        mine,
        lax.ppermute(mine, "section", [(0, 1), (1, 0)]),
    )


def shards(
    tokens, cotangent, patch_mask, text_mask, qkv_weight, qv_bias, out_weight, out_bias, norm_gain, norm_bias,
    up_table, up_bias, down_table, down_bias,
):
    is_first = lax.axis_index("section") == 0
    items, length, width = tokens.shape
    positions = jnp.arange(length, dtype=jnp.int32)
    chosen = jnp.any(positions[None, :, None] == patch_mask[:, None, :], axis=2) | jnp.any(
        positions[None, :, None] == text_mask[:, None, :], axis=2
    )
    targets = text_first(cotangent * chosen.astype(jnp.bfloat16)[..., None])
    own = text_first(tokens)
    params = dict(
        in_qkv=qkv_weight, in_out=out_weight, in_up=up_table, in_down=down_table, qv=qv_bias[0], proj=out_bias,
        gain=norm_gain[0], shift=norm_bias[0], up_b=up_bias, down_b=down_bias,
    )

    def named(made, start, names):
        return {name: made[start + name] for name in names}

    front, kept, back, returned, arrived, deltas = {}, {}, {}, {}, {}, {}
    sums_first, sums_second = [], []
    for at in range(2 * items):
        plan = {}
        if at < items:
            plan.update(first="front", x_first=own[at])
        else:
            item = at - items
            plan.update(
                first="back", x_back=own[item], g_first=returned[item], kept=kept[item], back_first=back[item]
            )
        second = 1 <= at <= items
        if second:
            plan.update(
                second=True, x_second=arrived[at - 1], g_second=targets[at - 1], front_second=front[at - 1]
            )
        made = tick(params, length, **plan)
        if at < items:
            front[at] = named(made, "front_first_", FRONT)
            kept[at] = named(made, "kept_", KEPT)
            arrived[at] = passed_along(made["passed"], "section", 1)
        else:
            back[at - items] = named(made, "back_first_", BACK)
            deltas[at - items] = made["input_delta"]
            sums_first.append((made["sums"], made["up_sums"]))
        if second:
            front[at - 1] = named(made, "front_second_", FRONT)
            back[at - 1] = named(made, "back_second_", BACK)
            returned[at - 1] = passed_along(made["sent_back"], "section", -1)
            sums_second.append((made["sums"], made["up_sums"]))
    total = [
        jnp.where(is_first, sum(one[n] for one in sums_first), sum(one[n] for one in sums_second)) for n in range(2)
    ]
    small = small_rows(*total)
    front = [front[item] for item in range(items)]
    back = [back[item] for item in range(items)]
    half = width // 2
    input_delta = patches_first(jnp.stack([deltas[item] for item in range(items)]), length)
    moved_half = passed_along(input_delta[..., half:].astype(jnp.bfloat16), "section", 1)
    branch_delta = jnp.where(
        is_first, jnp.concatenate([returned[item] for item in range(items)]), targets.reshape(-1, width)
    )
    lefts = left_parts(front, branch_delta, is_first)
    grads = large_grads if lax.axis_size("dp") == 16 else large_grads_plain
    qkv, out, up, down, mine, other = grads(lefts, front, back, small, is_first)
    wide, ff = width // lax.axis_size("dp"), up_bias.shape[1] // lax.axis_size("dp")
    qv_part, proj_part, gain_part, shift_part, up_part, down_part = small_outs(mine, other, is_first, wide, ff)
    input_grad = jnp.where(is_first, input_delta[..., :half], moved_half.astype(jnp.float32))
    return (
        input_grad, qkv[None], qv_part[None], out[None], proj_part, gain_part[None], shift_part[None],
        up, up_part, down, down_part,
    )


def solution(mesh):
    return jax.shard_map(
        shards,
        mesh=mesh,
        in_specs=(
            P("dp", None, None), P("dp", None, None), P("dp", None), P("dp", None),
            P("section", None, None), P("section", None, None), P("section", None, None), P("section", None),
            P("section", None, None), P("section", None, None), P(), P(), P(), P(),
        ),
        out_specs=(
            P("dp", None, "section"), P("section", None, "dp"), P("section", None, "dp"), P("section", None, "dp"),
            P("section", "dp"), P("section", None, "dp"), P("section", None, "dp"),
            P(None, None, "dp"), P(None, "dp"), P(None, "dp", None), P(None, "dp"),
        ),
        check_vma=False,
    )
```

```python
import functools

import jax
import jax.numpy as jnp
from jax import lax
from jax.experimental import pallas as pl
from jax.experimental.pallas import tpu as pltpu
from jax.sharding import PartitionSpec as P

HEAD_DIM = 64
PATCHES = 197
EPSILON = 1e-05
BLOCK = 384
RING = 3
TEXT = 64
ROWS = 272
MESH = pl.DeviceIdType.MESH


def sum_kernel(
    lt_ref, small_ref, hd_ref, act_ref, mix_ref, proj_ref, res_ref, small_out,
    rt, part, xs, xr, yr, zr, zl, small_sum, small_in, small_send, small_recv,
    rt_sem, core_send, core_recv, y_send, y_recv, right_send, right_recv, left_send, left_recv,
    own_sem, peer_send, peer_recv, cross_send, cross_recv, hand_send, hand_recv, credit,
):
    section = lax.axis_index("section")
    me = lax.axis_index("dp")
    z, y, core = me // 4, (me // 2) % 2, me % 2
    peer = (section, me + 1 - 2 * core)
    beside = (section, me + 2 - 4 * y)
    right = (section, me + 4)
    left = (section, me - 4)
    across = (1 - section, me)
    units = jnp.where(section == 0, 20, 12)
    other_kinds = jnp.where(section == 0, 2, 4)

    def kind_of(u):
        q = u // 4
        return jnp.where((section == 1) & (q == 2), 4, q)

    def plane_of(u):
        o = u % 4
        return jnp.where(o == 0, 0, jnp.where(o == 1, 3, o - 1))

    def remote(src, dst, send, recv, device):
        return pltpu.make_async_remote_copy(
            src_ref=src, dst_ref=dst, send_sem=send, recv_sem=recv, device_id=device, device_id_type=MESH
        )

    def core_copy(u, b):
        slot = u % RING
        return remote(xs.at[slot, b], xr.at[slot, b], core_send.at[u, b], core_recv.at[u, b], peer)

    def y_copy(u):
        return remote(part.at[u, 0], yr.at[u], y_send.at[u], y_recv.at[u], beside)

    def right_copy(u):
        return remote(part.at[u, 1], zr.at[u], right_send.at[u], right_recv.at[u], right)

    def left_copy(u):
        return remote(part.at[u, 1], zl.at[u], left_send.at[u], left_recv.at[u], left)

    def own_copy(u):
        k = kind_of(u)
        return pltpu.make_async_copy(part.at[u, 1], res_ref.at[0, core, k], own_sem.at[k])

    def peer_copy(u):
        k = kind_of(u)
        return remote(part.at[u, 1], res_ref.at[0, core, k], peer_send.at[k], peer_recv.at[k], peer)

    def cross_copy(u):
        k = kind_of(u)
        return remote(part.at[u, 1], res_ref.at[1, core, k], cross_send.at[k], cross_recv.at[k], across)

    def cross_arrival(k):
        return remote(part.at[0, 1], res_ref.at[1, core, k], cross_send.at[k], cross_recv.at[k], across)

    def hand_copy(k):
        return remote(res_ref.at[1, core, k], res_ref.at[1, core, k], hand_send.at[k], hand_recv.at[k], peer)

    def tile_copies(s):
        u, b, slot = s // 2, s % 2, s % 2
        k = kind_of(u)
        t = plane_of(u) * 2 + jnp.where(b == 0, 1 - y, y)
        columns = pl.ds(pl.multiple_of(t * BLOCK, 128), BLOCK)
        cases = []
        for ref, which, here in (
            (hd_ref, 0, (k == 0) | (k == 2)),
            (act_ref, 0, (k == 1) | (k == 3)),
            (mix_ref, 0, k == 4),
            (proj_ref, 1, k == 4),
        ):
            cases.append((here, pltpu.make_async_copy(ref.at[:, columns], rt.at[slot, which], rt_sem.at[slot, which])))
        return cases

    def start_tile(s):
        for here, copy in tile_copies(s):
            pl.when(here)(copy.start)

    def wait_tile(s):
        for here, copy in tile_copies(s):
            pl.when(here)(copy.wait)

    def add_into(target, source):
        target[...] = (target[...].astype(jnp.float32) + source[...].astype(jnp.float32)).astype(jnp.bfloat16)

    def rows(half):
        return pl.ds(pl.multiple_of(half * BLOCK, BLOCK), BLOCK)

    def dot(index, half, tile):
        return jnp.dot(lt_ref[index, rows(half), :], tile[...], preferred_element_type=jnp.float32)

    def compute(u):
        k = kind_of(u)
        ring = u % RING

        @pl.when(u >= RING)
        def _():
            core_copy(u - RING, 0).wait_send()
            core_copy(u - RING, 1).wait_send()
            pl.semaphore_wait(credit, 1)

        def block(b, carry):
            s = 2 * u + b
            slot = s % 2

            @pl.when(s + 1 < 2 * units)
            def _():
                start_tile(s + 1)

            wait_tile(s)

            @pl.when(k < 4)
            def _():
                xs[ring, b] = dot(k, 1 - core, rt.at[slot, 0]).astype(jnp.bfloat16)

            @pl.when(k == 4)
            def _():
                value = dot(4, 1 - core, rt.at[slot, 0]) + dot(5, 1 - core, rt.at[slot, 1])
                xs[ring, b] = value.astype(jnp.bfloat16)

            core_copy(u, b).start()

            @pl.when(k < 4)
            def _():
                part[u, b] = dot(k, core, rt.at[slot, 0]).astype(jnp.bfloat16)

            @pl.when(k == 4)
            def _():
                value = dot(4, core, rt.at[slot, 0]) + dot(5, core, rt.at[slot, 1])
                part[u, b] = value.astype(jnp.bfloat16)

            return carry

        lax.fori_loop(0, 2, block, 0)

    def join_core(u):
        ring = u % RING
        core_copy(u, 0).wait_recv()
        add_into(part.at[u, 0], xr.at[ring, 0])
        y_copy(u).start()
        core_copy(u, 1).wait_recv()
        add_into(part.at[u, 1], xr.at[ring, 1])

        @pl.when(u + RING < units)
        def _():
            pl.semaphore_signal(credit, inc=1, device_id=peer, device_id_type=MESH)

    def join_y(u):
        y_copy(u).wait_recv()
        add_into(part.at[u, 1], yr.at[u])

    def take_right(u):
        right_copy(u).wait_recv()
        add_into(part.at[u, 1], zr.at[u])

    def take_left(u):
        left_copy(u).wait_recv()
        add_into(part.at[u, 1], zl.at[u])

    def pass_right(u):
        pl.when(z > 0)(lambda: take_right(u))
        right_copy(u).start()

    def pass_left(u):
        pl.when(z < 3)(lambda: take_left(u))
        left_copy(u).start()

    def finish(u):
        pl.when(z > 0)(lambda: take_right(u))
        pl.when(z < 3)(lambda: take_left(u))
        own_copy(u).start()
        peer_copy(u).start()

        @pl.when(kind_of(u) < 4)
        def _():
            cross_copy(u).start()

    flips = (peer, beside, (section, me + 4 - 8 * (z % 2)), (section, me + 8 - 16 * (z // 2)), across)

    def small_copy(j):
        return remote(small_sum.at[j], small_in.at[j], small_send.at[j], small_recv.at[j], flips[j])

    def small_step(j):
        if j == 0:
            small_sum[0] = small_ref[...]
        else:
            small_copy(j - 1).wait_recv()
            if j == 5:
                small_out[0] = small_sum[4]
                small_out[1] = small_in[4]
            else:
                small_sum[j] = small_sum[j - 1] + small_in[j - 1]
        if j < 5:
            small_copy(j).start()

    def within(u):
        return (u >= 0) & (u < units)

    def when_in(u, condition, action):
        @pl.when(within(u) & condition)
        def _():
            action(u)

    barrier = pltpu.get_barrier_semaphore()
    for device in (peer, beside, across, flips[3]):
        pl.semaphore_signal(barrier, inc=1, device_id=device, device_id_type=MESH)

    @pl.when(z < 3)
    def _():
        pl.semaphore_signal(barrier, inc=1, device_id=right, device_id_type=MESH)

    @pl.when(z > 0)
    def _():
        pl.semaphore_signal(barrier, inc=1, device_id=left, device_id_type=MESH)

    start_tile(0)
    pl.semaphore_wait(barrier, 4 + jnp.where(z < 3, 1, 0) + jnp.where(z > 0, 1, 0))

    def step(i, carry):
        pl.when(i < units)(lambda: compute(i))
        when_in(i - 1, True, join_core)
        when_in(i - 4, True, join_y)
        u = i - 4 - 2 * z
        when_in(u, plane_of(jnp.maximum(u, 0)) > z, pass_right)
        u = i - 10 + 2 * z
        when_in(u, plane_of(jnp.maximum(u, 0)) < z, pass_left)
        u = i - 12
        when_in(u, plane_of(jnp.maximum(u, 0)) == z, finish)
        for j in range(6):
            pl.when(i == 2 + j)(functools.partial(small_step, j))
        return carry

    lax.fori_loop(0, units + 12, step, 0)

    def settle(u, carry):
        @pl.when(u >= units - RING)
        def _():
            core_copy(u, 0).wait_send()
            core_copy(u, 1).wait_send()

        y_copy(u).wait_send()
        plane = plane_of(u)

        @pl.when(plane > z)
        def _():
            right_copy(u).wait_send()

        @pl.when(plane < z)
        def _():
            left_copy(u).wait_send()

        @pl.when(plane == z)
        def _():
            own_copy(u).wait()
            peer_copy(u).wait()

            @pl.when(kind_of(u) < 4)
            def _():
                cross_copy(u).wait_send()

        return carry

    def hand(k, carry):
        cross_arrival(k).wait_recv()
        hand_copy(k).start()
        return carry

    lax.fori_loop(0, other_kinds, hand, 0)
    lax.fori_loop(0, units, settle, 0)

    def handed(k, carry):
        hand_copy(k).wait()
        return carry

    lax.fori_loop(0, other_kinds, handed, 0)
    for j in range(5):
        small_copy(j).wait_send()


def summed_blocks(left, small, hidden_delta, active, mixed, proj):
    dma = pltpu.SemaphoreType.DMA
    depth = left.shape[2]
    tile = (BLOCK, BLOCK)
    vmem, anywhere = pl.BlockSpec(memory_space=pltpu.VMEM), pl.BlockSpec(memory_space=pl.ANY)
    return pl.pallas_call(
        sum_kernel,
        out_shape=[
            jax.ShapeDtypeStruct((2, 2, 5) + tile, jnp.bfloat16),
            jax.ShapeDtypeStruct((2,) + small.shape, jnp.float32),
        ],
        in_specs=[vmem] * 2 + [anywhere] * 4,
        out_specs=[anywhere, vmem],
        scratch_shapes=[
            pltpu.VMEM((2, 2, depth, BLOCK), jnp.bfloat16),
            pltpu.VMEM((20, 2) + tile, jnp.bfloat16),
            pltpu.VMEM((RING, 2) + tile, jnp.bfloat16),
            pltpu.VMEM((RING, 2) + tile, jnp.bfloat16),
            pltpu.VMEM((20,) + tile, jnp.bfloat16),
            pltpu.VMEM((20,) + tile, jnp.bfloat16),
            pltpu.VMEM((20,) + tile, jnp.bfloat16),
            pltpu.VMEM((5,) + small.shape, jnp.float32),
            pltpu.VMEM((5,) + small.shape, jnp.float32),
            dma((5,)),
            dma((5,)),
            dma((2, 2)),
            dma((20, 2)),
            dma((20, 2)),
        ]
        + [dma((20,))] * 6
        + [dma((5,))] * 7
        + [pltpu.SemaphoreType.REGULAR],
        compiler_params=pltpu.CompilerParams(
            collective_id=0, has_side_effects=True, vmem_limit_bytes=56 * 1024 * 1024
        ),
        cost_estimate=pl.CostEstimate(flops=48 * 2 * 768 * 384 * depth, bytes_accessed=40_000_000, transcendentals=0),
    )(left, small, hidden_delta, active, mixed, proj)


CHUNK = 768
KEY_SPLIT = 256
TAIL = (0.319381530, -0.356563782, 1.781477937, -1.821255978, 1.330274429)
PEAK = 0.3989422804014327


def normal_parts(z):
    size = jnp.abs(z)
    scale = 1.0 + 0.2316419 * size
    t = pl.reciprocal(scale, approx=True)
    t = t * (2.0 - scale * t)
    bell = jnp.exp(-0.5 * z * z) * PEAK
    series = TAIL[4]
    for factor in TAIL[3::-1]:
        series = series * t + factor
    upper = bell * (series * t)
    return jnp.where(z >= 0, 1.0 - upper, upper), bell


def matmul(left, right):
    return jnp.dot(left, right, preferred_element_type=jnp.float32)


def matmul_turned(left, right):
    return lax.dot_general(left, right, (((1,), (1,)), ((), ())), preferred_element_type=jnp.float32)


def standardized(values):
    centre = values - jnp.mean(values, -1, keepdims=True)
    inverse = lax.rsqrt(jnp.mean(centre * centre, -1, keepdims=True) + EPSILON)
    return centre * inverse, inverse


def norm_step_back(delta, values, gain_row):
    standard, inverse = standardized(values)
    scaled = delta * gain_row
    moved = inverse * (
        scaled - jnp.mean(scaled, -1, keepdims=True) - standard * jnp.mean(scaled * standard, -1, keepdims=True)
    )
    return moved, jnp.sum(delta * standard, 0, keepdims=True), jnp.sum(delta, 0, keepdims=True)


def half_mask(half):
    lanes = lax.broadcasted_iota(jnp.int32, (1, 128), 1)
    return (lanes < 64) if half == 0 else (lanes >= 64)


def attention_forward(m, length):
    rows = m.qkv.shape[0]
    width = m.att.shape[1]

    def pair(p, carry):
        at = pl.multiple_of(p * 128, 128)
        q2 = m.qkv[:, pl.ds(at, 128)]
        k2 = m.qkv[:, pl.ds(pl.multiple_of(width + at, 128), 128)]
        v2 = m.qkv[:, pl.ds(pl.multiple_of(2 * width + at, 128), 128)]
        v_turned = v2.T
        parts = []
        for half in range(2):
            kh = jnp.where(half_mask(half), k2, jnp.zeros_like(k2))
            top = matmul_turned(kh[:KEY_SPLIT], q2)
            low = matmul_turned(kh[KEY_SPLIT:], q2)
            key_row = KEY_SPLIT + lax.broadcasted_iota(jnp.int32, low.shape, 0)
            low = jnp.where(key_row < length, low, -1e30)
            peak = jnp.maximum(jnp.max(top, 0, keepdims=True), jnp.max(low, 0, keepdims=True))
            top = jnp.exp(top - peak)
            low = jnp.exp(low - peak)
            over = 1.0 / (jnp.sum(top, 0, keepdims=True) + jnp.sum(low, 0, keepdims=True))
            probs = jnp.concatenate([(top * over).astype(jnp.bfloat16), (low * over).astype(jnp.bfloat16)], axis=0)
            m.probs[2 * p + half] = probs
            parts.append(matmul(v_turned[64 * half : 64 * half + 64], probs))
        turned = jnp.concatenate(parts, axis=0)
        m.att_turned[pl.ds(at, 128), :] = turned.astype(jnp.bfloat16)
        m.att[:, pl.ds(at, 128)] = turned.T.astype(jnp.bfloat16)
        return carry

    lax.fori_loop(0, width // 128, pair, 0)


def attention_back(m):
    width = m.att.shape[1]

    def pair(p, carry):
        at = pl.multiple_of(p * 128, 128)
        k_at = pl.ds(pl.multiple_of(width + at, 128), 128)
        v_at = pl.ds(pl.multiple_of(2 * width + at, 128), 128)
        q2 = m.qkv[:, pl.ds(at, 128)]
        k2 = m.qkv[:, k_at]
        v2 = m.qkv[:, v_at]
        d2 = m.att_delta[:, pl.ds(at, 128)]
        d_turned = d2.T
        k_turned = k2.T
        product = d_turned.astype(jnp.float32) * m.att_turned[pl.ds(at, 128), :].astype(jnp.float32)
        values, keys, queries = [], [], []
        for half in range(2):
            vh = jnp.where(half_mask(half), v2, jnp.zeros_like(v2))
            probs = m.probs[2 * p + half]
            inner = jnp.sum(product[64 * half : 64 * half + 64], 0, keepdims=True)
            score = (probs.astype(jnp.float32) * (matmul(vh, d_turned) - inner)).astype(jnp.bfloat16)
            values.append(matmul(probs, d2))
            keys.append(matmul(score, q2))
            queries.append(matmul(k_turned[64 * half : 64 * half + 64], score))
        dq = (jnp.concatenate(queries, axis=0).T * HEAD_DIM ** (-0.5)).astype(jnp.bfloat16)
        dk = jnp.where(half_mask(0), keys[0], keys[1]).astype(jnp.bfloat16)
        dv = jnp.where(half_mask(0), values[0], values[1]).astype(jnp.bfloat16)
        m.mixed[:, pl.ds(at, 128)] = dq
        m.mixed[:, k_at] = dk
        m.mixed[:, v_at] = dv
        m.sums[2:3, pl.ds(at, 128)] += jnp.sum(dq.astype(jnp.float32), 0, keepdims=True)
        m.sums[3:4, pl.ds(at, 128)] += jnp.sum(dv.astype(jnp.float32), 0, keepdims=True)
        return carry

    lax.fori_loop(0, width // 128, pair, 0)


def forward_front(m, x_ref, length):
    x = x_ref[...].astype(jnp.float32)
    standard, unused = standardized(x)
    m.n1[...] = (standard * m.gain[0:1] + m.shift[0:1]).astype(jnp.bfloat16)
    width = x.shape[1]
    m.need(m.qkv_w)
    n1 = m.n1[...]
    for part in range(3):
        value = matmul(n1, m.qkv_w[:, part * width : (part + 1) * width])
        if part == 0:
            value = (value + m.qv[0:1]).astype(jnp.bfloat16) * jnp.bfloat16(HEAD_DIM ** (-0.5))
        elif part == 2:
            value = value + m.qv[1:2]
        m.qkv[:, part * width : (part + 1) * width] = value.astype(jnp.bfloat16)
    attention_forward(m, length)
    m.need(m.out_w)
    middle = x_ref[...].astype(jnp.float32) + matmul(m.att[...], m.out_w[...]) + m.proj[0:1]
    m.middle[...] = middle
    standard, unused = standardized(middle)
    m.n2[...] = (standard * m.gain[1:2] + m.shift[1:2]).astype(jnp.bfloat16)


def back_tail(m, x_ref, g_ref, n2_delta, keep):
    middle_part, gain, shift = norm_step_back(n2_delta, m.middle[...], m.gain[1:2])
    m.sums[6:7] += gain
    m.sums[8:9] += shift
    middle_delta = g_ref[...].astype(jnp.float32) + middle_part
    proj_delta = middle_delta.astype(jnp.bfloat16)
    m.sums[4:5] += jnp.sum(proj_delta.astype(jnp.float32), 0, keepdims=True)
    m.proj_delta[...] = proj_delta
    m.middle_delta[...] = middle_delta
    m.att_delta[...] = matmul_turned(proj_delta, m.out_w[...]).astype(jnp.bfloat16)
    attention_back(m)
    width = m.att.shape[1]
    total = None
    for part in range(3):
        columns = slice(part * width, (part + 1) * width)
        piece = matmul_turned(m.mixed[:, columns], m.qkv_w[:, columns])
        total = piece if total is None else total + piece
    input_part, gain, shift = norm_step_back(total, x_ref[...].astype(jnp.float32), m.gain[0:1])
    m.sums[5:6] += gain
    m.sums[7:8] += shift
    keep(m.middle_delta[...] + input_part)


def forward_expert(m, slot, begin, end):
    steps = m.up_w.shape[2] // CHUNK

    def step(j, carry):
        columns = pl.ds(pl.multiple_of(j * CHUNK, CHUNK), CHUNK)
        hidden = matmul(m.n2[begin:end], m.up_w[slot, :, columns]) + m.up_b[slot : slot + 1, columns]
        below, bell = normal_parts(hidden)
        active = (hidden * below).astype(jnp.bfloat16)
        m.active[begin:end, columns] = active
        m.slope[begin:end, columns] = (below + hidden * bell).astype(jnp.bfloat16)
        m.total[begin:end] += matmul(active, m.down_w[slot, columns, :])
        return carry

    m.total[begin:end] = m.middle[begin:end] + m.down_b[slot : slot + 1]
    lax.fori_loop(0, steps, step, 0)


def back_expert(m, g_ref, slot, begin, end):
    steps = m.up_w.shape[2] // CHUNK
    m.total[begin:end] = jnp.zeros((end - begin, m.total.shape[1]), jnp.float32)
    m.sums[slot : slot + 1] += jnp.sum(g_ref[begin:end].astype(jnp.float32), 0, keepdims=True)

    def step(j, carry):
        columns = pl.ds(pl.multiple_of(j * CHUNK, CHUNK), CHUNK)
        active_delta = matmul_turned(g_ref[begin:end], m.down_w[slot, columns, :])
        hidden_delta = (active_delta * m.slope[begin:end, columns].astype(jnp.float32)).astype(jnp.bfloat16)
        m.hidden_delta[begin:end, columns] = hidden_delta
        m.sums[pl.ds(9 + 4 * slot + j, 1)] += jnp.sum(hidden_delta.astype(jnp.float32), 0, keepdims=True)
        m.total[begin:end] += matmul_turned(hidden_delta, m.up_w[slot, :, columns])
        return carry

    lax.fori_loop(0, steps, step, 0)


def both_expert(m, g_ref):
    steps = m.up_w.shape[2] // CHUNK
    m.total[...] = jnp.zeros(m.total.shape, jnp.float32)
    m.sums[0:1] += jnp.sum(g_ref[...].astype(jnp.float32), 0, keepdims=True)

    def step(j, carry):
        columns = pl.ds(pl.multiple_of(j * CHUNK, CHUNK), CHUNK)
        active_delta = matmul_turned(g_ref[...], m.down_w[0, columns, :])
        hidden = matmul(m.n2[...], m.up_w[0, :, columns]) + m.up_b[2:3, columns]
        below, bell = normal_parts(hidden)
        m.active[:, columns] = (hidden * below).astype(jnp.bfloat16)
        hidden_delta = (active_delta * (below + hidden * bell)).astype(jnp.bfloat16)
        m.hidden_delta[:, columns] = hidden_delta
        m.sums[pl.ds(9 + j, 1)] += jnp.sum(hidden_delta.astype(jnp.float32), 0, keepdims=True)
        m.total[...] += matmul_turned(hidden_delta, m.up_w[0, :, columns])
        return carry

    lax.fori_loop(0, steps, step, 0)


class Refs:
    pass


def layers_kernel(names, length, *refs):
    m = Refs()
    for name, ref in zip(names, refs):
        setattr(m, name, ref)
    items = m.tokens.shape[0]
    half = m.total.shape[1] // 2
    section = lax.axis_index("section")
    across = (1 - section, lax.axis_index("dp"))

    def send(i):
        return pltpu.make_async_remote_copy(
            src_ref=m.leaving.at[i], dst_ref=m.landed.at[i], send_sem=m.send_sem.at[i], recv_sem=m.recv_sem.at[i],
            device_id=across, device_id_type=MESH,
        )

    def send_half(i):
        return pltpu.make_async_remote_copy(
            src_ref=m.half_out.at[i], dst_ref=m.high.at[i], send_sem=m.half_send.at[i], recv_sem=m.half_recv.at[i],
            device_id=across, device_id_type=MESH,
        )

    def local(source, target, number):
        return pltpu.make_async_copy(source, target, m.copy_sem.at[number])

    def branch_copy(source, i):
        return pltpu.make_async_copy(source.at[i], m.branch.at[i], m.branch_sem.at[i])

    def weights(experts):
        found = [
            (m.qkv_w, [local(m.in_qkv.at[0], m.qkv_w, 0)]),
            (m.out_w, [local(m.in_out.at[0], m.out_w, 1)]),
            (m.up_w, []),
            (m.down_w, []),
        ]
        for slot, expert in enumerate(experts):
            found[2][1].append(local(m.in_up.at[expert], m.up_w.at[slot], 2 + slot))
            found[3][1].append(local(m.in_down.at[expert], m.down_w.at[slot], 4 + slot))
        return found

    def start_weights(found):
        copies = found[0][1] + found[1][1]
        for pair in zip(found[2][1], found[3][1]):
            copies += pair
        for copy in copies:
            copy.start()

    def needs(found, i):
        def need(ref):
            for here, copies in found:
                if here is ref:

                    @pl.when(i == 0)
                    def _():
                        for copy in copies:
                            copy.wait()

        return need

    leaving = (
        (m.n1, m.out_n1), (m.att, m.out_att), (m.n2, m.out_n2), (m.active, m.out_active), (m.qkv, m.kept_qkv),
        (m.probs, m.kept_probs), (m.att_turned, m.kept_turned), (m.middle, m.kept_middle), (m.slope, m.kept_slope),
        (m.mixed, m.out_mixed), (m.proj_delta, m.out_proj), (m.hidden_delta, m.out_hidden),
    )
    n1, att, n2, active, qkv, probs, turned, middle, slope, mixed, proj, hidden = range(len(leaving))

    def puts(i):
        return lambda number: local(leaving[number][0], leaving[number][1].at[i], 6 + number)

    def gets(i):
        return lambda number: local(leaving[number][1].at[i], leaving[number][0], 14 + number)

    def start(copies, *which):
        for number in which:
            copies(number).start()

    def wait(copies, *which):
        for number in which:
            copies(number).wait()

    def settle(i, *which):
        @pl.when(i > 0)
        def _():
            wait(puts(i), *which)

    def first_front(found, i, carry):
        m.need = needs(found, i)
        settle(i, n1, att, n2, qkv, probs, turned, middle)
        forward_front(m, m.tokens.at[i], length)
        start(puts(i), n1, att, n2, qkv, probs, turned, middle)
        settle(i, active, slope)
        m.need(m.up_w)
        m.need(m.down_w)
        forward_expert(m, 1, 0, TEXT)
        forward_expert(m, 0, TEXT, ROWS)
        m.leaving[i] = m.total[...].astype(jnp.bfloat16)
        send(i).start()
        start(puts(i), active, slope)
        return carry

    def first_back(i, carry):
        start(gets(i), slope, middle, turned, qkv, probs)

        @pl.when(i > 0)
        def _():
            send(i - 1).wait_send()

        send(i).wait_recv()
        branch_copy(m.landed, i).start()
        settle(i, hidden)
        wait(gets(i), slope)
        gradient = m.landed.at[i]
        back_expert(m, gradient, 1, 0, TEXT)
        back_expert(m, gradient, 0, TEXT, ROWS)
        start(puts(i), hidden)
        settle(i, mixed, proj)
        wait(gets(i), middle, turned, qkv, probs)

        def keep(value):
            m.low[i] = value[:, :half]
            m.half_out[i] = value[:, half:].astype(jnp.bfloat16)

        back_tail(m, m.tokens.at[i], gradient, m.total[...], keep)
        send_half(i).start()
        start(puts(i), mixed, proj)
        branch_copy(m.landed, i).wait()
        return carry

    def second_both(found, i, carry):
        m.need = needs(found, i)
        branch_copy(m.targets, i).start()
        send(i).wait_recv()
        settle(i, n1, att, n2)
        arrived = m.landed.at[i]
        forward_front(m, arrived, length)
        start(puts(i), n1, att, n2)
        settle(i, active, hidden)
        m.need(m.up_w)
        m.need(m.down_w)
        gradient = m.targets.at[i]
        both_expert(m, gradient)
        start(puts(i), active, hidden)
        settle(i, mixed, proj)

        def keep(value):
            m.leaving[i] = value.astype(jnp.bfloat16)

        back_tail(m, arrived, gradient, m.total[...], keep)
        send(i).start()
        start(puts(i), mixed, proj)
        branch_copy(m.targets, i).wait()
        return carry

    m.sums[...] = jnp.zeros(m.sums.shape, jnp.float32)
    barrier = pltpu.get_barrier_semaphore()
    pl.semaphore_signal(barrier, inc=1, device_id=across, device_id_type=MESH)

    @pl.when(section == 0)
    def _():
        found = weights((0, 1))
        start_weights(found)
        pl.semaphore_wait(barrier, 1)
        lax.fori_loop(0, items, functools.partial(first_front, found), 0)
        wait(puts(0), n1, att, n2, active, qkv, probs, turned, middle, slope)
        lax.fori_loop(0, items, first_back, 0)
        wait(puts(0), mixed, proj, hidden)
        send(items - 1).wait_send()
        for i in range(items):
            send_half(i).wait_send()

    @pl.when(section == 1)
    def _():
        found = weights((2,))
        start_weights(found)
        pl.semaphore_wait(barrier, 1)
        lax.fori_loop(0, items, functools.partial(second_both, found), 0)
        wait(puts(0), n1, att, n2, active, mixed, proj, hidden)
        for i in range(items):
            send(i).wait_send()
            send_half(i).wait_recv()


def both_layers(tokens, targets, qkv_weight, out_weight, up_table, down_table, qv, proj, gain, shift, up_b, down_b, length):
    items, rows, width = tokens.shape
    ff = up_b.shape[1]
    heads = width // HEAD_DIM
    bf16, f32 = jnp.bfloat16, jnp.float32
    dma = pltpu.SemaphoreType.DMA
    vmem, anywhere = pl.BlockSpec(memory_space=pltpu.VMEM), pl.BlockSpec(memory_space=pl.ANY)
    ins = dict(
        tokens=(tokens, vmem), targets=(targets, vmem), in_qkv=(qkv_weight, anywhere), in_out=(out_weight, anywhere),
        in_up=(up_table, anywhere), in_down=(down_table, anywhere), qv=(qv, vmem), proj=(proj, vmem), gain=(gain, vmem),
        shift=(shift, vmem), up_b=(up_b, vmem), down_b=(down_b, vmem),
    )

    def made(*shape, kind=bf16, spec=anywhere):
        return jax.ShapeDtypeStruct((items,) + shape, kind), spec

    outs = dict(
        out_n1=made(rows, width), out_att=made(rows, width), out_n2=made(rows, width), out_active=made(rows, ff),
        out_mixed=made(rows, 3 * width), out_proj=made(rows, width), out_hidden=made(rows, ff), branch=made(rows, width),
        kept_qkv=made(rows, 3 * width), kept_probs=made(heads, rows, rows), kept_turned=made(width, rows),
        kept_middle=made(rows, width, kind=f32), kept_slope=made(rows, ff),
        low=made(rows, width // 2, kind=f32, spec=vmem), high=made(rows, width // 2),
        sums=(jax.ShapeDtypeStruct((24, width), f32), vmem),
    )
    low_row, wide_row = ((rows, width), bf16), ((rows, ff), bf16)
    buffers = dict(
        qkv_w=((width, 3 * width), bf16), out_w=((width, width), bf16), up_w=((2, width, ff), bf16),
        down_w=((2, ff, width), bf16), n1=low_row, att=low_row, n2=low_row, active=wide_row,
        qkv=((rows, 3 * width), bf16), probs=((heads, rows, rows), bf16), att_turned=((width, rows), bf16),
        middle=((rows, width), f32), slope=wide_row, total=((rows, width), f32), mixed=((rows, 3 * width), bf16),
        proj_delta=low_row, hidden_delta=wide_row, att_delta=low_row, middle_delta=((rows, width), f32),
        leaving=((items, rows, width), bf16), landed=((items, rows, width), bf16),
        half_out=((items, rows, width // 2), bf16),
    )
    semaphores = dict(
        copy_sem=dma((23,)), branch_sem=dma((items,)), send_sem=dma((items,)), recv_sem=dma((items,)),
        half_send=dma((items,)), half_recv=dma((items,)),
    )
    names = list(ins) + list(outs) + list(buffers) + list(semaphores)
    results = pl.pallas_call(
        functools.partial(layers_kernel, names, length),
        out_shape=[shape for shape, spec in outs.values()],
        in_specs=[spec for value, spec in ins.values()],
        out_specs=[spec for shape, spec in outs.values()],
        scratch_shapes=[pltpu.VMEM(*kind) for kind in buffers.values()] + list(semaphores.values()),
        compiler_params=pltpu.CompilerParams(
            collective_id=1, has_side_effects=True, vmem_limit_bytes=60 * 1024 * 1024
        ),
        cost_estimate=pl.CostEstimate(flops=40_000_000_000, bytes_accessed=100_000_000, transcendentals=0),
    )(*[value for value, spec in ins.values()])
    m = Refs()
    for name, result in zip(outs, results):
        setattr(m, name, result)
    return m


def text_first(values):
    pad = jnp.zeros((values.shape[0], ROWS - values.shape[1]) + values.shape[2:], values.dtype)
    return jnp.concatenate([values[:, PATCHES:], values[:, :PATCHES], pad], axis=1)


def patches_first(values, length):
    return jnp.concatenate([values[:, TEXT:length], values[:, :TEXT]], axis=1)


def small_outs(own, other, is_first):
    first = jnp.where(is_first, own, other)
    second = jnp.where(is_first, other, own)
    me = lax.axis_index("dp")

    def columns(rows):
        wide = rows.shape[-1] // lax.axis_size("dp")
        return lax.dynamic_slice_in_dim(rows, me * wide, wide, rows.ndim - 1)

    down = columns(jnp.concatenate([first[:2], second[:1]]))
    up = columns(jnp.concatenate([first[9:17].reshape(2, -1), second[9:13].reshape(1, -1)]))
    own = columns(own[2:9])
    return own[0:2], own[2:3], own[3:5], own[5:7], up, down


def flat(value):
    return value.reshape((-1, value.shape[-1]))


def left_parts(m, is_first):
    n1, att, n2, branch_delta = (flat(part) for part in (m.out_n1, m.out_att, m.out_n2, m.branch))
    text = (jnp.arange(n1.shape[0]) % ROWS < TEXT)[:, None]
    vision = jnp.logical_not(text & is_first).astype(jnp.bfloat16)
    text = text.astype(jnp.bfloat16)
    return [
        piece.T for piece in (n2 * vision, branch_delta * vision, n2 * text, branch_delta * text, n1, att)
    ]


def large_grads(m, is_first):
    lefts = left_parts(m, is_first)
    width = lefts[0].shape[0]
    chips = 8
    core = lax.axis_index("dp") % 2

    def spread(value, before, after):
        value = flat(value)
        split = value.reshape(value.shape[0], chips, -1)
        return jnp.pad(split, ((0, 0), (0, 0), (before, after))).reshape(value.shape[0], -1)

    mixed, proj = spread(m.out_mixed, 0, 96), spread(m.out_proj, 288, 0)
    blocks, smalls = summed_blocks(jnp.stack(lefts), m.sums, flat(m.out_hidden), flat(m.out_active), mixed, proj)
    own, other = blocks[0], blocks[1]

    def whole(block, begin, wide):
        both = block.reshape(width, BLOCK)
        return lax.dynamic_slice_in_dim(both, begin + core * wide, wide, 1).astype(jnp.float32)

    first = [jnp.where(is_first, own[:, k], other[:, k]) for k in range(4)]
    second = [jnp.where(is_first, other[:, k], own[:, k]) for k in range(2)]
    up = jnp.stack([whole(block, 0, 192) for block in (first[0], first[2], second[0])])
    down = jnp.stack([whole(block, 0, 192).T for block in (first[1], first[3], second[1])])
    return whole(own[:, 4], 0, 144), whole(own[:, 4], 288, 48), up, down, smalls[0], smalls[1]


def large_grads_plain(m, is_first):
    lefts = left_parts(m, is_first)
    hidden_delta, active = flat(m.out_hidden), flat(m.out_active)

    def total_of(left, right):
        product = jnp.dot(left, right, preferred_element_type=jnp.float32).astype(jnp.bfloat16)
        return lax.psum_scatter(product, "dp", scatter_dimension=1, tiled=True)

    def table(vision_part, text_part):
        def swapped(part):
            return lax.psum(part, "section").astype(jnp.float32)

        return jnp.stack(
            [
                swapped(jnp.where(is_first, vision_part, 0)),
                swapped(jnp.where(is_first, text_part, 0)),
                swapped(jnp.where(is_first, 0, vision_part)),
            ]
        )

    up = table(total_of(lefts[0], hidden_delta), total_of(lefts[2], hidden_delta))
    down = table(total_of(lefts[1], active), total_of(lefts[3], active))
    small = lax.psum(m.sums, "dp")
    return (
        total_of(lefts[4], flat(m.out_mixed)).astype(jnp.float32),
        total_of(lefts[5], flat(m.out_proj)).astype(jnp.float32),
        up,
        down.transpose(0, 2, 1),
        small,
        lax.ppermute(small, "section", [(0, 1), (1, 0)]),
    )


def shards(
    tokens, cotangent, patch_mask, text_mask, qkv_weight, qv_bias, out_weight, out_bias, norm_gain, norm_bias,
    up_table, up_bias, down_table, down_bias,
):
    is_first = lax.axis_index("section") == 0
    length = tokens.shape[1]
    positions = jnp.arange(length, dtype=jnp.int32)
    chosen = jnp.any(positions[None, :, None] == patch_mask[:, None, :], axis=2) | jnp.any(
        positions[None, :, None] == text_mask[:, None, :], axis=2
    )
    targets = text_first(cotangent * chosen.astype(jnp.bfloat16)[..., None])
    m = both_layers(
        text_first(tokens), targets, qkv_weight, out_weight, up_table, down_table, qv_bias[0], out_bias, norm_gain[0],
        norm_bias[0], up_bias, down_bias, length,
    )
    grads = large_grads if lax.axis_size("dp") == 16 else large_grads_plain
    qkv, out, up, down, own, other = grads(m, is_first)
    qv_part, proj_part, gain_part, shift_part, up_part, down_part = small_outs(own, other, is_first)
    input_grad = patches_first(jnp.where(is_first, m.low, m.high.astype(jnp.float32)), length)
    return (
        input_grad, qkv[None], qv_part[None], out[None], proj_part, gain_part[None], shift_part[None],
        up, up_part, down, down_part,
    )


def solution(mesh):
    items, layers = P("dp"), P("section")
    return jax.shard_map(
        shards,
        mesh=mesh,
        in_specs=(items,) * 4 + (layers,) * 6 + (P(),) * 4,
        out_specs=(
            P("dp", None, "section"), P("section", None, "dp"), P("section", None, "dp"), P("section", None, "dp"),
            P("section", "dp"), P("section", None, "dp"), P("section", None, "dp"),
            P(None, None, "dp"), P(None, "dp"), P(None, "dp", None), P(None, "dp"),
        ),
        check_vma=False,
    )
```

```python
import functools

import jax
import jax.numpy as jnp
from jax import lax
from jax.experimental import pallas as pl
from jax.experimental.pallas import tpu as pltpu
from jax.sharding import PartitionSpec as P

HEAD_DIM = 64
PATCHES = 197
EPSILON = 1e-05
BLOCK = 384
RING = 3
TEXT = 64
ROWS = 272
MESH = pl.DeviceIdType.MESH


class Refs:
    pass


def sum_kernel(names, *refs):
    m = Refs()
    for name, ref in zip(names, refs):
        setattr(m, name, ref)
    section = lax.axis_index("section")
    me = lax.axis_index("dp")
    z, y, core = me // 4, (me // 2) % 2, me % 2
    peer = (section, me + 1 - 2 * core)
    beside = (section, me + 2 - 4 * y)
    right = (section, me + 4)
    left = (section, me - 4)
    across = (1 - section, me)
    on_first = section == 0
    units = jnp.where(on_first, 20, 16)
    computed = jnp.where(on_first, 20, 12)

    class Unit:
        def __init__(self, u):
            self.u = u
            self.group = jnp.where(on_first, u // 5, u // 4)
            turn = jnp.where(on_first, u % 5, u % 4)
            self.z_first = turn == 0
            self.handed_on = on_first & (turn == 1)
            self.j = jnp.maximum(3 * self.group + turn - jnp.where(on_first, 2, 1), 0)
            third = self.j // 4
            later = jnp.where(on_first, jnp.where(third == 1, 2, 4), jnp.where(third == 1, 4, 3))
            kind = jnp.where(third == 0, 1, later)
            self.kind = jnp.where(self.z_first, 0, jnp.where(self.handed_on, 3, kind))
            self.handed_in = jnp.logical_not(on_first) & (self.kind == 3)
            self.y_first = jnp.logical_not(self.z_first | self.handed_on)
            o = jnp.where(self.z_first | self.handed_on, self.group, self.j % 4)
            self.o = o
            self.plane = jnp.where(o == 0, 0, jnp.where(o == 1, 3, o - 1))
            self.y_slot = jnp.where(self.z_first, 12 + self.group, self.j)
            self.order = u - jnp.where((section == 1) & (u > 11), 1, 0)

    def remote(src, dst, send, recv, device):
        return pltpu.make_async_remote_copy(
            src_ref=src, dst_ref=dst, send_sem=send, recv_sem=recv, device_id=device, device_id_type=MESH
        )

    def core_copy(n, b):
        slot = n.order % RING
        return remote(m.xs.at[slot, b], m.xr.at[slot, b], m.core_send.at[n.order, b], m.core_recv.at[n.order, b], peer)

    def y_copy(n):
        return remote(m.part.at[n.u, 0], m.yr.at[n.y_slot], m.y_send.at[n.y_slot], m.y_recv.at[n.y_slot], beside)

    def right_copy(n):
        return remote(m.part.at[n.u, 1], m.zr.at[n.j], m.right_send.at[n.j], m.right_recv.at[n.j], right)

    def left_copy(n):
        return remote(m.part.at[n.u, 1], m.zl.at[n.j], m.left_send.at[n.j], m.left_recv.at[n.j], left)

    def right_pair(n):
        g = n.group
        return remote(m.part.at[n.u], m.wr.at[g], m.right_send.at[12 + g], m.right_recv.at[12 + g], right)

    def left_pair(n):
        g = n.group
        return remote(m.part.at[n.u], m.wl.at[g], m.left_send.at[12 + g], m.left_recv.at[12 + g], left)

    def over_copy(o, source, target):
        return remote(m.part.at[source], m.part.at[target], m.over_send.at[o], m.over_recv.at[o], across)

    def over_target(o):
        return jnp.where(o == 0, 11, 12 + o)

    def peer_copy(k):
        return remote(m.fin.at[0, core, k], m.fin.at[0, core, k], m.peer_send.at[k], m.peer_recv.at[k], peer)

    def cross_copy(k):
        return remote(m.fin.at[0, core, k], m.fin.at[1, core, k], m.cross_send.at[k], m.cross_recv.at[k], across)

    def hand_copy(k):
        return remote(m.fin.at[1, core, k], m.fin.at[1, core, k], m.hand_send.at[k], m.hand_recv.at[k], peer)

    def chip_of(n, b):
        return n.plane * 2 + jnp.where(b == 0, 1 - y, y)

    def mixed_start(t):
        return pl.multiple_of((9 * t // 4) * 128, 128)

    def proj_start(t):
        return pl.multiple_of(jnp.minimum(3 * t // 4, 3) * 128, 128)

    def tile_copies(n, b):
        t = chip_of(n, b)
        k = n.kind
        plain = pl.multiple_of(t * BLOCK, 128)
        cases = []
        for ref, which, here, begin in (
            (m.hidden, 0, (k == 0) | (k == 2), plain),
            (m.active, 0, (k == 1) | (k == 3), plain),
            (m.mixed, 0, k == 4, mixed_start(t)),
            (m.proj, 1, k == 4, proj_start(t)),
        ):
            copy = pltpu.make_async_copy(ref.at[:, pl.ds(begin, BLOCK)], m.rt.at[b, which], m.rt_sem.at[b, which])
            cases.append((here, copy))
        return cases

    def start_tile(n, b):
        for here, copy in tile_copies(n, b):
            pl.when(here)(copy.start)

    def wait_tile(n, b):
        for here, copy in tile_copies(n, b):
            pl.when(here)(copy.wait)

    def add_into(target, source):
        target[...] = (target[...].astype(jnp.float32) + source[...].astype(jnp.float32)).astype(jnp.bfloat16)

    def rows(half):
        return pl.ds(pl.multiple_of(half * BLOCK, BLOCK), BLOCK)

    def dot(index, half, tile):
        return jnp.dot(m.lt[index, rows(half), :], tile[...], preferred_element_type=jnp.float32)

    def attention_block(half, b, t):
        mixed_shift = (BLOCK - (288 * t - mixed_start(t))) % BLOCK
        proj_shift = 288 - (96 * t - proj_start(t))
        mixed = pltpu.roll(dot(4, half, m.rt.at[b, 0]), mixed_shift, 1)
        proj = pltpu.roll(dot(5, half, m.rt.at[b, 1]), proj_shift, 1)
        lanes = lax.broadcasted_iota(jnp.int32, (1, BLOCK), 1)
        return jnp.where(lanes < 288, mixed, proj)

    def compute(n):
        k = n.kind
        slot = n.order % RING

        @pl.when(n.order >= RING)
        def _():
            back = Unit(n.u - RING - jnp.where((section == 1) & (n.u == 12), 1, 0))
            core_copy(back, 0).wait_send()
            core_copy(back, 1).wait_send()
            pl.semaphore_wait(m.credit, 1)

        def block(b, carry):
            @pl.when(b == 0)
            def _():
                start_tile(n, 1)

            @pl.when((b == 1) & (n.order + 1 < computed))
            def _():
                start_tile(Unit(n.u + 1 + jnp.where((section == 1) & (n.u == 10), 1, 0)), 0)

            wait_tile(n, b)
            t = chip_of(n, b)
            tile = m.rt.at[b, 0]

            @pl.when(k < 4)
            def _():
                m.xs[slot, b] = dot(k, 1 - core, tile).astype(jnp.bfloat16)

            @pl.when(k == 4)
            def _():
                m.xs[slot, b] = attention_block(1 - core, b, t).astype(jnp.bfloat16)

            core_copy(n, b).start()

            @pl.when(k < 4)
            def _():
                m.part[n.u, b] = dot(k, core, tile).astype(jnp.bfloat16)

            @pl.when(k == 4)
            def _():
                m.part[n.u, b] = attention_block(core, b, t).astype(jnp.bfloat16)

            return carry

        lax.fori_loop(0, 2, block, 0)

    def join_core(n):
        slot = n.order % RING

        @pl.when(n.handed_in)
        def _():
            over_copy(n.o, 0, n.u).wait_recv()

        @pl.when(jnp.logical_not(n.handed_in))
        def _():
            core_copy(n, 0).wait_recv()
            add_into(m.part.at[n.u, 0], m.xr.at[slot, 0])

        pl.when(n.y_first)(lambda: y_copy(n).start())

        @pl.when(jnp.logical_not(n.handed_in))
        def _():
            core_copy(n, 1).wait_recv()
            add_into(m.part.at[n.u, 1], m.xr.at[slot, 1])

            @pl.when(n.order + RING < computed)
            def _():
                pl.semaphore_signal(m.credit, inc=1, device_id=peer, device_id_type=MESH)

        pl.when(n.handed_on)(lambda: over_copy(n.o, n.u, over_target(n.o)).start())

    def join_y(n):
        y_copy(n).wait_recv()
        add_into(m.part.at[n.u, 1], m.yr.at[n.y_slot])

    def take(n, one, pair, single_from, pair_from):
        @pl.when(n.y_first)
        def _():
            one(n).wait_recv()
            add_into(m.part.at[n.u, 1], single_from.at[n.j])

        @pl.when(n.z_first)
        def _():
            pair(n).wait_recv()
            add_into(m.part.at[n.u], pair_from.at[n.group])

    def take_right(n):
        take(n, right_copy, right_pair, m.zr, m.wr)

    def take_left(n):
        take(n, left_copy, left_pair, m.zl, m.wl)

    def pass_right(n):
        pl.when(z > 0)(lambda: take_right(n))
        pl.when(n.y_first)(lambda: right_copy(n).start())
        pl.when(n.z_first)(lambda: right_pair(n).start())

    def pass_left(n):
        pl.when(z < 3)(lambda: take_left(n))
        pl.when(n.y_first)(lambda: left_copy(n).start())
        pl.when(n.z_first)(lambda: left_pair(n).start())

    def give(n):
        k = n.kind
        m.fin[0, core, k] = m.part[n.u, 1]
        peer_copy(k).start()
        pl.when(k < 4)(lambda: cross_copy(k).start())

    def meet(n):
        pl.when(z > 0)(lambda: take_right(n))
        pl.when(z < 3)(lambda: take_left(n))
        pl.when(n.z_first)(lambda: y_copy(n).start())
        pl.when(n.y_first)(lambda: give(n))

    def meet_late(n):
        join_y(n)
        give(n)

    flips = (peer, beside, (section, me + 4 - 8 * (z % 2)), (section, me + 8 - 16 * (z // 2)), across)

    def small_copy(j):
        return remote(m.small_sum.at[j], m.small_in.at[j], m.small_send.at[j], m.small_recv.at[j], flips[j])

    def small_step(j):
        if j == 0:
            m.small_sum[0] = m.small[...]
        else:
            small_copy(j - 1).wait_recv()
            if j == 5:
                m.small_out[0] = m.small_sum[4]
                m.small_out[1] = m.small_in[4]
            else:
                m.small_sum[j] = m.small_sum[j - 1] + m.small_in[j - 1]
        if j < 5:
            small_copy(j).start()

    depth = m.stage.shape[0]
    lanes = lax.broadcasted_iota(jnp.int32, (1, depth), 1)
    is_text = lanes % ROWS < TEXT
    vision = jnp.where(is_text & on_first, 0.0, 1.0)
    text = jnp.where(is_text, 1.0, 0.0)
    stages = ((m.n2, 0, 2), (m.branch, 1, 3), (m.n1, 4, None), (m.att, 5, None))

    def stage_copy(number):
        return pltpu.make_async_copy(stages[number][0], m.stage, m.stage_sem.at[0])

    def prepare(number):
        stage_copy(number).wait()
        unused, first, second = stages[number]

        def part(c, carry):
            at = pl.ds(pl.multiple_of(c * 128, 128), 128)
            turned = m.stage[:, at].T
            if second is None:
                m.lt[first, at, :] = turned
            else:
                wide = turned.astype(jnp.float32)
                m.lt[first, at, :] = (wide * vision).astype(jnp.bfloat16)
                m.lt[second, at, :] = (wide * text).astype(jnp.bfloat16)
            return carry

        lax.fori_loop(0, m.stage.shape[1] // 128, part, 0)
        if number < 3:
            stage_copy(number + 1).start()

    barrier = pltpu.get_barrier_semaphore()
    for device in (peer, beside, across, flips[3]):
        pl.semaphore_signal(barrier, inc=1, device_id=device, device_id_type=MESH)

    @pl.when(z < 3)
    def _():
        pl.semaphore_signal(barrier, inc=1, device_id=right, device_id_type=MESH)

    @pl.when(z > 0)
    def _():
        pl.semaphore_signal(barrier, inc=1, device_id=left, device_id_type=MESH)

    stage_copy(0).start()
    start_tile(Unit(jnp.int32(0)), 0)
    prepare(0)
    pl.semaphore_wait(barrier, 4 + jnp.where(z < 3, 1, 0) + jnp.where(z > 0, 1, 0))

    def at_unit(u, condition, action):
        n = Unit(jnp.maximum(u, 0))

        @pl.when((u >= 0) & (u < units) & condition(n))
        def _():
            action(n)

    def in_flow(n):
        return jnp.logical_not(n.handed_on)

    def step(i, carry):
        at_unit(i, lambda n: jnp.logical_not(n.handed_in), compute)
        for number in range(3):
            pl.when(i == number)(functools.partial(prepare, number + 1))
        at_unit(i - 1, lambda n: True, join_core)
        at_unit(i - 4, lambda n: n.y_first, join_y)
        at_unit(i - 4 - 3 * z, lambda n: in_flow(n) & (n.plane > z), pass_right)
        at_unit(i - 13 + 3 * z, lambda n: in_flow(n) & (n.plane < z), pass_left)
        at_unit(i - 14, lambda n: in_flow(n) & (n.plane == z), meet)
        at_unit(i - 16, lambda n: n.z_first & (n.plane == z), meet_late)
        for j in range(6):
            pl.when(i == 3 + j)(functools.partial(small_step, j))
        return carry

    lax.fori_loop(0, units + 16, step, 0)

    def third_kind(k):
        return jnp.where(k == 2, 2 + section, k)

    def their_kind(k):
        return jnp.where(k == 2, 3 - section, k)

    for k in range(3):
        cross_copy(their_kind(jnp.int32(k))).wait_recv()
        hand_copy(their_kind(jnp.int32(k))).start()

    def settle(u, carry):
        n = Unit(u)

        @pl.when(jnp.logical_not(n.handed_in) & (n.order >= computed - RING))
        def _():
            core_copy(n, 0).wait_send()
            core_copy(n, 1).wait_send()

        pl.when(n.handed_on)(lambda: over_copy(n.o, n.u, over_target(n.o)).wait_send())
        pl.when(n.y_first | (n.z_first & (n.plane == z)))(lambda: y_copy(n).wait_send())
        pl.when(n.y_first & (n.plane > z))(lambda: right_copy(n).wait_send())
        pl.when(n.z_first & (n.plane > z))(lambda: right_pair(n).wait_send())
        pl.when(n.y_first & (n.plane < z))(lambda: left_copy(n).wait_send())
        pl.when(n.z_first & (n.plane < z))(lambda: left_pair(n).wait_send())
        return carry

    lax.fori_loop(0, units, settle, 0)
    for j in range(5):
        small_copy(j).wait_send()
    for k in range(3):
        peer_copy(third_kind(jnp.int32(k))).wait()
        cross_copy(third_kind(jnp.int32(k))).wait_send()
        hand_copy(their_kind(jnp.int32(k))).wait()
    peer_copy(4).wait()

    def write(c):
        def columns(side, half, k, begin, wide):
            return m.fin[side, half, k, :, begin + c * wide : begin + (c + 1) * wide]

        first, second = section, 1 - section
        for half in range(2):
            at = slice(half * BLOCK, (half + 1) * BLOCK)
            m.qkv_out[at, :] = columns(0, half, 4, 0, 144)
            m.out_out[at, :] = columns(0, half, 4, 288, 48)
            for expert, side, k in ((0, first, 0), (1, first, 2), (2, second, 0)):
                m.up_out[expert, at, :] = columns(side, half, k, 0, 192)
            for expert, side, k in ((0, first, 1), (1, second, 3), (2, second, 1)):
                m.down_out[expert, :, at] = columns(side, half, k, 0, 192).T

    for c in range(2):
        pl.when(core == c)(functools.partial(write, c))


def summed_grads(n1, att, n2, branch, hidden, active, mixed, proj, small):
    dma = pltpu.SemaphoreType.DMA
    depth, width = n1.shape
    bf16, f32 = jnp.bfloat16, jnp.float32
    tile = (BLOCK, BLOCK)
    vmem, anywhere = pl.BlockSpec(memory_space=pltpu.VMEM), pl.BlockSpec(memory_space=pl.ANY)
    ins = dict(n1=n1, att=att, n2=n2, branch=branch, hidden=hidden, active=active, mixed=mixed, proj=proj, small=small)
    outs = dict(
        up_out=((3, width, 192), bf16), down_out=((3, 192, width), bf16), qkv_out=((width, 144), bf16),
        out_out=((width, 48), bf16), small_out=((2,) + small.shape, f32),
    )
    buffers = dict(
        rt=((2, 2, depth, BLOCK), bf16), part=((20, 2) + tile, bf16), xs=((RING, 2) + tile, bf16),
        xr=((RING, 2) + tile, bf16), yr=((16,) + tile, bf16), zr=((12,) + tile, bf16), zl=((12,) + tile, bf16),
        wr=((4, 2) + tile, bf16), wl=((4, 2) + tile, bf16), fin=((2, 2, 5) + tile, bf16),
        lt=((6, width, depth), bf16), stage=((depth, width), bf16), small_sum=((5,) + small.shape, f32),
        small_in=((5,) + small.shape, f32),
    )
    semaphores = dict(
        small_send=dma((5,)), small_recv=dma((5,)), rt_sem=dma((2, 2)), stage_sem=dma((1,)), core_send=dma((20, 2)),
        core_recv=dma((20, 2)), y_send=dma((16,)), y_recv=dma((16,)), right_send=dma((16,)), right_recv=dma((16,)),
        left_send=dma((16,)), left_recv=dma((16,)), over_send=dma((4,)), over_recv=dma((4,)), peer_send=dma((5,)),
        peer_recv=dma((5,)), cross_send=dma((5,)), cross_recv=dma((5,)), hand_send=dma((5,)), hand_recv=dma((5,)),
        credit=pltpu.SemaphoreType.REGULAR,
    )
    names = list(ins) + list(outs) + list(buffers) + list(semaphores)
    return pl.pallas_call(
        functools.partial(sum_kernel, names),
        out_shape=[jax.ShapeDtypeStruct(*kind) for kind in outs.values()],
        in_specs=[anywhere] * 8 + [vmem],
        out_specs=[vmem] * len(outs),
        scratch_shapes=[pltpu.VMEM(*kind) for kind in buffers.values()] + list(semaphores.values()),
        compiler_params=pltpu.CompilerParams(
            collective_id=0, has_side_effects=True, vmem_limit_bytes=60 * 1024 * 1024
        ),
        cost_estimate=pl.CostEstimate(flops=48 * 2 * 768 * 384 * depth, bytes_accessed=40_000_000, transcendentals=0),
    )(*ins.values())


CHUNK = 768
KEY_SPLIT = 256
TAIL = (0.319381530, -0.356563782, 1.781477937, -1.821255978, 1.330274429)
PEAK = 0.3989422804014327


def normal_parts(z):
    size = jnp.abs(z)
    scale = 1.0 + 0.2316419 * size
    t = pl.reciprocal(scale, approx=True)
    t = t * (2.0 - scale * t)
    bell = jnp.exp(-0.5 * z * z) * PEAK
    series = TAIL[4]
    for factor in TAIL[3::-1]:
        series = series * t + factor
    upper = bell * (series * t)
    return jnp.where(z >= 0, 1.0 - upper, upper), bell


def matmul(left, right):
    return jnp.dot(left, right, preferred_element_type=jnp.float32)


def matmul_turned(left, right):
    return lax.dot_general(left, right, (((1,), (1,)), ((), ())), preferred_element_type=jnp.float32)


def standardized(values):
    centre = values - jnp.mean(values, -1, keepdims=True)
    inverse = lax.rsqrt(jnp.mean(centre * centre, -1, keepdims=True) + EPSILON)
    return centre * inverse, inverse


def norm_step_back(delta, values, gain_row):
    standard, inverse = standardized(values)
    scaled = delta * gain_row
    moved = inverse * (
        scaled - jnp.mean(scaled, -1, keepdims=True) - standard * jnp.mean(scaled * standard, -1, keepdims=True)
    )
    return moved, jnp.sum(delta * standard, 0, keepdims=True), jnp.sum(delta, 0, keepdims=True)


def half_mask(half):
    lanes = lax.broadcasted_iota(jnp.int32, (1, 128), 1)
    return (lanes < 64) if half == 0 else (lanes >= 64)


def attention_forward(m, length):
    rows = m.qkv.shape[0]
    width = m.att.shape[1]

    def pair(p, carry):
        at = pl.multiple_of(p * 128, 128)
        q2 = m.qkv[:, pl.ds(at, 128)]
        k2 = m.qkv[:, pl.ds(pl.multiple_of(width + at, 128), 128)]
        v2 = m.qkv[:, pl.ds(pl.multiple_of(2 * width + at, 128), 128)]
        v_turned = v2.T
        parts = []
        for half in range(2):
            kh = jnp.where(half_mask(half), k2, jnp.zeros_like(k2))
            top = matmul_turned(kh[:KEY_SPLIT], q2)
            low = matmul_turned(kh[KEY_SPLIT:], q2)
            key_row = KEY_SPLIT + lax.broadcasted_iota(jnp.int32, low.shape, 0)
            low = jnp.where(key_row < length, low, -1e30)
            peak = jnp.maximum(jnp.max(top, 0, keepdims=True), jnp.max(low, 0, keepdims=True))
            top = jnp.exp(top - peak)
            low = jnp.exp(low - peak)
            over = 1.0 / (jnp.sum(top, 0, keepdims=True) + jnp.sum(low, 0, keepdims=True))
            probs = jnp.concatenate([(top * over).astype(jnp.bfloat16), (low * over).astype(jnp.bfloat16)], axis=0)
            m.probs[2 * p + half] = probs
            parts.append(matmul(v_turned[64 * half : 64 * half + 64], probs))
        turned = jnp.concatenate(parts, axis=0)
        m.att_turned[pl.ds(at, 128), :] = turned.astype(jnp.bfloat16)
        m.att[:, pl.ds(at, 128)] = turned.T.astype(jnp.bfloat16)
        return carry

    lax.fori_loop(0, width // 128, pair, 0, unroll=3)


def attention_back(m):
    width = m.att.shape[1]

    def pair(p, carry):
        at = pl.multiple_of(p * 128, 128)
        k_at = pl.ds(pl.multiple_of(width + at, 128), 128)
        v_at = pl.ds(pl.multiple_of(2 * width + at, 128), 128)
        q2 = m.qkv[:, pl.ds(at, 128)]
        k2 = m.qkv[:, k_at]
        v2 = m.qkv[:, v_at]
        d2 = m.att_delta[:, pl.ds(at, 128)]
        d_turned = d2.T
        k_turned = k2.T
        product = d_turned.astype(jnp.float32) * m.att_turned[pl.ds(at, 128), :].astype(jnp.float32)
        values, keys, queries = [], [], []
        for half in range(2):
            vh = jnp.where(half_mask(half), v2, jnp.zeros_like(v2))
            probs = m.probs[2 * p + half]
            inner = jnp.sum(product[64 * half : 64 * half + 64], 0, keepdims=True)
            score = (probs.astype(jnp.float32) * (matmul(vh, d_turned) - inner)).astype(jnp.bfloat16)
            values.append(matmul(probs, d2))
            keys.append(matmul(score, q2))
            queries.append(matmul(k_turned[64 * half : 64 * half + 64], score))
        dq = (jnp.concatenate(queries, axis=0).T * HEAD_DIM ** (-0.5)).astype(jnp.bfloat16)
        dk = jnp.where(half_mask(0), keys[0], keys[1]).astype(jnp.bfloat16)
        dv = jnp.where(half_mask(0), values[0], values[1]).astype(jnp.bfloat16)
        m.mixed[:, pl.ds(at, 128)] = dq
        m.mixed[:, k_at] = dk
        m.mixed[:, v_at] = dv
        m.sums[2:3, pl.ds(at, 128)] += jnp.sum(dq.astype(jnp.float32), 0, keepdims=True)
        m.sums[3:4, pl.ds(at, 128)] += jnp.sum(dv.astype(jnp.float32), 0, keepdims=True)
        return carry

    lax.fori_loop(0, width // 128, pair, 0, unroll=3)


def forward_front(m, x_ref, length):
    x = x_ref[...].astype(jnp.float32)
    standard, unused = standardized(x)
    m.n1[...] = (standard * m.gain[0:1] + m.shift[0:1]).astype(jnp.bfloat16)
    width = x.shape[1]
    m.need(m.qkv_w)
    n1 = m.n1[...]
    for part in range(3):
        value = matmul(n1, m.qkv_w[:, part * width : (part + 1) * width])
        if part == 0:
            value = (value + m.qv[0:1]).astype(jnp.bfloat16) * jnp.bfloat16(HEAD_DIM ** (-0.5))
        elif part == 2:
            value = value + m.qv[1:2]
        m.qkv[:, part * width : (part + 1) * width] = value.astype(jnp.bfloat16)
    attention_forward(m, length)
    m.need(m.out_w)
    middle = x_ref[...].astype(jnp.float32) + matmul(m.att[...], m.out_w[...]) + m.proj[0:1]
    m.middle[...] = middle
    standard, unused = standardized(middle)
    m.n2[...] = (standard * m.gain[1:2] + m.shift[1:2]).astype(jnp.bfloat16)


def back_tail(m, x_ref, g_ref, n2_delta, keep):
    middle_part, gain, shift = norm_step_back(n2_delta, m.middle[...], m.gain[1:2])
    m.sums[6:7] += gain
    m.sums[8:9] += shift
    middle_delta = g_ref[...].astype(jnp.float32) + middle_part
    proj_delta = middle_delta.astype(jnp.bfloat16)
    m.sums[4:5] += jnp.sum(proj_delta.astype(jnp.float32), 0, keepdims=True)
    m.proj_delta[...] = proj_delta
    m.middle_delta[...] = middle_delta
    m.att_delta[...] = matmul_turned(proj_delta, m.out_w[...]).astype(jnp.bfloat16)
    attention_back(m)
    width = m.att.shape[1]
    total = None
    for part in range(3):
        columns = slice(part * width, (part + 1) * width)
        piece = matmul_turned(m.mixed[:, columns], m.qkv_w[:, columns])
        total = piece if total is None else total + piece
    input_part, gain, shift = norm_step_back(total, x_ref[...].astype(jnp.float32), m.gain[0:1])
    m.sums[5:6] += gain
    m.sums[7:8] += shift
    keep(m.middle_delta[...] + input_part)


def forward_expert(m, slot, begin, end):
    steps = m.up_w.shape[2] // CHUNK

    def step(j, carry):
        columns = pl.ds(pl.multiple_of(j * CHUNK, CHUNK), CHUNK)
        hidden = matmul(m.n2[begin:end], m.up_w[slot, :, columns]) + m.up_b[slot : slot + 1, columns]
        below, bell = normal_parts(hidden)
        active = (hidden * below).astype(jnp.bfloat16)
        m.active[begin:end, columns] = active
        m.slope[begin:end, columns] = (below + hidden * bell).astype(jnp.bfloat16)
        m.total[begin:end] += matmul(active, m.down_w[slot, columns, :])
        return carry

    m.total[begin:end] = m.middle[begin:end] + m.down_b[slot : slot + 1]
    lax.fori_loop(0, steps, step, 0, unroll=True)


def back_expert(m, g_ref, slot, begin, end):
    steps = m.up_w.shape[2] // CHUNK
    m.total[begin:end] = jnp.zeros((end - begin, m.total.shape[1]), jnp.float32)
    m.sums[slot : slot + 1] += jnp.sum(g_ref[begin:end].astype(jnp.float32), 0, keepdims=True)

    def step(j, carry):
        columns = pl.ds(pl.multiple_of(j * CHUNK, CHUNK), CHUNK)
        active_delta = matmul_turned(g_ref[begin:end], m.down_w[slot, columns, :])
        hidden_delta = (active_delta * m.slope[begin:end, columns].astype(jnp.float32)).astype(jnp.bfloat16)
        m.hidden_delta[begin:end, columns] = hidden_delta
        m.sums[pl.ds(9 + 4 * slot + j, 1)] += jnp.sum(hidden_delta.astype(jnp.float32), 0, keepdims=True)
        m.total[begin:end] += matmul_turned(hidden_delta, m.up_w[slot, :, columns])
        return carry

    lax.fori_loop(0, steps, step, 0, unroll=True)


def both_expert(m, g_ref):
    steps = m.up_w.shape[2] // CHUNK
    m.total[...] = jnp.zeros(m.total.shape, jnp.float32)
    m.sums[0:1] += jnp.sum(g_ref[...].astype(jnp.float32), 0, keepdims=True)

    def step(j, carry):
        columns = pl.ds(pl.multiple_of(j * CHUNK, CHUNK), CHUNK)
        active_delta = matmul_turned(g_ref[...], m.down_w[0, columns, :])
        hidden = matmul(m.n2[...], m.up_w[0, :, columns]) + m.up_b[2:3, columns]
        below, bell = normal_parts(hidden)
        m.active[:, columns] = (hidden * below).astype(jnp.bfloat16)
        hidden_delta = (active_delta * (below + hidden * bell)).astype(jnp.bfloat16)
        m.hidden_delta[:, columns] = hidden_delta
        m.sums[pl.ds(9 + j, 1)] += jnp.sum(hidden_delta.astype(jnp.float32), 0, keepdims=True)
        m.total[...] += matmul_turned(hidden_delta, m.up_w[0, :, columns])
        return carry

    lax.fori_loop(0, steps, step, 0, unroll=True)


def layers_kernel(names, length, *refs):
    m = Refs()
    for name, ref in zip(names, refs):
        setattr(m, name, ref)
    items = m.tokens.shape[0]
    half = m.total.shape[1] // 2
    section = lax.axis_index("section")
    across = (1 - section, lax.axis_index("dp"))

    def send(i):
        return pltpu.make_async_remote_copy(
            src_ref=m.leaving.at[i], dst_ref=m.landed.at[i], send_sem=m.send_sem.at[i], recv_sem=m.recv_sem.at[i],
            device_id=across, device_id_type=MESH,
        )

    def send_half(i):
        return pltpu.make_async_remote_copy(
            src_ref=m.half_out.at[i], dst_ref=m.high.at[i], send_sem=m.half_send.at[i], recv_sem=m.half_recv.at[i],
            device_id=across, device_id_type=MESH,
        )

    def local(source, target, number):
        return pltpu.make_async_copy(source, target, m.copy_sem.at[number])

    def branch_copy(source, i):
        return pltpu.make_async_copy(source.at[i], m.branch.at[i], m.branch_sem.at[i])

    def weights(experts):
        found = [
            (m.qkv_w, [local(m.in_qkv.at[0], m.qkv_w, 0)]),
            (m.out_w, [local(m.in_out.at[0], m.out_w, 1)]),
            (m.up_w, []),
            (m.down_w, []),
        ]
        for slot, expert in enumerate(experts):
            found[2][1].append(local(m.in_up.at[expert], m.up_w.at[slot], 2 + slot))
            found[3][1].append(local(m.in_down.at[expert], m.down_w.at[slot], 4 + slot))
        return found

    def start_weights(found):
        copies = found[0][1] + found[1][1]
        for pair in zip(found[2][1], found[3][1]):
            copies += pair
        for copy in copies:
            copy.start()

    def needs(found, i):
        def need(ref):
            for here, copies in found:
                if here is ref:

                    @pl.when(i == 0)
                    def _():
                        for copy in copies:
                            copy.wait()

        return need

    leaving = (
        (m.n1, m.out_n1), (m.att, m.out_att), (m.n2, m.out_n2), (m.active, m.out_active), (m.qkv, m.kept_qkv),
        (m.probs, m.kept_probs), (m.att_turned, m.kept_turned), (m.middle, m.kept_middle), (m.slope, m.kept_slope),
        (m.mixed, m.out_mixed), (m.proj_delta, m.out_proj), (m.hidden_delta, m.out_hidden),
    )
    n1, att, n2, active, qkv, probs, turned, middle, slope, mixed, proj, hidden = range(len(leaving))

    def puts(i):
        return lambda number: local(leaving[number][0], leaving[number][1].at[i], 6 + number)

    def gets(i):
        return lambda number: local(leaving[number][1].at[i], leaving[number][0], 14 + number)

    def start(copies, *which):
        for number in which:
            copies(number).start()

    def wait(copies, *which):
        for number in which:
            copies(number).wait()

    def settle(i, *which):
        @pl.when(i > 0)
        def _():
            wait(puts(i), *which)

    def first_front(found, i, carry):
        m.need = needs(found, i)
        settle(i, n1, att, n2, qkv, probs, turned, middle)
        forward_front(m, m.tokens.at[i], length)
        start(puts(i), n1, att, n2, qkv, probs, turned, middle)
        settle(i, active, slope)
        m.need(m.up_w)
        m.need(m.down_w)
        forward_expert(m, 1, 0, TEXT)
        forward_expert(m, 0, TEXT, ROWS)
        m.leaving[i] = m.total[...].astype(jnp.bfloat16)
        send(i).start()
        start(puts(i), active, slope)
        return carry

    def first_back(i, carry):
        start(gets(i), slope, middle, turned, qkv, probs)

        @pl.when(i > 0)
        def _():
            send(i - 1).wait_send()

        send(i).wait_recv()
        branch_copy(m.landed, i).start()
        settle(i, hidden)
        wait(gets(i), slope)
        gradient = m.landed.at[i]
        back_expert(m, gradient, 1, 0, TEXT)
        back_expert(m, gradient, 0, TEXT, ROWS)
        start(puts(i), hidden)
        settle(i, mixed, proj)
        wait(gets(i), middle, turned, qkv, probs)

        def keep(value):
            m.low[i] = value[:, :half]
            m.half_out[i] = value[:, half:].astype(jnp.bfloat16)

        back_tail(m, m.tokens.at[i], gradient, m.total[...], keep)
        send_half(i).start()
        start(puts(i), mixed, proj)
        branch_copy(m.landed, i).wait()
        return carry

    def second_both(found, i, carry):
        m.need = needs(found, i)
        branch_copy(m.targets, i).start()
        send(i).wait_recv()
        settle(i, n1, att, n2)
        arrived = m.landed.at[i]
        forward_front(m, arrived, length)
        start(puts(i), n1, att, n2)
        settle(i, active, hidden)
        m.need(m.up_w)
        m.need(m.down_w)
        gradient = m.targets.at[i]
        both_expert(m, gradient)
        start(puts(i), active, hidden)
        settle(i, mixed, proj)

        def keep(value):
            m.leaving[i] = value.astype(jnp.bfloat16)

        back_tail(m, arrived, gradient, m.total[...], keep)
        send(i).start()
        start(puts(i), mixed, proj)
        branch_copy(m.targets, i).wait()
        return carry

    m.sums[...] = jnp.zeros(m.sums.shape, jnp.float32)
    barrier = pltpu.get_barrier_semaphore()
    pl.semaphore_signal(barrier, inc=1, device_id=across, device_id_type=MESH)

    @pl.when(section == 0)
    def _():
        found = weights((0, 1))
        start_weights(found)
        pl.semaphore_wait(barrier, 1)
        lax.fori_loop(0, items, functools.partial(first_front, found), 0)
        wait(puts(0), n1, att, n2, active, qkv, probs, turned, middle, slope)
        lax.fori_loop(0, items, first_back, 0)
        wait(puts(0), mixed, proj, hidden)
        send(items - 1).wait_send()
        for i in range(items):
            send_half(i).wait_send()

    @pl.when(section == 1)
    def _():
        found = weights((2,))
        start_weights(found)
        pl.semaphore_wait(barrier, 1)
        lax.fori_loop(0, items, functools.partial(second_both, found), 0)
        wait(puts(0), n1, att, n2, active, mixed, proj, hidden)
        for i in range(items):
            send(i).wait_send()
            send_half(i).wait_recv()


def both_layers(tokens, targets, qkv_weight, out_weight, up_table, down_table, qv, proj, gain, shift, up_b, down_b, length):
    items, rows, width = tokens.shape
    ff = up_b.shape[1]
    heads = width // HEAD_DIM
    bf16, f32 = jnp.bfloat16, jnp.float32
    dma = pltpu.SemaphoreType.DMA
    vmem, anywhere = pl.BlockSpec(memory_space=pltpu.VMEM), pl.BlockSpec(memory_space=pl.ANY)
    ins = dict(
        tokens=(tokens, vmem), targets=(targets, vmem), in_qkv=(qkv_weight, anywhere), in_out=(out_weight, anywhere),
        in_up=(up_table, anywhere), in_down=(down_table, anywhere), qv=(qv, vmem), proj=(proj, vmem), gain=(gain, vmem),
        shift=(shift, vmem), up_b=(up_b, vmem), down_b=(down_b, vmem),
    )

    def made(*shape, kind=bf16, spec=anywhere):
        return jax.ShapeDtypeStruct((items,) + shape, kind), spec

    outs = dict(
        out_n1=made(rows, width), out_att=made(rows, width), out_n2=made(rows, width), out_active=made(rows, ff),
        out_mixed=made(rows, 3 * width), out_proj=made(rows, width), out_hidden=made(rows, ff), branch=made(rows, width),
        kept_qkv=made(rows, 3 * width), kept_probs=made(heads, rows, rows), kept_turned=made(width, rows),
        kept_middle=made(rows, width, kind=f32), kept_slope=made(rows, ff),
        low=made(rows, width // 2, kind=f32, spec=vmem), high=made(rows, width // 2),
        sums=(jax.ShapeDtypeStruct((24, width), f32), vmem),
    )
    low_row, wide_row = ((rows, width), bf16), ((rows, ff), bf16)
    buffers = dict(
        qkv_w=((width, 3 * width), bf16), out_w=((width, width), bf16), up_w=((2, width, ff), bf16),
        down_w=((2, ff, width), bf16), n1=low_row, att=low_row, n2=low_row, active=wide_row,
        qkv=((rows, 3 * width), bf16), probs=((heads, rows, rows), bf16), att_turned=((width, rows), bf16),
        middle=((rows, width), f32), slope=wide_row, total=((rows, width), f32), mixed=((rows, 3 * width), bf16),
        proj_delta=low_row, hidden_delta=wide_row, att_delta=low_row, middle_delta=((rows, width), f32),
        leaving=((items, rows, width), bf16), landed=((items, rows, width), bf16),
        half_out=((items, rows, width // 2), bf16),
    )
    semaphores = dict(
        copy_sem=dma((23,)), branch_sem=dma((items,)), send_sem=dma((items,)), recv_sem=dma((items,)),
        half_send=dma((items,)), half_recv=dma((items,)),
    )
    names = list(ins) + list(outs) + list(buffers) + list(semaphores)
    results = pl.pallas_call(
        functools.partial(layers_kernel, names, length),
        out_shape=[shape for shape, spec in outs.values()],
        in_specs=[spec for value, spec in ins.values()],
        out_specs=[spec for shape, spec in outs.values()],
        scratch_shapes=[pltpu.VMEM(*kind) for kind in buffers.values()] + list(semaphores.values()),
        compiler_params=pltpu.CompilerParams(
            collective_id=1, has_side_effects=True, vmem_limit_bytes=60 * 1024 * 1024
        ),
        cost_estimate=pl.CostEstimate(flops=40_000_000_000, bytes_accessed=100_000_000, transcendentals=0),
    )(*[value for value, spec in ins.values()])
    m = Refs()
    for name, result in zip(outs, results):
        setattr(m, name, result)
    return m


def text_first(values):
    pad = jnp.zeros((values.shape[0], ROWS - values.shape[1]) + values.shape[2:], values.dtype)
    return jnp.concatenate([values[:, PATCHES:], values[:, :PATCHES], pad], axis=1)


def patches_first(values, length):
    return jnp.concatenate([values[:, TEXT:length], values[:, :TEXT]], axis=1)


def small_outs(own, other, is_first):
    first = jnp.where(is_first, own, other)
    second = jnp.where(is_first, other, own)
    me = lax.axis_index("dp")

    def columns(rows):
        wide = rows.shape[-1] // lax.axis_size("dp")
        return lax.dynamic_slice_in_dim(rows, me * wide, wide, rows.ndim - 1)

    down = columns(jnp.concatenate([first[:2], second[:1]]))
    up = columns(jnp.concatenate([first[9:17].reshape(2, -1), second[9:13].reshape(1, -1)]))
    own = columns(own[2:9])
    return own[0:2], own[2:3], own[3:5], own[5:7], up, down


def flat(value):
    return value.reshape((-1, value.shape[-1]))


def left_parts(m, is_first):
    n1, att, n2, branch_delta = (flat(part) for part in (m.out_n1, m.out_att, m.out_n2, m.branch))
    text = (jnp.arange(n1.shape[0]) % ROWS < TEXT)[:, None]
    vision = jnp.logical_not(text & is_first).astype(jnp.bfloat16)
    text = text.astype(jnp.bfloat16)
    return [
        piece.T for piece in (n2 * vision, branch_delta * vision, n2 * text, branch_delta * text, n1, att)
    ]


def large_grads(m, is_first):
    up, down, qkv, out, smalls = summed_grads(
        flat(m.out_n1), flat(m.out_att), flat(m.out_n2), flat(m.branch), flat(m.out_hidden), flat(m.out_active),
        flat(m.out_mixed), flat(m.out_proj), m.sums,
    )
    qkv, out, up, down = (part.astype(jnp.float32) for part in (qkv, out, up, down))
    return qkv, out, up, down, smalls[0], smalls[1]


def large_grads_plain(m, is_first):
    lefts = left_parts(m, is_first)
    hidden_delta, active = flat(m.out_hidden), flat(m.out_active)

    def total_of(left, right):
        product = jnp.dot(left, right, preferred_element_type=jnp.float32).astype(jnp.bfloat16)
        return lax.psum_scatter(product, "dp", scatter_dimension=1, tiled=True)

    def table(vision_part, text_part):
        def swapped(part):
            return lax.psum(part, "section").astype(jnp.float32)

        return jnp.stack(
            [
                swapped(jnp.where(is_first, vision_part, 0)),
                swapped(jnp.where(is_first, text_part, 0)),
                swapped(jnp.where(is_first, 0, vision_part)),
            ]
        )

    up = table(total_of(lefts[0], hidden_delta), total_of(lefts[2], hidden_delta))
    down = table(total_of(lefts[1], active), total_of(lefts[3], active))
    small = lax.psum(m.sums, "dp")
    return (
        total_of(lefts[4], flat(m.out_mixed)).astype(jnp.float32),
        total_of(lefts[5], flat(m.out_proj)).astype(jnp.float32),
        up,
        down.transpose(0, 2, 1),
        small,
        lax.ppermute(small, "section", [(0, 1), (1, 0)]),
    )


def shards(
    tokens, cotangent, patch_mask, text_mask, qkv_weight, qv_bias, out_weight, out_bias, norm_gain, norm_bias,
    up_table, up_bias, down_table, down_bias,
):
    is_first = lax.axis_index("section") == 0
    length = tokens.shape[1]
    positions = jnp.arange(length, dtype=jnp.int32)
    chosen = jnp.any(positions[None, :, None] == patch_mask[:, None, :], axis=2) | jnp.any(
        positions[None, :, None] == text_mask[:, None, :], axis=2
    )
    targets = text_first(cotangent * chosen.astype(jnp.bfloat16)[..., None])
    m = both_layers(
        text_first(tokens), targets, qkv_weight, out_weight, up_table, down_table, qv_bias[0], out_bias, norm_gain[0],
        norm_bias[0], up_bias, down_bias, length,
    )
    grads = large_grads if lax.axis_size("dp") == 16 else large_grads_plain
    qkv, out, up, down, own, other = grads(m, is_first)
    qv_part, proj_part, gain_part, shift_part, up_part, down_part = small_outs(own, other, is_first)
    input_grad = patches_first(jnp.where(is_first, m.low, m.high.astype(jnp.float32)), length)
    return (
        input_grad, qkv[None], qv_part[None], out[None], proj_part, gain_part[None], shift_part[None],
        up, up_part, down, down_part,
    )


def solution(mesh):
    items, layers = P("dp"), P("section")
    return jax.shard_map(
        shards,
        mesh=mesh,
        in_specs=(items,) * 4 + (layers,) * 6 + (P(),) * 4,
        out_specs=(
            P("dp", None, "section"), P("section", None, "dp"), P("section", None, "dp"), P("section", None, "dp"),
            P("section", "dp"), P("section", None, "dp"), P("section", None, "dp"),
            P(None, None, "dp"), P(None, "dp"), P(None, "dp", None), P(None, "dp"),
        ),
        check_vma=False,
    )
```

```python
import functools

import jax
import jax.numpy as jnp
from jax import lax
from jax.experimental import pallas as pl
from jax.experimental.pallas import tpu as pltpu
from jax.sharding import PartitionSpec as P

HEAD_DIM = 64
PATCHES = 197
EPSILON = 1e-05
BLOCK = 384
WINDOW = 640
RING = 3
TEXT = 64
ROWS = 272
MESH = pl.DeviceIdType.MESH


class Refs:
    pass


def sum_kernel(names, *refs):
    m = Refs()
    for name, ref in zip(names, refs):
        setattr(m, name, ref)
    section = lax.axis_index("section")
    me = lax.axis_index("dp")
    z, y, core = me // 4, (me // 2) % 2, me % 2
    peer = (section, me + 1 - 2 * core)
    beside = (section, me + 2 - 4 * y)
    right = (section, me + 4)
    left = (section, me - 4)
    across = (1 - section, me)
    on_first = section == 0
    units = jnp.where(on_first, 20, 16)
    computed = jnp.where(on_first, 20, 12)

    class Unit:
        def __init__(self, u):
            self.u = u
            self.group = jnp.where(on_first, u // 5, u // 4)
            turn = jnp.where(on_first, u % 5, u % 4)
            self.z_first = turn == 0
            self.handed_on = on_first & (turn == 1)
            self.j = jnp.maximum(3 * self.group + turn - jnp.where(on_first, 2, 1), 0)
            third = self.j // 4
            later = jnp.where(on_first, jnp.where(third == 1, 2, 4), jnp.where(third == 1, 4, 3))
            kind = jnp.where(third == 0, 1, later)
            self.kind = jnp.where(self.z_first, 0, jnp.where(self.handed_on, 3, kind))
            self.handed_in = jnp.logical_not(on_first) & (self.kind == 3)
            self.y_first = jnp.logical_not(self.z_first | self.handed_on)
            o = jnp.where(self.z_first | self.handed_on, self.group, self.j % 4)
            self.o = o
            self.plane = jnp.where(o == 0, 0, jnp.where(o == 1, 3, o - 1))
            self.y_slot = jnp.where(self.z_first, 12 + self.group, self.j)
            self.uses_text = jnp.logical_not(on_first) | (self.kind > 1)
            self.uses_patches = jnp.logical_not(on_first) | (self.kind < 2) | (self.kind == 4)
            self.order = u - jnp.where((section == 1) & (u > 11), 1, 0)

    def remote(src, dst, send, recv, device):
        return pltpu.make_async_remote_copy(
            src_ref=src, dst_ref=dst, send_sem=send, recv_sem=recv, device_id=device, device_id_type=MESH
        )

    def core_copy(n, b):
        slot = n.order % RING
        return remote(m.xs.at[slot, b], m.xr.at[slot, b], m.core_send.at[n.order, b], m.core_recv.at[n.order, b], peer)

    def y_copy(n):
        return remote(m.part.at[n.u, 0], m.yr.at[n.y_slot], m.y_send.at[n.y_slot], m.y_recv.at[n.y_slot], beside)

    def right_copy(n):
        return remote(m.part.at[n.u, 1], m.zr.at[n.j], m.right_send.at[n.j], m.right_recv.at[n.j], right)

    def left_copy(n):
        return remote(m.part.at[n.u, 1], m.zl.at[n.j], m.left_send.at[n.j], m.left_recv.at[n.j], left)

    def right_pair(n):
        g = n.group
        return remote(m.part.at[n.u], m.wr.at[g], m.right_send.at[12 + g], m.right_recv.at[12 + g], right)

    def left_pair(n):
        g = n.group
        return remote(m.part.at[n.u], m.wl.at[g], m.left_send.at[12 + g], m.left_recv.at[12 + g], left)

    def over_copy(o, source, target):
        return remote(m.part.at[source], m.part.at[target], m.over_send.at[o], m.over_recv.at[o], across)

    def over_target(o):
        return jnp.where(o == 0, 11, 12 + o)

    def peer_copy(k):
        return remote(m.fin.at[0, core, k], m.fin.at[0, core, k], m.peer_send.at[k], m.peer_recv.at[k], peer)

    def cross_copy(k):
        return remote(m.fin.at[0, core, k], m.fin.at[1, core, k], m.cross_send.at[k], m.cross_recv.at[k], across)

    def hand_copy(k):
        return remote(m.fin.at[1, core, k], m.fin.at[1, core, k], m.hand_send.at[k], m.hand_recv.at[k], peer)

    def mixed_start(plane):
        return pl.multiple_of((9 * plane // 2) * 128, 128)

    def proj_start(plane):
        return pl.multiple_of((3 * plane // 2) * 128, 128)

    def tile_copies(n):
        k = n.kind
        slot = n.order % 2
        plain = pl.multiple_of(n.plane * 2 * BLOCK, 128)
        wide = pl.ds(plain, 2 * BLOCK)
        cases = []
        for ref, number, here, source, target in (
            (m.hidden, 0, (k == 0) | (k == 2), wide, slice(0, 2 * BLOCK)),
            (m.active, 0, (k == 1) | (k == 3), wide, slice(0, 2 * BLOCK)),
            (m.mixed, 0, k == 4, pl.ds(mixed_start(n.plane), WINDOW), slice(0, WINDOW)),
            (m.proj, 1, k == 4, pl.ds(proj_start(n.plane), 256), slice(WINDOW, WINDOW + 256)),
        ):
            copy = pltpu.make_async_copy(
                ref.at[:, :TEXT, source], m.text_tile.at[slot, :, :, target], m.text_sem.at[slot, number]
            )
            cases.append((here & n.uses_text, copy))
            copy = pltpu.make_async_copy(
                ref.at[:, TEXT:, source], m.patch_tile.at[slot, :, :, target], m.patch_sem.at[slot, number]
            )
            cases.append((here & n.uses_patches, copy))
        return cases

    def start_tile(n):
        for here, copy in tile_copies(n):
            pl.when(here)(copy.start)

    def wait_tile(n):
        for here, copy in tile_copies(n):
            pl.when(here)(copy.wait)

    def add_into(target, source):
        target[...] = target[...] + source[...]

    def rows(half):
        return pl.ds(pl.multiple_of(half * BLOCK, BLOCK), BLOCK)

    def tile_rows(tile, slot, begin, end):
        value = tile[slot, :, :, begin:end]
        return value.reshape(-1, end - begin)

    def text_dot(index, half, slot, begin, end):
        return matmul(m.text_left[index, rows(half), :], tile_rows(m.text_tile, slot, begin, end))

    def patch_dot(index, half, slot, begin, end):
        return matmul(m.patch_left[index, rows(half), :], tile_rows(m.patch_tile, slot, begin, end))

    def both_dot(index, half, slot, begin, end):
        return patch_dot(index, half, slot, begin, end) + text_dot(index, half, slot, begin, end)

    def attention_columns(half, slot, plane):
        mixed = both_dot(2, half, slot, 0, WINDOW)
        proj = both_dot(3, half, slot, WINDOW, WINDOW + 256)
        mixed_at = 576 * plane - mixed_start(plane)
        proj_at = 192 * plane - proj_start(plane)
        lanes = lax.broadcasted_iota(jnp.int32, (1, 128), 1)
        found = []
        for side in range(2):
            own = pltpu.roll(mixed, (WINDOW - mixed_at - 288 * side) % WINDOW, 1)
            last = pltpu.roll(proj, (256 + 32 - proj_at - 96 * side) % 256, 1)
            found.append((own[:, :256], jnp.where(lanes < 32, own[:, 256:384], last[:, :128])))
        return found

    def compute(n):
        k = n.kind
        slot = n.order % RING

        @pl.when(n.order >= RING)
        def _():
            back = Unit(n.u - RING - jnp.where((section == 1) & (n.u == 12), 1, 0))
            core_copy(back, 0).wait_send()
            core_copy(back, 1).wait_send()
            pl.semaphore_wait(m.credit, 1)

        @pl.when(n.order + 1 < computed)
        def _():
            start_tile(Unit(n.u + 1 + jnp.where((section == 1) & (n.u == 10), 1, 0)))

        wait_tile(n)
        tile = n.order % 2
        for part in range(2):
            half = (1 - core) if part == 0 else core
            target = m.xs.at[slot] if part == 0 else m.part.at[n.u]

            def put(value):
                for side in range(2):
                    target[jnp.where(y == side, 1, 0)] = value[:, side * BLOCK : (side + 1) * BLOCK].astype(jnp.bfloat16)

            @pl.when((k < 4) & jnp.logical_not(n.uses_text))
            def _():
                put(patch_dot(k % 2, half, tile, 0, 2 * BLOCK))

            @pl.when((k < 4) & jnp.logical_not(n.uses_patches))
            def _():
                put(text_dot(k % 2, half, tile, 0, 2 * BLOCK))

            @pl.when((k < 4) & n.uses_text & n.uses_patches)
            def _():
                put(both_dot(k % 2, half, tile, 0, 2 * BLOCK))

            @pl.when(k == 4)
            def _():
                for side, (front, back) in enumerate(attention_columns(half, tile, n.plane)):
                    at = jnp.where(y == side, 1, 0)
                    target[at, :, :256] = front.astype(jnp.bfloat16)
                    target[at, :, 256:] = back.astype(jnp.bfloat16)

            if part == 0:
                core_copy(n, 0).start()
                core_copy(n, 1).start()

    def join_core(n):
        slot = n.order % RING

        @pl.when(n.handed_in)
        def _():
            over_copy(n.o, 0, n.u).wait_recv()

        @pl.when(jnp.logical_not(n.handed_in))
        def _():
            core_copy(n, 0).wait_recv()
            add_into(m.part.at[n.u, 0], m.xr.at[slot, 0])

        pl.when(n.y_first)(lambda: y_copy(n).start())

        @pl.when(jnp.logical_not(n.handed_in))
        def _():
            core_copy(n, 1).wait_recv()
            add_into(m.part.at[n.u, 1], m.xr.at[slot, 1])

            @pl.when(n.order + RING < computed)
            def _():
                pl.semaphore_signal(m.credit, inc=1, device_id=peer, device_id_type=MESH)

        pl.when(n.handed_on)(lambda: over_copy(n.o, n.u, over_target(n.o)).start())

    def join_y(n):
        y_copy(n).wait_recv()
        add_into(m.part.at[n.u, 1], m.yr.at[n.y_slot])

    def take(n, one, pair, single_from, pair_from):
        @pl.when(n.y_first)
        def _():
            one(n).wait_recv()
            add_into(m.part.at[n.u, 1], single_from.at[n.j])

        @pl.when(n.z_first)
        def _():
            pair(n).wait_recv()
            add_into(m.part.at[n.u], pair_from.at[n.group])

    def take_right(n):
        take(n, right_copy, right_pair, m.zr, m.wr)

    def take_left(n):
        take(n, left_copy, left_pair, m.zl, m.wl)

    def pass_right(n):
        pl.when(z > 0)(lambda: take_right(n))
        pl.when(n.y_first)(lambda: right_copy(n).start())
        pl.when(n.z_first)(lambda: right_pair(n).start())

    def pass_left(n):
        pl.when(z < 3)(lambda: take_left(n))
        pl.when(n.y_first)(lambda: left_copy(n).start())
        pl.when(n.z_first)(lambda: left_pair(n).start())

    def give(n):
        k = n.kind
        m.fin[0, core, k] = m.part[n.u, 1]
        peer_copy(k).start()
        pl.when(k < 4)(lambda: cross_copy(k).start())

    def meet(n):
        pl.when(z > 0)(lambda: take_right(n))
        pl.when(z < 3)(lambda: take_left(n))
        pl.when(n.z_first)(lambda: y_copy(n).start())
        pl.when(n.y_first)(lambda: give(n))

    def meet_late(n):
        join_y(n)
        give(n)

    flips = (peer, beside, (section, me + 4 - 8 * (z % 2)), (section, me + 8 - 16 * (z // 2)), across)

    def small_copy(j):
        return remote(m.small_sum.at[j], m.small_in.at[j], m.small_send.at[j], m.small_recv.at[j], flips[j])

    def small_step(j):
        if j == 0:
            m.small_sum[0] = m.small[...]
        else:
            small_copy(j - 1).wait_recv()
            if j == 5:
                m.small_out[0] = m.small_sum[4]
                m.small_out[1] = m.small_in[4]
            else:
                m.small_sum[j] = m.small_sum[j - 1] + m.small_in[j - 1]
        if j < 5:
            small_copy(j).start()

    stages = (m.n2, m.branch, m.n1, m.att)

    def stage_copy(number):
        return pltpu.make_async_copy(stages[number], m.stage, m.stage_sem.at[0])

    def prepare(number):
        stage_copy(number).wait()

        def part(c, carry):
            at = pl.ds(pl.multiple_of(c * 128, 128), 128)
            m.text_left[number, at, :] = m.stage[:, :TEXT, at].reshape(-1, 128).T
            m.patch_left[number, at, :] = m.stage[:, TEXT:, at].reshape(-1, 128).T
            return carry

        lax.fori_loop(0, m.stage.shape[2] // 128, part, 0)
        if number < 3:
            stage_copy(number + 1).start()

    barrier = pltpu.get_barrier_semaphore()
    for device in (peer, beside, across, flips[3]):
        pl.semaphore_signal(barrier, inc=1, device_id=device, device_id_type=MESH)

    @pl.when(z < 3)
    def _():
        pl.semaphore_signal(barrier, inc=1, device_id=right, device_id_type=MESH)

    @pl.when(z > 0)
    def _():
        pl.semaphore_signal(barrier, inc=1, device_id=left, device_id_type=MESH)

    stage_copy(0).start()
    start_tile(Unit(jnp.int32(0)))
    prepare(0)
    pl.semaphore_wait(barrier, 4 + jnp.where(z < 3, 1, 0) + jnp.where(z > 0, 1, 0))

    def at_unit(u, condition, action):
        n = Unit(jnp.maximum(u, 0))

        @pl.when((u >= 0) & (u < units) & condition(n))
        def _():
            action(n)

    def in_flow(n):
        return jnp.logical_not(n.handed_on)

    def step(i, carry):
        at_unit(i, lambda n: jnp.logical_not(n.handed_in), compute)
        for number in range(3):
            pl.when(i == number)(functools.partial(prepare, number + 1))
        at_unit(i - 1, lambda n: True, join_core)
        at_unit(i - 4, lambda n: n.y_first, join_y)
        at_unit(i - 4 - 3 * z, lambda n: in_flow(n) & (n.plane > z), pass_right)
        at_unit(i - 13 + 3 * z, lambda n: in_flow(n) & (n.plane < z), pass_left)
        at_unit(i - 14, lambda n: in_flow(n) & (n.plane == z), meet)
        at_unit(i - 16, lambda n: n.z_first & (n.plane == z), meet_late)
        for j in range(6):
            pl.when(i == 3 + j)(functools.partial(small_step, j))
        return carry

    lax.fori_loop(0, units + 16, step, 0)

    def third_kind(k):
        return jnp.where(k == 2, 2 + section, k)

    def their_kind(k):
        return jnp.where(k == 2, 3 - section, k)

    for k in range(3):
        cross_copy(their_kind(jnp.int32(k))).wait_recv()
        hand_copy(their_kind(jnp.int32(k))).start()

    def settle(u, carry):
        n = Unit(u)

        @pl.when(jnp.logical_not(n.handed_in) & (n.order >= computed - RING))
        def _():
            core_copy(n, 0).wait_send()
            core_copy(n, 1).wait_send()

        pl.when(n.handed_on)(lambda: over_copy(n.o, n.u, over_target(n.o)).wait_send())
        pl.when(n.y_first | (n.z_first & (n.plane == z)))(lambda: y_copy(n).wait_send())
        pl.when(n.y_first & (n.plane > z))(lambda: right_copy(n).wait_send())
        pl.when(n.z_first & (n.plane > z))(lambda: right_pair(n).wait_send())
        pl.when(n.y_first & (n.plane < z))(lambda: left_copy(n).wait_send())
        pl.when(n.z_first & (n.plane < z))(lambda: left_pair(n).wait_send())
        return carry

    lax.fori_loop(0, units, settle, 0)
    for j in range(5):
        small_copy(j).wait_send()
    for k in range(3):
        peer_copy(third_kind(jnp.int32(k))).wait()
        cross_copy(third_kind(jnp.int32(k))).wait_send()
        hand_copy(their_kind(jnp.int32(k))).wait()
    peer_copy(4).wait()

    def write(c):
        def columns(side, half, k, begin, wide):
            return m.fin[side, half, k, :, begin + c * wide : begin + (c + 1) * wide]

        first, second = section, 1 - section
        for half in range(2):
            at = slice(half * BLOCK, (half + 1) * BLOCK)
            m.qkv_out[at, :] = columns(0, half, 4, 0, 144)
            m.out_out[at, :] = columns(0, half, 4, 288, 48)
            for expert, side, k in ((0, first, 0), (1, first, 2), (2, second, 0)):
                m.up_out[expert, at, :] = columns(side, half, k, 0, 192)
            for expert, side, k in ((0, first, 1), (1, second, 3), (2, second, 1)):
                m.down_out[expert, :, at] = columns(side, half, k, 0, 192).T

    for c in range(2):
        pl.when(core == c)(functools.partial(write, c))


def summed_grads(n1, att, n2, branch, hidden, active, mixed, proj, small):
    dma = pltpu.SemaphoreType.DMA
    items, depth, width = n1.shape
    bf16, f32 = jnp.bfloat16, jnp.float32
    tile = (BLOCK, BLOCK)
    vmem, anywhere = pl.BlockSpec(memory_space=pltpu.VMEM), pl.BlockSpec(memory_space=pl.ANY)
    ins = dict(n1=n1, att=att, n2=n2, branch=branch, hidden=hidden, active=active, mixed=mixed, proj=proj, small=small)
    outs = dict(
        up_out=((3, width, 192), bf16), down_out=((3, 192, width), bf16), qkv_out=((width, 144), bf16),
        out_out=((width, 48), bf16), small_out=((2,) + small.shape, f32),
    )
    buffers = dict(
        text_tile=((2, items, TEXT, WINDOW + 256), bf16), patch_tile=((2, items, depth - TEXT, WINDOW + 256), bf16), part=((20, 2) + tile, bf16), xs=((RING, 2) + tile, bf16),
        xr=((RING, 2) + tile, bf16), yr=((16,) + tile, bf16), zr=((12,) + tile, bf16), zl=((12,) + tile, bf16),
        wr=((4, 2) + tile, bf16), wl=((4, 2) + tile, bf16), fin=((2, 2, 5) + tile, bf16),
        text_left=((4, width, items * TEXT), bf16), patch_left=((4, width, items * (depth - TEXT)), bf16), stage=((items, depth, width), bf16), small_sum=((5,) + small.shape, f32),
        small_in=((5,) + small.shape, f32),
    )
    semaphores = dict(
        small_send=dma((5,)), small_recv=dma((5,)), text_sem=dma((2, 2)), patch_sem=dma((2, 2)), stage_sem=dma((1,)), core_send=dma((20, 2)),
        core_recv=dma((20, 2)), y_send=dma((16,)), y_recv=dma((16,)), right_send=dma((16,)), right_recv=dma((16,)),
        left_send=dma((16,)), left_recv=dma((16,)), over_send=dma((4,)), over_recv=dma((4,)), peer_send=dma((5,)),
        peer_recv=dma((5,)), cross_send=dma((5,)), cross_recv=dma((5,)), hand_send=dma((5,)), hand_recv=dma((5,)),
        credit=pltpu.SemaphoreType.REGULAR,
    )
    names = list(ins) + list(outs) + list(buffers) + list(semaphores)
    return pl.pallas_call(
        functools.partial(sum_kernel, names),
        out_shape=[jax.ShapeDtypeStruct(*kind) for kind in outs.values()],
        in_specs=[anywhere] * 8 + [vmem],
        out_specs=[vmem] * len(outs),
        scratch_shapes=[pltpu.VMEM(*kind) for kind in buffers.values()] + list(semaphores.values()),
        compiler_params=pltpu.CompilerParams(
            collective_id=0, has_side_effects=True, vmem_limit_bytes=60 * 1024 * 1024
        ),
        cost_estimate=pl.CostEstimate(flops=48 * 2 * 768 * 384 * items * depth, bytes_accessed=40_000_000, transcendentals=0),
    )(*ins.values())


CHUNK = 768
KEY_SPLIT = 256
TAIL = (0.319381530, -0.356563782, 1.781477937, -1.821255978, 1.330274429)
PEAK = 0.3989422804014327


def normal_parts(z):
    size = jnp.abs(z)
    scale = 1.0 + 0.2316419 * size
    t = pl.reciprocal(scale, approx=True)
    t = t * (2.0 - scale * t)
    bell = jnp.exp(-0.5 * z * z) * PEAK
    series = TAIL[4]
    for factor in TAIL[3::-1]:
        series = series * t + factor
    upper = bell * (series * t)
    return jnp.where(z >= 0, 1.0 - upper, upper), bell


def matmul(left, right):
    return jnp.dot(left, right, preferred_element_type=jnp.float32)


def matmul_turned(left, right):
    return lax.dot_general(left, right, (((1,), (1,)), ((), ())), preferred_element_type=jnp.float32)


def standardized(values):
    centre = values - jnp.mean(values, -1, keepdims=True)
    inverse = lax.rsqrt(jnp.mean(centre * centre, -1, keepdims=True) + EPSILON)
    return centre * inverse, inverse


def norm_step_back(delta, values, gain_row):
    standard, inverse = standardized(values)
    scaled = delta * gain_row
    moved = inverse * (
        scaled - jnp.mean(scaled, -1, keepdims=True) - standard * jnp.mean(scaled * standard, -1, keepdims=True)
    )
    return moved, jnp.sum(delta * standard, 0, keepdims=True), jnp.sum(delta, 0, keepdims=True)


def half_mask(half):
    lanes = lax.broadcasted_iota(jnp.int32, (1, 128), 1)
    return (lanes < 64) if half == 0 else (lanes >= 64)


def attention_forward(m, length):
    rows = m.qkv.shape[0]
    width = m.att.shape[1]

    def pair(p, carry):
        at = pl.multiple_of(p * 128, 128)
        q2 = m.qkv[:, pl.ds(at, 128)]
        k2 = m.qkv[:, pl.ds(pl.multiple_of(width + at, 128), 128)]
        v2 = m.qkv[:, pl.ds(pl.multiple_of(2 * width + at, 128), 128)]
        v_turned = v2.T
        parts = []
        for half in range(2):
            kh = jnp.where(half_mask(half), k2, jnp.zeros_like(k2))
            top = matmul_turned(kh[:KEY_SPLIT], q2)
            low = matmul_turned(kh[KEY_SPLIT:], q2)
            key_row = KEY_SPLIT + lax.broadcasted_iota(jnp.int32, low.shape, 0)
            low = jnp.where(key_row < length, low, -1e30)
            peak = jnp.maximum(jnp.max(top, 0, keepdims=True), jnp.max(low, 0, keepdims=True))
            top = jnp.exp(top - peak)
            low = jnp.exp(low - peak)
            over = 1.0 / (jnp.sum(top, 0, keepdims=True) + jnp.sum(low, 0, keepdims=True))
            probs = jnp.concatenate([(top * over).astype(jnp.bfloat16), (low * over).astype(jnp.bfloat16)], axis=0)
            m.probs[2 * p + half] = probs
            parts.append(matmul(v_turned[64 * half : 64 * half + 64], probs))
        turned = jnp.concatenate(parts, axis=0)
        m.att_turned[pl.ds(at, 128), :] = turned.astype(jnp.bfloat16)
        m.att[:, pl.ds(at, 128)] = turned.T.astype(jnp.bfloat16)
        return carry

    lax.fori_loop(0, width // 128, pair, 0, unroll=3)


def attention_back(m):
    width = m.att.shape[1]

    def pair(p, carry):
        at = pl.multiple_of(p * 128, 128)
        k_at = pl.ds(pl.multiple_of(width + at, 128), 128)
        v_at = pl.ds(pl.multiple_of(2 * width + at, 128), 128)
        q2 = m.qkv[:, pl.ds(at, 128)]
        k2 = m.qkv[:, k_at]
        v2 = m.qkv[:, v_at]
        d2 = m.att_delta[:, pl.ds(at, 128)]
        d_turned = d2.T
        k_turned = k2.T
        product = d_turned.astype(jnp.float32) * m.att_turned[pl.ds(at, 128), :].astype(jnp.float32)
        values, keys, queries = [], [], []
        for half in range(2):
            vh = jnp.where(half_mask(half), v2, jnp.zeros_like(v2))
            probs = m.probs[2 * p + half]
            inner = jnp.sum(product[64 * half : 64 * half + 64], 0, keepdims=True)
            score = (probs.astype(jnp.float32) * (matmul(vh, d_turned) - inner)).astype(jnp.bfloat16)
            values.append(matmul(probs, d2))
            keys.append(matmul(score, q2))
            queries.append(matmul(k_turned[64 * half : 64 * half + 64], score))
        dq = (jnp.concatenate(queries, axis=0).T * HEAD_DIM ** (-0.5)).astype(jnp.bfloat16)
        dk = jnp.where(half_mask(0), keys[0], keys[1]).astype(jnp.bfloat16)
        dv = jnp.where(half_mask(0), values[0], values[1]).astype(jnp.bfloat16)
        m.mixed[:, pl.ds(at, 128)] = dq
        m.mixed[:, k_at] = dk
        m.mixed[:, v_at] = dv
        m.sums[2:3, pl.ds(at, 128)] += jnp.sum(dq.astype(jnp.float32), 0, keepdims=True)
        m.sums[3:4, pl.ds(at, 128)] += jnp.sum(dv.astype(jnp.float32), 0, keepdims=True)
        return carry

    lax.fori_loop(0, width // 128, pair, 0, unroll=3)


def forward_front(m, x_ref, length):
    x = x_ref[...].astype(jnp.float32)
    standard, unused = standardized(x)
    m.n1[...] = (standard * m.gain[0:1] + m.shift[0:1]).astype(jnp.bfloat16)
    width = x.shape[1]
    m.need(m.qkv_w)
    n1 = m.n1[...]
    for part in range(3):
        value = matmul(n1, m.qkv_w[:, part * width : (part + 1) * width])
        if part == 0:
            value = (value + m.qv[0:1]).astype(jnp.bfloat16) * jnp.bfloat16(HEAD_DIM ** (-0.5))
        elif part == 2:
            value = value + m.qv[1:2]
        m.qkv[:, part * width : (part + 1) * width] = value.astype(jnp.bfloat16)
    attention_forward(m, length)
    m.need(m.out_w)
    middle = x_ref[...].astype(jnp.float32) + matmul(m.att[...], m.out_w[...]) + m.proj[0:1]
    m.middle[...] = middle
    standard, unused = standardized(middle)
    m.n2[...] = (standard * m.gain[1:2] + m.shift[1:2]).astype(jnp.bfloat16)


def back_tail(m, x_ref, g_ref, n2_delta, keep):
    middle_part, gain, shift = norm_step_back(n2_delta, m.middle[...], m.gain[1:2])
    m.sums[6:7] += gain
    m.sums[8:9] += shift
    middle_delta = g_ref[...].astype(jnp.float32) + middle_part
    proj_delta = middle_delta.astype(jnp.bfloat16)
    m.sums[4:5] += jnp.sum(proj_delta.astype(jnp.float32), 0, keepdims=True)
    m.proj_delta[...] = proj_delta
    m.middle_delta[...] = middle_delta
    m.att_delta[...] = matmul_turned(proj_delta, m.out_w[...]).astype(jnp.bfloat16)
    attention_back(m)
    width = m.att.shape[1]
    total = None
    for part in range(3):
        columns = slice(part * width, (part + 1) * width)
        piece = matmul_turned(m.mixed[:, columns], m.qkv_w[:, columns])
        total = piece if total is None else total + piece
    input_part, gain, shift = norm_step_back(total, x_ref[...].astype(jnp.float32), m.gain[0:1])
    m.sums[5:6] += gain
    m.sums[7:8] += shift
    keep(m.middle_delta[...] + input_part)


def forward_expert(m, slot, begin, end):
    steps = m.up_w.shape[2] // CHUNK

    def step(j, carry):
        columns = pl.ds(pl.multiple_of(j * CHUNK, CHUNK), CHUNK)
        hidden = matmul(m.n2[begin:end], m.up_w[slot, :, columns]) + m.up_b[slot : slot + 1, columns]
        below, bell = normal_parts(hidden)
        active = (hidden * below).astype(jnp.bfloat16)
        m.active[begin:end, columns] = active
        m.slope[begin:end, columns] = (below + hidden * bell).astype(jnp.bfloat16)
        m.total[begin:end] += matmul(active, m.down_w[slot, columns, :])
        return carry

    m.total[begin:end] = m.middle[begin:end] + m.down_b[slot : slot + 1]
    lax.fori_loop(0, steps, step, 0, unroll=True)


def back_expert(m, g_ref, slot, begin, end):
    steps = m.up_w.shape[2] // CHUNK
    m.total[begin:end] = jnp.zeros((end - begin, m.total.shape[1]), jnp.float32)
    m.sums[slot : slot + 1] += jnp.sum(g_ref[begin:end].astype(jnp.float32), 0, keepdims=True)

    def step(j, carry):
        columns = pl.ds(pl.multiple_of(j * CHUNK, CHUNK), CHUNK)
        active_delta = matmul_turned(g_ref[begin:end], m.down_w[slot, columns, :])
        hidden_delta = (active_delta * m.slope[begin:end, columns].astype(jnp.float32)).astype(jnp.bfloat16)
        m.hidden_delta[begin:end, columns] = hidden_delta
        m.sums[pl.ds(9 + 4 * slot + j, 1)] += jnp.sum(hidden_delta.astype(jnp.float32), 0, keepdims=True)
        m.total[begin:end] += matmul_turned(hidden_delta, m.up_w[slot, :, columns])
        return carry

    lax.fori_loop(0, steps, step, 0, unroll=True)


def both_expert(m, g_ref):
    steps = m.up_w.shape[2] // CHUNK
    m.total[...] = jnp.zeros(m.total.shape, jnp.float32)
    m.sums[0:1] += jnp.sum(g_ref[...].astype(jnp.float32), 0, keepdims=True)

    def step(j, carry):
        columns = pl.ds(pl.multiple_of(j * CHUNK, CHUNK), CHUNK)
        active_delta = matmul_turned(g_ref[...], m.down_w[0, columns, :])
        hidden = matmul(m.n2[...], m.up_w[0, :, columns]) + m.up_b[2:3, columns]
        below, bell = normal_parts(hidden)
        m.active[:, columns] = (hidden * below).astype(jnp.bfloat16)
        hidden_delta = (active_delta * (below + hidden * bell)).astype(jnp.bfloat16)
        m.hidden_delta[:, columns] = hidden_delta
        m.sums[pl.ds(9 + j, 1)] += jnp.sum(hidden_delta.astype(jnp.float32), 0, keepdims=True)
        m.total[...] += matmul_turned(hidden_delta, m.up_w[0, :, columns])
        return carry

    lax.fori_loop(0, steps, step, 0, unroll=True)


def layers_kernel(names, *refs):
    m = Refs()
    for name, ref in zip(names, refs):
        setattr(m, name, ref)
    items, length = m.in_tokens.shape[:2]
    half = m.total.shape[1] // 2
    section = lax.axis_index("section")
    across = (1 - section, lax.axis_index("dp"))

    def send(i):
        return pltpu.make_async_remote_copy(
            src_ref=m.leaving.at[i], dst_ref=m.landed.at[i], send_sem=m.send_sem.at[i], recv_sem=m.recv_sem.at[i],
            device_id=across, device_id_type=MESH,
        )

    def send_half(i):
        return pltpu.make_async_remote_copy(
            src_ref=m.half_out.at[i], dst_ref=m.half_in.at[i], send_sem=m.half_send.at[i], recv_sem=m.half_recv.at[i],
            device_id=across, device_id_type=MESH,
        )

    def local(source, target, number):
        return pltpu.make_async_copy(source, target, m.copy_sem.at[number])

    def branch_copy(source, i):
        return pltpu.make_async_copy(source.at[i], m.branch.at[i], m.branch_sem.at[i])

    def weights(experts):
        found = [
            (m.qkv_w, [local(m.in_qkv.at[0], m.qkv_w, 0)]),
            (m.out_w, [local(m.in_out.at[0], m.out_w, 1)]),
            (m.up_w, []),
            (m.down_w, []),
        ]
        for slot, expert in enumerate(experts):
            found[2][1].append(local(m.in_up.at[expert], m.up_w.at[slot], 2 + slot))
            found[3][1].append(local(m.in_down.at[expert], m.down_w.at[slot], 4 + slot))
        return found

    def start_weights(found):
        copies = found[0][1] + found[1][1]
        for pair in zip(found[2][1], found[3][1]):
            copies += pair
        for copy in copies:
            copy.start()

    def needs(found, i):
        def need(ref):
            for here, copies in found:
                if here is ref:

                    @pl.when(i == 0)
                    def _():
                        for copy in copies:
                            copy.wait()

        return need

    leaving = (
        (m.n1, m.out_n1), (m.att, m.out_att), (m.n2, m.out_n2), (m.active, m.out_active), (m.qkv, m.kept_qkv),
        (m.probs, m.kept_probs), (m.att_turned, m.kept_turned), (m.middle, m.kept_middle), (m.slope, m.kept_slope),
        (m.mixed, m.out_mixed), (m.proj_delta, m.out_proj), (m.hidden_delta, m.out_hidden),
    )
    n1, att, n2, active, qkv, probs, turned, middle, slope, mixed, proj, hidden = range(len(leaving))

    def puts(i):
        return lambda number: local(leaving[number][0], leaving[number][1].at[i], 6 + number)

    def gets(i):
        return lambda number: local(leaving[number][1].at[i], leaving[number][0], 14 + number)

    def start(copies, *which):
        for number in which:
            copies(number).start()

    def wait(copies, *which):
        for number in which:
            copies(number).wait()

    def settle(i, *which):
        @pl.when(i > 0)
        def _():
            wait(puts(i), *which)

    def text_first(target, source, i):
        value = source[i].astype(jnp.float32)
        pad = jnp.zeros((ROWS - length, value.shape[1]), jnp.float32)
        target[i, :TEXT] = value[PATCHES:].astype(jnp.bfloat16)
        target[i, TEXT:] = jnp.concatenate([value[:PATCHES], pad], axis=0).astype(jnp.bfloat16)

    def mask_targets(i):
        row = lax.broadcasted_iota(jnp.int32, (ROWS, 1), 0)
        position = jnp.where(row < TEXT, row + PATCHES, jnp.where(row < length, row - TEXT, length))
        chosen = jnp.zeros((ROWS, 1), jnp.float32)
        for mask in (m.patch_mask, m.text_mask):
            same = jnp.where(position == mask[i : i + 1, :], 1.0, 0.0)
            chosen = jnp.maximum(chosen, jnp.max(same, 1, keepdims=True))
        m.targets[i] = (m.targets[i].astype(jnp.float32) * chosen).astype(jnp.bfloat16)

    def place(i, value):
        m.input_grad[i, :PATCHES] = value[TEXT:length]
        m.input_grad[i, PATCHES:] = value[:TEXT]

    def first_front(found, i, carry):
        m.need = needs(found, i)
        text_first(m.tokens, m.in_tokens, i)
        settle(i, n1, att, n2, qkv, probs, turned, middle)
        forward_front(m, m.tokens.at[i], length)
        start(puts(i), n1, att, n2, qkv, probs, turned, middle)
        settle(i, active, slope)
        m.need(m.up_w)
        m.need(m.down_w)
        forward_expert(m, 1, 0, TEXT)
        forward_expert(m, 0, TEXT, ROWS)
        m.leaving[i] = m.total[...].astype(jnp.bfloat16)
        send(i).start()
        start(puts(i), active, slope)
        return carry

    def first_back(i, carry):
        start(gets(i), slope, middle, turned, qkv, probs)

        @pl.when(i > 0)
        def _():
            send(i - 1).wait_send()

        send(i).wait_recv()
        branch_copy(m.landed, i).start()
        settle(i, hidden)
        wait(gets(i), slope)
        gradient = m.landed.at[i]
        back_expert(m, gradient, 1, 0, TEXT)
        back_expert(m, gradient, 0, TEXT, ROWS)
        start(puts(i), hidden)
        settle(i, mixed, proj)
        wait(gets(i), middle, turned, qkv, probs)

        def keep(value):
            place(i, value[:, :half])
            m.half_out[i] = value[:, half:].astype(jnp.bfloat16)

        back_tail(m, m.tokens.at[i], gradient, m.total[...], keep)
        send_half(i).start()
        start(puts(i), mixed, proj)
        branch_copy(m.landed, i).wait()
        return carry

    def second_both(found, i, carry):
        m.need = needs(found, i)
        branch_copy(m.targets, i).start()
        send(i).wait_recv()
        settle(i, n1, att, n2)
        arrived = m.landed.at[i]
        forward_front(m, arrived, length)
        start(puts(i), n1, att, n2)
        settle(i, active, hidden)
        m.need(m.up_w)
        m.need(m.down_w)
        gradient = m.targets.at[i]
        both_expert(m, gradient)
        start(puts(i), active, hidden)
        settle(i, mixed, proj)

        def keep(value):
            m.leaving[i] = value.astype(jnp.bfloat16)

        back_tail(m, arrived, gradient, m.total[...], keep)
        send(i).start()
        start(puts(i), mixed, proj)
        branch_copy(m.targets, i).wait()
        return carry

    m.sums[...] = jnp.zeros(m.sums.shape, jnp.float32)
    barrier = pltpu.get_barrier_semaphore()
    pl.semaphore_signal(barrier, inc=1, device_id=across, device_id_type=MESH)

    @pl.when(section == 0)
    def _():
        found = weights((0, 1))
        start_weights(found)
        pl.semaphore_wait(barrier, 1)
        lax.fori_loop(0, items, functools.partial(first_front, found), 0)
        wait(puts(0), n1, att, n2, active, qkv, probs, turned, middle, slope)
        lax.fori_loop(0, items, first_back, 0)
        wait(puts(0), mixed, proj, hidden)
        send(items - 1).wait_send()
        for i in range(items):
            send_half(i).wait_send()

    @pl.when(section == 1)
    def _():
        found = weights((2,))
        start_weights(found)
        for i in range(items):
            text_first(m.targets, m.cotangent, i)
            mask_targets(i)
        pl.semaphore_wait(barrier, 1)
        lax.fori_loop(0, items, functools.partial(second_both, found), 0)
        wait(puts(0), n1, att, n2, active, mixed, proj, hidden)
        for i in range(items):
            send(i).wait_send()
            send_half(i).wait_recv()
            place(i, m.half_in[i].astype(jnp.float32))


def both_layers(
    tokens, cotangent, patch_mask, text_mask, qkv_weight, out_weight, up_table, down_table, qv, proj, gain, shift, up_b, down_b
):
    items, length, width = tokens.shape
    rows = ROWS
    ff = up_b.shape[1]
    heads = width // HEAD_DIM
    bf16, f32 = jnp.bfloat16, jnp.float32
    dma = pltpu.SemaphoreType.DMA
    vmem, anywhere = pl.BlockSpec(memory_space=pltpu.VMEM), pl.BlockSpec(memory_space=pl.ANY)
    ins = dict(
        in_tokens=(tokens, vmem), cotangent=(cotangent, vmem), patch_mask=(patch_mask, vmem), text_mask=(text_mask, vmem), in_qkv=(qkv_weight, anywhere), in_out=(out_weight, anywhere),
        in_up=(up_table, anywhere), in_down=(down_table, anywhere), qv=(qv, vmem), proj=(proj, vmem), gain=(gain, vmem),
        shift=(shift, vmem), up_b=(up_b, vmem), down_b=(down_b, vmem),
    )

    def made(*shape, kind=bf16, spec=anywhere):
        return jax.ShapeDtypeStruct((items,) + shape, kind), spec

    outs = dict(
        out_n1=made(rows, width), out_att=made(rows, width), out_n2=made(rows, width), out_active=made(rows, ff),
        out_mixed=made(rows, 3 * width), out_proj=made(rows, width), out_hidden=made(rows, ff), branch=made(rows, width),
        kept_qkv=made(rows, 3 * width), kept_probs=made(heads, rows, rows), kept_turned=made(width, rows),
        kept_middle=made(rows, width, kind=f32), kept_slope=made(rows, ff),
        input_grad=made(length, width // 2, kind=f32, spec=vmem),
        sums=(jax.ShapeDtypeStruct((24, width), f32), vmem),
    )
    low_row, wide_row = ((rows, width), bf16), ((rows, ff), bf16)
    buffers = dict(
        qkv_w=((width, 3 * width), bf16), out_w=((width, width), bf16), up_w=((2, width, ff), bf16),
        down_w=((2, ff, width), bf16), n1=low_row, att=low_row, n2=low_row, active=wide_row,
        qkv=((rows, 3 * width), bf16), probs=((heads, rows, rows), bf16), att_turned=((width, rows), bf16),
        middle=((rows, width), f32), slope=wide_row, total=((rows, width), f32), mixed=((rows, 3 * width), bf16),
        proj_delta=low_row, hidden_delta=wide_row, att_delta=low_row, middle_delta=((rows, width), f32),
        leaving=((items, rows, width), bf16), landed=((items, rows, width), bf16),
        half_out=((items, rows, width // 2), bf16), half_in=((items, rows, width // 2), bf16),
        tokens=((items, rows, width), bf16), targets=((items, rows, width), bf16),
    )
    semaphores = dict(
        copy_sem=dma((23,)), branch_sem=dma((items,)), send_sem=dma((items,)), recv_sem=dma((items,)),
        half_send=dma((items,)), half_recv=dma((items,)),
    )
    names = list(ins) + list(outs) + list(buffers) + list(semaphores)
    results = pl.pallas_call(
        functools.partial(layers_kernel, names),
        out_shape=[shape for shape, spec in outs.values()],
        in_specs=[spec for value, spec in ins.values()],
        out_specs=[spec for shape, spec in outs.values()],
        scratch_shapes=[pltpu.VMEM(*kind) for kind in buffers.values()] + list(semaphores.values()),
        compiler_params=pltpu.CompilerParams(
            collective_id=1, has_side_effects=True, vmem_limit_bytes=60 * 1024 * 1024
        ),
        cost_estimate=pl.CostEstimate(flops=40_000_000_000, bytes_accessed=100_000_000, transcendentals=0),
    )(*[value for value, spec in ins.values()])
    m = Refs()
    for name, result in zip(outs, results):
        setattr(m, name, result)
    return m


def small_outs(own, other, is_first):
    first = jnp.where(is_first, own, other)
    second = jnp.where(is_first, other, own)
    me = lax.axis_index("dp")

    def columns(rows):
        wide = rows.shape[-1] // lax.axis_size("dp")
        return lax.dynamic_slice_in_dim(rows, me * wide, wide, rows.ndim - 1)

    down = columns(jnp.concatenate([first[:2], second[:1]]))
    up = columns(jnp.concatenate([first[9:17].reshape(2, -1), second[9:13].reshape(1, -1)]))
    own = columns(own[2:9])
    return own[0:2], own[2:3], own[3:5], own[5:7], up, down


def flat(value):
    return value.reshape((-1, value.shape[-1]))


def left_parts(m, is_first):
    n1, att, n2, branch_delta = (flat(part) for part in (m.out_n1, m.out_att, m.out_n2, m.branch))
    text = (jnp.arange(n1.shape[0]) % ROWS < TEXT)[:, None]
    vision = jnp.logical_not(text & is_first).astype(jnp.bfloat16)
    text = text.astype(jnp.bfloat16)
    return [
        piece.T for piece in (n2 * vision, branch_delta * vision, n2 * text, branch_delta * text, n1, att)
    ]


def large_grads(m, is_first):
    up, down, qkv, out, smalls = summed_grads(
        m.out_n1, m.out_att, m.out_n2, m.branch, m.out_hidden, m.out_active, m.out_mixed, m.out_proj, m.sums,
    )
    qkv, out, up, down = (part.astype(jnp.float32) for part in (qkv, out, up, down))
    return qkv, out, up, down, smalls[0], smalls[1]


def large_grads_plain(m, is_first):
    lefts = left_parts(m, is_first)
    hidden_delta, active = flat(m.out_hidden), flat(m.out_active)

    def total_of(left, right):
        product = jnp.dot(left, right, preferred_element_type=jnp.float32).astype(jnp.bfloat16)
        return lax.psum_scatter(product, "dp", scatter_dimension=1, tiled=True)

    def table(vision_part, text_part):
        def swapped(part):
            return lax.psum(part, "section").astype(jnp.float32)

        return jnp.stack(
            [
                swapped(jnp.where(is_first, vision_part, 0)),
                swapped(jnp.where(is_first, text_part, 0)),
                swapped(jnp.where(is_first, 0, vision_part)),
            ]
        )

    up = table(total_of(lefts[0], hidden_delta), total_of(lefts[2], hidden_delta))
    down = table(total_of(lefts[1], active), total_of(lefts[3], active))
    small = lax.psum(m.sums, "dp")
    return (
        total_of(lefts[4], flat(m.out_mixed)).astype(jnp.float32),
        total_of(lefts[5], flat(m.out_proj)).astype(jnp.float32),
        up,
        down.transpose(0, 2, 1),
        small,
        lax.ppermute(small, "section", [(0, 1), (1, 0)]),
    )


def shards(
    tokens, cotangent, patch_mask, text_mask, qkv_weight, qv_bias, out_weight, out_bias, norm_gain, norm_bias,
    up_table, up_bias, down_table, down_bias,
):
    is_first = lax.axis_index("section") == 0
    m = both_layers(
        tokens, cotangent, patch_mask, text_mask, qkv_weight, out_weight, up_table, down_table, qv_bias[0], out_bias,
        norm_gain[0], norm_bias[0], up_bias, down_bias,
    )
    grads = large_grads if lax.axis_size("dp") == 16 else large_grads_plain
    qkv, out, up, down, own, other = grads(m, is_first)
    qv_part, proj_part, gain_part, shift_part, up_part, down_part = small_outs(own, other, is_first)
    return (
        m.input_grad, qkv[None], qv_part[None], out[None], proj_part, gain_part[None], shift_part[None],
        up, up_part, down, down_part,
    )


def solution(mesh):
    items, layers = P("dp"), P("section")
    return jax.shard_map(
        shards,
        mesh=mesh,
        in_specs=(items,) * 4 + (layers,) * 6 + (P(),) * 4,
        out_specs=(
            P("dp", None, "section"), P("section", None, "dp"), P("section", None, "dp"), P("section", None, "dp"),
            P("section", "dp"), P("section", None, "dp"), P("section", None, "dp"),
            P(None, None, "dp"), P(None, "dp"), P(None, "dp", None), P(None, "dp"),
        ),
        check_vma=False,
    )
```

```python
import functools

import jax
import jax.numpy as jnp
from jax import lax
from jax.experimental import pallas as pl
from jax.experimental.pallas import tpu as pltpu
from jax.sharding import PartitionSpec as P

HEAD_DIM = 64
PATCHES = 197
EPSILON = 1e-05
BLOCK = 384
WINDOW = 640
RING = 3
TEXT = 64
ROWS = 272
MESH = pl.DeviceIdType.MESH


UNITS = (
    (
        (3, 1, 0), (0, 1, 0), (3, 3, 0), (2, 1, 0), (3, 0, 0), (0, 3, 0), (2, 0, 1), (3, 2, 0), (0,
        0, 0), (2, 3, 1), (1, 2, 0), (0, 2, 0), (1, 0, 0), (4, 0, 1), (4, 3, 0), (4, 1, 0), (1, 3,
        0), (2, 2, 0), (1, 1, 0), (4, 2, 0),
    ),
    (
        (0, 2, 0), (0, 1, 0), (0, 3, 0), (3, 1, 0), (0, 0, 1), (1, 2, 0), (1, 3, 1), (1, 0, 0), (3,
        3, 0), (3, 0, 0), (4, 3, 1), (3, 2, 0), (1, 1, 0), (4, 2, 0), (4, 0, 0), (4, 1, 0),
    ),
)
WAIT = 3
HOP = 2
LEFT_OF = ((0,), (1,), (0,), (1,), (2, 3))


def packed(units, handed_on):
    counts = [0, 0]
    codes = []
    for kind, plane, z_first in units:
        slot = 0
        if not (handed_on and kind == 3):
            slot = counts[z_first]
            counts[z_first] += 1
        codes.append(kind | plane << 3 | z_first << 5 | slot << 6)
    codes += [0] * (-len(codes) % 3)
    return [codes[i] | codes[i + 1] << 10 | codes[i + 2] << 20 for i in range(0, len(codes), 3)], counts


PACKED, COUNTS = zip(*(packed(units, side == 0) for side, units in enumerate(UNITS)))
Y_UNITS, Z_UNITS = (max(COUNTS[0][way], COUNTS[1][way], 1) for way in range(2))


def look_up(words, u):
    word = words[0]
    for n in range(1, len(words)):
        word = jnp.where(u // 3 == n, words[n], word)
    return word >> (10 * (u % 3))


class Refs:
    pass


def sum_kernel(names, *refs):
    m = Refs()
    for name, ref in zip(names, refs):
        setattr(m, name, ref)
    section = lax.axis_index("section")
    me = lax.axis_index("dp")
    z, y, core = me // 4, (me // 2) % 2, me % 2
    peer = (section, me + 1 - 2 * core)
    beside = (section, me + 2 - 4 * y)
    right = (section, me + 4)
    left = (section, me - 4)
    across = (1 - section, me)
    on_first = section == 0
    units = jnp.where(on_first, len(UNITS[0]), len(UNITS[1]))
    computed = jnp.where(on_first, len(UNITS[0]), len(UNITS[1]) - 4)

    arrivals = [u for u, (kind, plane, z_first) in enumerate(UNITS[1]) if kind == 3]

    class Unit:
        def __init__(self, u):
            self.u = u
            code = jnp.where(on_first, look_up(PACKED[0], u), look_up(PACKED[1], u))
            self.kind = code & 7
            self.plane = (code >> 3) & 3
            self.z_first = ((code >> 5) & 1) == 1
            self.slot = (code >> 6) & 15
            self.handed_on = on_first & (self.kind == 3)
            self.handed_in = jnp.logical_not(on_first) & (self.kind == 3)
            self.y_first = jnp.logical_not(self.z_first | self.handed_on)
            self.y_slot = self.slot + jnp.where(self.z_first, Y_UNITS, 0)
            self.uses_text = jnp.logical_not(on_first) | (self.kind > 1)
            self.uses_patches = jnp.logical_not(on_first) | (self.kind < 2) | (self.kind == 4)
            self.order = u
            for at in arrivals:
                self.order = self.order - jnp.where((section == 1) & (u > at), 1, 0)

    def following(u):
        u = u + 1
        for at in arrivals:
            u = u + jnp.where((section == 1) & (u == at), 1, 0)
        return u

    def remote(src, dst, send, recv, device):
        return pltpu.make_async_remote_copy(
            src_ref=src, dst_ref=dst, send_sem=send, recv_sem=recv, device_id=device, device_id_type=MESH
        )

    def core_copy(order, b):
        slot = order % RING
        return remote(m.xs.at[slot, b], m.xr.at[slot, b], m.core_send.at[order, b], m.core_recv.at[order, b], peer)

    def y_copy(n):
        return remote(m.part.at[n.u, 0], m.yr.at[n.y_slot], m.y_send.at[n.y_slot], m.y_recv.at[n.y_slot], beside)

    def right_copy(n):
        return remote(m.part.at[n.u, 1], m.zr.at[n.slot], m.right_send.at[n.slot], m.right_recv.at[n.slot], right)

    def left_copy(n):
        return remote(m.part.at[n.u, 1], m.zl.at[n.slot], m.left_send.at[n.slot], m.left_recv.at[n.slot], left)

    def right_pair(n):
        g = n.slot
        return remote(m.part.at[n.u], m.wr.at[g], m.right_send.at[Y_UNITS + g], m.right_recv.at[Y_UNITS + g], right)

    def left_pair(n):
        g = n.slot
        return remote(m.part.at[n.u], m.wl.at[g], m.left_send.at[Y_UNITS + g], m.left_recv.at[Y_UNITS + g], left)

    def over_copy(plane, source, target):
        return remote(m.part.at[source], m.part.at[target], m.over_send.at[plane], m.over_recv.at[plane], across)

    def over_target(plane):
        target = 0
        for at in arrivals:
            target = target + jnp.where(plane == UNITS[1][at][1], at, 0)
        return target

    def peer_copy(k):
        return remote(m.fin.at[0, core, k], m.fin.at[0, core, k], m.peer_send.at[k], m.peer_recv.at[k], peer)

    def cross_copy(k):
        return remote(m.fin.at[0, core, k], m.fin.at[1, core, k], m.cross_send.at[k], m.cross_recv.at[k], across)

    def hand_copy(k):
        return remote(m.fin.at[1, core, k], m.fin.at[1, core, k], m.hand_send.at[k], m.hand_recv.at[k], peer)

    def mixed_start(plane):
        return pl.multiple_of((9 * plane // 2) * 128, 128)

    def proj_start(plane):
        return pl.multiple_of((3 * plane // 2) * 128, 128)

    def tile_copies(n):
        k = n.kind
        slot = n.order % 2
        plain = pl.multiple_of(n.plane * 2 * BLOCK, 128)
        wide = pl.ds(plain, 2 * BLOCK)
        cases = []
        for ref, number, here, source, target in (
            (m.hidden, 0, (k == 0) | (k == 2), wide, slice(0, 2 * BLOCK)),
            (m.active, 0, (k == 1) | (k == 3), wide, slice(0, 2 * BLOCK)),
            (m.mixed, 0, k == 4, pl.ds(mixed_start(n.plane), WINDOW), slice(0, WINDOW)),
            (m.proj, 1, k == 4, pl.ds(proj_start(n.plane), 256), slice(WINDOW, WINDOW + 256)),
        ):
            copy = pltpu.make_async_copy(
                ref.at[:, :TEXT, source], m.text_tile.at[slot, :, :, target], m.text_sem.at[slot, number]
            )
            cases.append((here & n.uses_text, copy))
            copy = pltpu.make_async_copy(
                ref.at[:, TEXT:, source], m.patch_tile.at[slot, :, :, target], m.patch_sem.at[slot, number]
            )
            cases.append((here & n.uses_patches, copy))
        return cases

    def start_tile(n):
        for here, copy in tile_copies(n):
            pl.when(here)(copy.start)

    def wait_tile(n):
        for here, copy in tile_copies(n):
            pl.when(here)(copy.wait)

    def add_into(target, source):
        target[...] = target[...] + source[...]

    def rows(half):
        return pl.ds(pl.multiple_of(half * BLOCK, BLOCK), BLOCK)

    def tile_rows(tile, slot, begin, end):
        value = tile[slot, :, :, begin:end]
        return value.reshape(-1, end - begin)

    def text_dot(index, half, slot, begin, end):
        return matmul(m.text_left[index, rows(half), :], tile_rows(m.text_tile, slot, begin, end))

    def patch_dot(index, half, slot, begin, end):
        return matmul(m.patch_left[index, rows(half), :], tile_rows(m.patch_tile, slot, begin, end))

    def both_dot(index, half, slot, begin, end):
        return patch_dot(index, half, slot, begin, end) + text_dot(index, half, slot, begin, end)

    def attention_columns(half, slot, plane):
        mixed = both_dot(2, half, slot, 0, WINDOW)
        proj = both_dot(3, half, slot, WINDOW, WINDOW + 256)
        mixed_at = 576 * plane - mixed_start(plane)
        proj_at = 192 * plane - proj_start(plane)
        lanes = lax.broadcasted_iota(jnp.int32, (1, 128), 1)
        found = []
        for side in range(2):
            own = pltpu.roll(mixed, (WINDOW - mixed_at - 288 * side) % WINDOW, 1)
            last = pltpu.roll(proj, (256 + 32 - proj_at - 96 * side) % 256, 1)
            found.append((own[:, :256], jnp.where(lanes < 32, own[:, 256:384], last[:, :128])))
        return found

    def compute(n):
        k = n.kind
        slot = n.order % RING

        @pl.when(n.order >= RING)
        def _():
            core_copy(n.order - RING, 0).wait_send()
            core_copy(n.order - RING, 1).wait_send()
            pl.semaphore_wait(m.credit, 1)

        @pl.when(n.order + 1 < computed)
        def _():
            start_tile(Unit(following(n.u)))

        wait_tile(n)
        tile = n.order % 2
        for part in range(2):
            half = (1 - core) if part == 0 else core
            target = m.xs.at[slot] if part == 0 else m.part.at[n.u]

            def put(value):
                for side in range(2):
                    target[jnp.where(y == side, 1, 0)] = value[:, side * BLOCK : (side + 1) * BLOCK].astype(jnp.bfloat16)

            @pl.when((k < 4) & jnp.logical_not(n.uses_text))
            def _():
                put(patch_dot(k % 2, half, tile, 0, 2 * BLOCK))

            @pl.when((k < 4) & jnp.logical_not(n.uses_patches))
            def _():
                put(text_dot(k % 2, half, tile, 0, 2 * BLOCK))

            @pl.when((k < 4) & n.uses_text & n.uses_patches)
            def _():
                put(both_dot(k % 2, half, tile, 0, 2 * BLOCK))

            @pl.when(k == 4)
            def _():
                for side, (front, back) in enumerate(attention_columns(half, tile, n.plane)):
                    at = jnp.where(y == side, 1, 0)
                    target[at, :, :256] = front.astype(jnp.bfloat16)
                    target[at, :, 256:] = back.astype(jnp.bfloat16)

            if part == 0:
                core_copy(n.order, 0).start()
                core_copy(n.order, 1).start()

    def join_core(n):
        slot = n.order % RING

        @pl.when(n.handed_in)
        def _():
            over_copy(n.plane, 0, n.u).wait_recv()

        @pl.when(jnp.logical_not(n.handed_in))
        def _():
            core_copy(n.order, 0).wait_recv()
            add_into(m.part.at[n.u, 0], m.xr.at[slot, 0])

        pl.when(n.y_first)(lambda: y_copy(n).start())

        @pl.when(jnp.logical_not(n.handed_in))
        def _():
            core_copy(n.order, 1).wait_recv()
            add_into(m.part.at[n.u, 1], m.xr.at[slot, 1])

            @pl.when(n.order + RING < computed)
            def _():
                pl.semaphore_signal(m.credit, inc=1, device_id=peer, device_id_type=MESH)

        pl.when(n.handed_on)(lambda: over_copy(n.plane, n.u, over_target(n.plane)).start())

    def join_y(n):
        y_copy(n).wait_recv()
        add_into(m.part.at[n.u, 1], m.yr.at[n.y_slot])

    def take(n, one, pair, single_from, pair_from):
        @pl.when(n.y_first)
        def _():
            one(n).wait_recv()
            add_into(m.part.at[n.u, 1], single_from.at[n.slot])

        @pl.when(n.z_first)
        def _():
            pair(n).wait_recv()
            add_into(m.part.at[n.u], pair_from.at[n.slot])

    def take_right(n):
        take(n, right_copy, right_pair, m.zr, m.wr)

    def take_left(n):
        take(n, left_copy, left_pair, m.zl, m.wl)

    def pass_right(n):
        pl.when(z > 0)(lambda: take_right(n))
        pl.when(n.y_first)(lambda: right_copy(n).start())
        pl.when(n.z_first)(lambda: right_pair(n).start())

    def pass_left(n):
        pl.when(z < 3)(lambda: take_left(n))
        pl.when(n.y_first)(lambda: left_copy(n).start())
        pl.when(n.z_first)(lambda: left_pair(n).start())

    def give(n):
        k = n.kind
        m.fin[0, core, k] = m.part[n.u, 1]
        peer_copy(k).start()
        pl.when(k < 4)(lambda: cross_copy(k).start())

    def meet(n):
        pl.when(z > 0)(lambda: take_right(n))
        pl.when(z < 3)(lambda: take_left(n))
        pl.when(n.z_first)(lambda: y_copy(n).start())
        pl.when(n.y_first)(lambda: give(n))

    def meet_late(n):
        join_y(n)
        give(n)

    flips = (peer, beside, (section, me + 4 - 8 * (z % 2)), (section, me + 8 - 16 * (z // 2)), across)

    def small_copy(j):
        return remote(m.small_sum.at[j], m.small_in.at[j], m.small_send.at[j], m.small_recv.at[j], flips[j])

    def small_step(j):
        if j == 0:
            m.small_sum[0] = m.small[...]
        else:
            small_copy(j - 1).wait_recv()
            if j == 5:
                m.small_out[0] = m.small_sum[4]
                m.small_out[1] = m.small_in[4]
            else:
                m.small_sum[j] = m.small_sum[j - 1] + m.small_in[j - 1]
        if j < 5:
            small_copy(j).start()

    lefts = (m.n2, m.branch, m.n1, m.att)
    turns = [[], []]
    for side in range(2):
        for kind, plane, z_first in UNITS[side]:
            for index in LEFT_OF[kind] if (side, kind) != (1, 3) else ():
                if index not in turns[side]:
                    turns[side].append(index)

    def stage_copy(index):
        return pltpu.make_async_copy(lefts[index], m.stage, m.stage_sem.at[0])

    def start_stage(turn):
        for side in range(2):
            pl.when(section == side)(stage_copy(turns[side][turn]).start)

    def prepare(turn):
        stage_copy(0).wait()
        number = jnp.where(on_first, turns[0][turn], turns[1][turn])

        def part(c, carry):
            at = pl.ds(pl.multiple_of(c * 128, 128), 128)
            m.text_left[number, at, :] = m.stage[:, :TEXT, at].reshape(-1, 128).T
            m.patch_left[number, at, :] = m.stage[:, TEXT:, at].reshape(-1, 128).T
            return carry

        lax.fori_loop(0, m.stage.shape[2] // 128, part, 0)
        if turn < 3:
            start_stage(turn + 1)

    barrier = pltpu.get_barrier_semaphore()
    for device in (peer, beside, across, flips[3]):
        pl.semaphore_signal(barrier, inc=1, device_id=device, device_id_type=MESH)

    @pl.when(z < 3)
    def _():
        pl.semaphore_signal(barrier, inc=1, device_id=right, device_id_type=MESH)

    @pl.when(z > 0)
    def _():
        pl.semaphore_signal(barrier, inc=1, device_id=left, device_id_type=MESH)

    start_stage(0)
    start_tile(Unit(jnp.int32(0)))
    prepare(0)
    pl.semaphore_wait(barrier, 4 + jnp.where(z < 3, 1, 0) + jnp.where(z > 0, 1, 0))

    def at_unit(u, condition, action):
        n = Unit(jnp.maximum(u, 0))

        @pl.when((u >= 0) & (u < units) & condition(n))
        def _():
            action(n)

    def in_flow(n):
        return jnp.logical_not(n.handed_on)

    def step(i, carry):
        at_unit(i, lambda n: jnp.logical_not(n.handed_in), compute)
        for number in range(3):
            pl.when(i == number)(functools.partial(prepare, number + 1))
        at_unit(i - 1, lambda n: n.kind >= 0, join_core)
        at_unit(i - WAIT, lambda n: n.y_first, join_y)
        at_unit(i - WAIT - HOP * z, lambda n: in_flow(n) & (n.plane > z), pass_right)
        at_unit(i - WAIT - HOP * (3 - z), lambda n: in_flow(n) & (n.plane < z), pass_left)
        at_unit(i - WAIT - 3 * HOP - 1, lambda n: in_flow(n) & (n.plane == z), meet)
        at_unit(i - WAIT - 3 * HOP - 3, lambda n: n.z_first & (n.plane == z), meet_late)
        for j in range(6):
            pl.when(i == 3 + j)(functools.partial(small_step, j))
        return carry

    lax.fori_loop(0, units + WAIT + 3 * HOP + 3, step, 0)

    def third_kind(k):
        return jnp.where(k == 2, 2 + section, k)

    def their_kind(k):
        return jnp.where(k == 2, 3 - section, k)

    for k in range(3):
        cross_copy(their_kind(jnp.int32(k))).wait_recv()
        hand_copy(their_kind(jnp.int32(k))).start()

    def settle(u, carry):
        n = Unit(u)

        @pl.when(jnp.logical_not(n.handed_in) & (n.order >= computed - RING))
        def _():
            core_copy(n.order, 0).wait_send()
            core_copy(n.order, 1).wait_send()

        pl.when(n.handed_on)(lambda: over_copy(n.plane, n.u, over_target(n.plane)).wait_send())
        pl.when(n.y_first | (n.z_first & (n.plane == z)))(lambda: y_copy(n).wait_send())
        pl.when(n.y_first & (n.plane > z))(lambda: right_copy(n).wait_send())
        pl.when(n.z_first & (n.plane > z))(lambda: right_pair(n).wait_send())
        pl.when(n.y_first & (n.plane < z))(lambda: left_copy(n).wait_send())
        pl.when(n.z_first & (n.plane < z))(lambda: left_pair(n).wait_send())
        return carry

    lax.fori_loop(0, units, settle, 0)
    for j in range(5):
        small_copy(j).wait_send()
    for k in range(3):
        peer_copy(third_kind(jnp.int32(k))).wait()
        cross_copy(third_kind(jnp.int32(k))).wait_send()
        hand_copy(their_kind(jnp.int32(k))).wait()
    peer_copy(4).wait()

    def write(c):
        def columns(side, half, k, begin, wide):
            return m.fin[side, half, k, :, begin + c * wide : begin + (c + 1) * wide]

        first, second = section, 1 - section
        for half in range(2):
            at = slice(half * BLOCK, (half + 1) * BLOCK)
            m.qkv_out[at, :] = columns(0, half, 4, 0, 144)
            m.out_out[at, :] = columns(0, half, 4, 288, 48)
            for expert, side, k in ((0, first, 0), (1, first, 2), (2, second, 0)):
                m.up_out[expert, at, :] = columns(side, half, k, 0, 192)
            for expert, side, k in ((0, first, 1), (1, second, 3), (2, second, 1)):
                m.down_out[expert, :, at] = columns(side, half, k, 0, 192).T

    for c in range(2):
        pl.when(core == c)(functools.partial(write, c))


def summed_grads(n1, att, n2, branch, hidden, active, mixed, proj, small):
    dma = pltpu.SemaphoreType.DMA
    items, depth, width = n1.shape
    bf16, f32 = jnp.bfloat16, jnp.float32
    tile = (BLOCK, BLOCK)
    vmem, anywhere = pl.BlockSpec(memory_space=pltpu.VMEM), pl.BlockSpec(memory_space=pl.ANY)
    ins = dict(n1=n1, att=att, n2=n2, branch=branch, hidden=hidden, active=active, mixed=mixed, proj=proj, small=small)
    outs = dict(
        up_out=((3, width, 192), bf16), down_out=((3, 192, width), bf16), qkv_out=((width, 144), bf16),
        out_out=((width, 48), bf16), small_out=((2,) + small.shape, f32),
    )
    buffers = dict(
        text_tile=((2, items, TEXT, WINDOW + 256), bf16), patch_tile=((2, items, depth - TEXT, WINDOW + 256), bf16), part=((20, 2) + tile, bf16), xs=((RING, 2) + tile, bf16),
        xr=((RING, 2) + tile, bf16), yr=((Y_UNITS + Z_UNITS,) + tile, bf16), zr=((Y_UNITS,) + tile, bf16), zl=((Y_UNITS,) + tile, bf16),
        wr=((Z_UNITS, 2) + tile, bf16), wl=((Z_UNITS, 2) + tile, bf16), fin=((2, 2, 5) + tile, bf16),
        text_left=((4, width, items * TEXT), bf16), patch_left=((4, width, items * (depth - TEXT)), bf16), stage=((items, depth, width), bf16), small_sum=((5,) + small.shape, f32),
        small_in=((5,) + small.shape, f32),
    )
    semaphores = dict(
        small_send=dma((5,)), small_recv=dma((5,)), text_sem=dma((2, 2)), patch_sem=dma((2, 2)), stage_sem=dma((1,)), core_send=dma((20, 2)),
        core_recv=dma((20, 2)), y_send=dma((Y_UNITS + Z_UNITS,)), y_recv=dma((Y_UNITS + Z_UNITS,)), right_send=dma((Y_UNITS + Z_UNITS,)), right_recv=dma((Y_UNITS + Z_UNITS,)),
        left_send=dma((Y_UNITS + Z_UNITS,)), left_recv=dma((Y_UNITS + Z_UNITS,)), over_send=dma((4,)), over_recv=dma((4,)), peer_send=dma((5,)),
        peer_recv=dma((5,)), cross_send=dma((5,)), cross_recv=dma((5,)), hand_send=dma((5,)), hand_recv=dma((5,)),
        credit=pltpu.SemaphoreType.REGULAR,
    )
    names = list(ins) + list(outs) + list(buffers) + list(semaphores)
    return pl.pallas_call(
        functools.partial(sum_kernel, names),
        out_shape=[jax.ShapeDtypeStruct(*kind) for kind in outs.values()],
        in_specs=[anywhere] * 8 + [vmem],
        out_specs=[vmem] * len(outs),
        scratch_shapes=[pltpu.VMEM(*kind) for kind in buffers.values()] + list(semaphores.values()),
        compiler_params=pltpu.CompilerParams(
            collective_id=0, has_side_effects=True, vmem_limit_bytes=60 * 1024 * 1024
        ),
        cost_estimate=pl.CostEstimate(flops=48 * 2 * 768 * 384 * items * depth, bytes_accessed=40_000_000, transcendentals=0),
    )(*ins.values())


CHUNK = 1024
KEY_SPLIT = 256
TAIL = (0.319381530, -0.356563782, 1.781477937, -1.821255978, 1.330274429)
PEAK = 0.3989422804014327


def normal_parts(z):
    size = jnp.abs(z)
    scale = 1.0 + 0.2316419 * size
    t = pl.reciprocal(scale, approx=True)
    t = t * (2.0 - scale * t)
    bell = jnp.exp(-0.5 * z * z) * PEAK
    series = TAIL[4]
    for factor in TAIL[3::-1]:
        series = series * t + factor
    upper = bell * (series * t)
    return jnp.where(z >= 0, 1.0 - upper, upper), bell


def matmul(left, right):
    return jnp.dot(left, right, preferred_element_type=jnp.float32)


def matmul_turned(left, right):
    return lax.dot_general(left, right, (((1,), (1,)), ((), ())), preferred_element_type=jnp.float32)


def standardized(values):
    centre = values - jnp.mean(values, -1, keepdims=True)
    inverse = lax.rsqrt(jnp.mean(centre * centre, -1, keepdims=True) + EPSILON)
    return centre * inverse, inverse


def norm_step_back(delta, values, gain_row):
    standard, inverse = standardized(values)
    scaled = delta * gain_row
    moved = inverse * (
        scaled - jnp.mean(scaled, -1, keepdims=True) - standard * jnp.mean(scaled * standard, -1, keepdims=True)
    )
    return moved, jnp.sum(delta * standard, 0, keepdims=True), jnp.sum(delta, 0, keepdims=True)


def half_mask(half):
    lanes = lax.broadcasted_iota(jnp.int32, (1, 128), 1)
    return (lanes < 64) if half == 0 else (lanes >= 64)


def attention_forward(m, length):
    rows = m.qkv.shape[0]
    width = m.att.shape[1]

    def pair(p, carry):
        at = pl.multiple_of(p * 128, 128)
        q2 = m.qkv[:, pl.ds(at, 128)]
        k2 = m.qkv[:, pl.ds(pl.multiple_of(width + at, 128), 128)]
        v2 = m.qkv[:, pl.ds(pl.multiple_of(2 * width + at, 128), 128)]
        v_turned = v2.T
        parts = []
        for half in range(2):
            kh = jnp.where(half_mask(half), k2, jnp.zeros_like(k2))
            top = matmul_turned(kh[:KEY_SPLIT], q2)
            low = matmul_turned(kh[KEY_SPLIT:], q2)
            key_row = KEY_SPLIT + lax.broadcasted_iota(jnp.int32, low.shape, 0)
            low = jnp.where(key_row < length, low, -1e30)
            peak = jnp.maximum(jnp.max(top, 0, keepdims=True), jnp.max(low, 0, keepdims=True))
            top = jnp.exp(top - peak)
            low = jnp.exp(low - peak)
            over = 1.0 / (jnp.sum(top, 0, keepdims=True) + jnp.sum(low, 0, keepdims=True))
            probs = jnp.concatenate([(top * over).astype(jnp.bfloat16), (low * over).astype(jnp.bfloat16)], axis=0)
            m.probs[2 * p + half] = probs
            parts.append(matmul(v_turned[64 * half : 64 * half + 64], probs))
        turned = jnp.concatenate(parts, axis=0)
        m.att_turned[pl.ds(at, 128), :] = turned.astype(jnp.bfloat16)
        m.att[:, pl.ds(at, 128)] = turned.T.astype(jnp.bfloat16)
        return carry

    lax.fori_loop(0, width // 128, pair, 0, unroll=True)


def attention_back(m):
    width = m.att.shape[1]

    def pair(p, carry):
        at = pl.multiple_of(p * 128, 128)
        k_at = pl.ds(pl.multiple_of(width + at, 128), 128)
        v_at = pl.ds(pl.multiple_of(2 * width + at, 128), 128)
        q2 = m.qkv[:, pl.ds(at, 128)]
        k2 = m.qkv[:, k_at]
        v2 = m.qkv[:, v_at]
        d2 = m.att_delta[:, pl.ds(at, 128)]
        d_turned = d2.T
        k_turned = k2.T
        product = d_turned.astype(jnp.float32) * m.att_turned[pl.ds(at, 128), :].astype(jnp.float32)
        values, keys, queries = [], [], []
        for half in range(2):
            vh = jnp.where(half_mask(half), v2, jnp.zeros_like(v2))
            probs = m.probs[2 * p + half]
            inner = jnp.sum(product[64 * half : 64 * half + 64], 0, keepdims=True)
            score = (probs.astype(jnp.float32) * (matmul(vh, d_turned) - inner)).astype(jnp.bfloat16)
            values.append(matmul(probs, d2))
            keys.append(matmul(score, q2))
            queries.append(matmul(k_turned[64 * half : 64 * half + 64], score))
        dq = (jnp.concatenate(queries, axis=0).T * HEAD_DIM ** (-0.5)).astype(jnp.bfloat16)
        dk = jnp.where(half_mask(0), keys[0], keys[1]).astype(jnp.bfloat16)
        dv = jnp.where(half_mask(0), values[0], values[1]).astype(jnp.bfloat16)
        m.mixed[:, pl.ds(at, 128)] = dq
        m.mixed[:, k_at] = dk
        m.mixed[:, v_at] = dv
        m.sums[2:3, pl.ds(at, 128)] += jnp.sum(dq.astype(jnp.float32), 0, keepdims=True)
        m.sums[3:4, pl.ds(at, 128)] += jnp.sum(dv.astype(jnp.float32), 0, keepdims=True)
        return carry

    lax.fori_loop(0, width // 128, pair, 0, unroll=True)


def forward_front(m, x_ref, length):
    x = x_ref[...].astype(jnp.float32)
    standard, unused = standardized(x)
    m.n1[...] = (standard * m.gain[0:1] + m.shift[0:1]).astype(jnp.bfloat16)
    width = x.shape[1]
    m.need(m.qkv_w)
    value = matmul(m.n1[...], m.qkv_w[...])
    query = (value[:, :width] + m.qv[0:1]).astype(jnp.bfloat16)
    m.qkv[:, :width] = query * jnp.bfloat16(HEAD_DIM ** (-0.5))
    m.qkv[:, width : 2 * width] = value[:, width : 2 * width].astype(jnp.bfloat16)
    m.qkv[:, 2 * width :] = (value[:, 2 * width :] + m.qv[1:2]).astype(jnp.bfloat16)
    attention_forward(m, length)
    m.need(m.out_w)
    middle = x_ref[...].astype(jnp.float32) + matmul(m.att[...], m.out_w[...]) + m.proj[0:1]
    m.middle[...] = middle
    standard, unused = standardized(middle)
    m.n2[...] = (standard * m.gain[1:2] + m.shift[1:2]).astype(jnp.bfloat16)


def back_tail(m, x_ref, g_ref, n2_delta, keep):
    middle_part, gain, shift = norm_step_back(n2_delta, m.middle[...], m.gain[1:2])
    m.sums[6:7, :gain.shape[1]] += gain
    m.sums[8:9, :gain.shape[1]] += shift
    middle_delta = g_ref[...].astype(jnp.float32) + middle_part
    proj_delta = middle_delta.astype(jnp.bfloat16)
    m.sums[4:5, :gain.shape[1]] += jnp.sum(proj_delta.astype(jnp.float32), 0, keepdims=True)
    m.proj_delta[...] = proj_delta
    m.middle_delta[...] = middle_delta
    m.att_delta[...] = matmul_turned(proj_delta, m.out_w[...]).astype(jnp.bfloat16)
    attention_back(m)
    total = matmul_turned(m.mixed[...], m.qkv_w[...])
    input_part, gain, shift = norm_step_back(total, x_ref[...].astype(jnp.float32), m.gain[0:1])
    m.sums[5:6, :gain.shape[1]] += gain
    m.sums[7:8, :gain.shape[1]] += shift
    keep(m.middle_delta[...] + input_part)


def forward_expert(m, slot, begin, end):
    steps = m.up_w.shape[2] // CHUNK

    def step(j, carry):
        columns = pl.ds(pl.multiple_of(j * CHUNK, CHUNK), CHUNK)
        hidden = matmul(m.n2[begin:end], m.up_w[slot, :, columns]) + m.up_b[slot : slot + 1, columns]
        below, bell = normal_parts(hidden)
        active = (hidden * below).astype(jnp.bfloat16)
        m.active[begin:end, columns] = active
        m.slope[begin:end, columns] = (below + hidden * bell).astype(jnp.bfloat16)
        return carry

    lax.fori_loop(0, steps, step, 0, unroll=True)
    result = matmul(m.active[begin:end], m.down_w[slot])
    m.total[begin:end] = m.middle[begin:end] + result + m.down_b[slot : slot + 1]


def back_expert(m, g_ref, slot, begin, end):
    steps = m.up_w.shape[2] // CHUNK
    m.sums[slot : slot + 1, : g_ref.shape[1]] += jnp.sum(g_ref[begin:end].astype(jnp.float32), 0, keepdims=True)

    def step(j, carry):
        columns = pl.ds(pl.multiple_of(j * CHUNK, CHUNK), CHUNK)
        active_delta = matmul_turned(g_ref[begin:end], m.down_w[slot, columns, :])
        hidden_delta = (active_delta * m.slope[begin:end, columns].astype(jnp.float32)).astype(jnp.bfloat16)
        m.hidden_delta[begin:end, columns] = hidden_delta
        m.sums[pl.ds(9 + 3 * slot + j, 1)] += jnp.sum(hidden_delta.astype(jnp.float32), 0, keepdims=True)
        return carry

    lax.fori_loop(0, steps, step, 0, unroll=True)
    m.total[begin:end] = matmul_turned(m.hidden_delta[begin:end], m.up_w[slot])


def both_expert(m, g_ref):
    steps = m.up_w.shape[2] // CHUNK
    m.sums[0:1, :g_ref.shape[1]] += jnp.sum(g_ref[...].astype(jnp.float32), 0, keepdims=True)

    def step(j, carry):
        columns = pl.ds(pl.multiple_of(j * CHUNK, CHUNK), CHUNK)
        active_delta = matmul_turned(g_ref[...], m.down_w[0, columns, :])
        hidden = matmul(m.n2[...], m.up_w[0, :, columns]) + m.up_b[2:3, columns]
        below, bell = normal_parts(hidden)
        m.active[:, columns] = (hidden * below).astype(jnp.bfloat16)
        hidden_delta = (active_delta * (below + hidden * bell)).astype(jnp.bfloat16)
        m.hidden_delta[:, columns] = hidden_delta
        m.sums[pl.ds(9 + j, 1)] += jnp.sum(hidden_delta.astype(jnp.float32), 0, keepdims=True)
        return carry

    lax.fori_loop(0, steps, step, 0, unroll=True)
    m.total[...] = matmul_turned(m.hidden_delta[...], m.up_w[0])


def layers_kernel(names, *refs):
    m = Refs()
    for name, ref in zip(names, refs):
        setattr(m, name, ref)
    items, length = m.in_tokens.shape[:2]
    half = m.total.shape[1] // 2
    section = lax.axis_index("section")
    across = (1 - section, lax.axis_index("dp"))

    def send(i):
        return pltpu.make_async_remote_copy(
            src_ref=m.leaving.at[i], dst_ref=m.landed.at[i], send_sem=m.send_sem.at[i], recv_sem=m.recv_sem.at[i],
            device_id=across, device_id_type=MESH,
        )

    def send_half(i):
        return pltpu.make_async_remote_copy(
            src_ref=m.half_out.at[i], dst_ref=m.half_in.at[i], send_sem=m.half_send.at[i], recv_sem=m.half_recv.at[i],
            device_id=across, device_id_type=MESH,
        )

    def local(source, target, number):
        return pltpu.make_async_copy(source, target, m.copy_sem.at[number])

    def branch_copy(source, i):
        return pltpu.make_async_copy(source.at[i], m.branch.at[i], m.branch_sem.at[i])

    def weights(experts):
        found = [
            (m.qkv_w, [local(m.in_qkv.at[0], m.qkv_w, 0)]),
            (m.out_w, [local(m.in_out.at[0], m.out_w, 1)]),
            (m.up_w, []),
            (m.down_w, []),
        ]
        for slot, expert in enumerate(experts):
            found[2][1].append(local(m.in_up.at[expert], m.up_w.at[slot], 2 + slot))
            found[3][1].append(local(m.in_down.at[expert], m.down_w.at[slot], 4 + slot))
        return found

    def start_weights(found):
        copies = found[0][1] + found[1][1]
        for pair in zip(found[2][1], found[3][1]):
            copies += pair
        for copy in copies:
            copy.start()

    def needs(found, i):
        def need(ref):
            for here, copies in found:
                if here is ref:

                    @pl.when(i == 0)
                    def _():
                        for copy in copies:
                            copy.wait()

        return need

    leaving = (
        (m.n1, m.out_n1), (m.att, m.out_att), (m.n2, m.out_n2), (m.active, m.out_active), (m.qkv, m.kept_qkv),
        (m.probs, m.kept_probs), (m.att_turned, m.kept_turned), (m.middle, m.kept_middle), (m.slope, m.kept_slope),
        (m.mixed, m.out_mixed), (m.proj_delta, m.out_proj), (m.hidden_delta, m.out_hidden),
    )
    n1, att, n2, active, qkv, probs, turned, middle, slope, mixed, proj, hidden = range(len(leaving))

    def puts(i):
        return lambda number: local(leaving[number][0], leaving[number][1].at[i], 6 + number)

    def gets(i):
        return lambda number: local(leaving[number][1].at[i], leaving[number][0], 14 + number)

    def start(copies, *which):
        for number in which:
            copies(number).start()

    def wait(copies, *which):
        for number in which:
            copies(number).wait()

    def settle(i, *which):
        @pl.when(i > 0)
        def _():
            wait(puts(i), *which)

    def text_first(target, source, i):
        value = source[i].astype(jnp.float32)
        pad = jnp.zeros((ROWS - length, value.shape[1]), jnp.float32)
        target[i, :TEXT] = value[PATCHES:].astype(jnp.bfloat16)
        target[i, TEXT:] = jnp.concatenate([value[:PATCHES], pad], axis=0).astype(jnp.bfloat16)

    def mask_targets(i):
        row = lax.broadcasted_iota(jnp.int32, (ROWS, 1), 0)
        position = jnp.where(row < TEXT, row + PATCHES, jnp.where(row < length, row - TEXT, length))
        chosen = jnp.zeros((ROWS, 1), jnp.float32)
        for mask in (m.patch_mask, m.text_mask):
            same = jnp.where(position == mask[i : i + 1, :], 1.0, 0.0)
            chosen = jnp.maximum(chosen, jnp.max(same, 1, keepdims=True))
        m.targets[i] = (m.targets[i].astype(jnp.float32) * chosen).astype(jnp.bfloat16)

    def place(i, value):
        m.input_grad[i, :PATCHES] = value[TEXT:length]
        m.input_grad[i, PATCHES:] = value[:TEXT]

    def first_front(found, i, carry):
        m.need = needs(found, i)
        text_first(m.tokens, m.in_tokens, i)
        settle(i, n1, att, n2, qkv, probs, turned, middle)
        forward_front(m, m.tokens.at[i], length)
        start(puts(i), n1, att, n2, qkv, probs, turned, middle)
        settle(i, active, slope)
        m.need(m.up_w)
        m.need(m.down_w)
        forward_expert(m, 1, 0, TEXT)
        forward_expert(m, 0, TEXT, ROWS)
        m.leaving[i] = m.total[...].astype(jnp.bfloat16)
        send(i).start()
        start(puts(i), active, slope)
        return carry

    def first_back(i, carry):
        start(gets(i), slope, middle, turned, qkv, probs)

        @pl.when(i > 0)
        def _():
            send(i - 1).wait_send()

        send(i).wait_recv()
        branch_copy(m.landed, i).start()
        settle(i, hidden)
        wait(gets(i), slope)
        gradient = m.landed.at[i]
        back_expert(m, gradient, 1, 0, TEXT)
        back_expert(m, gradient, 0, TEXT, ROWS)
        start(puts(i), hidden)
        settle(i, mixed, proj)
        wait(gets(i), middle, turned, qkv, probs)

        def keep(value):
            place(i, value[:, :half])
            m.half_out[i] = value[:, half:].astype(jnp.bfloat16)

        back_tail(m, m.tokens.at[i], gradient, m.total[...], keep)
        send_half(i).start()
        start(puts(i), mixed, proj)
        branch_copy(m.landed, i).wait()
        return carry

    def second_both(found, i, carry):
        m.need = needs(found, i)
        branch_copy(m.targets, i).start()
        send(i).wait_recv()
        settle(i, n1, att, n2)
        arrived = m.landed.at[i]
        forward_front(m, arrived, length)
        start(puts(i), n1, att, n2)
        settle(i, active, hidden)
        m.need(m.up_w)
        m.need(m.down_w)
        gradient = m.targets.at[i]
        both_expert(m, gradient)
        start(puts(i), active, hidden)
        settle(i, mixed, proj)

        def keep(value):
            m.leaving[i] = value.astype(jnp.bfloat16)

        back_tail(m, arrived, gradient, m.total[...], keep)
        send(i).start()
        start(puts(i), mixed, proj)
        branch_copy(m.targets, i).wait()
        return carry

    m.sums[...] = jnp.zeros(m.sums.shape, jnp.float32)
    barrier = pltpu.get_barrier_semaphore()
    pl.semaphore_signal(barrier, inc=1, device_id=across, device_id_type=MESH)

    @pl.when(section == 0)
    def _():
        found = weights((0, 1))
        start_weights(found)
        pl.semaphore_wait(barrier, 1)
        lax.fori_loop(0, items, functools.partial(first_front, found), 0)
        wait(puts(0), n1, att, n2, active, qkv, probs, turned, middle, slope)
        lax.fori_loop(0, items, first_back, 0)
        wait(puts(0), mixed, proj, hidden)
        send(items - 1).wait_send()
        for i in range(items):
            send_half(i).wait_send()

    @pl.when(section == 1)
    def _():
        found = weights((2,))
        start_weights(found)
        for i in range(items):
            text_first(m.targets, m.cotangent, i)
            mask_targets(i)
        pl.semaphore_wait(barrier, 1)
        lax.fori_loop(0, items, functools.partial(second_both, found), 0)
        wait(puts(0), n1, att, n2, active, mixed, proj, hidden)
        for i in range(items):
            send(i).wait_send()
            send_half(i).wait_recv()
            place(i, m.half_in[i].astype(jnp.float32))


def both_layers(
    tokens, cotangent, patch_mask, text_mask, qkv_weight, out_weight, up_table, down_table, qv, proj, gain, shift, up_b, down_b
):
    items, length, width = tokens.shape
    rows = ROWS
    ff = up_b.shape[1]
    heads = width // HEAD_DIM
    bf16, f32 = jnp.bfloat16, jnp.float32
    dma = pltpu.SemaphoreType.DMA
    vmem, anywhere = pl.BlockSpec(memory_space=pltpu.VMEM), pl.BlockSpec(memory_space=pl.ANY)
    ins = dict(
        in_tokens=(tokens, vmem), cotangent=(cotangent, vmem), patch_mask=(patch_mask, vmem), text_mask=(text_mask, vmem), in_qkv=(qkv_weight, anywhere), in_out=(out_weight, anywhere),
        in_up=(up_table, anywhere), in_down=(down_table, anywhere), qv=(qv, vmem), proj=(proj, vmem), gain=(gain, vmem),
        shift=(shift, vmem), up_b=(up_b, vmem), down_b=(down_b, vmem),
    )

    def made(*shape, kind=bf16, spec=anywhere):
        return jax.ShapeDtypeStruct((items,) + shape, kind), spec

    outs = dict(
        out_n1=made(rows, width), out_att=made(rows, width), out_n2=made(rows, width), out_active=made(rows, ff),
        out_mixed=made(rows, 3 * width), out_proj=made(rows, width), out_hidden=made(rows, ff), branch=made(rows, width),
        kept_qkv=made(rows, 3 * width), kept_probs=made(heads, rows, rows), kept_turned=made(width, rows),
        kept_middle=made(rows, width, kind=f32), kept_slope=made(rows, ff),
        input_grad=made(length, width // 2, kind=f32, spec=vmem),
        sums=(jax.ShapeDtypeStruct((16, CHUNK), f32), vmem),
    )
    low_row, wide_row = ((rows, width), bf16), ((rows, ff), bf16)
    buffers = dict(
        qkv_w=((width, 3 * width), bf16), out_w=((width, width), bf16), up_w=((2, width, ff), bf16),
        down_w=((2, ff, width), bf16), n1=low_row, att=low_row, n2=low_row, active=wide_row,
        qkv=((rows, 3 * width), bf16), probs=((heads, rows, rows), bf16), att_turned=((width, rows), bf16),
        middle=((rows, width), f32), slope=wide_row, total=((rows, width), f32), mixed=((rows, 3 * width), bf16),
        proj_delta=low_row, hidden_delta=wide_row, att_delta=low_row, middle_delta=((rows, width), f32),
        leaving=((items, rows, width), bf16), landed=((items, rows, width), bf16),
        half_out=((items, rows, width // 2), bf16), half_in=((items, rows, width // 2), bf16),
        tokens=((items, rows, width), bf16), targets=((items, rows, width), bf16),
    )
    semaphores = dict(
        copy_sem=dma((23,)), branch_sem=dma((items,)), send_sem=dma((items,)), recv_sem=dma((items,)),
        half_send=dma((items,)), half_recv=dma((items,)),
    )
    names = list(ins) + list(outs) + list(buffers) + list(semaphores)
    results = pl.pallas_call(
        functools.partial(layers_kernel, names),
        out_shape=[shape for shape, spec in outs.values()],
        in_specs=[spec for value, spec in ins.values()],
        out_specs=[spec for shape, spec in outs.values()],
        scratch_shapes=[pltpu.VMEM(*kind) for kind in buffers.values()] + list(semaphores.values()),
        compiler_params=pltpu.CompilerParams(
            collective_id=1, has_side_effects=True, vmem_limit_bytes=60 * 1024 * 1024
        ),
        cost_estimate=pl.CostEstimate(flops=40_000_000_000, bytes_accessed=100_000_000, transcendentals=0),
    )(*[value for value, spec in ins.values()])
    m = Refs()
    for name, result in zip(outs, results):
        setattr(m, name, result)
    return m


def small_outs(own, other, is_first, width):
    first = jnp.where(is_first, own, other)
    second = jnp.where(is_first, other, own)
    me = lax.axis_index("dp")

    def columns(rows):
        wide = rows.shape[-1] // lax.axis_size("dp")
        return lax.dynamic_slice_in_dim(rows, me * wide, wide, rows.ndim - 1)

    down = columns(jnp.concatenate([first[:2], second[:1]])[:, :width])
    up = columns(jnp.concatenate([first[9:15].reshape(2, -1), second[9:12].reshape(1, -1)]))
    own = columns(own[2:9, :width])
    return own[0:2], own[2:3], own[3:5], own[5:7], up, down


def flat(value):
    return value.reshape((-1, value.shape[-1]))


def left_parts(m, is_first):
    n1, att, n2, branch_delta = (flat(part) for part in (m.out_n1, m.out_att, m.out_n2, m.branch))
    text = (jnp.arange(n1.shape[0]) % ROWS < TEXT)[:, None]
    vision = jnp.logical_not(text & is_first).astype(jnp.bfloat16)
    text = text.astype(jnp.bfloat16)
    return [
        piece.T for piece in (n2 * vision, branch_delta * vision, n2 * text, branch_delta * text, n1, att)
    ]


def large_grads(m, is_first):
    up, down, qkv, out, smalls = summed_grads(
        m.out_n1, m.out_att, m.out_n2, m.branch, m.out_hidden, m.out_active, m.out_mixed, m.out_proj, m.sums,
    )
    qkv, out, up, down = (part.astype(jnp.float32) for part in (qkv, out, up, down))
    return qkv, out, up, down, smalls[0], smalls[1]


def large_grads_plain(m, is_first):
    lefts = left_parts(m, is_first)
    hidden_delta, active = flat(m.out_hidden), flat(m.out_active)

    def total_of(left, right):
        product = jnp.dot(left, right, preferred_element_type=jnp.float32).astype(jnp.bfloat16)
        return lax.psum_scatter(product, "dp", scatter_dimension=1, tiled=True)

    def table(vision_part, text_part):
        def swapped(part):
            return lax.psum(part, "section").astype(jnp.float32)

        return jnp.stack(
            [
                swapped(jnp.where(is_first, vision_part, 0)),
                swapped(jnp.where(is_first, text_part, 0)),
                swapped(jnp.where(is_first, 0, vision_part)),
            ]
        )

    up = table(total_of(lefts[0], hidden_delta), total_of(lefts[2], hidden_delta))
    down = table(total_of(lefts[1], active), total_of(lefts[3], active))
    small = lax.psum(m.sums, "dp")
    return (
        total_of(lefts[4], flat(m.out_mixed)).astype(jnp.float32),
        total_of(lefts[5], flat(m.out_proj)).astype(jnp.float32),
        up,
        down.transpose(0, 2, 1),
        small,
        lax.ppermute(small, "section", [(0, 1), (1, 0)]),
    )


def shards(
    tokens, cotangent, patch_mask, text_mask, qkv_weight, qv_bias, out_weight, out_bias, norm_gain, norm_bias,
    up_table, up_bias, down_table, down_bias,
):
    is_first = lax.axis_index("section") == 0
    m = both_layers(
        tokens, cotangent, patch_mask, text_mask, qkv_weight, out_weight, up_table, down_table, qv_bias[0], out_bias,
        norm_gain[0], norm_bias[0], up_bias, down_bias,
    )
    grads = large_grads if lax.axis_size("dp") == 16 else large_grads_plain
    qkv, out, up, down, own, other = grads(m, is_first)
    qv_part, proj_part, gain_part, shift_part, up_part, down_part = small_outs(own, other, is_first, tokens.shape[2])
    return (
        m.input_grad, qkv[None], qv_part[None], out[None], proj_part, gain_part[None], shift_part[None],
        up, up_part, down, down_part,
    )


def solution(mesh):
    items, layers = P("dp"), P("section")
    return jax.shard_map(
        shards,
        mesh=mesh,
        in_specs=(items,) * 4 + (layers,) * 6 + (P(),) * 4,
        out_specs=(
            P("dp", None, "section"), P("section", None, "dp"), P("section", None, "dp"), P("section", None, "dp"),
            P("section", "dp"), P("section", None, "dp"), P("section", None, "dp"),
            P(None, None, "dp"), P(None, "dp"), P(None, "dp", None), P(None, "dp"),
        ),
        check_vma=False,
    )
```

```python
import functools

import jax
import jax.numpy as jnp
from jax import lax
from jax.experimental import pallas as pl
from jax.experimental.pallas import tpu as pltpu
from jax.sharding import PartitionSpec as P

HEAD_DIM = 64
PATCHES = 197
EPSILON = 1e-05
BLOCK = 384
RING = 3
TEXT = 64
ROWS = 272
MESH = pl.DeviceIdType.MESH


UNITS = (
    (
        (3, 1, 0), (0, 1, 0), (3, 3, 0), (2, 1, 0), (3, 0, 0), (0, 3, 0), (2, 0, 1), (3, 2, 0), (0,
        0, 0), (2, 3, 1), (1, 2, 0), (0, 2, 0), (1, 0, 0), (4, 0, 1), (4, 3, 0), (4, 1, 0), (1, 3,
        0), (2, 2, 0), (1, 1, 0), (4, 2, 0),
    ),
    (
        (0, 2, 0), (0, 1, 0), (0, 3, 0), (3, 1, 0), (0, 0, 1), (1, 2, 0), (1, 3, 1), (1, 0, 0), (3,
        3, 0), (3, 0, 0), (4, 3, 1), (3, 2, 0), (1, 1, 0), (4, 2, 0), (4, 0, 0), (4, 1, 0),
    ),
)
WAIT = 3
HOP = 2
LEFT_OF = ((0,), (1,), (0,), (1,), (2, 3))


def packed(units, handed_on):
    counts = [0, 0]
    codes = []
    for kind, plane, z_first in units:
        slot = 0
        if not (handed_on and kind == 3):
            slot = counts[z_first]
            counts[z_first] += 1
        codes.append(kind | plane << 3 | z_first << 5 | slot << 6)
    codes += [0] * (-len(codes) % 3)
    return [codes[i] | codes[i + 1] << 10 | codes[i + 2] << 20 for i in range(0, len(codes), 3)], counts


PACKED, COUNTS = zip(*(packed(units, side == 0) for side, units in enumerate(UNITS)))
Y_UNITS, Z_UNITS = (max(COUNTS[0][way], COUNTS[1][way], 1) for way in range(2))


def look_up(words, u):
    word = words[0]
    for n in range(1, len(words)):
        word = jnp.where(u // 3 == n, words[n], word)
    return word >> (10 * (u % 3))


class Refs:
    pass


def sum_kernel(names, *refs):
    m = Refs()
    for name, ref in zip(names, refs):
        setattr(m, name, ref)
    section = lax.axis_index("section")
    me = lax.axis_index("dp")
    z, y, core = me // 4, (me // 2) % 2, me % 2
    peer = (section, me + 1 - 2 * core)
    beside = (section, me + 2 - 4 * y)
    right = (section, me + 4)
    left = (section, me - 4)
    across = (1 - section, me)
    on_first = section == 0
    units = jnp.where(on_first, len(UNITS[0]), len(UNITS[1]))
    computed = jnp.where(on_first, len(UNITS[0]), len(UNITS[1]) - 4)

    arrivals = [u for u, (kind, plane, z_first) in enumerate(UNITS[1]) if kind == 3]

    class Unit:
        def __init__(self, u):
            self.u = u
            code = jnp.where(on_first, look_up(PACKED[0], u), look_up(PACKED[1], u))
            self.kind = code & 7
            self.plane = (code >> 3) & 3
            self.z_first = ((code >> 5) & 1) == 1
            self.slot = (code >> 6) & 15
            self.handed_on = on_first & (self.kind == 3)
            self.handed_in = jnp.logical_not(on_first) & (self.kind == 3)
            self.y_first = jnp.logical_not(self.z_first | self.handed_on)
            self.y_slot = self.slot + jnp.where(self.z_first, Y_UNITS, 0)
            self.uses_text = jnp.logical_not(on_first) | (self.kind > 1)
            self.uses_patches = jnp.logical_not(on_first) | (self.kind < 2) | (self.kind == 4)
            self.order = u
            for at in arrivals:
                self.order = self.order - jnp.where((section == 1) & (u > at), 1, 0)

    def following(u):
        u = u + 1
        for at in arrivals:
            u = u + jnp.where((section == 1) & (u == at), 1, 0)
        return u

    def remote(src, dst, send, recv, device):
        return pltpu.make_async_remote_copy(
            src_ref=src, dst_ref=dst, send_sem=send, recv_sem=recv, device_id=device, device_id_type=MESH
        )

    def core_copy(order, b):
        slot = order % RING
        return remote(m.made.at[slot, 1 - core, b], m.xr.at[slot, b], m.core_send.at[order, b], m.core_recv.at[order, b], peer)

    def y_copy(n):
        return remote(m.part.at[n.u, 0], m.yr.at[n.y_slot], m.y_send.at[n.y_slot], m.y_recv.at[n.y_slot], beside)

    def right_copy(n):
        return remote(m.part.at[n.u, 1], m.zr.at[n.slot], m.right_send.at[n.slot], m.right_recv.at[n.slot], right)

    def left_copy(n):
        return remote(m.part.at[n.u, 1], m.zl.at[n.slot], m.left_send.at[n.slot], m.left_recv.at[n.slot], left)

    def right_pair(n):
        g = n.slot
        return remote(m.part.at[n.u], m.wr.at[g], m.right_send.at[Y_UNITS + g], m.right_recv.at[Y_UNITS + g], right)

    def left_pair(n):
        g = n.slot
        return remote(m.part.at[n.u], m.wl.at[g], m.left_send.at[Y_UNITS + g], m.left_recv.at[Y_UNITS + g], left)

    def over_copy(plane, source, target):
        return remote(m.part.at[source], m.part.at[target], m.over_send.at[plane], m.over_recv.at[plane], across)

    def over_target(plane):
        target = 0
        for at in arrivals:
            target = target + jnp.where(plane == UNITS[1][at][1], at, 0)
        return target

    def peer_copy(k):
        return remote(m.fin.at[0, core, k], m.fin.at[0, core, k], m.peer_send.at[k], m.peer_recv.at[k], peer)

    def cross_copy(k):
        return remote(m.fin.at[0, core, k], m.fin.at[1, core, k], m.cross_send.at[k], m.cross_recv.at[k], across)

    def hand_copy(k):
        return remote(m.fin.at[1, core, k], m.fin.at[1, core, k], m.hand_send.at[k], m.hand_recv.at[k], peer)

    def tile_copies(n):
        k = n.kind
        slot = n.order % 2
        wide = pl.ds(pl.multiple_of(n.plane * 2 * BLOCK, 128), 2 * BLOCK)
        cases = []
        for ref, here in ((m.hidden, (k == 0) | (k == 2)), (m.active, (k == 1) | (k == 3)), (m.joint, k == 4)):
            copy = pltpu.make_async_copy(ref.at[:, :TEXT, wide], m.text_tile.at[slot], m.text_sem.at[slot])
            cases.append((here & n.uses_text, copy))
            copy = pltpu.make_async_copy(ref.at[:, TEXT:, wide], m.patch_tile.at[slot], m.patch_sem.at[slot])
            cases.append((here & n.uses_patches, copy))
        return cases

    def start_tile(n):
        for here, copy in tile_copies(n):
            pl.when(here)(copy.start)

    def wait_tile(n):
        for here, copy in tile_copies(n):
            pl.when(here)(copy.wait)

    def add_into(target, source):
        target[...] = target[...] + source[...]

    def text_dot(index, slot, *columns):
        tile = jnp.concatenate([m.text_tile[slot, :, :, at] for at in columns], axis=2)
        return matmul(m.text_left[index], tile.reshape(-1, tile.shape[2]))

    def patch_dot(index, slot, *columns):
        tile = jnp.concatenate([m.patch_tile[slot, :, :, at] for at in columns], axis=2)
        return matmul(m.patch_left[index], tile.reshape(-1, tile.shape[2]))

    def both_dot(index, slot, *columns):
        return patch_dot(index, slot, *columns) + text_dot(index, slot, *columns)

    def compute(n):
        k = n.kind
        slot = n.order % RING

        @pl.when(n.order >= RING)
        def _():
            core_copy(n.order - RING, 0).wait_send()
            core_copy(n.order - RING, 1).wait_send()
            pl.semaphore_wait(m.credit, 1)

        @pl.when(n.order + 1 < computed)
        def _():
            start_tile(Unit(following(n.u)))

        wait_tile(n)
        tile = n.order % 2
        everything = slice(0, 2 * BLOCK)

        def put(value, columns, begin):
            for half in range(2):
                for side in range(2):
                    piece = value[half * BLOCK : (half + 1) * BLOCK, columns[side]]
                    at = slice(begin, begin + piece.shape[1])
                    m.made[slot, half, jnp.where(y == side, 1, 0), :, at] = piece.astype(jnp.bfloat16)

        sides = (slice(0, BLOCK), slice(BLOCK, 2 * BLOCK))

        @pl.when((k < 4) & jnp.logical_not(n.uses_text))
        def _():
            put(patch_dot(k % 2, tile, everything), sides, 0)

        @pl.when((k < 4) & jnp.logical_not(n.uses_patches))
        def _():
            put(text_dot(k % 2, tile, everything), sides, 0)

        @pl.when((k < 4) & n.uses_text & n.uses_patches)
        def _():
            put(both_dot(k % 2, tile, everything), sides, 0)

        @pl.when(k == 4)
        def _():
            ends = (slice(256, BLOCK), slice(BLOCK + 256, 2 * BLOCK))
            mixed = both_dot(2, tile, everything)
            proj = both_dot(3, tile, *ends)
            put(mixed, (slice(0, 256), slice(BLOCK, BLOCK + 256)), 0)
            lanes = lax.broadcasted_iota(jnp.int32, (1, 128), 1)
            last = [jnp.where(lanes < 32, mixed[:, ends[side]], proj[:, 128 * side : 128 * side + 128]) for side in range(2)]
            put(jnp.concatenate(last, axis=1), (slice(0, 128), slice(128, 256)), 256)

        core_copy(n.order, 0).start()
        core_copy(n.order, 1).start()

    def join_core(n):
        slot = n.order % RING

        @pl.when(n.handed_in)
        def _():
            over_copy(n.plane, 0, n.u).wait_recv()

        @pl.when(jnp.logical_not(n.handed_in))
        def _():
            core_copy(n.order, 0).wait_recv()
            m.part[n.u, 0] = m.made[slot, core, 0] + m.xr[slot, 0]

        pl.when(n.y_first)(lambda: y_copy(n).start())

        @pl.when(jnp.logical_not(n.handed_in))
        def _():
            core_copy(n.order, 1).wait_recv()
            m.part[n.u, 1] = m.made[slot, core, 1] + m.xr[slot, 1]

            @pl.when(n.order + RING < computed)
            def _():
                pl.semaphore_signal(m.credit, inc=1, device_id=peer, device_id_type=MESH)

        pl.when(n.handed_on)(lambda: over_copy(n.plane, n.u, over_target(n.plane)).start())

    def join_y(n):
        y_copy(n).wait_recv()
        add_into(m.part.at[n.u, 1], m.yr.at[n.y_slot])

    def take(n, one, pair, single_from, pair_from):
        @pl.when(n.y_first)
        def _():
            one(n).wait_recv()
            add_into(m.part.at[n.u, 1], single_from.at[n.slot])

        @pl.when(n.z_first)
        def _():
            pair(n).wait_recv()
            add_into(m.part.at[n.u], pair_from.at[n.slot])

    def take_right(n):
        take(n, right_copy, right_pair, m.zr, m.wr)

    def take_left(n):
        take(n, left_copy, left_pair, m.zl, m.wl)

    def pass_right(n):
        pl.when(z > 0)(lambda: take_right(n))
        pl.when(n.y_first)(lambda: right_copy(n).start())
        pl.when(n.z_first)(lambda: right_pair(n).start())

    def pass_left(n):
        pl.when(z < 3)(lambda: take_left(n))
        pl.when(n.y_first)(lambda: left_copy(n).start())
        pl.when(n.z_first)(lambda: left_pair(n).start())

    def give(n):
        k = n.kind
        m.fin[0, core, k] = m.part[n.u, 1]
        peer_copy(k).start()
        pl.when(k < 4)(lambda: cross_copy(k).start())

    def meet(n):
        pl.when(z > 0)(lambda: take_right(n))
        pl.when(z < 3)(lambda: take_left(n))
        pl.when(n.z_first)(lambda: y_copy(n).start())
        pl.when(n.y_first)(lambda: give(n))

    def meet_late(n):
        join_y(n)
        give(n)

    flips = (peer, beside, (section, me + 4 - 8 * (z % 2)), (section, me + 8 - 16 * (z // 2)), across)

    def small_copy(j):
        return remote(m.small_sum.at[j], m.small_in.at[j], m.small_send.at[j], m.small_recv.at[j], flips[j])

    def small_step(j):
        if j == 0:
            m.small_sum[0] = m.small[...]
        else:
            small_copy(j - 1).wait_recv()
            if j == 5:
                m.small_out[0] = m.small_sum[4]
                m.small_out[1] = m.small_in[4]
            else:
                m.small_sum[j] = m.small_sum[j - 1] + m.small_in[j - 1]
        if j < 5:
            small_copy(j).start()

    lefts = (m.n2, m.branch, m.n1, m.att)
    turns = [[], []]
    for side in range(2):
        for kind, plane, z_first in UNITS[side]:
            for index in LEFT_OF[kind] if (side, kind) != (1, 3) else ():
                if index not in turns[side]:
                    turns[side].append(index)

    def stage_copy(index):
        return pltpu.make_async_copy(lefts[index], m.stage, m.stage_sem.at[0])

    def start_stage(turn):
        for side in range(2):
            pl.when(section == side)(stage_copy(turns[side][turn]).start)

    def prepare(turn):
        stage_copy(0).wait()
        number = jnp.where(on_first, turns[0][turn], turns[1][turn])

        def part(c, carry):
            at = pl.ds(pl.multiple_of(c * 128, 128), 128)
            m.text_left[number, at, :] = m.stage[:, :TEXT, at].reshape(-1, 128).T
            m.patch_left[number, at, :] = m.stage[:, TEXT:, at].reshape(-1, 128).T
            return carry

        lax.fori_loop(0, m.stage.shape[2] // 128, part, 0)
        if turn < 3:
            start_stage(turn + 1)

    barrier = pltpu.get_barrier_semaphore()
    for device in (peer, beside, across, flips[3]):
        pl.semaphore_signal(barrier, inc=1, device_id=device, device_id_type=MESH)

    @pl.when(z < 3)
    def _():
        pl.semaphore_signal(barrier, inc=1, device_id=right, device_id_type=MESH)

    @pl.when(z > 0)
    def _():
        pl.semaphore_signal(barrier, inc=1, device_id=left, device_id_type=MESH)

    start_stage(0)
    start_tile(Unit(jnp.int32(0)))
    prepare(0)
    pl.semaphore_wait(barrier, 4 + jnp.where(z < 3, 1, 0) + jnp.where(z > 0, 1, 0))

    def at_unit(u, condition, action):
        n = Unit(jnp.maximum(u, 0))

        @pl.when((u >= 0) & (u < units) & condition(n))
        def _():
            action(n)

    def in_flow(n):
        return jnp.logical_not(n.handed_on)

    def step(i, carry):
        at_unit(i, lambda n: jnp.logical_not(n.handed_in), compute)
        for number in range(3):
            pl.when(i == number)(functools.partial(prepare, number + 1))
        at_unit(i - 1, lambda n: n.kind >= 0, join_core)
        at_unit(i - WAIT, lambda n: n.y_first, join_y)
        at_unit(i - WAIT - HOP * z, lambda n: in_flow(n) & (n.plane > z), pass_right)
        at_unit(i - WAIT - HOP * (3 - z), lambda n: in_flow(n) & (n.plane < z), pass_left)
        at_unit(i - WAIT - 3 * HOP - 1, lambda n: in_flow(n) & (n.plane == z), meet)
        at_unit(i - WAIT - 3 * HOP - 3, lambda n: n.z_first & (n.plane == z), meet_late)
        for j in range(6):
            pl.when(i == 3 + j)(functools.partial(small_step, j))
        return carry

    lax.fori_loop(0, units + WAIT + 3 * HOP + 3, step, 0)

    def third_kind(k):
        return jnp.where(k == 2, 2 + section, k)

    def their_kind(k):
        return jnp.where(k == 2, 3 - section, k)

    for k in range(3):
        cross_copy(their_kind(jnp.int32(k))).wait_recv()
        hand_copy(their_kind(jnp.int32(k))).start()

    def settle(u, carry):
        n = Unit(u)

        @pl.when(jnp.logical_not(n.handed_in) & (n.order >= computed - RING))
        def _():
            core_copy(n.order, 0).wait_send()
            core_copy(n.order, 1).wait_send()

        pl.when(n.handed_on)(lambda: over_copy(n.plane, n.u, over_target(n.plane)).wait_send())
        pl.when(n.y_first | (n.z_first & (n.plane == z)))(lambda: y_copy(n).wait_send())
        pl.when(n.y_first & (n.plane > z))(lambda: right_copy(n).wait_send())
        pl.when(n.z_first & (n.plane > z))(lambda: right_pair(n).wait_send())
        pl.when(n.y_first & (n.plane < z))(lambda: left_copy(n).wait_send())
        pl.when(n.z_first & (n.plane < z))(lambda: left_pair(n).wait_send())
        return carry

    lax.fori_loop(0, units, settle, 0)
    for j in range(5):
        small_copy(j).wait_send()
    for k in range(3):
        peer_copy(third_kind(jnp.int32(k))).wait()
        cross_copy(third_kind(jnp.int32(k))).wait_send()
        hand_copy(their_kind(jnp.int32(k))).wait()
    peer_copy(4).wait()

    def write(c):
        def columns(side, half, k, begin, wide):
            return m.fin[side, half, k, :, begin + c * wide : begin + (c + 1) * wide]

        first, second = section, 1 - section
        for half in range(2):
            at = slice(half * BLOCK, (half + 1) * BLOCK)
            m.qkv_out[at, :] = columns(0, half, 4, 0, 144)
            m.out_out[at, :] = columns(0, half, 4, 288, 48)
            for expert, side, k in ((0, first, 0), (1, first, 2), (2, second, 0)):
                m.up_out[expert, at, :] = columns(side, half, k, 0, 192)
            for expert, side, k in ((0, first, 1), (1, second, 3), (2, second, 1)):
                m.down_out[expert, :, at] = columns(side, half, k, 0, 192).T

    for c in range(2):
        pl.when(core == c)(functools.partial(write, c))


def summed_grads(n1, att, n2, branch, hidden, active, joint, small):
    dma = pltpu.SemaphoreType.DMA
    items, depth, width = n1.shape
    bf16, f32 = jnp.bfloat16, jnp.float32
    tile = (BLOCK, BLOCK)
    vmem, anywhere = pl.BlockSpec(memory_space=pltpu.VMEM), pl.BlockSpec(memory_space=pl.ANY)
    ins = dict(n1=n1, att=att, n2=n2, branch=branch, hidden=hidden, active=active, joint=joint, small=small)
    outs = dict(
        up_out=((3, width, 192), bf16), down_out=((3, 192, width), bf16), qkv_out=((width, 144), bf16),
        out_out=((width, 48), bf16), small_out=((2,) + small.shape, f32),
    )
    buffers = dict(
        text_tile=((2, items, TEXT, 2 * BLOCK), bf16), patch_tile=((2, items, depth - TEXT, 2 * BLOCK), bf16), part=((20, 2) + tile, bf16), made=((RING, 2, 2) + tile, bf16),
        xr=((RING, 2) + tile, bf16), yr=((Y_UNITS + Z_UNITS,) + tile, bf16), zr=((Y_UNITS,) + tile, bf16), zl=((Y_UNITS,) + tile, bf16),
        wr=((Z_UNITS, 2) + tile, bf16), wl=((Z_UNITS, 2) + tile, bf16), fin=((2, 2, 5) + tile, bf16),
        text_left=((4, width, items * TEXT), bf16), patch_left=((4, width, items * (depth - TEXT)), bf16), stage=((items, depth, width), bf16), small_sum=((5,) + small.shape, f32),
        small_in=((5,) + small.shape, f32),
    )
    semaphores = dict(
        small_send=dma((5,)), small_recv=dma((5,)), text_sem=dma((2,)), patch_sem=dma((2,)), stage_sem=dma((1,)), core_send=dma((20, 2)),
        core_recv=dma((20, 2)), y_send=dma((Y_UNITS + Z_UNITS,)), y_recv=dma((Y_UNITS + Z_UNITS,)), right_send=dma((Y_UNITS + Z_UNITS,)), right_recv=dma((Y_UNITS + Z_UNITS,)),
        left_send=dma((Y_UNITS + Z_UNITS,)), left_recv=dma((Y_UNITS + Z_UNITS,)), over_send=dma((4,)), over_recv=dma((4,)), peer_send=dma((5,)),
        peer_recv=dma((5,)), cross_send=dma((5,)), cross_recv=dma((5,)), hand_send=dma((5,)), hand_recv=dma((5,)),
        credit=pltpu.SemaphoreType.REGULAR,
    )
    names = list(ins) + list(outs) + list(buffers) + list(semaphores)
    return pl.pallas_call(
        functools.partial(sum_kernel, names),
        out_shape=[jax.ShapeDtypeStruct(*kind) for kind in outs.values()],
        in_specs=[anywhere] * 7 + [vmem],
        out_specs=[vmem] * len(outs),
        scratch_shapes=[pltpu.VMEM(*kind) for kind in buffers.values()] + list(semaphores.values()),
        compiler_params=pltpu.CompilerParams(
            collective_id=0, has_side_effects=True, vmem_limit_bytes=60 * 1024 * 1024
        ),
        cost_estimate=pl.CostEstimate(flops=48 * 2 * 768 * 384 * items * depth, bytes_accessed=40_000_000, transcendentals=0),
    )(*ins.values())


CHUNK = 1024
PIECE = 512
KEY_SPLIT = 256
TAIL = (0.319381530, -0.356563782, 1.781477937, -1.821255978, 1.330274429)
PEAK = 0.3989422804014327


def normal_parts(z):
    size = jnp.abs(z)
    scale = 1.0 + 0.2316419 * size
    t = pl.reciprocal(scale, approx=True)
    t = t * (2.0 - scale * t)
    bell = jnp.exp(-0.5 * z * z) * PEAK
    series = TAIL[4]
    for factor in TAIL[3::-1]:
        series = series * t + factor
    upper = bell * (series * t)
    return jnp.where(z >= 0, 1.0 - upper, upper), bell


def matmul(left, right):
    return jnp.dot(left, right, preferred_element_type=jnp.float32)


def matmul_turned(left, right):
    return lax.dot_general(left, right, (((1,), (1,)), ((), ())), preferred_element_type=jnp.float32)


def standardized(values):
    centre = values - jnp.mean(values, -1, keepdims=True)
    inverse = lax.rsqrt(jnp.mean(centre * centre, -1, keepdims=True) + EPSILON)
    return centre * inverse, inverse


def norm_step_back(delta, values, gain_row):
    standard, inverse = standardized(values)
    scaled = delta * gain_row
    moved = inverse * (
        scaled - jnp.mean(scaled, -1, keepdims=True) - standard * jnp.mean(scaled * standard, -1, keepdims=True)
    )
    return moved, jnp.sum(delta * standard, 0, keepdims=True), jnp.sum(delta, 0, keepdims=True)


def half_mask(half):
    lanes = lax.broadcasted_iota(jnp.int32, (1, 128), 1)
    return (lanes < 64) if half == 0 else (lanes >= 64)


def pair_columns(p, part, width):
    return slice(part * width + p * 128, part * width + p * 128 + 128)


def both_halves(pair):
    return jnp.concatenate([jnp.where(half_mask(half), pair, jnp.zeros_like(pair)) for half in range(2)], axis=0)


def in_turn(count, *stages):
    for turn in range(count + len(stages) - 1):
        for number, stage in enumerate(stages):
            if 0 <= turn - number < count:
                stage(turn - number)


def attention_forward(m, length):
    rows, width = m.att.shape

    def scores(p):
        q2 = m.qkv[:, pair_columns(p, 0, width)]
        k2 = m.qkv[:, pair_columns(p, 1, width)]
        m.scores[p % 2] = matmul_turned(both_halves(k2), q2).reshape(2, rows, rows)

    def soften(p):
        for half in range(2):
            top = m.scores[p % 2, half, :KEY_SPLIT]
            low = m.scores[p % 2, half, KEY_SPLIT:]
            key_row = KEY_SPLIT + lax.broadcasted_iota(jnp.int32, low.shape, 0)
            low = jnp.where(key_row < length, low, -1e30)
            peak = jnp.maximum(jnp.max(top, 0, keepdims=True), jnp.max(low, 0, keepdims=True))
            top = jnp.exp(top - peak)
            low = jnp.exp(low - peak)
            over = 1.0 / (jnp.sum(top, 0, keepdims=True) + jnp.sum(low, 0, keepdims=True))
            m.probs[2 * p + half, :KEY_SPLIT] = (top * over).astype(jnp.bfloat16)
            m.probs[2 * p + half, KEY_SPLIT:] = (low * over).astype(jnp.bfloat16)

    def blend(p):
        v_turned = m.qkv[:, pair_columns(p, 2, width)].T
        parts = [matmul(v_turned[64 * half : 64 * half + 64], m.probs[2 * p + half]) for half in range(2)]
        turned = jnp.concatenate(parts, axis=0)
        m.att_turned[p * 128 : p * 128 + 128, :] = turned.astype(jnp.bfloat16)
        m.att[:, p * 128 : p * 128 + 128] = turned.T.astype(jnp.bfloat16)

    in_turn(width // 128, scores, soften, blend)


def attention_back(m):
    rows, width = m.att.shape

    def probs_back(p):
        v2 = m.qkv[:, pair_columns(p, 2, width)]
        d_turned = m.att_delta[:, pair_columns(p, 0, width)].T
        m.scores[p % 2] = matmul(both_halves(v2), d_turned).reshape(2, rows, rows)
        product = d_turned.astype(jnp.float32) * m.att_turned[p * 128 : p * 128 + 128, :].astype(jnp.float32)
        for half in range(2):
            m.inner[p % 2, half] = jnp.sum(product[64 * half : 64 * half + 64], 0, keepdims=True)

    def scores_back(p):
        for half in range(2):
            probs = m.probs[2 * p + half].astype(jnp.float32)
            m.score_delta[p % 2, half] = (probs * (m.scores[p % 2, half] - m.inner[p % 2, half])).astype(jnp.bfloat16)

    def heads_back(p):
        q_at, k_at, v_at = (pair_columns(p, part, width) for part in range(3))
        score = m.score_delta[p % 2]
        probs = m.probs[2 * p : 2 * p + 2].reshape(2 * rows, rows)
        k_turned = m.qkv[:, k_at].T
        value = matmul(probs, m.att_delta[:, q_at])
        key = matmul(score.reshape(2 * rows, rows), m.qkv[:, q_at])
        query = jnp.concatenate(
            [matmul(k_turned[64 * half : 64 * half + 64], score[half]) for half in range(2)], axis=0
        )
        dq = (query.T * HEAD_DIM ** (-0.5)).astype(jnp.bfloat16)
        dk = jnp.where(half_mask(0), key[:rows], key[rows:]).astype(jnp.bfloat16)
        dv = jnp.where(half_mask(0), value[:rows], value[rows:]).astype(jnp.bfloat16)
        m.mixed[:, q_at] = dq
        m.mixed[:, k_at] = dk
        m.mixed[:, v_at] = dv
        m.sums[2:3, q_at] += jnp.sum(dq.astype(jnp.float32), 0, keepdims=True)
        m.sums[3:4, q_at] += jnp.sum(dv.astype(jnp.float32), 0, keepdims=True)

    in_turn(width // 128, probs_back, scores_back, heads_back)


def forward_front(m, x_ref, length):
    x = x_ref[...].astype(jnp.float32)
    standard, unused = standardized(x)
    m.n1[...] = (standard * m.gain[0:1] + m.shift[0:1]).astype(jnp.bfloat16)
    width = x.shape[1]
    m.need(m.qkv_w)
    value = matmul(m.n1[...], m.qkv_w[...])
    query = (value[:, :width] + m.qv[0:1]).astype(jnp.bfloat16)
    m.qkv[:, :width] = query * jnp.bfloat16(HEAD_DIM ** (-0.5))
    m.qkv[:, width : 2 * width] = value[:, width : 2 * width].astype(jnp.bfloat16)
    m.qkv[:, 2 * width :] = (value[:, 2 * width :] + m.qv[1:2]).astype(jnp.bfloat16)
    attention_forward(m, length)
    m.need(m.out_w)
    middle = x_ref[...].astype(jnp.float32) + matmul(m.att[...], m.out_w[...]) + m.proj[0:1]
    m.middle[...] = middle
    standard, unused = standardized(middle)
    m.n2[...] = (standard * m.gain[1:2] + m.shift[1:2]).astype(jnp.bfloat16)


def back_tail(m, x_ref, g_ref, n2_delta, keep):
    middle_part, gain, shift = norm_step_back(n2_delta, m.middle[...], m.gain[1:2])
    m.sums[6:7, :gain.shape[1]] += gain
    m.sums[8:9, :gain.shape[1]] += shift
    middle_delta = g_ref[...].astype(jnp.float32) + middle_part
    proj_delta = middle_delta.astype(jnp.bfloat16)
    m.sums[4:5, :gain.shape[1]] += jnp.sum(proj_delta.astype(jnp.float32), 0, keepdims=True)
    m.proj_delta[...] = proj_delta
    m.middle_delta[...] = middle_delta
    m.att_delta[...] = matmul_turned(proj_delta, m.out_w[...]).astype(jnp.bfloat16)
    attention_back(m)
    total = matmul_turned(m.mixed[...], m.qkv_w[...])
    input_part, gain, shift = norm_step_back(total, x_ref[...].astype(jnp.float32), m.gain[0:1])
    m.sums[5:6, :gain.shape[1]] += gain
    m.sums[7:8, :gain.shape[1]] += shift
    keep(m.middle_delta[...] + input_part)


def forward_expert(m, slot, begin, end):
    def columns(j):
        return slice(j * PIECE, (j + 1) * PIECE)

    def widen(j):
        hidden = matmul(m.n2[begin:end], m.up_w[slot, :, columns(j)])
        m.hidden[j % 2, begin:end] = hidden + m.up_b[slot : slot + 1, columns(j)]

    def bend(j):
        hidden = m.hidden[j % 2, begin:end]
        below, bell = normal_parts(hidden)
        m.active[begin:end, columns(j)] = (hidden * below).astype(jnp.bfloat16)
        m.slope[begin:end, columns(j)] = (below + hidden * bell).astype(jnp.bfloat16)

    in_turn(m.up_w.shape[2] // PIECE, widen, bend)
    result = matmul(m.active[begin:end], m.down_w[slot])
    m.total[begin:end] = m.middle[begin:end] + result + m.down_b[slot : slot + 1]


def add_up_sums(m, slot, begin, end):
    for j in range(m.up_w.shape[2] // CHUNK):
        piece = m.hidden_delta[begin:end, j * CHUNK : (j + 1) * CHUNK].astype(jnp.float32)
        m.sums[9 + 3 * slot + j : 10 + 3 * slot + j] += jnp.sum(piece, 0, keepdims=True)


def back_expert(m, g_ref, slot, begin, end):
    m.sums[slot : slot + 1, : g_ref.shape[1]] += jnp.sum(g_ref[begin:end].astype(jnp.float32), 0, keepdims=True)
    active_delta = matmul_turned(g_ref[begin:end], m.down_w[slot])
    m.hidden_delta[begin:end] = (active_delta * m.slope[begin:end].astype(jnp.float32)).astype(jnp.bfloat16)
    m.total[begin:end] = matmul_turned(m.hidden_delta[begin:end], m.up_w[slot])
    add_up_sums(m, slot, begin, end)


def both_expert(m, g_ref):
    m.sums[0:1, : g_ref.shape[1]] += jnp.sum(g_ref[...].astype(jnp.float32), 0, keepdims=True)

    def columns(j):
        return slice(j * PIECE, (j + 1) * PIECE)

    def widen(j):
        m.hidden[j % 2] = matmul(m.n2[...], m.up_w[0, :, columns(j)]) + m.up_b[2:3, columns(j)]
        m.active_delta[j % 2] = matmul_turned(g_ref[...], m.down_w[0, columns(j), :])

    def bend(j):
        hidden = m.hidden[j % 2]
        below, bell = normal_parts(hidden)
        m.active[:, columns(j)] = (hidden * below).astype(jnp.bfloat16)
        slope = below + hidden * bell
        m.hidden_delta[:, columns(j)] = (m.active_delta[j % 2] * slope).astype(jnp.bfloat16)

    in_turn(m.up_w.shape[2] // PIECE, widen, bend)
    m.total[...] = matmul_turned(m.hidden_delta[...], m.up_w[0])
    add_up_sums(m, 0, 0, ROWS)


def join_columns(m):
    chips = m.joint.shape[1] // BLOCK
    mixed, proj = m.mixed.shape[1] // chips, m.proj_delta.shape[1] // chips
    for t in range(chips):
        m.joint[:, t * BLOCK : t * BLOCK + mixed] = m.mixed[:, t * mixed : (t + 1) * mixed]
        m.joint[:, t * BLOCK + mixed : (t + 1) * BLOCK] = m.proj_delta[:, t * proj : (t + 1) * proj]


def layers_kernel(names, *refs):
    m = Refs()
    for name, ref in zip(names, refs):
        setattr(m, name, ref)
    items, length = m.in_tokens.shape[:2]
    half = m.total.shape[1] // 2
    section = lax.axis_index("section")
    across = (1 - section, lax.axis_index("dp"))

    def send(i):
        return pltpu.make_async_remote_copy(
            src_ref=m.leaving.at[i], dst_ref=m.landed.at[i], send_sem=m.send_sem.at[i], recv_sem=m.recv_sem.at[i],
            device_id=across, device_id_type=MESH,
        )

    def send_half(i):
        return pltpu.make_async_remote_copy(
            src_ref=m.half_out.at[i], dst_ref=m.half_in.at[i], send_sem=m.half_send.at[i], recv_sem=m.half_recv.at[i],
            device_id=across, device_id_type=MESH,
        )

    def local(source, target, number):
        return pltpu.make_async_copy(source, target, m.copy_sem.at[number])

    def branch_copy(source, i):
        return pltpu.make_async_copy(source.at[i], m.branch.at[i], m.branch_sem.at[i])

    def weights(experts):
        found = [
            (m.qkv_w, [local(m.in_qkv.at[0], m.qkv_w, 0)]),
            (m.out_w, [local(m.in_out.at[0], m.out_w, 1)]),
            (m.up_w, []),
            (m.down_w, []),
        ]
        for slot, expert in enumerate(experts):
            found[2][1].append(local(m.in_up.at[expert], m.up_w.at[slot], 2 + slot))
            found[3][1].append(local(m.in_down.at[expert], m.down_w.at[slot], 4 + slot))
        return found

    def start_weights(found):
        copies = found[0][1] + found[1][1]
        for pair in zip(found[2][1], found[3][1]):
            copies += pair
        for copy in copies:
            copy.start()

    def needs(found, i):
        def need(ref):
            for here, copies in found:
                if here is ref:

                    @pl.when(i == 0)
                    def _():
                        for copy in copies:
                            copy.wait()

        return need

    leaving = (
        (m.n1, m.out_n1), (m.att, m.out_att), (m.n2, m.out_n2), (m.active, m.out_active), (m.qkv, m.kept_qkv),
        (m.probs, m.kept_probs), (m.att_turned, m.kept_turned), (m.middle, m.kept_middle), (m.slope, m.kept_slope),
        (m.joint, m.out_joint), (m.hidden_delta, m.out_hidden),
    )
    n1, att, n2, active, qkv, probs, turned, middle, slope, joint, hidden = range(len(leaving))

    def puts(i):
        return lambda number: local(leaving[number][0], leaving[number][1].at[i], 6 + number)

    def gets(i):
        return lambda number: local(leaving[number][1].at[i], leaving[number][0], 14 + number)

    def start(copies, *which):
        for number in which:
            copies(number).start()

    def wait(copies, *which):
        for number in which:
            copies(number).wait()

    def settle(i, *which):
        @pl.when(i > 0)
        def _():
            wait(puts(i), *which)

    def text_first(target, source, i):
        value = source[i].astype(jnp.float32)
        pad = jnp.zeros((ROWS - length, value.shape[1]), jnp.float32)
        target[i, :TEXT] = value[PATCHES:].astype(jnp.bfloat16)
        target[i, TEXT:] = jnp.concatenate([value[:PATCHES], pad], axis=0).astype(jnp.bfloat16)

    def mask_targets(i):
        row = lax.broadcasted_iota(jnp.int32, (ROWS, 1), 0)
        position = jnp.where(row < TEXT, row + PATCHES, jnp.where(row < length, row - TEXT, length))
        chosen = jnp.zeros((ROWS, 1), jnp.float32)
        for mask in (m.patch_mask, m.text_mask):
            same = jnp.where(position == mask[i : i + 1, :], 1.0, 0.0)
            chosen = jnp.maximum(chosen, jnp.max(same, 1, keepdims=True))
        m.targets[i] = (m.targets[i].astype(jnp.float32) * chosen).astype(jnp.bfloat16)

    def place(i, value):
        m.input_grad[i, :PATCHES] = value[TEXT:length]
        m.input_grad[i, PATCHES:] = value[:TEXT]

    def first_front(found, i, carry):
        m.need = needs(found, i)
        text_first(m.tokens, m.in_tokens, i)
        settle(i, n1, att, n2, qkv, probs, turned, middle)
        forward_front(m, m.tokens.at[i], length)
        start(puts(i), n1, att, n2, qkv, probs, turned, middle)
        settle(i, active, slope)
        m.need(m.up_w)
        m.need(m.down_w)
        forward_expert(m, 1, 0, TEXT)
        forward_expert(m, 0, TEXT, ROWS)
        m.leaving[i] = m.total[...].astype(jnp.bfloat16)
        send(i).start()
        start(puts(i), active, slope)
        return carry

    def first_back(i, carry):
        start(gets(i), slope, middle, turned, qkv, probs)

        @pl.when(i > 0)
        def _():
            send(i - 1).wait_send()

        send(i).wait_recv()
        branch_copy(m.landed, i).start()
        settle(i, hidden)
        wait(gets(i), slope)
        gradient = m.landed.at[i]
        back_expert(m, gradient, 1, 0, TEXT)
        back_expert(m, gradient, 0, TEXT, ROWS)
        start(puts(i), hidden)
        wait(gets(i), middle, turned, qkv, probs)

        def keep(value):
            place(i, value[:, :half])
            m.half_out[i] = value[:, half:].astype(jnp.bfloat16)

        back_tail(m, m.tokens.at[i], gradient, m.total[...], keep)
        send_half(i).start()
        settle(i, joint)
        join_columns(m)
        start(puts(i), joint)
        branch_copy(m.landed, i).wait()
        return carry

    def second_both(found, i, carry):
        m.need = needs(found, i)
        branch_copy(m.targets, i).start()
        send(i).wait_recv()
        settle(i, n1, att, n2)
        arrived = m.landed.at[i]
        forward_front(m, arrived, length)
        start(puts(i), n1, att, n2)
        settle(i, active, hidden)
        m.need(m.up_w)
        m.need(m.down_w)
        gradient = m.targets.at[i]
        both_expert(m, gradient)
        start(puts(i), active, hidden)

        def keep(value):
            m.leaving[i] = value.astype(jnp.bfloat16)

        back_tail(m, arrived, gradient, m.total[...], keep)
        send(i).start()
        settle(i, joint)
        join_columns(m)
        start(puts(i), joint)
        branch_copy(m.targets, i).wait()
        return carry

    m.sums[...] = jnp.zeros(m.sums.shape, jnp.float32)
    barrier = pltpu.get_barrier_semaphore()
    pl.semaphore_signal(barrier, inc=1, device_id=across, device_id_type=MESH)

    @pl.when(section == 0)
    def _():
        found = weights((0, 1))
        start_weights(found)
        pl.semaphore_wait(barrier, 1)
        lax.fori_loop(0, items, functools.partial(first_front, found), 0)
        wait(puts(0), n1, att, n2, active, qkv, probs, turned, middle, slope)
        lax.fori_loop(0, items, first_back, 0)
        wait(puts(0), joint, hidden)
        send(items - 1).wait_send()
        for i in range(items):
            send_half(i).wait_send()

    @pl.when(section == 1)
    def _():
        found = weights((2,))
        start_weights(found)
        for i in range(items):
            text_first(m.targets, m.cotangent, i)
            mask_targets(i)
        pl.semaphore_wait(barrier, 1)
        lax.fori_loop(0, items, functools.partial(second_both, found), 0)
        wait(puts(0), n1, att, n2, active, joint, hidden)
        for i in range(items):
            send(i).wait_send()
            send_half(i).wait_recv()
            place(i, m.half_in[i].astype(jnp.float32))


def both_layers(
    tokens, cotangent, patch_mask, text_mask, qkv_weight, out_weight, up_table, down_table, qv, proj, gain, shift, up_b, down_b
):
    items, length, width = tokens.shape
    rows = ROWS
    ff = up_b.shape[1]
    heads = width // HEAD_DIM
    bf16, f32 = jnp.bfloat16, jnp.float32
    dma = pltpu.SemaphoreType.DMA
    vmem, anywhere = pl.BlockSpec(memory_space=pltpu.VMEM), pl.BlockSpec(memory_space=pl.ANY)
    ins = dict(
        in_tokens=(tokens, vmem), cotangent=(cotangent, vmem), patch_mask=(patch_mask, vmem), text_mask=(text_mask, vmem), in_qkv=(qkv_weight, anywhere), in_out=(out_weight, anywhere),
        in_up=(up_table, anywhere), in_down=(down_table, anywhere), qv=(qv, vmem), proj=(proj, vmem), gain=(gain, vmem),
        shift=(shift, vmem), up_b=(up_b, vmem), down_b=(down_b, vmem),
    )

    def made(*shape, kind=bf16, spec=anywhere):
        return jax.ShapeDtypeStruct((items,) + shape, kind), spec

    outs = dict(
        out_n1=made(rows, width), out_att=made(rows, width), out_n2=made(rows, width), out_active=made(rows, ff),
        out_joint=made(rows, 4 * width), out_hidden=made(rows, ff), branch=made(rows, width),
        kept_qkv=made(rows, 3 * width), kept_probs=made(heads, rows, rows), kept_turned=made(width, rows),
        kept_middle=made(rows, width, kind=f32), kept_slope=made(rows, ff),
        input_grad=made(length, width // 2, kind=f32, spec=vmem),
        sums=(jax.ShapeDtypeStruct((16, CHUNK), f32), vmem),
    )
    low_row, wide_row = ((rows, width), bf16), ((rows, ff), bf16)
    buffers = dict(
        qkv_w=((width, 3 * width), bf16), out_w=((width, width), bf16), up_w=((2, width, ff), bf16),
        down_w=((2, ff, width), bf16), n1=low_row, att=low_row, n2=low_row, active=wide_row,
        qkv=((rows, 3 * width), bf16), probs=((heads, rows, rows), bf16), att_turned=((width, rows), bf16),
        middle=((rows, width), f32), slope=wide_row, total=((rows, width), f32), mixed=((rows, 3 * width), bf16),
        proj_delta=low_row, joint=((rows, 4 * width), bf16), scores=((2, 2, rows, rows), f32),
        score_delta=((2, 2, rows, rows), bf16), inner=((2, 2, 1, rows), f32), hidden=((2, rows, PIECE), f32),
        active_delta=((2, rows, PIECE), f32), hidden_delta=wide_row, att_delta=low_row, middle_delta=((rows, width), f32),
        leaving=((items, rows, width), bf16), landed=((items, rows, width), bf16),
        half_out=((items, rows, width // 2), bf16), half_in=((items, rows, width // 2), bf16),
        tokens=((items, rows, width), bf16), targets=((items, rows, width), bf16),
    )
    semaphores = dict(
        copy_sem=dma((23,)), branch_sem=dma((items,)), send_sem=dma((items,)), recv_sem=dma((items,)),
        half_send=dma((items,)), half_recv=dma((items,)),
    )
    names = list(ins) + list(outs) + list(buffers) + list(semaphores)
    results = pl.pallas_call(
        functools.partial(layers_kernel, names),
        out_shape=[shape for shape, spec in outs.values()],
        in_specs=[spec for value, spec in ins.values()],
        out_specs=[spec for shape, spec in outs.values()],
        scratch_shapes=[pltpu.VMEM(*kind) for kind in buffers.values()] + list(semaphores.values()),
        compiler_params=pltpu.CompilerParams(
            collective_id=1, has_side_effects=True, vmem_limit_bytes=60 * 1024 * 1024
        ),
        cost_estimate=pl.CostEstimate(flops=40_000_000_000, bytes_accessed=100_000_000, transcendentals=0),
    )(*[value for value, spec in ins.values()])
    m = Refs()
    for name, result in zip(outs, results):
        setattr(m, name, result)
    return m


def small_outs(own, other, is_first, width):
    first = jnp.where(is_first, own, other)
    second = jnp.where(is_first, other, own)
    me = lax.axis_index("dp")

    def columns(rows):
        wide = rows.shape[-1] // lax.axis_size("dp")
        return lax.dynamic_slice_in_dim(rows, me * wide, wide, rows.ndim - 1)

    down = columns(jnp.concatenate([first[:2], second[:1]])[:, :width])
    up = columns(jnp.concatenate([first[9:15].reshape(2, -1), second[9:12].reshape(1, -1)]))
    own = columns(own[2:9, :width])
    return own[0:2], own[2:3], own[3:5], own[5:7], up, down


def flat(value):
    return value.reshape((-1, value.shape[-1]))


def left_parts(m, is_first):
    n1, att, n2, branch_delta = (flat(part) for part in (m.out_n1, m.out_att, m.out_n2, m.branch))
    text = (jnp.arange(n1.shape[0]) % ROWS < TEXT)[:, None]
    vision = jnp.logical_not(text & is_first).astype(jnp.bfloat16)
    text = text.astype(jnp.bfloat16)
    return [
        piece.T for piece in (n2 * vision, branch_delta * vision, n2 * text, branch_delta * text, n1, att)
    ]


def large_grads(m, is_first):
    up, down, qkv, out, smalls = summed_grads(
        m.out_n1, m.out_att, m.out_n2, m.branch, m.out_hidden, m.out_active, m.out_joint, m.sums,
    )
    qkv, out, up, down = (part.astype(jnp.float32) for part in (qkv, out, up, down))
    return qkv, out, up, down, smalls[0], smalls[1]


def large_grads_plain(m, is_first):
    lefts = left_parts(m, is_first)
    hidden_delta, active = flat(m.out_hidden), flat(m.out_active)

    def total_of(left, right):
        product = jnp.dot(left, right, preferred_element_type=jnp.float32).astype(jnp.bfloat16)
        return lax.psum_scatter(product, "dp", scatter_dimension=1, tiled=True)

    def table(vision_part, text_part):
        def swapped(part):
            return lax.psum(part, "section").astype(jnp.float32)

        return jnp.stack(
            [
                swapped(jnp.where(is_first, vision_part, 0)),
                swapped(jnp.where(is_first, text_part, 0)),
                swapped(jnp.where(is_first, 0, vision_part)),
            ]
        )

    up = table(total_of(lefts[0], hidden_delta), total_of(lefts[2], hidden_delta))
    down = table(total_of(lefts[1], active), total_of(lefts[3], active))
    small = lax.psum(m.sums, "dp")
    joint = flat(m.out_joint)
    joint = joint.reshape(joint.shape[0], -1, BLOCK)
    mixed, proj = (part.reshape(joint.shape[0], -1) for part in (joint[:, :, :288], joint[:, :, 288:]))
    return (
        total_of(lefts[4], mixed).astype(jnp.float32),
        total_of(lefts[5], proj).astype(jnp.float32),
        up,
        down.transpose(0, 2, 1),
        small,
        lax.ppermute(small, "section", [(0, 1), (1, 0)]),
    )


def shards(
    tokens, cotangent, patch_mask, text_mask, qkv_weight, qv_bias, out_weight, out_bias, norm_gain, norm_bias,
    up_table, up_bias, down_table, down_bias,
):
    is_first = lax.axis_index("section") == 0
    m = both_layers(
        tokens, cotangent, patch_mask, text_mask, qkv_weight, out_weight, up_table, down_table, qv_bias[0], out_bias,
        norm_gain[0], norm_bias[0], up_bias, down_bias,
    )
    grads = large_grads if lax.axis_size("dp") == 16 else large_grads_plain
    qkv, out, up, down, own, other = grads(m, is_first)
    qv_part, proj_part, gain_part, shift_part, up_part, down_part = small_outs(own, other, is_first, tokens.shape[2])
    return (
        m.input_grad, qkv[None], qv_part[None], out[None], proj_part, gain_part[None], shift_part[None],
        up, up_part, down, down_part,
    )


def solution(mesh):
    items, layers = P("dp"), P("section")
    return jax.shard_map(
        shards,
        mesh=mesh,
        in_specs=(items,) * 4 + (layers,) * 6 + (P(),) * 4,
        out_specs=(
            P("dp", None, "section"), P("section", None, "dp"), P("section", None, "dp"), P("section", None, "dp"),
            P("section", "dp"), P("section", None, "dp"), P("section", None, "dp"),
            P(None, None, "dp"), P(None, "dp"), P(None, "dp", None), P(None, "dp"),
        ),
        check_vma=False,
    )
```

```python
import functools

import jax
import jax.numpy as jnp
from jax import lax
from jax.experimental import pallas as pl
from jax.experimental.pallas import tpu as pltpu
from jax.sharding import PartitionSpec as P

HEAD_DIM = 64
PATCHES = 197
EPSILON = 1e-05
BLOCK = 384
RING = 3
TEXT = 64
ROWS = 272
MESH = pl.DeviceIdType.MESH


UNITS = (
    (
        (2, 2, 0), (3, 0, 0), (2, 3, 1), (1, 1, 0), (1, 0, 1), (3, 1, 0), (2, 1, 0), (0, 2, 0), (3,
        3, 0), (0, 0, 0), (0, 3, 1), (2, 0, 0), (1, 3, 0), (4, 0, 1), (4, 3, 0), (3, 2, 0), (0, 1,
        0), (1, 2, 0), (4, 1, 0), (4, 2, 0),
    ),
    (
        (1, 2, 0), (0, 3, 1), (0, 0, 0), (0, 1, 0), (1, 1, 0), (1, 0, 0), (3, 0, 1), (1, 3, 0), (4,
        3, 0), (4, 0, 1), (3, 3, 0), (0, 2, 0), (3, 1, 0), (4, 1, 0), (3, 2, 0), (4, 2, 0),
    ),
)
WAIT = 4
HOP = 3
LEFT_OF = ((0,), (1,), (0,), (1,), (2, 3))


def packed(units, handed_on):
    counts = [0, 0]
    codes = []
    for kind, plane, z_first in units:
        slot = 0
        if not (handed_on and kind == 3):
            slot = counts[z_first]
            counts[z_first] += 1
        codes.append(kind | plane << 3 | z_first << 5 | slot << 6)
    codes += [0] * (-len(codes) % 3)
    return [codes[i] | codes[i + 1] << 10 | codes[i + 2] << 20 for i in range(0, len(codes), 3)], counts


PACKED, COUNTS = zip(*(packed(units, side == 0) for side, units in enumerate(UNITS)))
Y_UNITS, Z_UNITS = (max(COUNTS[0][way], COUNTS[1][way], 1) for way in range(2))


def look_up(words, u):
    word = words[0]
    for n in range(1, len(words)):
        word = jnp.where(u // 3 == n, words[n], word)
    return word >> (10 * (u % 3))


class Refs:
    pass


def sum_kernel(names, *refs):
    m = Refs()
    for name, ref in zip(names, refs):
        setattr(m, name, ref)
    section = lax.axis_index("section")
    me = lax.axis_index("dp")
    z, y, core = me // 4, (me // 2) % 2, me % 2
    peer = (section, me + 1 - 2 * core)
    beside = (section, me + 2 - 4 * y)
    right = (section, me + 4)
    left = (section, me - 4)
    across = (1 - section, me)
    on_first = section == 0
    units = jnp.where(on_first, len(UNITS[0]), len(UNITS[1]))
    computed = jnp.where(on_first, len(UNITS[0]), len(UNITS[1]) - 4)

    arrivals = [u for u, (kind, plane, z_first) in enumerate(UNITS[1]) if kind == 3]

    class Unit:
        def __init__(self, u):
            self.u = u
            code = jnp.where(on_first, look_up(PACKED[0], u), look_up(PACKED[1], u))
            self.kind = code & 7
            self.plane = (code >> 3) & 3
            self.z_first = ((code >> 5) & 1) == 1
            self.slot = (code >> 6) & 15
            self.handed_on = on_first & (self.kind == 3)
            self.handed_in = jnp.logical_not(on_first) & (self.kind == 3)
            self.y_first = jnp.logical_not(self.z_first | self.handed_on)
            self.y_slot = self.slot + jnp.where(self.z_first, Y_UNITS, 0)
            self.uses_text = jnp.logical_not(on_first) | (self.kind > 1)
            self.uses_patches = jnp.logical_not(on_first) | (self.kind < 2) | (self.kind == 4)
            self.order = u
            for at in arrivals:
                self.order = self.order - jnp.where((section == 1) & (u > at), 1, 0)

    def following(u):
        u = u + 1
        for at in arrivals:
            u = u + jnp.where((section == 1) & (u == at), 1, 0)
        return u

    def remote(src, dst, send, recv, device):
        return pltpu.make_async_remote_copy(
            src_ref=src, dst_ref=dst, send_sem=send, recv_sem=recv, device_id=device, device_id_type=MESH
        )

    def core_copy(order, b):
        slot = order % RING
        return remote(m.made.at[slot, 1 - core, b], m.xr.at[slot, b], m.core_send.at[order, b], m.core_recv.at[order, b], peer)

    def y_copy(n):
        return remote(m.part.at[n.u, 0], m.yr.at[n.y_slot], m.y_send.at[n.y_slot], m.y_recv.at[n.y_slot], beside)

    def right_copy(n):
        return remote(m.part.at[n.u, 1], m.zr.at[n.slot], m.right_send.at[n.slot], m.right_recv.at[n.slot], right)

    def left_copy(n):
        return remote(m.part.at[n.u, 1], m.zl.at[n.slot], m.left_send.at[n.slot], m.left_recv.at[n.slot], left)

    def right_pair(n):
        g = n.slot
        return remote(m.part.at[n.u], m.wr.at[g], m.right_send.at[Y_UNITS + g], m.right_recv.at[Y_UNITS + g], right)

    def left_pair(n):
        g = n.slot
        return remote(m.part.at[n.u], m.wl.at[g], m.left_send.at[Y_UNITS + g], m.left_recv.at[Y_UNITS + g], left)

    def over_copy(plane, source, target):
        return remote(m.part.at[source], m.part.at[target], m.over_send.at[plane], m.over_recv.at[plane], across)

    def over_target(plane):
        target = 0
        for at in arrivals:
            target = target + jnp.where(plane == UNITS[1][at][1], at, 0)
        return target

    def peer_copy(k):
        return remote(m.fin.at[0, core, k], m.fin.at[0, core, k], m.peer_send.at[k], m.peer_recv.at[k], peer)

    def cross_copy(k):
        return remote(m.fin.at[0, core, k], m.fin.at[1, core, k], m.cross_send.at[k], m.cross_recv.at[k], across)

    def hand_copy(k):
        return remote(m.fin.at[1, core, k], m.fin.at[1, core, k], m.hand_send.at[k], m.hand_recv.at[k], peer)

    def tile_copies(n):
        k = n.kind
        slot = n.order % 2
        wide = pl.ds(pl.multiple_of(n.plane * 2 * BLOCK, 128), 2 * BLOCK)
        cases = []
        for ref, here in ((m.hidden, (k == 0) | (k == 2)), (m.active, (k == 1) | (k == 3)), (m.joint, k == 4)):
            copy = pltpu.make_async_copy(ref.at[:, :TEXT, wide], m.text_tile.at[slot], m.text_sem.at[slot])
            cases.append((here & n.uses_text, copy))
            copy = pltpu.make_async_copy(ref.at[:, TEXT:, wide], m.patch_tile.at[slot], m.patch_sem.at[slot])
            cases.append((here & n.uses_patches, copy))
        return cases

    def start_tile(n):
        for here, copy in tile_copies(n):
            pl.when(here)(copy.start)

    def wait_tile(n):
        for here, copy in tile_copies(n):
            pl.when(here)(copy.wait)

    def add_into(target, source):
        target[...] = target[...] + source[...]

    def text_dot(index, slot, *columns):
        tile = jnp.concatenate([m.text_tile[slot, :, :, at] for at in columns], axis=2)
        return matmul(m.text_left[index], tile.reshape(-1, tile.shape[2]))

    def patch_dot(index, slot, *columns):
        tile = jnp.concatenate([m.patch_tile[slot, :, :, at] for at in columns], axis=2)
        return matmul(m.patch_left[index], tile.reshape(-1, tile.shape[2]))

    def both_dot(index, slot, *columns):
        return patch_dot(index, slot, *columns) + text_dot(index, slot, *columns)

    def compute(n):
        k = n.kind
        slot = n.order % RING

        @pl.when(n.order >= RING)
        def _():
            core_copy(n.order - RING, 0).wait_send()
            core_copy(n.order - RING, 1).wait_send()
            pl.semaphore_wait(m.credit, 1)

        @pl.when(n.order + 1 < computed)
        def _():
            start_tile(Unit(following(n.u)))

        wait_tile(n)
        tile = n.order % 2
        everything = slice(0, 2 * BLOCK)

        def put(value, columns, begin):
            for half in range(2):
                for side in range(2):
                    piece = value[half * BLOCK : (half + 1) * BLOCK, columns[side]]
                    at = slice(begin, begin + piece.shape[1])
                    m.made[slot, half, jnp.where(y == side, 1, 0), :, at] = piece.astype(jnp.bfloat16)

        sides = (slice(0, BLOCK), slice(BLOCK, 2 * BLOCK))

        @pl.when((k < 4) & jnp.logical_not(n.uses_text))
        def _():
            put(patch_dot(k % 2, tile, everything), sides, 0)

        @pl.when((k < 4) & jnp.logical_not(n.uses_patches))
        def _():
            put(text_dot(k % 2, tile, everything), sides, 0)

        @pl.when((k < 4) & n.uses_text & n.uses_patches)
        def _():
            put(both_dot(k % 2, tile, everything), sides, 0)

        @pl.when(k == 4)
        def _():
            ends = (slice(256, BLOCK), slice(BLOCK + 256, 2 * BLOCK))
            mixed = both_dot(2, tile, everything)
            proj = both_dot(3, tile, *ends)
            put(mixed, (slice(0, 256), slice(BLOCK, BLOCK + 256)), 0)
            lanes = lax.broadcasted_iota(jnp.int32, (1, 128), 1)
            last = [jnp.where(lanes < 32, mixed[:, ends[side]], proj[:, 128 * side : 128 * side + 128]) for side in range(2)]
            put(jnp.concatenate(last, axis=1), (slice(0, 128), slice(128, 256)), 256)

        core_copy(n.order, 0).start()
        core_copy(n.order, 1).start()

    def join_core(n):
        slot = n.order % RING

        @pl.when(n.handed_in)
        def _():
            over_copy(n.plane, 0, n.u).wait_recv()

        @pl.when(jnp.logical_not(n.handed_in))
        def _():
            core_copy(n.order, 0).wait_recv()
            m.part[n.u, 0] = m.made[slot, core, 0] + m.xr[slot, 0]

        pl.when(n.y_first)(lambda: y_copy(n).start())

        @pl.when(jnp.logical_not(n.handed_in))
        def _():
            core_copy(n.order, 1).wait_recv()
            m.part[n.u, 1] = m.made[slot, core, 1] + m.xr[slot, 1]

            @pl.when(n.order + RING < computed)
            def _():
                pl.semaphore_signal(m.credit, inc=1, device_id=peer, device_id_type=MESH)

        pl.when(n.handed_on)(lambda: over_copy(n.plane, n.u, over_target(n.plane)).start())

    def join_y(n):
        y_copy(n).wait_recv()
        add_into(m.part.at[n.u, 1], m.yr.at[n.y_slot])

    def take(n, one, pair, single_from, pair_from):
        @pl.when(n.y_first)
        def _():
            one(n).wait_recv()
            add_into(m.part.at[n.u, 1], single_from.at[n.slot])

        @pl.when(n.z_first)
        def _():
            pair(n).wait_recv()
            add_into(m.part.at[n.u], pair_from.at[n.slot])

    def take_right(n):
        take(n, right_copy, right_pair, m.zr, m.wr)

    def take_left(n):
        take(n, left_copy, left_pair, m.zl, m.wl)

    def pass_right(n):
        pl.when(z > 0)(lambda: take_right(n))
        pl.when(n.y_first)(lambda: right_copy(n).start())
        pl.when(n.z_first)(lambda: right_pair(n).start())

    def pass_left(n):
        pl.when(z < 3)(lambda: take_left(n))
        pl.when(n.y_first)(lambda: left_copy(n).start())
        pl.when(n.z_first)(lambda: left_pair(n).start())

    def give(n):
        k = n.kind
        m.fin[0, core, k] = m.part[n.u, 1]
        peer_copy(k).start()
        pl.when(k < 4)(lambda: cross_copy(k).start())

    def meet(n):
        pl.when(z > 0)(lambda: take_right(n))
        pl.when(z < 3)(lambda: take_left(n))
        pl.when(n.z_first)(lambda: y_copy(n).start())
        pl.when(n.y_first)(lambda: give(n))

    def meet_late(n):
        join_y(n)
        give(n)

    flips = (peer, beside, (section, me + 4 - 8 * (z % 2)), (section, me + 8 - 16 * (z // 2)), across)

    def small_copy(j):
        return remote(m.small_sum.at[j], m.small_in.at[j], m.small_send.at[j], m.small_recv.at[j], flips[j])

    def small_step(j):
        if j == 0:
            m.small_sum[0] = m.small[...]
        else:
            small_copy(j - 1).wait_recv()
            if j == 5:
                m.small_out[0] = m.small_sum[4]
                m.small_out[1] = m.small_in[4]
            else:
                m.small_sum[j] = m.small_sum[j - 1] + m.small_in[j - 1]
        if j < 5:
            small_copy(j).start()

    lefts = (m.n2, m.branch, m.n1, m.att)
    turns = [[], []]
    for side in range(2):
        for kind, plane, z_first in UNITS[side]:
            for index in LEFT_OF[kind] if (side, kind) != (1, 3) else ():
                if index not in turns[side]:
                    turns[side].append(index)

    def stage_copy(index):
        return pltpu.make_async_copy(lefts[index], m.stage, m.stage_sem.at[0])

    def start_stage(turn):
        for side in range(2):
            pl.when(section == side)(stage_copy(turns[side][turn]).start)

    def prepare(turn):
        stage_copy(0).wait()
        number = jnp.where(on_first, turns[0][turn], turns[1][turn])

        def part(c, carry):
            at = pl.ds(pl.multiple_of(c * 128, 128), 128)
            m.text_left[number, at, :] = m.stage[:, :TEXT, at].reshape(-1, 128).T
            m.patch_left[number, at, :] = m.stage[:, TEXT:, at].reshape(-1, 128).T
            return carry

        lax.fori_loop(0, m.stage.shape[2] // 128, part, 0)
        if turn < 3:
            start_stage(turn + 1)

    barrier = pltpu.get_barrier_semaphore()
    for device in (peer, beside, across, flips[3]):
        pl.semaphore_signal(barrier, inc=1, device_id=device, device_id_type=MESH)

    @pl.when(z < 3)
    def _():
        pl.semaphore_signal(barrier, inc=1, device_id=right, device_id_type=MESH)

    @pl.when(z > 0)
    def _():
        pl.semaphore_signal(barrier, inc=1, device_id=left, device_id_type=MESH)

    start_stage(0)
    start_tile(Unit(jnp.int32(0)))
    prepare(0)
    pl.semaphore_wait(barrier, 4 + jnp.where(z < 3, 1, 0) + jnp.where(z > 0, 1, 0))

    def at_unit(u, condition, action):
        n = Unit(jnp.maximum(u, 0))

        @pl.when((u >= 0) & (u < units) & condition(n))
        def _():
            action(n)

    def in_flow(n):
        return jnp.logical_not(n.handed_on)

    def step(i, carry):
        at_unit(i, lambda n: jnp.logical_not(n.handed_in), compute)
        for number in range(3):
            pl.when(i == number)(functools.partial(prepare, number + 1))
        at_unit(i - 1, lambda n: n.kind >= 0, join_core)
        at_unit(i - WAIT, lambda n: n.y_first, join_y)
        at_unit(i - WAIT - HOP * z, lambda n: in_flow(n) & (n.plane > z), pass_right)
        at_unit(i - WAIT - HOP * (3 - z), lambda n: in_flow(n) & (n.plane < z), pass_left)
        at_unit(i - WAIT - 3 * HOP - 1, lambda n: in_flow(n) & (n.plane == z), meet)
        at_unit(i - WAIT - 3 * HOP - 3, lambda n: n.z_first & (n.plane == z), meet_late)
        for j in range(6):
            pl.when(i == 3 + j)(functools.partial(small_step, j))
        return carry

    lax.fori_loop(0, units + WAIT + 3 * HOP + 3, step, 0)

    def third_kind(k):
        return jnp.where(k == 2, 2 + section, k)

    def their_kind(k):
        return jnp.where(k == 2, 3 - section, k)

    for k in range(3):
        cross_copy(their_kind(jnp.int32(k))).wait_recv()
        hand_copy(their_kind(jnp.int32(k))).start()

    def settle(u, carry):
        n = Unit(u)

        @pl.when(jnp.logical_not(n.handed_in) & (n.order >= computed - RING))
        def _():
            core_copy(n.order, 0).wait_send()
            core_copy(n.order, 1).wait_send()

        pl.when(n.handed_on)(lambda: over_copy(n.plane, n.u, over_target(n.plane)).wait_send())
        pl.when(n.y_first | (n.z_first & (n.plane == z)))(lambda: y_copy(n).wait_send())
        pl.when(n.y_first & (n.plane > z))(lambda: right_copy(n).wait_send())
        pl.when(n.z_first & (n.plane > z))(lambda: right_pair(n).wait_send())
        pl.when(n.y_first & (n.plane < z))(lambda: left_copy(n).wait_send())
        pl.when(n.z_first & (n.plane < z))(lambda: left_pair(n).wait_send())
        return carry

    lax.fori_loop(0, units, settle, 0)
    for j in range(5):
        small_copy(j).wait_send()
    for k in range(3):
        peer_copy(third_kind(jnp.int32(k))).wait()
        cross_copy(third_kind(jnp.int32(k))).wait_send()
        hand_copy(their_kind(jnp.int32(k))).wait()
    peer_copy(4).wait()

    def write(c):
        def turned(side, half, k, begin, wide):
            return m.fin[side, half, k, :, begin + c * wide : begin + (c + 1) * wide].T

        first, second = section, 1 - section
        for half in range(2):
            at = slice(half * BLOCK, (half + 1) * BLOCK)
            m.qkv_out[:, at] = turned(0, half, 4, 0, 144)
            m.out_out[:, at] = turned(0, half, 4, 288, 48)
            for expert, side, k in ((0, first, 0), (1, first, 2), (2, second, 0)):
                m.up_out[expert, :, at] = turned(side, half, k, 0, 192)
            for expert, side, k in ((0, first, 1), (1, second, 3), (2, second, 1)):
                m.down_out[expert, :, at] = turned(side, half, k, 0, 192)

    for c in range(2):
        pl.when(core == c)(functools.partial(write, c))


def summed_grads(n1, att, n2, branch, hidden, active, joint, small):
    dma = pltpu.SemaphoreType.DMA
    items, depth, width = n1.shape
    bf16, f32 = jnp.bfloat16, jnp.float32
    tile = (BLOCK, BLOCK)
    vmem, anywhere = pl.BlockSpec(memory_space=pltpu.VMEM), pl.BlockSpec(memory_space=pl.ANY)
    ins = dict(n1=n1, att=att, n2=n2, branch=branch, hidden=hidden, active=active, joint=joint, small=small)
    outs = dict(
        up_out=((3, 192, width), bf16), down_out=((3, 192, width), bf16), qkv_out=((144, width), bf16),
        out_out=((48, width), bf16), small_out=((2,) + small.shape, f32),
    )
    buffers = dict(
        text_tile=((2, items, TEXT, 2 * BLOCK), bf16), patch_tile=((2, items, depth - TEXT, 2 * BLOCK), bf16), part=((20, 2) + tile, bf16), made=((RING, 2, 2) + tile, bf16),
        xr=((RING, 2) + tile, bf16), yr=((Y_UNITS + Z_UNITS,) + tile, bf16), zr=((Y_UNITS,) + tile, bf16), zl=((Y_UNITS,) + tile, bf16),
        wr=((Z_UNITS, 2) + tile, bf16), wl=((Z_UNITS, 2) + tile, bf16), fin=((2, 2, 5) + tile, bf16),
        text_left=((4, width, items * TEXT), bf16), patch_left=((4, width, items * (depth - TEXT)), bf16), stage=((items, depth, width), bf16), small_sum=((5,) + small.shape, f32),
        small_in=((5,) + small.shape, f32),
    )
    semaphores = dict(
        small_send=dma((5,)), small_recv=dma((5,)), text_sem=dma((2,)), patch_sem=dma((2,)), stage_sem=dma((1,)), core_send=dma((20, 2)),
        core_recv=dma((20, 2)), y_send=dma((Y_UNITS + Z_UNITS,)), y_recv=dma((Y_UNITS + Z_UNITS,)), right_send=dma((Y_UNITS + Z_UNITS,)), right_recv=dma((Y_UNITS + Z_UNITS,)),
        left_send=dma((Y_UNITS + Z_UNITS,)), left_recv=dma((Y_UNITS + Z_UNITS,)), over_send=dma((4,)), over_recv=dma((4,)), peer_send=dma((5,)),
        peer_recv=dma((5,)), cross_send=dma((5,)), cross_recv=dma((5,)), hand_send=dma((5,)), hand_recv=dma((5,)),
        credit=pltpu.SemaphoreType.REGULAR,
    )
    names = list(ins) + list(outs) + list(buffers) + list(semaphores)
    return pl.pallas_call(
        functools.partial(sum_kernel, names),
        out_shape=[jax.ShapeDtypeStruct(*kind) for kind in outs.values()],
        in_specs=[anywhere] * 7 + [vmem],
        out_specs=[vmem] * len(outs),
        scratch_shapes=[pltpu.VMEM(*kind) for kind in buffers.values()] + list(semaphores.values()),
        compiler_params=pltpu.CompilerParams(
            collective_id=0, has_side_effects=True, vmem_limit_bytes=60 * 1024 * 1024
        ),
        cost_estimate=pl.CostEstimate(flops=48 * 2 * 768 * 384 * items * depth, bytes_accessed=40_000_000, transcendentals=0),
    )(*ins.values())


def finish_kernel(up, down, qkv, out, grad, small, up_out, down_out, qkv_out, out_out, grad_out, *small_outs):
    for source, target in ((up, up_out), (down, down_out), (qkv, qkv_out), (out, out_out), (grad, grad_out)):
        target[...] = source[...].astype(jnp.float32)
    section, me = lax.axis_index("section"), lax.axis_index("dp")
    width, wide = up.shape[2], up.shape[2] // 16
    ff = width * 4

    def columns(row, size):
        return pltpu.roll(row, (row.shape[1] - size * me) % row.shape[1], 1)[:, :size]

    def up_bias(side, slot):
        return columns(jnp.concatenate([small[side, 9 + 3 * slot + j : 10 + 3 * slot + j] for j in range(3)], axis=1), ff // 16)

    own = columns(small[0, :9, :width], wide)
    other = columns(small[1, :9, :width], wide)
    qv_out, proj_out, gain_out, shift_out, up_bias_out, down_bias_out = small_outs
    qv_out[...] = own[2:4]
    proj_out[...] = own[4:5]
    gain_out[...] = own[5:7]
    shift_out[...] = own[7:9]
    for side in range(2):
        mine, theirs = (own, other) if side == 0 else (other, own)

        @pl.when(section == side)
        def _():
            down_bias_out[0:2] = mine[0:2]
            down_bias_out[2:3] = theirs[0:1]
            up_bias_out[0:1] = up_bias(side, 0)
            up_bias_out[1:2] = up_bias(side, 1)
            up_bias_out[2:3] = up_bias(1 - side, 0)


def finished(up, down, qkv, out, small, grad):
    width = up.shape[2]
    shapes = [up.shape, down.shape, qkv.shape, out.shape, grad.shape]
    shapes += [(rows, width // 16) for rows in (2, 1, 2, 2)] + [(3, width // 4), (3, width // 16)]
    return pl.pallas_call(
        finish_kernel,
        out_shape=[jax.ShapeDtypeStruct(shape, jnp.float32) for shape in shapes],
        compiler_params=pltpu.CompilerParams(vmem_limit_bytes=40 * 1024 * 1024),
    )(up, down, qkv, out, grad, small)


CHUNK = 1024
PIECE = 512
KEY_SPLIT = 256
TAIL = (0.319381530, -0.356563782, 1.781477937, -1.821255978, 1.330274429)
PEAK = 0.3989422804014327


def normal_parts(z):
    size = jnp.abs(z)
    scale = 1.0 + 0.2316419 * size
    t = pl.reciprocal(scale, approx=True)
    t = t * (2.0 - scale * t)
    bell = jnp.exp(-0.5 * z * z) * PEAK
    series = TAIL[4]
    for factor in TAIL[3::-1]:
        series = series * t + factor
    upper = bell * (series * t)
    return jnp.where(z >= 0, 1.0 - upper, upper), bell


def matmul(left, right):
    return jnp.dot(left, right, preferred_element_type=jnp.float32)


def matmul_turned(left, right):
    return lax.dot_general(left, right, (((1,), (1,)), ((), ())), preferred_element_type=jnp.float32)


def standardized(values):
    centre = values - jnp.mean(values, -1, keepdims=True)
    inverse = lax.rsqrt(jnp.mean(centre * centre, -1, keepdims=True) + EPSILON)
    return centre * inverse, inverse


def norm_step_back(delta, values, gain_row):
    standard, inverse = standardized(values)
    scaled = delta * gain_row
    moved = inverse * (
        scaled - jnp.mean(scaled, -1, keepdims=True) - standard * jnp.mean(scaled * standard, -1, keepdims=True)
    )
    return moved, jnp.sum(delta * standard, 0, keepdims=True), jnp.sum(delta, 0, keepdims=True)


def half_mask(half):
    lanes = lax.broadcasted_iota(jnp.int32, (1, 128), 1)
    return (lanes < 64) if half == 0 else (lanes >= 64)


def pair_columns(p, part, width):
    return slice(part * width + p * 128, part * width + p * 128 + 128)


def both_halves(pair):
    return jnp.concatenate([jnp.where(half_mask(half), pair, jnp.zeros_like(pair)) for half in range(2)], axis=0)


def in_turn(count, *stages):
    for turn in range(count + len(stages) - 1):
        for number, stage in enumerate(stages):
            if 0 <= turn - number < count:
                stage(turn - number)


def attention_forward(m, length):
    rows, width = m.att.shape

    def scores(p):
        q2 = m.qkv[:, pair_columns(p, 0, width)]
        k2 = m.qkv[:, pair_columns(p, 1, width)]
        m.scores[p % 2] = matmul_turned(both_halves(k2), q2).reshape(2, rows, rows)

    def soften(p):
        for half in range(2):
            top = m.scores[p % 2, half, :KEY_SPLIT]
            low = m.scores[p % 2, half, KEY_SPLIT:]
            key_row = KEY_SPLIT + lax.broadcasted_iota(jnp.int32, low.shape, 0)
            low = jnp.where(key_row < length, low, -1e30)
            peak = jnp.maximum(jnp.max(top, 0, keepdims=True), jnp.max(low, 0, keepdims=True))
            top = jnp.exp(top - peak)
            low = jnp.exp(low - peak)
            over = 1.0 / (jnp.sum(top, 0, keepdims=True) + jnp.sum(low, 0, keepdims=True))
            m.probs[2 * p + half, :KEY_SPLIT] = (top * over).astype(jnp.bfloat16)
            m.probs[2 * p + half, KEY_SPLIT:] = (low * over).astype(jnp.bfloat16)

    def blend(p):
        v_turned = m.qkv[:, pair_columns(p, 2, width)].T
        parts = [matmul(v_turned[64 * half : 64 * half + 64], m.probs[2 * p + half]) for half in range(2)]
        turned = jnp.concatenate(parts, axis=0)
        m.att_turned[p * 128 : p * 128 + 128, :] = turned.astype(jnp.bfloat16)
        m.att[:, p * 128 : p * 128 + 128] = turned.T.astype(jnp.bfloat16)

    in_turn(width // 128, scores, soften, blend)


def attention_back(m):
    rows, width = m.att.shape

    def probs_back(p):
        v2 = m.qkv[:, pair_columns(p, 2, width)]
        d_turned = m.att_delta[:, pair_columns(p, 0, width)].T
        m.scores[p % 2] = matmul(both_halves(v2), d_turned).reshape(2, rows, rows)
        product = d_turned.astype(jnp.float32) * m.att_turned[p * 128 : p * 128 + 128, :].astype(jnp.float32)
        for half in range(2):
            m.inner[p % 2, half] = jnp.sum(product[64 * half : 64 * half + 64], 0, keepdims=True)

    def scores_back(p):
        for half in range(2):
            probs = m.probs[2 * p + half].astype(jnp.float32)
            m.score_delta[p % 2, half] = (probs * (m.scores[p % 2, half] - m.inner[p % 2, half])).astype(jnp.bfloat16)

    def heads_back(p):
        q_at, k_at, v_at = (pair_columns(p, part, width) for part in range(3))
        score = m.score_delta[p % 2]
        probs = m.probs[2 * p : 2 * p + 2].reshape(2 * rows, rows)
        k_turned = m.qkv[:, k_at].T
        value = matmul(probs, m.att_delta[:, q_at])
        key = matmul(score.reshape(2 * rows, rows), m.qkv[:, q_at])
        query = jnp.concatenate(
            [matmul(k_turned[64 * half : 64 * half + 64], score[half]) for half in range(2)], axis=0
        )
        dq = (query.T * HEAD_DIM ** (-0.5)).astype(jnp.bfloat16)
        dk = jnp.where(half_mask(0), key[:rows], key[rows:]).astype(jnp.bfloat16)
        dv = jnp.where(half_mask(0), value[:rows], value[rows:]).astype(jnp.bfloat16)
        m.mixed[:, q_at] = dq
        m.mixed[:, k_at] = dk
        m.mixed[:, v_at] = dv
        m.sums[2:3, q_at] += jnp.sum(dq.astype(jnp.float32), 0, keepdims=True)
        m.sums[3:4, q_at] += jnp.sum(dv.astype(jnp.float32), 0, keepdims=True)

    in_turn(width // 128, probs_back, scores_back, heads_back)


def forward_front(m, x_ref, length):
    x = x_ref[...].astype(jnp.float32)
    standard, unused = standardized(x)
    m.n1[...] = (standard * m.gain[0:1] + m.shift[0:1]).astype(jnp.bfloat16)
    width = x.shape[1]
    m.need(m.qkv_w)
    value = matmul(m.n1[...], m.qkv_w[...])
    query = (value[:, :width] + m.qv[0:1]).astype(jnp.bfloat16)
    m.qkv[:, :width] = query * jnp.bfloat16(HEAD_DIM ** (-0.5))
    m.qkv[:, width : 2 * width] = value[:, width : 2 * width].astype(jnp.bfloat16)
    m.qkv[:, 2 * width :] = (value[:, 2 * width :] + m.qv[1:2]).astype(jnp.bfloat16)
    attention_forward(m, length)
    m.need(m.out_w)
    middle = x_ref[...].astype(jnp.float32) + matmul(m.att[...], m.out_w[...]) + m.proj[0:1]
    m.middle[...] = middle
    standard, unused = standardized(middle)
    m.n2[...] = (standard * m.gain[1:2] + m.shift[1:2]).astype(jnp.bfloat16)


def back_tail(m, x_ref, g_ref, n2_delta, keep):
    middle_part, gain, shift = norm_step_back(n2_delta, m.middle[...], m.gain[1:2])
    m.sums[6:7, :gain.shape[1]] += gain
    m.sums[8:9, :gain.shape[1]] += shift
    middle_delta = g_ref[...].astype(jnp.float32) + middle_part
    proj_delta = middle_delta.astype(jnp.bfloat16)
    m.sums[4:5, :gain.shape[1]] += jnp.sum(proj_delta.astype(jnp.float32), 0, keepdims=True)
    m.proj_delta[...] = proj_delta
    m.middle_delta[...] = middle_delta
    m.att_delta[...] = matmul_turned(proj_delta, m.out_w[...]).astype(jnp.bfloat16)
    attention_back(m)
    total = matmul_turned(m.mixed[...], m.qkv_w[...])
    input_part, gain, shift = norm_step_back(total, x_ref[...].astype(jnp.float32), m.gain[0:1])
    m.sums[5:6, :gain.shape[1]] += gain
    m.sums[7:8, :gain.shape[1]] += shift
    keep(m.middle_delta[...] + input_part)


def forward_expert(m, slot, begin, end):
    def columns(j):
        return slice(j * PIECE, (j + 1) * PIECE)

    def widen(j):
        hidden = matmul(m.n2[begin:end], m.up_w[slot, :, columns(j)])
        m.hidden[j % 2, begin:end] = hidden + m.up_b[slot : slot + 1, columns(j)]

    def bend(j):
        hidden = m.hidden[j % 2, begin:end]
        below, bell = normal_parts(hidden)
        m.active[begin:end, columns(j)] = (hidden * below).astype(jnp.bfloat16)
        m.slope[begin:end, columns(j)] = (below + hidden * bell).astype(jnp.bfloat16)

    in_turn(m.up_w.shape[2] // PIECE, widen, bend)
    result = matmul(m.active[begin:end], m.down_w[slot])
    m.total[begin:end] = m.middle[begin:end] + result + m.down_b[slot : slot + 1]


def add_up_sums(m, slot, begin, end):
    for j in range(m.up_w.shape[2] // CHUNK):
        piece = m.hidden_delta[begin:end, j * CHUNK : (j + 1) * CHUNK].astype(jnp.float32)
        m.sums[9 + 3 * slot + j : 10 + 3 * slot + j] += jnp.sum(piece, 0, keepdims=True)


def back_expert(m, g_ref, slot, begin, end):
    m.sums[slot : slot + 1, : g_ref.shape[1]] += jnp.sum(g_ref[begin:end].astype(jnp.float32), 0, keepdims=True)
    active_delta = matmul_turned(g_ref[begin:end], m.down_w[slot])
    m.hidden_delta[begin:end] = (active_delta * m.slope[begin:end].astype(jnp.float32)).astype(jnp.bfloat16)
    m.total[begin:end] = matmul_turned(m.hidden_delta[begin:end], m.up_w[slot])
    add_up_sums(m, slot, begin, end)


def both_expert(m, g_ref):
    m.sums[0:1, : g_ref.shape[1]] += jnp.sum(g_ref[...].astype(jnp.float32), 0, keepdims=True)

    def columns(j):
        return slice(j * PIECE, (j + 1) * PIECE)

    def widen(j):
        m.hidden[j % 2] = matmul(m.n2[...], m.up_w[0, :, columns(j)]) + m.up_b[2:3, columns(j)]
        m.active_delta[j % 2] = matmul_turned(g_ref[...], m.down_w[0, columns(j), :])

    def bend(j):
        hidden = m.hidden[j % 2]
        below, bell = normal_parts(hidden)
        m.active[:, columns(j)] = (hidden * below).astype(jnp.bfloat16)
        slope = below + hidden * bell
        m.hidden_delta[:, columns(j)] = (m.active_delta[j % 2] * slope).astype(jnp.bfloat16)

    in_turn(m.up_w.shape[2] // PIECE, widen, bend)
    m.total[...] = matmul_turned(m.hidden_delta[...], m.up_w[0])
    add_up_sums(m, 0, 0, ROWS)


def join_columns(m):
    chips = m.joint.shape[1] // BLOCK
    mixed, proj = m.mixed.shape[1] // chips, m.proj_delta.shape[1] // chips
    for t in range(chips):
        m.joint[:, t * BLOCK : t * BLOCK + mixed] = m.mixed[:, t * mixed : (t + 1) * mixed]
        m.joint[:, t * BLOCK + mixed : (t + 1) * BLOCK] = m.proj_delta[:, t * proj : (t + 1) * proj]


def layers_kernel(names, *refs):
    m = Refs()
    for name, ref in zip(names, refs):
        setattr(m, name, ref)
    items, length = m.in_tokens.shape[:2]
    half = m.total.shape[1] // 2
    section = lax.axis_index("section")
    across = (1 - section, lax.axis_index("dp"))

    def send(i, part):
        rows = (slice(0, TEXT), slice(TEXT, ROWS))[part]
        return pltpu.make_async_remote_copy(
            src_ref=m.leaving.at[i, rows], dst_ref=m.landed.at[i, rows], send_sem=m.send_sem.at[i, part],
            recv_sem=m.recv_sem.at[i, part], device_id=across, device_id_type=MESH,
        )

    def send_half(i):
        return pltpu.make_async_remote_copy(
            src_ref=m.half_out.at[i], dst_ref=m.half_in.at[i], send_sem=m.half_send.at[i], recv_sem=m.half_recv.at[i],
            device_id=across, device_id_type=MESH,
        )

    def local(source, target, number):
        return pltpu.make_async_copy(source, target, m.copy_sem.at[number])

    def branch_copy(source, i):
        return pltpu.make_async_copy(source.at[i], m.branch.at[i], m.branch_sem.at[i])

    def weights(experts):
        found = [
            (m.qkv_w, [local(m.in_qkv.at[0], m.qkv_w, 0)]),
            (m.out_w, [local(m.in_out.at[0], m.out_w, 1)]),
            (m.up_w, []),
            (m.down_w, []),
        ]
        for slot, expert in enumerate(experts):
            found[2][1].append(local(m.in_up.at[expert], m.up_w.at[slot], 2 + slot))
            found[3][1].append(local(m.in_down.at[expert], m.down_w.at[slot], 4 + slot))
        return found

    def start_weights(found):
        copies = found[0][1] + found[1][1]
        for pair in zip(found[2][1], found[3][1]):
            copies += pair
        for copy in copies:
            copy.start()

    def needs(found, i):
        def need(ref):
            for here, copies in found:
                if here is ref:

                    @pl.when(i == 0)
                    def _():
                        for copy in copies:
                            copy.wait()

        return need

    leaving = (
        (m.n1, m.out_n1), (m.att, m.out_att), (m.n2, m.out_n2), (m.active, m.out_active), (m.qkv, m.kept_qkv),
        (m.probs, m.kept_probs), (m.att_turned, m.kept_turned), (m.middle, m.kept_middle), (m.slope, m.kept_slope),
        (m.joint, m.out_joint), (m.hidden_delta, m.out_hidden),
    )
    n1, att, n2, active, qkv, probs, turned, middle, slope, joint, hidden = range(len(leaving))

    def puts(i):
        return lambda number: local(leaving[number][0], leaving[number][1].at[i], 6 + number)

    def gets(i):
        return lambda number: local(leaving[number][1].at[i], leaving[number][0], 14 + number)

    def start(copies, *which):
        for number in which:
            copies(number).start()

    def wait(copies, *which):
        for number in which:
            copies(number).wait()

    def settle(i, *which):
        @pl.when(i > 0)
        def _():
            wait(puts(i), *which)

    def text_first(target, source, i):
        value = source[i].astype(jnp.float32)
        pad = jnp.zeros((ROWS - length, value.shape[1]), jnp.float32)
        target[i, :TEXT] = value[PATCHES:].astype(jnp.bfloat16)
        target[i, TEXT:] = jnp.concatenate([value[:PATCHES], pad], axis=0).astype(jnp.bfloat16)

    def mask_targets(i):
        row = lax.broadcasted_iota(jnp.int32, (ROWS, 1), 0)
        position = jnp.where(row < TEXT, row + PATCHES, jnp.where(row < length, row - TEXT, length))
        chosen = jnp.zeros((ROWS, 1), jnp.float32)
        for mask in (m.patch_mask, m.text_mask):
            same = jnp.where(position == mask[i : i + 1, :], 1.0, 0.0)
            chosen = jnp.maximum(chosen, jnp.max(same, 1, keepdims=True))
        m.targets[i] = (m.targets[i].astype(jnp.float32) * chosen).astype(jnp.bfloat16)

    def place(i, value):
        m.input_grad[i, :PATCHES] = value[TEXT:length]
        m.input_grad[i, PATCHES:] = value[:TEXT]

    def first_front(found, i, carry):
        m.need = needs(found, i)
        text_first(m.tokens, m.in_tokens, i)
        settle(i, n1, att, n2, qkv, probs, turned, middle)
        forward_front(m, m.tokens.at[i], length)
        start(puts(i), n1, att, n2, qkv, probs, turned, middle)
        settle(i, active, slope)
        m.need(m.up_w)
        m.need(m.down_w)
        forward_expert(m, 1, 0, TEXT)
        m.leaving[i, :TEXT] = m.total[:TEXT].astype(jnp.bfloat16)
        send(i, 0).start()
        forward_expert(m, 0, TEXT, ROWS)
        m.leaving[i, TEXT:] = m.total[TEXT:].astype(jnp.bfloat16)
        send(i, 1).start()
        start(puts(i), active, slope)
        return carry

    def first_back(i, carry):
        start(gets(i), slope, middle, turned, qkv, probs)

        @pl.when(i > 0)
        def _():
            send(i - 1, 0).wait_send()
            send(i - 1, 1).wait_send()

        settle(i, hidden)
        wait(gets(i), slope)
        gradient = m.landed.at[i]
        send(i, 0).wait_recv()
        back_expert(m, gradient, 1, 0, TEXT)
        send(i, 1).wait_recv()
        branch_copy(m.landed, i).start()
        back_expert(m, gradient, 0, TEXT, ROWS)
        start(puts(i), hidden)
        wait(gets(i), middle, turned, qkv, probs)

        def keep(value):
            place(i, value[:, :half])
            m.half_out[i] = value[:, half:].astype(jnp.bfloat16)

        back_tail(m, m.tokens.at[i], gradient, m.total[...], keep)
        send_half(i).start()
        settle(i, joint)
        join_columns(m)
        start(puts(i), joint)
        branch_copy(m.landed, i).wait()
        return carry

    def second_both(found, i, carry):
        m.need = needs(found, i)
        branch_copy(m.targets, i).start()
        send(i, 0).wait_recv()
        send(i, 1).wait_recv()
        settle(i, n1, att, n2)
        arrived = m.landed.at[i]
        forward_front(m, arrived, length)
        start(puts(i), n1, att, n2)
        settle(i, active, hidden)
        m.need(m.up_w)
        m.need(m.down_w)
        gradient = m.targets.at[i]
        both_expert(m, gradient)
        start(puts(i), active, hidden)

        def keep(value):
            m.leaving[i] = value.astype(jnp.bfloat16)

        back_tail(m, arrived, gradient, m.total[...], keep)
        send(i, 0).start()
        send(i, 1).start()
        settle(i, joint)
        join_columns(m)
        start(puts(i), joint)
        branch_copy(m.targets, i).wait()
        return carry

    m.sums[...] = jnp.zeros(m.sums.shape, jnp.float32)
    barrier = pltpu.get_barrier_semaphore()
    pl.semaphore_signal(barrier, inc=1, device_id=across, device_id_type=MESH)

    @pl.when(section == 0)
    def _():
        found = weights((0, 1))
        start_weights(found)
        pl.semaphore_wait(barrier, 1)
        lax.fori_loop(0, items, functools.partial(first_front, found), 0)
        wait(puts(0), n1, att, n2, active, qkv, probs, turned, middle, slope)
        lax.fori_loop(0, items, first_back, 0)
        wait(puts(0), joint, hidden)
        send(items - 1, 0).wait_send()
        send(items - 1, 1).wait_send()
        for i in range(items):
            send_half(i).wait_send()

    @pl.when(section == 1)
    def _():
        found = weights((2,))
        start_weights(found)
        for i in range(items):
            text_first(m.targets, m.cotangent, i)
            mask_targets(i)
        pl.semaphore_wait(barrier, 1)
        lax.fori_loop(0, items, functools.partial(second_both, found), 0)
        wait(puts(0), n1, att, n2, active, joint, hidden)
        for i in range(items):
            send(i, 0).wait_send()
            send(i, 1).wait_send()
            send_half(i).wait_recv()
            place(i, m.half_in[i].astype(jnp.float32))


def both_layers(
    tokens, cotangent, patch_mask, text_mask, qkv_weight, out_weight, up_table, down_table, qv, proj, gain, shift, up_b, down_b
):
    items, length, width = tokens.shape
    rows = ROWS
    ff = up_b.shape[1]
    heads = width // HEAD_DIM
    bf16, f32 = jnp.bfloat16, jnp.float32
    dma = pltpu.SemaphoreType.DMA
    vmem, anywhere = pl.BlockSpec(memory_space=pltpu.VMEM), pl.BlockSpec(memory_space=pl.ANY)
    ins = dict(
        in_tokens=(tokens, vmem), cotangent=(cotangent, vmem), patch_mask=(patch_mask, vmem), text_mask=(text_mask, vmem), in_qkv=(qkv_weight, anywhere), in_out=(out_weight, anywhere),
        in_up=(up_table, anywhere), in_down=(down_table, anywhere), qv=(qv, vmem), proj=(proj, vmem), gain=(gain, vmem),
        shift=(shift, vmem), up_b=(up_b, vmem), down_b=(down_b, vmem),
    )

    def made(*shape, kind=bf16, spec=anywhere):
        return jax.ShapeDtypeStruct((items,) + shape, kind), spec

    outs = dict(
        out_n1=made(rows, width), out_att=made(rows, width), out_n2=made(rows, width), out_active=made(rows, ff),
        out_joint=made(rows, 4 * width), out_hidden=made(rows, ff), branch=made(rows, width),
        kept_qkv=made(rows, 3 * width), kept_probs=made(heads, rows, rows), kept_turned=made(width, rows),
        kept_middle=made(rows, width, kind=f32), kept_slope=made(rows, ff),
        input_grad=made(length, width // 2, kind=f32, spec=vmem),
        sums=(jax.ShapeDtypeStruct((16, CHUNK), f32), vmem),
    )
    low_row, wide_row = ((rows, width), bf16), ((rows, ff), bf16)
    buffers = dict(
        qkv_w=((width, 3 * width), bf16), out_w=((width, width), bf16), up_w=((2, width, ff), bf16),
        down_w=((2, ff, width), bf16), n1=low_row, att=low_row, n2=low_row, active=wide_row,
        qkv=((rows, 3 * width), bf16), probs=((heads, rows, rows), bf16), att_turned=((width, rows), bf16),
        middle=((rows, width), f32), slope=wide_row, total=((rows, width), f32), mixed=((rows, 3 * width), bf16),
        proj_delta=low_row, joint=((rows, 4 * width), bf16), scores=((2, 2, rows, rows), f32),
        score_delta=((2, 2, rows, rows), bf16), inner=((2, 2, 1, rows), f32), hidden=((2, rows, PIECE), f32),
        active_delta=((2, rows, PIECE), f32), hidden_delta=wide_row, att_delta=low_row, middle_delta=((rows, width), f32),
        leaving=((items, rows, width), bf16), landed=((items, rows, width), bf16),
        half_out=((items, rows, width // 2), bf16), half_in=((items, rows, width // 2), bf16),
        tokens=((items, rows, width), bf16), targets=((items, rows, width), bf16),
    )
    semaphores = dict(
        copy_sem=dma((23,)), branch_sem=dma((items,)), send_sem=dma((items, 2)), recv_sem=dma((items, 2)),
        half_send=dma((items,)), half_recv=dma((items,)),
    )
    names = list(ins) + list(outs) + list(buffers) + list(semaphores)
    results = pl.pallas_call(
        functools.partial(layers_kernel, names),
        out_shape=[shape for shape, spec in outs.values()],
        in_specs=[spec for value, spec in ins.values()],
        out_specs=[spec for shape, spec in outs.values()],
        scratch_shapes=[pltpu.VMEM(*kind) for kind in buffers.values()] + list(semaphores.values()),
        compiler_params=pltpu.CompilerParams(
            collective_id=1, has_side_effects=True, vmem_limit_bytes=60 * 1024 * 1024
        ),
        cost_estimate=pl.CostEstimate(flops=40_000_000_000, bytes_accessed=100_000_000, transcendentals=0),
    )(*[value for value, spec in ins.values()])
    m = Refs()
    for name, result in zip(outs, results):
        setattr(m, name, result)
    return m


def small_outs(own, other, is_first, width):
    first = jnp.where(is_first, own, other)
    second = jnp.where(is_first, other, own)
    me = lax.axis_index("dp")

    def columns(rows):
        wide = rows.shape[-1] // lax.axis_size("dp")
        return lax.dynamic_slice_in_dim(rows, me * wide, wide, rows.ndim - 1)

    down = columns(jnp.concatenate([first[:2], second[:1]])[:, :width])
    up = columns(jnp.concatenate([first[9:15].reshape(2, -1), second[9:12].reshape(1, -1)]))
    own = columns(own[2:9, :width])
    return own[0:2], own[2:3], own[3:5], own[5:7], up, down


def flat(value):
    return value.reshape((-1, value.shape[-1]))


def left_parts(m, is_first):
    n1, att, n2, branch_delta = (flat(part) for part in (m.out_n1, m.out_att, m.out_n2, m.branch))
    text = (jnp.arange(n1.shape[0]) % ROWS < TEXT)[:, None]
    vision = jnp.logical_not(text & is_first).astype(jnp.bfloat16)
    text = text.astype(jnp.bfloat16)
    return [
        piece.T for piece in (n2 * vision, branch_delta * vision, n2 * text, branch_delta * text, n1, att)
    ]


def all_grads(m):
    up, down, qkv, out, input_grad, *small = finished(
        *summed_grads(m.out_n1, m.out_att, m.out_n2, m.branch, m.out_hidden, m.out_active, m.out_joint, m.sums),
        m.input_grad,
    )
    return qkv.T, out.T, up.transpose(0, 2, 1), down, small, input_grad


def large_grads_plain(m, is_first):
    lefts = left_parts(m, is_first)
    hidden_delta, active = flat(m.out_hidden), flat(m.out_active)

    def total_of(left, right):
        product = jnp.dot(left, right, preferred_element_type=jnp.float32).astype(jnp.bfloat16)
        return lax.psum_scatter(product, "dp", scatter_dimension=1, tiled=True)

    def table(vision_part, text_part):
        def swapped(part):
            return lax.psum(part, "section").astype(jnp.float32)

        return jnp.stack(
            [
                swapped(jnp.where(is_first, vision_part, 0)),
                swapped(jnp.where(is_first, text_part, 0)),
                swapped(jnp.where(is_first, 0, vision_part)),
            ]
        )

    up = table(total_of(lefts[0], hidden_delta), total_of(lefts[2], hidden_delta))
    down = table(total_of(lefts[1], active), total_of(lefts[3], active))
    small = lax.psum(m.sums, "dp")
    joint = flat(m.out_joint)
    joint = joint.reshape(joint.shape[0], -1, BLOCK)
    mixed, proj = (part.reshape(joint.shape[0], -1) for part in (joint[:, :, :288], joint[:, :, 288:]))
    return (
        total_of(lefts[4], mixed).astype(jnp.float32),
        total_of(lefts[5], proj).astype(jnp.float32),
        up,
        down.transpose(0, 2, 1),
        small,
        lax.ppermute(small, "section", [(0, 1), (1, 0)]),
    )


def shards(
    tokens, cotangent, patch_mask, text_mask, qkv_weight, qv_bias, out_weight, out_bias, norm_gain, norm_bias,
    up_table, up_bias, down_table, down_bias,
):
    is_first = lax.axis_index("section") == 0
    m = both_layers(
        tokens, cotangent, patch_mask, text_mask, qkv_weight, out_weight, up_table, down_table, qv_bias[0], out_bias,
        norm_gain[0], norm_bias[0], up_bias, down_bias,
    )
    if lax.axis_size("dp") == 16:
        qkv, out, up, down, small, input_grad = all_grads(m)
    else:
        qkv, out, up, down, own, other = large_grads_plain(m, is_first)
        small = small_outs(own, other, is_first, tokens.shape[2])
        input_grad = m.input_grad
    qv_part, proj_part, gain_part, shift_part, up_part, down_part = small
    return (
        input_grad, qkv[None], qv_part[None], out[None], proj_part, gain_part[None], shift_part[None],
        up, up_part, down, down_part,
    )


def solution(mesh):
    items, layers = P("dp"), P("section")
    return jax.shard_map(
        shards,
        mesh=mesh,
        in_specs=(items,) * 4 + (layers,) * 6 + (P(),) * 4,
        out_specs=(
            P("dp", None, "section"), P("section", None, "dp"), P("section", None, "dp"), P("section", None, "dp"),
            P("section", "dp"), P("section", None, "dp"), P("section", None, "dp"),
            P(None, None, "dp"), P(None, "dp"), P(None, "dp", None), P(None, "dp"),
        ),
        check_vma=False,
    )
```

```python
import functools

import jax
import jax.numpy as jnp
from jax import lax
from jax.experimental import pallas as pl
from jax.experimental.pallas import tpu as pltpu
from jax.sharding import PartitionSpec as P

HEAD_DIM = 64
PATCHES = 197
EPSILON = 1e-05
BLOCK = 384
RING = 3
TEXT = 64
ROWS = 272
MESH = pl.DeviceIdType.MESH


UNITS = (
    (
        (2, 2, 0), (3, 2, 0), (2, 3, 0), (3, 0, 0), (0, 1, 0), (3, 3, 0), (0, 2, 0), (3, 1, 0), (2,
        0, 0), (4, 3, 1), (1, 0, 0), (0, 3, 0), (0, 0, 1), (2, 1, 0), (1, 3, 0), (1, 1, 0), (4, 0,
        0), (4, 1, 0), (1, 2, 0), (4, 2, 0),
    ),
    (
        (0, 2, 0), (1, 0, 0), (1, 2, 0), (1, 1, 0), (0, 1, 0), (0, 3, 1), (4, 1, 1), (4, 2, 0), (1,
        3, 0), (0, 0, 0), (3, 0, 0), (4, 0, 0), (3, 2, 0), (3, 3, 0), (4, 3, 0), (3, 1, 0), (2, 1,
        0),
    ),
)
WAIT = 4
HOP = 3
MEET = WAIT + 3 * HOP + 1
MEET_LATE = MEET + 2
LEFT_OF = ((0,), (1,), (0,), (1,), (2, 3))
MOVED = [unit[:2] for unit in UNITS[1] if unit[0] in (2, 3)]
MOVED_BITS = sum(1 << (4 * kind + plane) for kind, plane in MOVED)
FIRST_MOVED = min(u for u, unit in enumerate(UNITS[1]) if unit[:2] in MOVED)


def packed(units, handed_on):
    counts = [0, 0]
    codes = []
    for kind, plane, z_first in units:
        slot = 0
        if not (handed_on and (kind, plane) in MOVED):
            slot = counts[z_first]
            counts[z_first] += 1
        codes.append(kind | plane << 3 | z_first << 5 | slot << 6)
    codes += [0] * (-len(codes) % 3)
    return [codes[i] | codes[i + 1] << 10 | codes[i + 2] << 20 for i in range(0, len(codes), 3)], counts


PACKED, COUNTS = zip(*(packed(units, side == 0) for side, units in enumerate(UNITS)))
Y_UNITS, Z_UNITS = (max(COUNTS[0][way], COUNTS[1][way], 1) for way in range(2))


def look_up(words, u):
    word = words[0]
    for n in range(1, len(words)):
        word = jnp.where(u // 3 == n, words[n], word)
    return word >> (10 * (u % 3))


class Refs:
    pass


def sum_kernel(names, *refs):
    m = Refs()
    for name, ref in zip(names, refs):
        setattr(m, name, ref)
    section = lax.axis_index("section")
    me = lax.axis_index("dp")
    z, y, core = me // 4, (me // 2) % 2, me % 2
    peer = (section, me + 1 - 2 * core)
    beside = (section, me + 2 - 4 * y)
    right = (section, me + 4)
    left = (section, me - 4)
    across = (1 - section, me)
    on_first = section == 0
    units = jnp.where(on_first, len(UNITS[0]), len(UNITS[1]))
    computed = jnp.where(on_first, len(UNITS[0]), len(UNITS[1]) - len(MOVED))

    arrivals = [u for u, unit in enumerate(UNITS[1]) if unit[:2] in MOVED]

    def is_moved(kind, plane):
        return ((MOVED_BITS >> (4 * kind + plane)) & 1) == 1

    class Unit:
        def __init__(self, u):
            self.u = u
            code = jnp.where(on_first, look_up(PACKED[0], u), look_up(PACKED[1], u))
            self.kind = code & 7
            self.plane = (code >> 3) & 3
            self.z_first = ((code >> 5) & 1) == 1
            self.slot = (code >> 6) & 15
            moved = is_moved(self.kind, self.plane)
            self.handed_on = on_first & moved
            self.handed_in = jnp.logical_not(on_first) & moved
            self.y_first = jnp.logical_not(self.z_first | self.handed_on)
            self.y_slot = self.slot + jnp.where(self.z_first, Y_UNITS, 0)
            self.uses_text = jnp.logical_not(on_first) | (self.kind > 1)
            self.uses_patches = jnp.logical_not(on_first) | (self.kind < 2) | (self.kind == 4)
            self.order = u
            for at in arrivals:
                self.order = self.order - jnp.where((section == 1) & (u > at), 1, 0)

    def following(u):
        u = u + 1
        for at in arrivals:
            u = u + jnp.where((section == 1) & (u == at), 1, 0)
        return u

    def remote(src, dst, send, recv, device):
        return pltpu.make_async_remote_copy(
            src_ref=src, dst_ref=dst, send_sem=send, recv_sem=recv, device_id=device, device_id_type=MESH
        )

    def core_copy(order, b):
        slot = order % RING
        return remote(m.made.at[slot, 1 - core, b], m.xr.at[slot, b], m.core_send.at[order, b], m.core_recv.at[order, b], peer)

    def y_copy(n):
        return remote(m.part.at[n.u, 0], m.yr.at[n.y_slot], m.y_send.at[n.y_slot], m.y_recv.at[n.y_slot], beside)

    def right_copy(n):
        return remote(m.part.at[n.u, 1], m.zr.at[n.slot], m.right_send.at[n.slot], m.right_recv.at[n.slot], right)

    def left_copy(n):
        return remote(m.part.at[n.u, 1], m.zl.at[n.slot], m.left_send.at[n.slot], m.left_recv.at[n.slot], left)

    def right_pair(n):
        g = n.slot
        return remote(m.part.at[n.u], m.wr.at[g], m.right_send.at[Y_UNITS + g], m.right_recv.at[Y_UNITS + g], right)

    def left_pair(n):
        g = n.slot
        return remote(m.part.at[n.u], m.wl.at[g], m.left_send.at[Y_UNITS + g], m.left_recv.at[Y_UNITS + g], left)

    def over_copy(n, source, target):
        number = 4 * (n.kind - 2) + n.plane
        return remote(m.part.at[source], m.part.at[target], m.over_send.at[number], m.over_recv.at[number], across)

    def over_target(n):
        target = 0
        for at in arrivals:
            kind, plane, unused = UNITS[1][at]
            target = target + jnp.where((n.kind == kind) & (n.plane == plane), at, 0)
        return target

    def half_copy():
        return remote(m.half, m.half_out, m.half_send.at[0], m.half_recv.at[0], across)

    def peer_copy(k):
        return remote(m.fin.at[0, core, k], m.fin.at[0, core, k], m.peer_send.at[k], m.peer_recv.at[k], peer)

    def cross_copy(k):
        return remote(m.fin.at[0, core, k], m.fin.at[1, core, k], m.cross_send.at[k], m.cross_recv.at[k], across)

    def hand_copy(k):
        return remote(m.fin.at[1, core, k], m.fin.at[1, core, k], m.hand_send.at[k], m.hand_recv.at[k], peer)

    def tile_copies(n):
        k = n.kind
        slot = n.order % 2
        wide = pl.ds(pl.multiple_of(n.plane * 2 * BLOCK, 128), 2 * BLOCK)
        cases = []
        for ref, here in ((m.hidden, (k == 0) | (k == 2)), (m.active, (k == 1) | (k == 3)), (m.joint, k == 4)):
            copy = pltpu.make_async_copy(ref.at[:, :TEXT, wide], m.text_tile.at[slot], m.text_sem.at[slot])
            cases.append((here & n.uses_text, copy))
            copy = pltpu.make_async_copy(ref.at[:, TEXT:, wide], m.patch_tile.at[slot], m.patch_sem.at[slot])
            cases.append((here & n.uses_patches, copy))
        return cases

    def start_tile(n):
        for here, copy in tile_copies(n):
            pl.when(here)(copy.start)

    def wait_tile(n):
        for here, copy in tile_copies(n):
            pl.when(here)(copy.wait)

    def add_into(target, source):
        target[...] = target[...] + source[...]

    def text_dot(index, slot, *columns):
        tile = jnp.concatenate([m.text_tile[slot, :, :, at] for at in columns], axis=2)
        return matmul(m.text_left[index], tile.reshape(-1, tile.shape[2]))

    def patch_dot(index, slot, *columns):
        tile = jnp.concatenate([m.patch_tile[slot, :, :, at] for at in columns], axis=2)
        return matmul(m.patch_left[index], tile.reshape(-1, tile.shape[2]))

    def both_dot(index, slot, *columns):
        return patch_dot(index, slot, *columns) + text_dot(index, slot, *columns)

    def compute(n):
        k = n.kind
        slot = n.order % RING

        @pl.when(n.order >= RING)
        def _():
            core_copy(n.order - RING, 0).wait_send()
            core_copy(n.order - RING, 1).wait_send()
            pl.semaphore_wait(m.credit, 1)

        @pl.when(n.order + 1 < computed)
        def _():
            start_tile(Unit(following(n.u)))

        wait_tile(n)
        tile = n.order % 2
        everything = slice(0, 2 * BLOCK)

        def put(value, columns, begin):
            for half in range(2):
                for side in range(2):
                    piece = value[half * BLOCK : (half + 1) * BLOCK, columns[side]]
                    at = slice(begin, begin + piece.shape[1])
                    m.made[slot, half, jnp.where(y == side, 1, 0), :, at] = piece.astype(jnp.bfloat16)

        sides = (slice(0, BLOCK), slice(BLOCK, 2 * BLOCK))

        @pl.when((k < 4) & jnp.logical_not(n.uses_text))
        def _():
            put(patch_dot(k % 2, tile, everything), sides, 0)

        @pl.when((k < 4) & jnp.logical_not(n.uses_patches))
        def _():
            put(text_dot(k % 2, tile, everything), sides, 0)

        @pl.when((k < 4) & n.uses_text & n.uses_patches)
        def _():
            put(both_dot(k % 2, tile, everything), sides, 0)

        @pl.when(k == 4)
        def _():
            ends = (slice(256, BLOCK), slice(BLOCK + 256, 2 * BLOCK))
            mixed = both_dot(2, tile, everything)
            proj = both_dot(3, tile, *ends)
            put(mixed, (slice(0, 256), slice(BLOCK, BLOCK + 256)), 0)
            lanes = lax.broadcasted_iota(jnp.int32, (1, 128), 1)
            last = [jnp.where(lanes < 32, mixed[:, ends[side]], proj[:, 128 * side : 128 * side + 128]) for side in range(2)]
            put(jnp.concatenate(last, axis=1), (slice(0, 128), slice(128, 256)), 256)

        core_copy(n.order, 0).start()
        core_copy(n.order, 1).start()

    def join_core(n):
        slot = n.order % RING

        @pl.when(n.handed_in)
        def _():
            over_copy(n, 0, n.u).wait_recv()

        @pl.when(jnp.logical_not(n.handed_in))
        def _():
            core_copy(n.order, 0).wait_recv()
            m.part[n.u, 0] = m.made[slot, core, 0] + m.xr[slot, 0]

        pl.when(n.y_first)(lambda: y_copy(n).start())

        @pl.when(jnp.logical_not(n.handed_in))
        def _():
            core_copy(n.order, 1).wait_recv()
            m.part[n.u, 1] = m.made[slot, core, 1] + m.xr[slot, 1]

            @pl.when(n.order + RING < computed)
            def _():
                pl.semaphore_signal(m.credit, inc=1, device_id=peer, device_id_type=MESH)

        pl.when(n.handed_on)(lambda: over_copy(n, n.u, over_target(n)).start())

    def join_y(n):
        y_copy(n).wait_recv()
        add_into(m.part.at[n.u, 1], m.yr.at[n.y_slot])

    def take(n, one, pair, single_from, pair_from):
        @pl.when(n.y_first)
        def _():
            one(n).wait_recv()
            add_into(m.part.at[n.u, 1], single_from.at[n.slot])

        @pl.when(n.z_first)
        def _():
            pair(n).wait_recv()
            add_into(m.part.at[n.u], pair_from.at[n.slot])

    def take_right(n):
        take(n, right_copy, right_pair, m.zr, m.wr)

    def take_left(n):
        take(n, left_copy, left_pair, m.zl, m.wl)

    def pass_right(n):
        pl.when(z > 0)(lambda: take_right(n))
        pl.when(n.y_first)(lambda: right_copy(n).start())
        pl.when(n.z_first)(lambda: right_pair(n).start())

    def pass_left(n):
        pl.when(z < 3)(lambda: take_left(n))
        pl.when(n.y_first)(lambda: left_copy(n).start())
        pl.when(n.z_first)(lambda: left_pair(n).start())

    def give(n, i):
        k = n.kind
        m.fin[0, core, k] = m.part[n.u, 1]
        peer_copy(k).start()
        pl.when((k < 4) & (on_first | (i > FIRST_MOVED)))(lambda: cross_copy(k).start())

    def write_table(side, k, c):
        by_second = (section == 1) ^ (side == 1)
        layer = jnp.where((k < 2) & by_second, 2, k // 2)
        at = layer + jnp.where(k % 2 == 1, 3, 0)
        for half in range(2):
            piece = m.fin[side, half, k, :, c * 192 : (c + 1) * 192]
            m.tables_out[at, :, half * BLOCK : (half + 1) * BLOCK] = piece.T

    def write_attention(c):
        for half in range(2):
            at = slice(half * BLOCK, (half + 1) * BLOCK)
            m.qkv_out[:, at] = m.fin[0, half, 4, :, c * 144 : (c + 1) * 144].T
            m.out_out[:, at] = m.fin[0, half, 4, :, 288 + c * 48 : 288 + (c + 1) * 48].T

    def write(side, k):
        for c in range(2):
            pl.when((core == c) & (k < 4))(functools.partial(write_table, side, k, c))
            if side == 0:
                pl.when((core == c) & (k == 4))(functools.partial(write_attention, c))

    def collect(n):
        peer_copy(n.kind).wait()
        write(0, n.kind)

    def greet_first(u, carry):
        n = Unit(u)
        ended = jnp.where(n.z_first, MEET_LATE, MEET) + u <= FIRST_MOVED
        pl.when(ended & (n.kind < 4) & (n.plane == z))(lambda: cross_copy(n.kind).start())
        return carry

    def meet(n, i):
        pl.when(z > 0)(lambda: take_right(n))
        pl.when(z < 3)(lambda: take_left(n))
        pl.when(n.z_first)(lambda: y_copy(n).start())
        pl.when(n.y_first)(lambda: give(n, i))

    def meet_late(n, i):
        join_y(n)
        give(n, i)

    flips = (peer, beside, (section, me + 4 - 8 * (z % 2)), (section, me + 8 - 16 * (z // 2)), across)

    def small_copy(j):
        return remote(m.small_sum.at[j], m.small_in.at[j], m.small_send.at[j], m.small_recv.at[j], flips[j])

    def small_step(j):
        if j == 0:
            m.small_sum[0] = m.small[...]
        else:
            small_copy(j - 1).wait_recv()
            if j == 5:
                m.small_out[0] = m.small_sum[4]
                m.small_out[1] = m.small_in[4]
            else:
                m.small_sum[j] = m.small_sum[j - 1] + m.small_in[j - 1]
        if j < 5:
            small_copy(j).start()

    lefts = (m.n2, m.branch, m.n1, m.att)
    turns = [[], []]
    for side in range(2):
        for kind, plane, z_first in UNITS[side]:
            for index in () if side == 1 and (kind, plane) in MOVED else LEFT_OF[kind]:
                if index not in turns[side]:
                    turns[side].append(index)

    def stage_copy(index):
        return pltpu.make_async_copy(lefts[index], m.stage, m.stage_sem.at[0])

    def start_stage(turn):
        for side in range(2):
            pl.when(section == side)(stage_copy(turns[side][turn]).start)

    def prepare(turn):
        stage_copy(0).wait()
        number = jnp.where(on_first, turns[0][turn], turns[1][turn])

        def part(c, carry):
            at = pl.ds(pl.multiple_of(c * 128, 128), 128)
            m.text_left[number, at, :] = m.stage[:, :TEXT, at].reshape(-1, 128).T
            m.patch_left[number, at, :] = m.stage[:, TEXT:, at].reshape(-1, 128).T
            return carry

        lax.fori_loop(0, m.stage.shape[2] // 128, part, 0)
        if turn < 3:
            start_stage(turn + 1)

    barrier = pltpu.get_barrier_semaphore()
    for device in (peer, beside, flips[3]):
        pl.semaphore_signal(barrier, inc=1, device_id=device, device_id_type=MESH)

    @pl.when(section == 1)
    def _():
        pl.semaphore_signal(barrier, inc=1, device_id=across, device_id_type=MESH)

    @pl.when(z < 3)
    def _():
        pl.semaphore_signal(barrier, inc=1, device_id=right, device_id_type=MESH)

    @pl.when(z > 0)
    def _():
        pl.semaphore_signal(barrier, inc=1, device_id=left, device_id_type=MESH)

    start_stage(0)
    start_tile(Unit(jnp.int32(0)))
    prepare(0)
    pl.semaphore_wait(barrier, 3 + jnp.where(on_first, 1, 0) + jnp.where(z < 3, 1, 0) + jnp.where(z > 0, 1, 0))

    @pl.when(on_first)
    def _():
        pl.semaphore_signal(m.ready, inc=1, device_id=across, device_id_type=MESH)
        half_copy().start()


    def at_unit(u, condition, action, *more):
        n = Unit(jnp.maximum(u, 0))

        @pl.when((u >= 0) & (u < units) & condition(n))
        def _():
            action(n, *more)

    def in_flow(n):
        return jnp.logical_not(n.handed_on)

    def step(i, carry):
        @pl.when((i == FIRST_MOVED + 1) & (section == 1))
        def _():
            pl.semaphore_wait(m.ready, 1)
            lax.fori_loop(0, units, greet_first, 0)

        at_unit(i, lambda n: jnp.logical_not(n.handed_in), compute)
        for number in range(3):
            pl.when(i == number)(functools.partial(prepare, number + 1))
        at_unit(i - 1, lambda n: n.kind >= 0, join_core)
        at_unit(i - WAIT, lambda n: n.y_first, join_y)
        at_unit(i - WAIT - HOP * z, lambda n: in_flow(n) & (n.plane > z), pass_right)
        at_unit(i - WAIT - HOP * (3 - z), lambda n: in_flow(n) & (n.plane < z), pass_left)
        at_unit(i - MEET, lambda n: in_flow(n) & (n.plane == z), meet, i)
        at_unit(i - MEET_LATE, lambda n: n.z_first & (n.plane == z), meet_late, i)
        at_unit(i - MEET_LATE - 1, lambda n: in_flow(n) & (n.plane == z), collect)
        for j in range(4):
            pl.when(i == 3 + j)(functools.partial(small_step, j))
        return carry

    lax.fori_loop(0, units + MEET_LATE + 1, step, 0)
    small_step(4)

    def ours(k):
        return True if k in (0, 1, 4) else is_moved(k, z) == (section == 1)

    def when_ours(k, wanted, action):
        pl.when(jnp.logical_not(ours(k) ^ wanted) if k in (2, 3) else True)(action)

    for k in range(4):

        def hand_on(k=k):
            cross_copy(k).wait_recv()
            hand_copy(k).start()

        when_ours(k, False, hand_on)
    small_step(5)

    def settle(u, carry):
        n = Unit(u)

        @pl.when(jnp.logical_not(n.handed_in) & (n.order >= computed - RING))
        def _():
            core_copy(n.order, 0).wait_send()
            core_copy(n.order, 1).wait_send()

        pl.when(n.handed_on)(lambda: over_copy(n, n.u, over_target(n)).wait_send())
        pl.when(n.y_first | (n.z_first & (n.plane == z)))(lambda: y_copy(n).wait_send())
        pl.when(n.y_first & (n.plane > z))(lambda: right_copy(n).wait_send())
        pl.when(n.z_first & (n.plane > z))(lambda: right_pair(n).wait_send())
        pl.when(n.y_first & (n.plane < z))(lambda: left_copy(n).wait_send())
        pl.when(n.z_first & (n.plane < z))(lambda: left_pair(n).wait_send())
        return carry

    lax.fori_loop(0, units, settle, 0)
    for j in range(5):
        small_copy(j).wait_send()
    for k in range(4):

        def handed(k=k):
            hand_copy(k).wait()
            write(1, jnp.int32(k))

        when_ours(k, False, handed)
        when_ours(k, True, lambda k=k: cross_copy(k).wait_send())

    @pl.when(on_first)
    def _():
        half_copy().wait_send()

    @pl.when(section == 1)
    def _():
        half_copy().wait_recv()

def summed_grads(n1, att, n2, branch, hidden, active, joint, half, small):
    dma = pltpu.SemaphoreType.DMA
    items, depth, width = n1.shape
    bf16, f32 = jnp.bfloat16, jnp.float32
    tile = (BLOCK, BLOCK)
    vmem, anywhere = pl.BlockSpec(memory_space=pltpu.VMEM), pl.BlockSpec(memory_space=pl.ANY)
    ins = dict(n1=n1, att=att, n2=n2, branch=branch, hidden=hidden, active=active, joint=joint, half=half, small=small)
    outs = dict(
        tables_out=((6, 192, width), bf16), qkv_out=((144, width), bf16),
        out_out=((48, width), bf16), small_out=((2,) + small.shape, f32), half_out=(half.shape, bf16),
    )
    buffers = dict(
        text_tile=((2, items, TEXT, 2 * BLOCK), bf16), patch_tile=((2, items, depth - TEXT, 2 * BLOCK), bf16), part=((20, 2) + tile, bf16), made=((RING, 2, 2) + tile, bf16),
        xr=((RING, 2) + tile, bf16), yr=((Y_UNITS + Z_UNITS,) + tile, bf16), zr=((Y_UNITS,) + tile, bf16), zl=((Y_UNITS,) + tile, bf16),
        wr=((Z_UNITS, 2) + tile, bf16), wl=((Z_UNITS, 2) + tile, bf16), fin=((2, 2, 5) + tile, bf16),
        text_left=((4, width, items * TEXT), bf16), patch_left=((4, width, items * (depth - TEXT)), bf16), stage=((items, depth, width), bf16), small_sum=((5,) + small.shape, f32),
        small_in=((5,) + small.shape, f32),
    )
    semaphores = dict(
        small_send=dma((5,)), small_recv=dma((5,)), text_sem=dma((2,)), patch_sem=dma((2,)), stage_sem=dma((1,)), core_send=dma((20, 2)),
        core_recv=dma((20, 2)), y_send=dma((Y_UNITS + Z_UNITS,)), y_recv=dma((Y_UNITS + Z_UNITS,)), right_send=dma((Y_UNITS + Z_UNITS,)), right_recv=dma((Y_UNITS + Z_UNITS,)),
        left_send=dma((Y_UNITS + Z_UNITS,)), left_recv=dma((Y_UNITS + Z_UNITS,)), over_send=dma((8,)), over_recv=dma((8,)), half_send=dma((1,)), half_recv=dma((1,)), peer_send=dma((5,)),
        peer_recv=dma((5,)), cross_send=dma((5,)), cross_recv=dma((5,)), hand_send=dma((5,)), hand_recv=dma((5,)),
        credit=pltpu.SemaphoreType.REGULAR, ready=pltpu.SemaphoreType.REGULAR,
    )
    names = list(ins) + list(outs) + list(buffers) + list(semaphores)
    return pl.pallas_call(
        functools.partial(sum_kernel, names),
        out_shape=[jax.ShapeDtypeStruct(*kind) for kind in outs.values()],
        in_specs=[anywhere] * 8 + [vmem],
        out_specs=[vmem] * (len(outs) - 1) + [anywhere],
        scratch_shapes=[pltpu.VMEM(*kind) for kind in buffers.values()] + list(semaphores.values()),
        compiler_params=pltpu.CompilerParams(
            collective_id=0, has_side_effects=True, vmem_limit_bytes=60 * 1024 * 1024
        ),
        cost_estimate=pl.CostEstimate(flops=48 * 2 * 768 * 384 * items * depth, bytes_accessed=40_000_000, transcendentals=0),
    )(*ins.values())


def finish_kernel(count, *refs):
    sources, targets, held = refs[:count], refs[count:-count - 1], refs[-count - 1 : -1]
    copies = [pltpu.make_async_copy(*pair, refs[-1].at[n]) for n, pair in enumerate(zip(sources, held))]
    for copy in copies:
        copy.start()
    for copy in copies:
        copy.wait()
    tables, qkv, out, small, half, grad = held
    up_out, down_out, qkv_out, out_out, grad_out, *small_outs = targets
    for source, target in ((tables.at[:3], up_out), (tables.at[3:], down_out), (qkv, qkv_out), (out, out_out)):
        target[...] = source[...].astype(jnp.float32)
    section, me = lax.axis_index("section"), lax.axis_index("dp")
    width, wide = tables.shape[2], tables.shape[2] // 16
    ff = width * 4

    def columns(row, size):
        return pltpu.roll(row, (row.shape[1] - size * me) % row.shape[1], 1)[:, :size]

    def up_bias(side, slot):
        return columns(jnp.concatenate([small[side, 9 + 3 * slot + j : 10 + 3 * slot + j] for j in range(3)], axis=1), ff // 16)

    own = columns(small[0, :9, :width], wide)
    other = columns(small[1, :9, :width], wide)
    qv_out, proj_out, gain_out, shift_out, up_bias_out, down_bias_out = small_outs
    qv_out[...] = own[2:4]
    proj_out[...] = own[4:5]
    gain_out[...] = own[5:7]
    shift_out[...] = own[7:9]
    for side in range(2):
        mine, theirs = (own, other) if side == 0 else (other, own)

        @pl.when(section == side)
        def _():
            for i in range(grad.shape[0]):
                place(grad_out, i, grad[i] if side == 0 else half[i].astype(jnp.float32))
            down_bias_out[0:2] = mine[0:2]
            down_bias_out[2:3] = theirs[0:1]
            up_bias_out[0:1] = up_bias(side, 0)
            up_bias_out[1:2] = up_bias(side, 1)
            up_bias_out[2:3] = up_bias(1 - side, 0)


def place(target, i, value):
    target[i, :PATCHES] = value[TEXT : target.shape[1]]
    target[i, PATCHES:] = value[:TEXT]


def finished(length, *sources):
    tables, qkv, out, small, half, grad = sources
    width = tables.shape[2]
    shapes = [(3,) + tables.shape[1:]] * 2 + [qkv.shape, out.shape, (grad.shape[0], length, grad.shape[2])]
    shapes += [(rows, width // 16) for rows in (2, 1, 2, 2)] + [(3, width // 4), (3, width // 16)]
    return pl.pallas_call(
        functools.partial(finish_kernel, len(sources)),
        out_shape=[jax.ShapeDtypeStruct(shape, jnp.float32) for shape in shapes],
        in_specs=[pl.BlockSpec(memory_space=pltpu.HBM)] * len(sources),
        scratch_shapes=[pltpu.VMEM(value.shape, value.dtype) for value in sources]
        + [pltpu.SemaphoreType.DMA((len(sources),))],
        compiler_params=pltpu.CompilerParams(vmem_limit_bytes=60 * 1024 * 1024),
    )(*sources)


CHUNK = 1024
PIECE = 512
KEY_SPLIT = 256
TAIL = (0.319381530, -0.356563782, 1.781477937, -1.821255978, 1.330274429)
PEAK = 0.3989422804014327


def normal_parts(z):
    size = jnp.abs(z)
    scale = 1.0 + 0.2316419 * size
    t = pl.reciprocal(scale, approx=True)
    t = t * (2.0 - scale * t)
    bell = jnp.exp(-0.5 * z * z) * PEAK
    series = TAIL[4]
    for factor in TAIL[3::-1]:
        series = series * t + factor
    upper = bell * (series * t)
    return jnp.where(z >= 0, 1.0 - upper, upper), bell


def matmul(left, right):
    return jnp.dot(left, right, preferred_element_type=jnp.float32)


def matmul_turned(left, right):
    return lax.dot_general(left, right, (((1,), (1,)), ((), ())), preferred_element_type=jnp.float32)


def standardized(values):
    centre = values - jnp.mean(values, -1, keepdims=True)
    inverse = lax.rsqrt(jnp.mean(centre * centre, -1, keepdims=True) + EPSILON)
    return centre * inverse, inverse


def norm_step_back(delta, values, gain_row):
    standard, inverse = standardized(values)
    scaled = delta * gain_row
    moved = inverse * (
        scaled - jnp.mean(scaled, -1, keepdims=True) - standard * jnp.mean(scaled * standard, -1, keepdims=True)
    )
    return moved, jnp.sum(delta * standard, 0, keepdims=True), jnp.sum(delta, 0, keepdims=True)


def half_mask(half):
    lanes = lax.broadcasted_iota(jnp.int32, (1, 128), 1)
    return (lanes < 64) if half == 0 else (lanes >= 64)


def pair_columns(p, part, width):
    return slice(part * width + p * 128, part * width + p * 128 + 128)


def both_halves(pair):
    return jnp.concatenate([jnp.where(half_mask(half), pair, jnp.zeros_like(pair)) for half in range(2)], axis=0)


def in_turn(count, *stages):
    for turn in range(count + len(stages) - 1):
        for number, stage in enumerate(stages):
            if 0 <= turn - number < count:
                stage(turn - number)


def attention_forward(m, length):
    rows, width = m.att.shape

    def scores(p):
        q2 = m.qkv[:, pair_columns(p, 0, width)]
        k2 = m.qkv[:, pair_columns(p, 1, width)]
        m.scores[p % 2] = matmul_turned(both_halves(k2), q2).reshape(2, rows, rows)

    def soften(p):
        for half in range(2):
            top = m.scores[p % 2, half, :KEY_SPLIT]
            low = m.scores[p % 2, half, KEY_SPLIT:]
            key_row = KEY_SPLIT + lax.broadcasted_iota(jnp.int32, low.shape, 0)
            low = jnp.where(key_row < length, low, -1e30)
            peak = jnp.maximum(jnp.max(top, 0, keepdims=True), jnp.max(low, 0, keepdims=True))
            top = jnp.exp(top - peak)
            low = jnp.exp(low - peak)
            over = 1.0 / (jnp.sum(top, 0, keepdims=True) + jnp.sum(low, 0, keepdims=True))
            m.probs[2 * p + half, :KEY_SPLIT] = (top * over).astype(jnp.bfloat16)
            m.probs[2 * p + half, KEY_SPLIT:] = (low * over).astype(jnp.bfloat16)

    def blend(p):
        v_turned = m.qkv[:, pair_columns(p, 2, width)].T
        parts = [matmul(v_turned[64 * half : 64 * half + 64], m.probs[2 * p + half]) for half in range(2)]
        turned = jnp.concatenate(parts, axis=0)
        m.att_turned[p * 128 : p * 128 + 128, :] = turned.astype(jnp.bfloat16)
        m.att[:, p * 128 : p * 128 + 128] = turned.T.astype(jnp.bfloat16)

    in_turn(width // 128, scores, soften, blend)


def attention_back(m):
    rows, width = m.att.shape

    def probs_back(p):
        v2 = m.qkv[:, pair_columns(p, 2, width)]
        d_turned = m.att_delta[:, pair_columns(p, 0, width)].T
        m.scores[p % 2] = matmul(both_halves(v2), d_turned).reshape(2, rows, rows)
        product = d_turned.astype(jnp.float32) * m.att_turned[p * 128 : p * 128 + 128, :].astype(jnp.float32)
        for half in range(2):
            m.inner[p % 2, half] = jnp.sum(product[64 * half : 64 * half + 64], 0, keepdims=True)

    def scores_back(p):
        for half in range(2):
            probs = m.probs[2 * p + half].astype(jnp.float32)
            m.score_delta[p % 2, half] = (probs * (m.scores[p % 2, half] - m.inner[p % 2, half])).astype(jnp.bfloat16)

    def heads_back(p):
        q_at, k_at, v_at = (pair_columns(p, part, width) for part in range(3))
        score = m.score_delta[p % 2]
        probs = m.probs[2 * p : 2 * p + 2].reshape(2 * rows, rows)
        k_turned = m.qkv[:, k_at].T
        value = matmul(probs, m.att_delta[:, q_at])
        key = matmul(score.reshape(2 * rows, rows), m.qkv[:, q_at])
        query = jnp.concatenate(
            [matmul(k_turned[64 * half : 64 * half + 64], score[half]) for half in range(2)], axis=0
        )
        dq = (query.T * HEAD_DIM ** (-0.5)).astype(jnp.bfloat16)
        dk = jnp.where(half_mask(0), key[:rows], key[rows:]).astype(jnp.bfloat16)
        dv = jnp.where(half_mask(0), value[:rows], value[rows:]).astype(jnp.bfloat16)
        m.mixed[:, q_at] = dq
        m.mixed[:, k_at] = dk
        m.mixed[:, v_at] = dv
        m.sums[2:3, q_at] += jnp.sum(dq.astype(jnp.float32), 0, keepdims=True)
        m.sums[3:4, q_at] += jnp.sum(dv.astype(jnp.float32), 0, keepdims=True)

    in_turn(width // 128, probs_back, scores_back, heads_back)


def forward_front(m, x_ref, length):
    x = x_ref[...].astype(jnp.float32)
    standard, unused = standardized(x)
    m.n1[...] = (standard * m.gain[0:1] + m.shift[0:1]).astype(jnp.bfloat16)
    width = x.shape[1]
    m.need(m.qkv_w)
    value = matmul(m.n1[...], m.qkv_w[...])
    query = (value[:, :width] + m.qv[0:1]).astype(jnp.bfloat16)
    m.qkv[:, :width] = query * jnp.bfloat16(HEAD_DIM ** (-0.5))
    m.qkv[:, width : 2 * width] = value[:, width : 2 * width].astype(jnp.bfloat16)
    m.qkv[:, 2 * width :] = (value[:, 2 * width :] + m.qv[1:2]).astype(jnp.bfloat16)
    attention_forward(m, length)
    m.need(m.out_w)
    middle = x_ref[...].astype(jnp.float32) + matmul(m.att[...], m.out_w[...]) + m.proj[0:1]
    m.middle[...] = middle
    standard, unused = standardized(middle)
    m.n2[...] = (standard * m.gain[1:2] + m.shift[1:2]).astype(jnp.bfloat16)


def back_tail(m, x_ref, g_ref, n2_delta, keep):
    middle_part, gain, shift = norm_step_back(n2_delta, m.middle[...], m.gain[1:2])
    m.sums[6:7, :gain.shape[1]] += gain
    m.sums[8:9, :gain.shape[1]] += shift
    middle_delta = g_ref[...].astype(jnp.float32) + middle_part
    proj_delta = middle_delta.astype(jnp.bfloat16)
    m.sums[4:5, :gain.shape[1]] += jnp.sum(proj_delta.astype(jnp.float32), 0, keepdims=True)
    m.proj_delta[...] = proj_delta
    m.middle_delta[...] = middle_delta
    m.att_delta[...] = matmul_turned(proj_delta, m.out_w[...]).astype(jnp.bfloat16)
    attention_back(m)
    total = matmul_turned(m.mixed[...], m.qkv_w[...])
    input_part, gain, shift = norm_step_back(total, x_ref[...].astype(jnp.float32), m.gain[0:1])
    m.sums[5:6, :gain.shape[1]] += gain
    m.sums[7:8, :gain.shape[1]] += shift
    keep(m.middle_delta[...] + input_part)


def forward_expert(m, slot, begin, end):
    def columns(j):
        return slice(j * PIECE, (j + 1) * PIECE)

    def widen(j):
        hidden = matmul(m.n2[begin:end], m.up_w[slot, :, columns(j)])
        m.hidden[j % 2, begin:end] = hidden + m.up_b[slot : slot + 1, columns(j)]

    def bend(j):
        hidden = m.hidden[j % 2, begin:end]
        below, bell = normal_parts(hidden)
        m.active[begin:end, columns(j)] = (hidden * below).astype(jnp.bfloat16)
        m.slope[begin:end, columns(j)] = (below + hidden * bell).astype(jnp.bfloat16)

    in_turn(m.up_w.shape[2] // PIECE, widen, bend)
    result = matmul(m.active[begin:end], m.down_w[slot])
    m.total[begin:end] = m.middle[begin:end] + result + m.down_b[slot : slot + 1]


def add_up_sums(m, slot, begin, end):
    for j in range(m.up_w.shape[2] // CHUNK):
        piece = m.hidden_delta[begin:end, j * CHUNK : (j + 1) * CHUNK].astype(jnp.float32)
        m.sums[9 + 3 * slot + j : 10 + 3 * slot + j] += jnp.sum(piece, 0, keepdims=True)


def back_expert(m, g_ref, slot, begin, end):
    m.sums[slot : slot + 1, : g_ref.shape[1]] += jnp.sum(g_ref[begin:end].astype(jnp.float32), 0, keepdims=True)
    active_delta = matmul_turned(g_ref[begin:end], m.down_w[slot])
    m.hidden_delta[begin:end] = (active_delta * m.slope[begin:end].astype(jnp.float32)).astype(jnp.bfloat16)
    m.total[begin:end] = matmul_turned(m.hidden_delta[begin:end], m.up_w[slot])
    add_up_sums(m, slot, begin, end)


def both_expert(m, g_ref):
    m.sums[0:1, : g_ref.shape[1]] += jnp.sum(g_ref[...].astype(jnp.float32), 0, keepdims=True)

    def columns(j):
        return slice(j * PIECE, (j + 1) * PIECE)

    def widen(j):
        m.hidden[j % 2] = matmul(m.n2[...], m.up_w[0, :, columns(j)]) + m.up_b[2:3, columns(j)]
        m.active_delta[j % 2] = matmul_turned(g_ref[...], m.down_w[0, columns(j), :])

    def bend(j):
        hidden = m.hidden[j % 2]
        below, bell = normal_parts(hidden)
        m.active[:, columns(j)] = (hidden * below).astype(jnp.bfloat16)
        slope = below + hidden * bell
        m.hidden_delta[:, columns(j)] = (m.active_delta[j % 2] * slope).astype(jnp.bfloat16)

    in_turn(m.up_w.shape[2] // PIECE, widen, bend)
    m.total[...] = matmul_turned(m.hidden_delta[...], m.up_w[0])
    add_up_sums(m, 0, 0, ROWS)


def join_columns(m):
    chips = m.joint.shape[1] // BLOCK
    mixed, proj = m.mixed.shape[1] // chips, m.proj_delta.shape[1] // chips
    for t in range(chips):
        m.joint[:, t * BLOCK : t * BLOCK + mixed] = m.mixed[:, t * mixed : (t + 1) * mixed]
        m.joint[:, t * BLOCK + mixed : (t + 1) * BLOCK] = m.proj_delta[:, t * proj : (t + 1) * proj]


def layers_kernel(names, *refs):
    m = Refs()
    for name, ref in zip(names, refs):
        setattr(m, name, ref)
    items, length = m.in_tokens.shape[:2]
    half = m.total.shape[1] // 2
    section = lax.axis_index("section")
    across = (1 - section, lax.axis_index("dp"))

    def send(i, part):
        rows = (slice(0, TEXT), slice(TEXT, ROWS))[part]
        return pltpu.make_async_remote_copy(
            src_ref=m.leaving.at[i, rows], dst_ref=m.landed.at[i, rows], send_sem=m.send_sem.at[i, part],
            recv_sem=m.recv_sem.at[i, part], device_id=across, device_id_type=MESH,
        )

    def local(source, target, number):
        return pltpu.make_async_copy(source, target, m.copy_sem.at[number])

    def branch_copy(source, i):
        return pltpu.make_async_copy(source.at[i], m.branch.at[i], m.branch_sem.at[i])

    def weights(experts):
        found = [
            (m.qkv_w, [local(m.in_qkv.at[0], m.qkv_w, 0)]),
            (m.out_w, [local(m.in_out.at[0], m.out_w, 1)]),
            (m.up_w, []),
            (m.down_w, []),
        ]
        for slot, expert in enumerate(experts):
            found[2][1].append(local(m.in_up.at[expert], m.up_w.at[slot], 2 + slot))
            found[3][1].append(local(m.in_down.at[expert], m.down_w.at[slot], 4 + slot))
        return found

    def start_weights(found):
        copies = found[0][1] + found[1][1]
        for pair in zip(found[2][1], found[3][1]):
            copies += pair
        for copy in copies:
            copy.start()

    def needs(found, i):
        def need(ref):
            for here, copies in found:
                if here is ref:

                    @pl.when(i == 0)
                    def _():
                        for copy in copies:
                            copy.wait()

        return need

    leaving = (
        (m.n1, m.out_n1), (m.att, m.out_att), (m.n2, m.out_n2), (m.active, m.out_active), (m.qkv, m.kept_qkv),
        (m.probs, m.kept_probs), (m.att_turned, m.kept_turned), (m.middle, m.kept_middle), (m.slope, m.kept_slope),
        (m.joint, m.out_joint), (m.hidden_delta, m.out_hidden),
    )
    n1, att, n2, active, qkv, probs, turned, middle, slope, joint, hidden = range(len(leaving))

    def puts(i):
        return lambda number: local(leaving[number][0], leaving[number][1].at[i], 6 + number)

    def gets(i):
        return lambda number: local(leaving[number][1].at[i], leaving[number][0], 14 + number)

    def start(copies, *which):
        for number in which:
            copies(number).start()

    def wait(copies, *which):
        for number in which:
            copies(number).wait()

    def settle(i, *which):
        @pl.when(i > 0)
        def _():
            wait(puts(i), *which)

    def text_first(target, source, i):
        value = source[i].astype(jnp.float32)
        pad = jnp.zeros((ROWS - length, value.shape[1]), jnp.float32)
        target[i, :TEXT] = value[PATCHES:].astype(jnp.bfloat16)
        target[i, TEXT:] = jnp.concatenate([value[:PATCHES], pad], axis=0).astype(jnp.bfloat16)

    def mask_targets(i):
        row = lax.broadcasted_iota(jnp.int32, (ROWS, 1), 0)
        position = jnp.where(row < TEXT, row + PATCHES, jnp.where(row < length, row - TEXT, length))
        chosen = jnp.zeros((ROWS, 1), jnp.float32)
        for mask in (m.patch_mask, m.text_mask):
            same = jnp.where(position == mask[i : i + 1, :], 1.0, 0.0)
            chosen = jnp.maximum(chosen, jnp.max(same, 1, keepdims=True))
        m.targets[i] = (m.targets[i].astype(jnp.float32) * chosen).astype(jnp.bfloat16)

    def first_front(found, i, carry):
        m.need = needs(found, i)
        text_first(m.tokens, m.in_tokens, i)
        settle(i, n1, att, n2, qkv, probs, turned, middle)
        forward_front(m, m.tokens.at[i], length)
        start(puts(i), n1, att, n2, qkv, probs, turned, middle)
        settle(i, active, slope)
        m.need(m.up_w)
        m.need(m.down_w)
        forward_expert(m, 1, 0, TEXT)
        m.leaving[i, :TEXT] = m.total[:TEXT].astype(jnp.bfloat16)
        send(i, 0).start()
        forward_expert(m, 0, TEXT, ROWS)
        m.leaving[i, TEXT:] = m.total[TEXT:].astype(jnp.bfloat16)
        send(i, 1).start()
        start(puts(i), active, slope)
        return carry

    def first_back(i, carry):
        start(gets(i), slope, middle, turned, qkv, probs)

        @pl.when(i > 0)
        def _():
            send(i - 1, 0).wait_send()
            send(i - 1, 1).wait_send()

        settle(i, hidden)
        wait(gets(i), slope)
        gradient = m.landed.at[i]
        send(i, 0).wait_recv()
        back_expert(m, gradient, 1, 0, TEXT)
        send(i, 1).wait_recv()
        branch_copy(m.landed, i).start()
        back_expert(m, gradient, 0, TEXT, ROWS)
        start(puts(i), hidden)
        wait(gets(i), middle, turned, qkv, probs)

        def keep(value):
            m.low[i] = value[:, :half]
            m.high[i] = value[:, half:].astype(jnp.bfloat16)

        back_tail(m, m.tokens.at[i], gradient, m.total[...], keep)
        settle(i, joint)
        join_columns(m)
        start(puts(i), joint)
        branch_copy(m.landed, i).wait()
        return carry

    def second_both(found, i, carry):
        m.need = needs(found, i)
        branch_copy(m.targets, i).start()
        send(i, 0).wait_recv()
        send(i, 1).wait_recv()
        settle(i, n1, att, n2)
        arrived = m.landed.at[i]
        forward_front(m, arrived, length)
        start(puts(i), n1, att, n2)
        settle(i, active, hidden)
        m.need(m.up_w)
        m.need(m.down_w)
        gradient = m.targets.at[i]
        both_expert(m, gradient)
        start(puts(i), active, hidden)

        def keep(value):
            m.leaving[i] = value.astype(jnp.bfloat16)

        back_tail(m, arrived, gradient, m.total[...], keep)
        send(i, 0).start()
        send(i, 1).start()
        settle(i, joint)
        join_columns(m)
        start(puts(i), joint)
        branch_copy(m.targets, i).wait()
        return carry

    m.sums[...] = jnp.zeros(m.sums.shape, jnp.float32)
    barrier = pltpu.get_barrier_semaphore()
    pl.semaphore_signal(barrier, inc=1, device_id=across, device_id_type=MESH)

    @pl.when(section == 0)
    def _():
        found = weights((0, 1))
        start_weights(found)
        pl.semaphore_wait(barrier, 1)
        lax.fori_loop(0, items, functools.partial(first_front, found), 0)
        wait(puts(0), n1, att, n2, active, qkv, probs, turned, middle, slope)
        lax.fori_loop(0, items, first_back, 0)
        wait(puts(0), joint, hidden)
        send(items - 1, 0).wait_send()
        send(items - 1, 1).wait_send()

    @pl.when(section == 1)
    def _():
        found = weights((2,))
        start_weights(found)
        for i in range(items):
            text_first(m.targets, m.cotangent, i)
            mask_targets(i)
        pl.semaphore_wait(barrier, 1)
        lax.fori_loop(0, items, functools.partial(second_both, found), 0)
        wait(puts(0), n1, att, n2, active, joint, hidden)
        for i in range(items):
            send(i, 0).wait_send()
            send(i, 1).wait_send()


def both_layers(
    tokens, cotangent, patch_mask, text_mask, qkv_weight, out_weight, up_table, down_table, qv, proj, gain, shift, up_b, down_b
):
    items, length, width = tokens.shape
    rows = ROWS
    ff = up_b.shape[1]
    heads = width // HEAD_DIM
    bf16, f32 = jnp.bfloat16, jnp.float32
    dma = pltpu.SemaphoreType.DMA
    vmem, anywhere = pl.BlockSpec(memory_space=pltpu.VMEM), pl.BlockSpec(memory_space=pl.ANY)
    ins = dict(
        in_tokens=(tokens, vmem), cotangent=(cotangent, vmem), patch_mask=(patch_mask, vmem), text_mask=(text_mask, vmem), in_qkv=(qkv_weight, anywhere), in_out=(out_weight, anywhere),
        in_up=(up_table, anywhere), in_down=(down_table, anywhere), qv=(qv, vmem), proj=(proj, vmem), gain=(gain, vmem),
        shift=(shift, vmem), up_b=(up_b, vmem), down_b=(down_b, vmem),
    )

    def made(*shape, kind=bf16, spec=anywhere):
        return jax.ShapeDtypeStruct((items,) + shape, kind), spec

    outs = dict(
        out_n1=made(rows, width), out_att=made(rows, width), out_n2=made(rows, width), out_active=made(rows, ff),
        out_joint=made(rows, 4 * width), out_hidden=made(rows, ff), branch=made(rows, width),
        kept_qkv=made(rows, 3 * width), kept_probs=made(heads, rows, rows), kept_turned=made(width, rows),
        kept_middle=made(rows, width, kind=f32), kept_slope=made(rows, ff),
        low=made(rows, width // 2, kind=f32, spec=vmem), high=made(rows, width // 2, spec=vmem),
        sums=(jax.ShapeDtypeStruct((16, CHUNK), f32), vmem),
    )
    low_row, wide_row = ((rows, width), bf16), ((rows, ff), bf16)
    buffers = dict(
        qkv_w=((width, 3 * width), bf16), out_w=((width, width), bf16), up_w=((2, width, ff), bf16),
        down_w=((2, ff, width), bf16), n1=low_row, att=low_row, n2=low_row, active=wide_row,
        qkv=((rows, 3 * width), bf16), probs=((heads, rows, rows), bf16), att_turned=((width, rows), bf16),
        middle=((rows, width), f32), slope=wide_row, total=((rows, width), f32), mixed=((rows, 3 * width), bf16),
        proj_delta=low_row, joint=((rows, 4 * width), bf16), scores=((2, 2, rows, rows), f32),
        score_delta=((2, 2, rows, rows), bf16), inner=((2, 2, 1, rows), f32), hidden=((2, rows, PIECE), f32),
        active_delta=((2, rows, PIECE), f32), hidden_delta=wide_row, att_delta=low_row, middle_delta=((rows, width), f32),
        leaving=((items, rows, width), bf16), landed=((items, rows, width), bf16),
        tokens=((items, rows, width), bf16), targets=((items, rows, width), bf16),
    )
    semaphores = dict(
        copy_sem=dma((23,)), branch_sem=dma((items,)), send_sem=dma((items, 2)), recv_sem=dma((items, 2)),
    )
    names = list(ins) + list(outs) + list(buffers) + list(semaphores)
    results = pl.pallas_call(
        functools.partial(layers_kernel, names),
        out_shape=[shape for shape, spec in outs.values()],
        in_specs=[spec for value, spec in ins.values()],
        out_specs=[spec for shape, spec in outs.values()],
        scratch_shapes=[pltpu.VMEM(*kind) for kind in buffers.values()] + list(semaphores.values()),
        compiler_params=pltpu.CompilerParams(
            collective_id=1, has_side_effects=True, vmem_limit_bytes=60 * 1024 * 1024
        ),
        cost_estimate=pl.CostEstimate(flops=40_000_000_000, bytes_accessed=100_000_000, transcendentals=0),
    )(*[value for value, spec in ins.values()])
    m = Refs()
    for name, result in zip(outs, results):
        setattr(m, name, result)
    return m


def small_outs(own, other, is_first, width):
    first = jnp.where(is_first, own, other)
    second = jnp.where(is_first, other, own)
    me = lax.axis_index("dp")

    def columns(rows):
        wide = rows.shape[-1] // lax.axis_size("dp")
        return lax.dynamic_slice_in_dim(rows, me * wide, wide, rows.ndim - 1)

    down = columns(jnp.concatenate([first[:2], second[:1]])[:, :width])
    up = columns(jnp.concatenate([first[9:15].reshape(2, -1), second[9:12].reshape(1, -1)]))
    own = columns(own[2:9, :width])
    return own[0:2], own[2:3], own[3:5], own[5:7], up, down


def flat(value):
    return value.reshape((-1, value.shape[-1]))


def left_parts(m, is_first):
    n1, att, n2, branch_delta = (flat(part) for part in (m.out_n1, m.out_att, m.out_n2, m.branch))
    text = (jnp.arange(n1.shape[0]) % ROWS < TEXT)[:, None]
    vision = jnp.logical_not(text & is_first).astype(jnp.bfloat16)
    text = text.astype(jnp.bfloat16)
    return [
        piece.T for piece in (n2 * vision, branch_delta * vision, n2 * text, branch_delta * text, n1, att)
    ]


def all_grads(m, length):
    up, down, qkv, out, input_grad, *small = finished(
        length,
        *summed_grads(m.out_n1, m.out_att, m.out_n2, m.branch, m.out_hidden, m.out_active, m.out_joint, m.high, m.sums),
        m.low,
    )
    return qkv.T, out.T, up.transpose(0, 2, 1), down, small, input_grad


def large_grads_plain(m, is_first):
    lefts = left_parts(m, is_first)
    hidden_delta, active = flat(m.out_hidden), flat(m.out_active)

    def total_of(left, right):
        product = jnp.dot(left, right, preferred_element_type=jnp.float32).astype(jnp.bfloat16)
        return lax.psum_scatter(product, "dp", scatter_dimension=1, tiled=True)

    def table(vision_part, text_part):
        def swapped(part):
            return lax.psum(part, "section").astype(jnp.float32)

        return jnp.stack(
            [
                swapped(jnp.where(is_first, vision_part, 0)),
                swapped(jnp.where(is_first, text_part, 0)),
                swapped(jnp.where(is_first, 0, vision_part)),
            ]
        )

    up = table(total_of(lefts[0], hidden_delta), total_of(lefts[2], hidden_delta))
    down = table(total_of(lefts[1], active), total_of(lefts[3], active))
    small = lax.psum(m.sums, "dp")
    joint = flat(m.out_joint)
    joint = joint.reshape(joint.shape[0], -1, BLOCK)
    mixed, proj = (part.reshape(joint.shape[0], -1) for part in (joint[:, :, :288], joint[:, :, 288:]))
    return (
        total_of(lefts[4], mixed).astype(jnp.float32),
        total_of(lefts[5], proj).astype(jnp.float32),
        up,
        down.transpose(0, 2, 1),
        small,
        lax.ppermute(small, "section", [(0, 1), (1, 0)]),
    )


def shards(
    tokens, cotangent, patch_mask, text_mask, qkv_weight, qv_bias, out_weight, out_bias, norm_gain, norm_bias,
    up_table, up_bias, down_table, down_bias,
):
    is_first = lax.axis_index("section") == 0
    m = both_layers(
        tokens, cotangent, patch_mask, text_mask, qkv_weight, out_weight, up_table, down_table, qv_bias[0], out_bias,
        norm_gain[0], norm_bias[0], up_bias, down_bias,
    )
    if lax.axis_size("dp") == 16:
        qkv, out, up, down, small, input_grad = all_grads(m, tokens.shape[1])
    else:
        qkv, out, up, down, own, other = large_grads_plain(m, is_first)
        small = small_outs(own, other, is_first, tokens.shape[2])
        high = lax.ppermute(m.high, "section", [(0, 1)])
        value = jnp.where(is_first, m.low, high.astype(jnp.float32))
        input_grad = jnp.concatenate([value[:, TEXT : tokens.shape[1]], value[:, :TEXT]], axis=1)
    qv_part, proj_part, gain_part, shift_part, up_part, down_part = small
    return (
        input_grad, qkv[None], qv_part[None], out[None], proj_part, gain_part[None], shift_part[None],
        up, up_part, down, down_part,
    )


def solution(mesh):
    items, layers = P("dp"), P("section")
    return jax.shard_map(
        shards,
        mesh=mesh,
        in_specs=(items,) * 4 + (layers,) * 6 + (P(),) * 4,
        out_specs=(
            P("dp", None, "section"), P("section", None, "dp"), P("section", None, "dp"), P("section", None, "dp"),
            P("section", "dp"), P("section", None, "dp"), P("section", None, "dp"),
            P(None, None, "dp"), P(None, "dp"), P(None, "dp", None), P(None, "dp"),
        ),
        check_vma=False,
    )
```

```python
import functools

import jax
import jax.numpy as jnp
from jax import lax
from jax.experimental import pallas as pl
from jax.experimental.pallas import tpu as pltpu
from jax.sharding import PartitionSpec as P

HEAD_DIM = 64
PATCHES = 197
EPSILON = 1e-05
BLOCK = 384
WINDOW = 640
RING = 3
TEXT = 64
ROWS = 272
MESH = pl.DeviceIdType.MESH


UNITS = (
    (
        (2, 2, 0), (3, 2, 0), (2, 3, 0), (3, 0, 0), (0, 1, 0), (3, 3, 0), (0, 2, 0), (3, 1, 0), (2,
        0, 0), (4, 3, 1), (1, 0, 0), (0, 3, 0), (0, 0, 1), (2, 1, 0), (1, 3, 0), (1, 1, 0), (4, 0,
        0), (4, 1, 0), (1, 2, 0), (4, 2, 0),
    ),
    (
        (0, 2, 0), (1, 0, 0), (1, 2, 0), (1, 1, 0), (0, 1, 0), (0, 3, 1), (4, 1, 1), (4, 2, 0), (1,
        3, 0), (0, 0, 0), (3, 0, 0), (4, 0, 0), (3, 2, 0), (3, 3, 0), (4, 3, 0), (3, 1, 0), (2, 1,
        0),
    ),
)
WAIT = 4
HOP = 3
MEET = WAIT + 3 * HOP + 1
MEET_LATE = MEET + 2
LEFT_OF = ((0,), (1,), (0,), (1,), (2, 3))
MOVED = [unit[:2] for unit in UNITS[1] if unit[0] in (2, 3)]
MOVED_BITS = sum(1 << (4 * kind + plane) for kind, plane in MOVED)
FIRST_MOVED = min(u for u, unit in enumerate(UNITS[1]) if unit[:2] in MOVED)


def packed(units, handed_on):
    counts = [0, 0]
    codes = []
    for kind, plane, z_first in units:
        slot = 0
        if not (handed_on and (kind, plane) in MOVED):
            slot = counts[z_first]
            counts[z_first] += 1
        codes.append(kind | plane << 3 | z_first << 5 | slot << 6)
    codes += [0] * (-len(codes) % 3)
    return [codes[i] | codes[i + 1] << 10 | codes[i + 2] << 20 for i in range(0, len(codes), 3)], counts


PACKED, COUNTS = zip(*(packed(units, side == 0) for side, units in enumerate(UNITS)))
Y_UNITS, Z_UNITS = (max(COUNTS[0][way], COUNTS[1][way], 1) for way in range(2))


def look_up(words, u):
    word = words[0]
    for n in range(1, len(words)):
        word = jnp.where(u // 3 == n, words[n], word)
    return word >> (10 * (u % 3))


class Refs:
    pass


def sum_kernel(names, *refs):
    m = Refs()
    for name, ref in zip(names, refs):
        setattr(m, name, ref)
    section = lax.axis_index("section")
    me = lax.axis_index("dp")
    z, y, core = me // 4, (me // 2) % 2, me % 2
    peer = (section, me + 1 - 2 * core)
    beside = (section, me + 2 - 4 * y)
    right = (section, me + 4)
    left = (section, me - 4)
    aslant = (1 - section, me + 1 - 2 * core)
    across = (1 - section, me)
    on_first = section == 0
    units = jnp.where(on_first, len(UNITS[0]), len(UNITS[1]))
    computed = jnp.where(on_first, len(UNITS[0]), len(UNITS[1]) - len(MOVED))

    arrivals = [u for u, unit in enumerate(UNITS[1]) if unit[:2] in MOVED]

    def is_moved(kind, plane):
        return ((MOVED_BITS >> (4 * kind + plane)) & 1) == 1

    class Unit:
        def __init__(self, u):
            self.u = u
            code = jnp.where(on_first, look_up(PACKED[0], u), look_up(PACKED[1], u))
            self.kind = code & 7
            self.plane = (code >> 3) & 3
            self.z_first = ((code >> 5) & 1) == 1
            self.slot = (code >> 6) & 15
            moved = is_moved(self.kind, self.plane)
            self.handed_on = on_first & moved
            self.handed_in = jnp.logical_not(on_first) & moved
            self.y_first = jnp.logical_not(self.z_first | self.handed_on)
            self.y_slot = self.slot + jnp.where(self.z_first, Y_UNITS, 0)
            self.uses_text = jnp.logical_not(on_first) | (self.kind > 1)
            self.uses_patches = jnp.logical_not(on_first) | (self.kind < 2) | (self.kind == 4)
            self.order = u
            for at in arrivals:
                self.order = self.order - jnp.where((section == 1) & (u > at), 1, 0)

    def following(u):
        u = u + 1
        for at in arrivals:
            u = u + jnp.where((section == 1) & (u == at), 1, 0)
        return u

    def remote(src, dst, send, recv, device):
        return pltpu.make_async_remote_copy(
            src_ref=src, dst_ref=dst, send_sem=send, recv_sem=recv, device_id=device, device_id_type=MESH
        )

    def core_copy(order, b):
        slot = order % RING
        return remote(m.made.at[slot, 1 - core, b], m.xr.at[slot, b], m.core_send.at[order, b], m.core_recv.at[order, b], peer)

    def y_copy(n):
        return remote(m.part.at[n.u, 0], m.yr.at[n.y_slot], m.y_send.at[n.y_slot], m.y_recv.at[n.y_slot], beside)

    def right_copy(n):
        return remote(m.part.at[n.u, 1], m.zr.at[n.slot], m.right_send.at[n.slot], m.right_recv.at[n.slot], right)

    def left_copy(n):
        return remote(m.part.at[n.u, 1], m.zl.at[n.slot], m.left_send.at[n.slot], m.left_recv.at[n.slot], left)

    def right_pair(n):
        g = n.slot
        return remote(m.part.at[n.u], m.wr.at[g], m.right_send.at[Y_UNITS + g], m.right_recv.at[Y_UNITS + g], right)

    def left_pair(n):
        g = n.slot
        return remote(m.part.at[n.u], m.wl.at[g], m.left_send.at[Y_UNITS + g], m.left_recv.at[Y_UNITS + g], left)

    def over_copy(n, source, target):
        number = 4 * (n.kind - 2) + n.plane
        return remote(m.part.at[source], m.part.at[target], m.over_send.at[number], m.over_recv.at[number], across)

    def over_target(n):
        target = 0
        for at in arrivals:
            kind, plane, unused = UNITS[1][at]
            target = target + jnp.where((n.kind == kind) & (n.plane == plane), at, 0)
        return target

    def half_copy():
        return remote(m.half, m.half_out, m.half_send.at[0], m.half_recv.at[0], across)

    def own_half():
        return pl.ds(pl.multiple_of(core * BLOCK, 128), BLOCK)

    def mine(size):
        return pl.ds(pl.multiple_of(core * size, 16), size)

    def theirs(size):
        return pl.ds(pl.multiple_of((1 - core) * size, 16), size)

    def table_of(k, by_second):
        return jnp.where((k < 2) & by_second, 2, k // 2) + jnp.where(k % 2 == 1, 3, 0)

    def table_rows(k, by_second):
        return m.tables_out.at[table_of(k, by_second), :, own_half()]

    def peer_copy(k):
        return remote(m.turned.at[k, theirs(192)], table_rows(k, section == 1), m.peer_send.at[k], m.peer_recv.at[k], peer)

    def cross_copy(k, by_second, other_core):
        source = theirs(192) if other_core else mine(192)
        device = aslant if other_core else across
        number = 1 if other_core else 0
        return remote(
            m.turned.at[k, source], table_rows(k, by_second), m.cross_send.at[number, k], m.cross_recv.at[number, k], device
        )

    def attention_copies():
        rows = pl.ds(pl.multiple_of(288 + (1 - core) * 48, 16), 48)
        return (
            remote(m.turned.at[4, theirs(144)], m.qkv_out.at[:, own_half()], m.peer_send.at[4], m.peer_recv.at[4], peer),
            remote(m.turned.at[4, rows], m.out_out.at[:, own_half()], m.peer_send.at[5], m.peer_recv.at[5], peer),
        )

    def start_cross(k):
        cross_copy(k, section == 1, False).start()
        cross_copy(k, section == 1, True).start()

    def mixed_start(plane):
        return pl.multiple_of((9 * plane // 2) * 128, 128)

    def proj_start(plane):
        return pl.multiple_of((3 * plane // 2) * 128, 128)

    def tile_copies(n):
        k = n.kind
        slot = n.order % 2
        wide = pl.ds(pl.multiple_of(n.plane * 2 * BLOCK, 128), 2 * BLOCK)
        cases = []
        for ref, number, here, source, target in (
            (m.hidden, 0, (k == 0) | (k == 2), wide, slice(0, 2 * BLOCK)),
            (m.active, 0, (k == 1) | (k == 3), wide, slice(0, 2 * BLOCK)),
            (m.mixed, 0, k == 4, pl.ds(mixed_start(n.plane), WINDOW), slice(0, WINDOW)),
            (m.proj, 1, k == 4, pl.ds(proj_start(n.plane), 256), slice(WINDOW, WINDOW + 256)),
        ):
            copy = pltpu.make_async_copy(
                ref.at[:, :TEXT, source], m.text_tile.at[slot, :, :, target], m.text_sem.at[slot, number]
            )
            cases.append((here & n.uses_text, copy))
            copy = pltpu.make_async_copy(
                ref.at[:, TEXT:, source], m.patch_tile.at[slot, :, :, target], m.patch_sem.at[slot, number]
            )
            cases.append((here & n.uses_patches, copy))
        return cases

    def join_columns(slot, begin):
        for tile, joint in ((m.text_tile, m.text_joint), (m.patch_tile, m.patch_joint)):
            for side in range(2):
                at, mixed, proj = side * BLOCK, begin + side * 288, WINDOW + begin + side * 96
                joint[:, :, at : at + 288] = tile[slot, :, :, mixed : mixed + 288]
                joint[:, :, at + 288 : at + BLOCK] = tile[slot, :, :, proj : proj + 96]

    def start_tile(n):
        for here, copy in tile_copies(n):
            pl.when(here)(copy.start)

    def wait_tile(n):
        for here, copy in tile_copies(n):
            pl.when(here)(copy.wait)

    def add_into(target, source):
        target[...] = target[...] + source[...]

    def rows_dot(left, tile, *columns):
        tile = jnp.concatenate([tile[:, :, at] for at in columns], axis=2)
        return matmul(left, tile.reshape(-1, tile.shape[2]))

    def text_dot(index, slot, *columns):
        return rows_dot(m.text_left[index], m.text_tile.at[slot], *columns)

    def patch_dot(index, slot, *columns):
        return rows_dot(m.patch_left[index], m.patch_tile.at[slot], *columns)

    def joint_dot(index, *columns):
        text = rows_dot(m.text_left[index], m.text_joint, *columns)
        return rows_dot(m.patch_left[index], m.patch_joint, *columns) + text

    def compute(n):
        k = n.kind
        slot = n.order % RING

        @pl.when(n.order >= RING)
        def _():
            core_copy(n.order - RING, 0).wait_send()
            core_copy(n.order - RING, 1).wait_send()
            pl.semaphore_wait(m.credit, 1)

        @pl.when(n.order + 1 < computed)
        def _():
            start_tile(Unit(following(n.u)))

        wait_tile(n)
        tile = n.order % 2
        everything = slice(0, 2 * BLOCK)

        def put(value, columns, begin):
            for half in range(2):
                for side in range(2):
                    piece = value[half * BLOCK : (half + 1) * BLOCK, columns[side]]
                    at = slice(begin, begin + piece.shape[1])
                    m.made[slot, half, jnp.where(y == side, 1, 0), :, at] = piece.astype(jnp.bfloat16)

        sides = (slice(0, BLOCK), slice(BLOCK, 2 * BLOCK))

        @pl.when((k < 4) & jnp.logical_not(n.uses_text))
        def _():
            put(patch_dot(k % 2, tile, everything), sides, 0)

        @pl.when((k < 4) & jnp.logical_not(n.uses_patches))
        def _():
            put(text_dot(k % 2, tile, everything), sides, 0)

        @pl.when((k < 4) & n.uses_text & n.uses_patches)
        def _():
            put(patch_dot(k % 2, tile, everything) + text_dot(k % 2, tile, everything), sides, 0)

        @pl.when(k == 4)
        def _():
            ends = (slice(256, BLOCK), slice(BLOCK + 256, 2 * BLOCK))
            for odd in range(2):
                pl.when(n.plane % 2 == odd)(functools.partial(join_columns, tile, 64 * odd))
            mixed = joint_dot(2, everything)
            proj = joint_dot(3, *ends)
            put(mixed, (slice(0, 256), slice(BLOCK, BLOCK + 256)), 0)
            lanes = lax.broadcasted_iota(jnp.int32, (1, 128), 1)
            last = [jnp.where(lanes < 32, mixed[:, ends[side]], proj[:, 128 * side : 128 * side + 128]) for side in range(2)]
            put(jnp.concatenate(last, axis=1), (slice(0, 128), slice(128, 256)), 256)

        core_copy(n.order, 0).start()
        core_copy(n.order, 1).start()

    def join_core(n):
        slot = n.order % RING

        @pl.when(n.handed_in)
        def _():
            over_copy(n, 0, n.u).wait_recv()

        @pl.when(jnp.logical_not(n.handed_in))
        def _():
            core_copy(n.order, 0).wait_recv()
            m.part[n.u, 0] = m.made[slot, core, 0] + m.xr[slot, 0]

        pl.when(n.y_first)(lambda: y_copy(n).start())

        @pl.when(jnp.logical_not(n.handed_in))
        def _():
            core_copy(n.order, 1).wait_recv()
            m.part[n.u, 1] = m.made[slot, core, 1] + m.xr[slot, 1]

            @pl.when(n.order + RING < computed)
            def _():
                pl.semaphore_signal(m.credit, inc=1, device_id=peer, device_id_type=MESH)

        pl.when(n.handed_on)(lambda: over_copy(n, n.u, over_target(n)).start())

    def join_y(n):
        y_copy(n).wait_recv()
        add_into(m.part.at[n.u, 1], m.yr.at[n.y_slot])

    def take(n, one, pair, single_from, pair_from):
        @pl.when(n.y_first)
        def _():
            one(n).wait_recv()
            add_into(m.part.at[n.u, 1], single_from.at[n.slot])

        @pl.when(n.z_first)
        def _():
            pair(n).wait_recv()
            add_into(m.part.at[n.u], pair_from.at[n.slot])

    def take_right(n):
        take(n, right_copy, right_pair, m.zr, m.wr)

    def take_left(n):
        take(n, left_copy, left_pair, m.zl, m.wl)

    def pass_right(n):
        pl.when(z > 0)(lambda: take_right(n))
        pl.when(n.y_first)(lambda: right_copy(n).start())
        pl.when(n.z_first)(lambda: right_pair(n).start())

    def pass_left(n):
        pl.when(z < 3)(lambda: take_left(n))
        pl.when(n.y_first)(lambda: left_copy(n).start())
        pl.when(n.z_first)(lambda: left_pair(n).start())

    def give(n, i):
        k = n.kind
        m.turned[k] = m.part[n.u, 1].T

        @pl.when(k < 4)
        def _():
            m.tables_out[table_of(k, section == 1), :, own_half()] = m.turned[k, mine(192), :]
            peer_copy(k).start()
            pl.when(on_first | (i > FIRST_MOVED))(lambda: start_cross(k))

        @pl.when(k == 4)
        def _():
            m.qkv_out[:, own_half()] = m.turned[4, mine(144), :]
            m.out_out[:, own_half()] = m.turned[4, pl.ds(pl.multiple_of(288 + core * 48, 16), 48), :]
            for copy in attention_copies():
                copy.start()

    def greet_first(u, carry):
        n = Unit(u)
        ended = jnp.where(n.z_first, MEET_LATE, MEET) + u <= FIRST_MOVED
        pl.when(ended & (n.kind < 4) & (n.plane == z))(lambda: start_cross(n.kind))
        return carry

    def meet(n, i):
        pl.when(z > 0)(lambda: take_right(n))
        pl.when(z < 3)(lambda: take_left(n))
        pl.when(n.z_first)(lambda: y_copy(n).start())
        pl.when(n.y_first)(lambda: give(n, i))

    def meet_late(n, i):
        join_y(n)
        give(n, i)

    flips = (peer, beside, (section, me + 4 - 8 * (z % 2)), (section, me + 8 - 16 * (z // 2)), across)

    def small_copy(j):
        return remote(m.small_sum.at[j], m.small_in.at[j], m.small_send.at[j], m.small_recv.at[j], flips[j])

    def small_step(j):
        if j == 0:
            m.small_sum[0] = m.small[...]
        else:
            small_copy(j - 1).wait_recv()
            if j == 5:
                m.small_out[0] = m.small_sum[4]
                m.small_out[1] = m.small_in[4]
            else:
                m.small_sum[j] = m.small_sum[j - 1] + m.small_in[j - 1]
        if j < 5:
            small_copy(j).start()

    lefts = (m.n2, m.branch, m.n1, m.att)
    turns = [[], []]
    for side in range(2):
        for kind, plane, z_first in UNITS[side]:
            for index in () if side == 1 and (kind, plane) in MOVED else LEFT_OF[kind]:
                if index not in turns[side]:
                    turns[side].append(index)

    def stage_copy(index):
        return pltpu.make_async_copy(lefts[index], m.stage, m.stage_sem.at[0])

    def start_stage(turn):
        for side in range(2):
            pl.when(section == side)(stage_copy(turns[side][turn]).start)

    def prepare(turn):
        stage_copy(0).wait()
        number = jnp.where(on_first, turns[0][turn], turns[1][turn])

        def part(c, carry):
            at = pl.ds(pl.multiple_of(c * 128, 128), 128)
            m.text_left[number, at, :] = m.stage[:, :TEXT, at].reshape(-1, 128).T
            m.patch_left[number, at, :] = m.stage[:, TEXT:, at].reshape(-1, 128).T
            return carry

        lax.fori_loop(0, m.stage.shape[2] // 128, part, 0)
        if turn < 3:
            start_stage(turn + 1)

    barrier = pltpu.get_barrier_semaphore()
    for device in (peer, beside, flips[3]):
        pl.semaphore_signal(barrier, inc=1, device_id=device, device_id_type=MESH)

    @pl.when(section == 1)
    def _():
        for device in (across, aslant):
            pl.semaphore_signal(barrier, inc=1, device_id=device, device_id_type=MESH)

    @pl.when(z < 3)
    def _():
        pl.semaphore_signal(barrier, inc=1, device_id=right, device_id_type=MESH)

    @pl.when(z > 0)
    def _():
        pl.semaphore_signal(barrier, inc=1, device_id=left, device_id_type=MESH)

    start_stage(0)
    start_tile(Unit(jnp.int32(0)))
    prepare(0)
    pl.semaphore_wait(barrier, 3 + jnp.where(on_first, 2, 0) + jnp.where(z < 3, 1, 0) + jnp.where(z > 0, 1, 0))

    @pl.when(on_first)
    def _():
        for device in (across, aslant):
            pl.semaphore_signal(m.ready, inc=1, device_id=device, device_id_type=MESH)
        half_copy().start()


    def at_unit(u, condition, action, *more):
        n = Unit(jnp.maximum(u, 0))

        @pl.when((u >= 0) & (u < units) & condition(n))
        def _():
            action(n, *more)

    def in_flow(n):
        return jnp.logical_not(n.handed_on)

    def step(i, carry):
        @pl.when((i == FIRST_MOVED + 1) & (section == 1))
        def _():
            pl.semaphore_wait(m.ready, 2)
            lax.fori_loop(0, units, greet_first, 0)

        at_unit(i, lambda n: jnp.logical_not(n.handed_in), compute)
        for number in range(3):
            pl.when(i == number)(functools.partial(prepare, number + 1))
        at_unit(i - 1, lambda n: n.kind >= 0, join_core)
        at_unit(i - WAIT, lambda n: n.y_first, join_y)
        at_unit(i - WAIT - HOP * z, lambda n: in_flow(n) & (n.plane > z), pass_right)
        at_unit(i - WAIT - HOP * (3 - z), lambda n: in_flow(n) & (n.plane < z), pass_left)
        at_unit(i - MEET, lambda n: in_flow(n) & (n.plane == z), meet, i)
        at_unit(i - MEET_LATE, lambda n: n.z_first & (n.plane == z), meet_late, i)
        for j in range(4):
            pl.when(i == 3 + j)(functools.partial(small_step, j))
        return carry

    lax.fori_loop(0, units + MEET_LATE, step, 0)
    small_step(4)

    def ours(k):
        return True if k in (0, 1, 4) else is_moved(k, z) == (section == 1)

    def when_ours(k, wanted, action):
        pl.when(jnp.logical_not(ours(k) ^ wanted) if k in (2, 3) else True)(action)

    small_step(5)

    def settle(u, carry):
        n = Unit(u)

        @pl.when(jnp.logical_not(n.handed_in) & (n.order >= computed - RING))
        def _():
            core_copy(n.order, 0).wait_send()
            core_copy(n.order, 1).wait_send()

        pl.when(n.handed_on)(lambda: over_copy(n, n.u, over_target(n)).wait_send())
        pl.when(n.y_first | (n.z_first & (n.plane == z)))(lambda: y_copy(n).wait_send())
        pl.when(n.y_first & (n.plane > z))(lambda: right_copy(n).wait_send())
        pl.when(n.z_first & (n.plane > z))(lambda: right_pair(n).wait_send())
        pl.when(n.y_first & (n.plane < z))(lambda: left_copy(n).wait_send())
        pl.when(n.z_first & (n.plane < z))(lambda: left_pair(n).wait_send())
        return carry

    lax.fori_loop(0, units, settle, 0)
    for j in range(5):
        small_copy(j).wait_send()
    for k in range(4):

        def arrived(k=k):
            for other_core in (False, True):
                cross_copy(k, section == 0, other_core).wait_recv()

        def sent(k=k):
            peer_copy(k).wait()
            for other_core in (False, True):
                cross_copy(k, section == 1, other_core).wait_send()

        when_ours(k, True, sent)
        when_ours(k, False, arrived)
    for copy in attention_copies():
        copy.wait()

    @pl.when(on_first)
    def _():
        half_copy().wait_send()

    @pl.when(section == 1)
    def _():
        half_copy().wait_recv()

def summed_grads(n1, att, n2, branch, hidden, active, mixed, proj, half, small):
    dma = pltpu.SemaphoreType.DMA
    items, depth, width = n1.shape
    bf16, f32 = jnp.bfloat16, jnp.float32
    tile = (BLOCK, BLOCK)
    vmem, anywhere = pl.BlockSpec(memory_space=pltpu.VMEM), pl.BlockSpec(memory_space=pl.ANY)
    ins = dict(n1=n1, att=att, n2=n2, branch=branch, hidden=hidden, active=active, mixed=mixed, proj=proj, half=half,
        small=small)
    outs = dict(
        tables_out=((6, 192, width), bf16), qkv_out=((144, width), bf16),
        out_out=((48, width), bf16), small_out=((2,) + small.shape, f32), half_out=(half.shape, bf16),
    )
    buffers = dict(
        text_tile=((2, items, TEXT, WINDOW + 256), bf16),
        patch_tile=((2, items, depth - TEXT, WINDOW + 256), bf16), text_joint=((items, TEXT, 2 * BLOCK), bf16),
        patch_joint=((items, depth - TEXT, 2 * BLOCK), bf16), part=((20, 2) + tile, bf16), made=((RING, 2, 2) + tile, bf16),
        xr=((RING, 2) + tile, bf16), yr=((Y_UNITS + Z_UNITS,) + tile, bf16), zr=((Y_UNITS,) + tile, bf16), zl=((Y_UNITS,) + tile, bf16),
        wr=((Z_UNITS, 2) + tile, bf16), wl=((Z_UNITS, 2) + tile, bf16), turned=((5,) + tile, bf16),
        text_left=((4, width, items * TEXT), bf16), patch_left=((4, width, items * (depth - TEXT)), bf16), stage=((items, depth, width), bf16), small_sum=((5,) + small.shape, f32),
        small_in=((5,) + small.shape, f32),
    )
    semaphores = dict(
        small_send=dma((5,)), small_recv=dma((5,)), text_sem=dma((2, 2)), patch_sem=dma((2, 2)), stage_sem=dma((1,)), core_send=dma((20, 2)),
        core_recv=dma((20, 2)), y_send=dma((Y_UNITS + Z_UNITS,)), y_recv=dma((Y_UNITS + Z_UNITS,)), right_send=dma((Y_UNITS + Z_UNITS,)), right_recv=dma((Y_UNITS + Z_UNITS,)),
        left_send=dma((Y_UNITS + Z_UNITS,)), left_recv=dma((Y_UNITS + Z_UNITS,)), over_send=dma((8,)), over_recv=dma((8,)), half_send=dma((1,)), half_recv=dma((1,)), peer_send=dma((6,)),
        peer_recv=dma((6,)), cross_send=dma((2, 4)), cross_recv=dma((2, 4)),
        credit=pltpu.SemaphoreType.REGULAR, ready=pltpu.SemaphoreType.REGULAR,
    )
    names = list(ins) + list(outs) + list(buffers) + list(semaphores)
    return pl.pallas_call(
        functools.partial(sum_kernel, names),
        out_shape=[jax.ShapeDtypeStruct(*kind) for kind in outs.values()],
        in_specs=[anywhere] * 9 + [vmem],
        out_specs=[vmem] * (len(outs) - 1) + [anywhere],
        scratch_shapes=[pltpu.VMEM(*kind) for kind in buffers.values()] + list(semaphores.values()),
        compiler_params=pltpu.CompilerParams(
            collective_id=0, has_side_effects=True, vmem_limit_bytes=60 * 1024 * 1024
        ),
        cost_estimate=pl.CostEstimate(flops=48 * 2 * 768 * 384 * items * depth, bytes_accessed=40_000_000, transcendentals=0),
    )(*ins.values())


def finish_kernel(count, *refs):
    sources, targets = refs[:count], refs[count : count + 11]
    held, made, (load_sem, store_sem) = refs[count + 11 : -7], refs[-7:-2], refs[-2:]
    loads = [pltpu.make_async_copy(*pair, load_sem.at[n]) for n, pair in enumerate(zip(sources, held))]
    stores = [pltpu.make_async_copy(*pair, store_sem.at[n]) for n, pair in enumerate(zip(made, targets[:5]))]
    for load in loads:
        load.start()
    tables, qkv, out, small, half, grad = held
    small_outs = targets[5:]
    loads[0].wait()
    for number, source in enumerate((tables.at[:3], tables.at[3:], qkv, out)):
        if number > 1:
            loads[number - 1].wait()
        made[number][...] = source[...].astype(jnp.float32)
        stores[number].start()
    for load in loads[3:]:
        load.wait()
    section, me = lax.axis_index("section"), lax.axis_index("dp")
    width, wide = tables.shape[2], tables.shape[2] // 16
    ff = width * 4

    def columns(row, size):
        return pltpu.roll(row, (row.shape[1] - size * me) % row.shape[1], 1)[:, :size]

    def up_bias(side, slot):
        return columns(jnp.concatenate([small[side, 9 + 3 * slot + j : 10 + 3 * slot + j] for j in range(3)], axis=1), ff // 16)

    own = columns(small[0, :9, :width], wide)
    other = columns(small[1, :9, :width], wide)
    qv_out, proj_out, gain_out, shift_out, up_bias_out, down_bias_out = small_outs
    qv_out[...] = own[2:4]
    proj_out[...] = own[4:5]
    gain_out[...] = own[5:7]
    shift_out[...] = own[7:9]
    for side in range(2):
        mine, theirs = (own, other) if side == 0 else (other, own)

        @pl.when(section == side)
        def _():
            for i in range(grad.shape[0]):
                place(made[4], i, grad[i] if side == 0 else half[i].astype(jnp.float32))
            stores[4].start()
            down_bias_out[0:2] = mine[0:2]
            down_bias_out[2:3] = theirs[0:1]
            up_bias_out[0:1] = up_bias(side, 0)
            up_bias_out[1:2] = up_bias(side, 1)
            up_bias_out[2:3] = up_bias(1 - side, 0)

    for store in stores:
        store.wait()


def place(target, i, value):
    target[i, :PATCHES] = value[TEXT : target.shape[1]]
    target[i, PATCHES:] = value[:TEXT]


def finished(length, *sources):
    tables, qkv, out, small, half, grad = sources
    width = tables.shape[2]
    shapes = [(3,) + tables.shape[1:]] * 2 + [qkv.shape, out.shape, (grad.shape[0], length, grad.shape[2])]
    shapes += [(rows, width // 16) for rows in (2, 1, 2, 2)] + [(3, width // 4), (3, width // 16)]
    return pl.pallas_call(
        functools.partial(finish_kernel, len(sources)),
        out_shape=[jax.ShapeDtypeStruct(shape, jnp.float32) for shape in shapes],
        in_specs=[pl.BlockSpec(memory_space=pltpu.HBM)] * len(sources),
        out_specs=[pl.BlockSpec(memory_space=pl.ANY)] * 5 + [pl.BlockSpec(memory_space=pltpu.VMEM)] * 6,
        scratch_shapes=[pltpu.VMEM(value.shape, value.dtype) for value in sources]
        + [pltpu.VMEM(shape, jnp.float32) for shape in shapes[:5]]
        + [pltpu.SemaphoreType.DMA((len(sources),)), pltpu.SemaphoreType.DMA((5,))],
        compiler_params=pltpu.CompilerParams(vmem_limit_bytes=60 * 1024 * 1024),
    )(*sources)


CHUNK = 1024
PIECE = 512
KEY_SPLIT = 256
TAIL = (0.319381530, -0.356563782, 1.781477937, -1.821255978, 1.330274429)
PEAK = 0.3989422804014327


def normal_parts(z):
    size = jnp.abs(z)
    scale = 1.0 + 0.2316419 * size
    t = pl.reciprocal(scale, approx=True)
    t = t * (2.0 - scale * t)
    bell = jnp.exp(-0.5 * z * z) * PEAK
    series = TAIL[4]
    for factor in TAIL[3::-1]:
        series = series * t + factor
    upper = bell * (series * t)
    return jnp.where(z >= 0, 1.0 - upper, upper), bell


def matmul(left, right):
    return jnp.dot(left, right, preferred_element_type=jnp.float32)


def matmul_turned(left, right):
    return lax.dot_general(left, right, (((1,), (1,)), ((), ())), preferred_element_type=jnp.float32)


def standardized(values):
    centre = values - jnp.mean(values, -1, keepdims=True)
    inverse = lax.rsqrt(jnp.mean(centre * centre, -1, keepdims=True) + EPSILON)
    return centre * inverse, inverse


def norm_step_back(delta, values, gain_row):
    standard, inverse = standardized(values)
    scaled = delta * gain_row
    moved = inverse * (
        scaled - jnp.mean(scaled, -1, keepdims=True) - standard * jnp.mean(scaled * standard, -1, keepdims=True)
    )
    return moved, jnp.sum(delta * standard, 0, keepdims=True), jnp.sum(delta, 0, keepdims=True)


def half_mask(half):
    lanes = lax.broadcasted_iota(jnp.int32, (1, 128), 1)
    return (lanes < 64) if half == 0 else (lanes >= 64)


def pair_columns(p, part, width):
    return slice(part * width + p * 128, part * width + p * 128 + 128)


def both_halves(pair):
    return jnp.concatenate([jnp.where(half_mask(half), pair, jnp.zeros_like(pair)) for half in range(2)], axis=0)


def in_turn(count, *stages):
    for turn in range(count + len(stages) - 1):
        for number, stage in enumerate(stages):
            if 0 <= turn - number < count:
                stage(turn - number)


def attention_forward(m, length):
    rows, width = m.att.shape

    def scores(p):
        q2 = m.qkv[:, pair_columns(p, 0, width)]
        k2 = m.qkv[:, pair_columns(p, 1, width)]
        m.scores[p % 2] = matmul_turned(both_halves(k2), q2).reshape(2, rows, rows)

    def soften(p):
        for half in range(2):
            top = m.scores[p % 2, half, :KEY_SPLIT]
            low = m.scores[p % 2, half, KEY_SPLIT:]
            key_row = KEY_SPLIT + lax.broadcasted_iota(jnp.int32, low.shape, 0)
            low = jnp.where(key_row < length, low, -1e30)
            peak = jnp.maximum(jnp.max(top, 0, keepdims=True), jnp.max(low, 0, keepdims=True))
            top = jnp.exp(top - peak)
            low = jnp.exp(low - peak)
            over = 1.0 / (jnp.sum(top, 0, keepdims=True) + jnp.sum(low, 0, keepdims=True))
            m.probs[2 * p + half, :KEY_SPLIT] = (top * over).astype(jnp.bfloat16)
            m.probs[2 * p + half, KEY_SPLIT:] = (low * over).astype(jnp.bfloat16)

    def blend(p):
        v_turned = m.qkv[:, pair_columns(p, 2, width)].T
        parts = [matmul(v_turned[64 * half : 64 * half + 64], m.probs[2 * p + half]) for half in range(2)]
        turned = jnp.concatenate(parts, axis=0)
        m.att_turned[p * 128 : p * 128 + 128, :] = turned.astype(jnp.bfloat16)
        m.att[:, p * 128 : p * 128 + 128] = turned.T.astype(jnp.bfloat16)

    in_turn(width // 128, scores, soften, blend)


def attention_back(m):
    rows, width = m.att.shape

    def probs_back(p):
        v2 = m.qkv[:, pair_columns(p, 2, width)]
        d_turned = m.att_delta[:, pair_columns(p, 0, width)].T
        m.scores[p % 2] = matmul(both_halves(v2), d_turned).reshape(2, rows, rows)
        product = d_turned.astype(jnp.float32) * m.att_turned[p * 128 : p * 128 + 128, :].astype(jnp.float32)
        for half in range(2):
            m.inner[p % 2, half] = jnp.sum(product[64 * half : 64 * half + 64], 0, keepdims=True)

    def scores_back(p):
        for half in range(2):
            probs = m.probs[2 * p + half].astype(jnp.float32)
            m.score_delta[p % 2, half] = (probs * (m.scores[p % 2, half] - m.inner[p % 2, half])).astype(jnp.bfloat16)

    def heads_back(p):
        q_at, k_at, v_at = (pair_columns(p, part, width) for part in range(3))
        score = m.score_delta[p % 2]
        probs = m.probs[2 * p : 2 * p + 2].reshape(2 * rows, rows)
        k_turned = m.qkv[:, k_at].T
        value = matmul(probs, m.att_delta[:, q_at])
        key = matmul(score.reshape(2 * rows, rows), m.qkv[:, q_at])
        query = jnp.concatenate(
            [matmul(k_turned[64 * half : 64 * half + 64], score[half]) for half in range(2)], axis=0
        )
        dq = (query.T * HEAD_DIM ** (-0.5)).astype(jnp.bfloat16)
        dk = jnp.where(half_mask(0), key[:rows], key[rows:]).astype(jnp.bfloat16)
        dv = jnp.where(half_mask(0), value[:rows], value[rows:]).astype(jnp.bfloat16)
        m.mixed[:, q_at] = dq
        m.mixed[:, k_at] = dk
        m.mixed[:, v_at] = dv
        m.sums[2:3, q_at] += jnp.sum(dq.astype(jnp.float32), 0, keepdims=True)
        m.sums[3:4, q_at] += jnp.sum(dv.astype(jnp.float32), 0, keepdims=True)

    in_turn(width // 128, probs_back, scores_back, heads_back)


def forward_front(m, x_ref, length):
    x = x_ref[...].astype(jnp.float32)
    standard, unused = standardized(x)
    m.n1[...] = (standard * m.gain[0:1] + m.shift[0:1]).astype(jnp.bfloat16)
    width = x.shape[1]
    m.need(m.qkv_w)
    value = matmul(m.n1[...], m.qkv_w[...])
    query = (value[:, :width] + m.qv[0:1]).astype(jnp.bfloat16)
    m.qkv[:, :width] = query * jnp.bfloat16(HEAD_DIM ** (-0.5))
    m.qkv[:, width : 2 * width] = value[:, width : 2 * width].astype(jnp.bfloat16)
    m.qkv[:, 2 * width :] = (value[:, 2 * width :] + m.qv[1:2]).astype(jnp.bfloat16)
    attention_forward(m, length)
    m.need(m.out_w)
    middle = x_ref[...].astype(jnp.float32) + matmul(m.att[...], m.out_w[...]) + m.proj[0:1]
    m.middle[...] = middle
    standard, unused = standardized(middle)
    m.n2[...] = (standard * m.gain[1:2] + m.shift[1:2]).astype(jnp.bfloat16)


def back_tail(m, x_ref, g_ref, n2_delta, keep):
    middle_part, gain, shift = norm_step_back(n2_delta, m.middle[...], m.gain[1:2])
    m.sums[6:7, :gain.shape[1]] += gain
    m.sums[8:9, :gain.shape[1]] += shift
    middle_delta = g_ref[...].astype(jnp.float32) + middle_part
    proj_delta = middle_delta.astype(jnp.bfloat16)
    m.sums[4:5, :gain.shape[1]] += jnp.sum(proj_delta.astype(jnp.float32), 0, keepdims=True)
    m.proj_delta[...] = proj_delta
    m.middle_delta[...] = middle_delta
    m.att_delta[...] = matmul_turned(proj_delta, m.out_w[...]).astype(jnp.bfloat16)
    attention_back(m)
    total = matmul_turned(m.mixed[...], m.qkv_w[...])
    input_part, gain, shift = norm_step_back(total, x_ref[...].astype(jnp.float32), m.gain[0:1])
    m.sums[5:6, :gain.shape[1]] += gain
    m.sums[7:8, :gain.shape[1]] += shift
    keep(m.middle_delta[...] + input_part)


def forward_expert(m, slot, begin, end):
    def columns(j):
        return slice(j * PIECE, (j + 1) * PIECE)

    def widen(j):
        hidden = matmul(m.n2[begin:end], m.up_w[slot, :, columns(j)])
        m.hidden[j % 2, begin:end] = hidden + m.up_b[slot : slot + 1, columns(j)]

    def bend(j):
        hidden = m.hidden[j % 2, begin:end]
        below, bell = normal_parts(hidden)
        m.active[begin:end, columns(j)] = (hidden * below).astype(jnp.bfloat16)
        m.slope[begin:end, columns(j)] = (below + hidden * bell).astype(jnp.bfloat16)

    in_turn(m.up_w.shape[2] // PIECE, widen, bend)
    result = matmul(m.active[begin:end], m.down_w[slot])
    m.total[begin:end] = m.middle[begin:end] + result + m.down_b[slot : slot + 1]


def add_up_sums(m, slot, begin, end):
    for j in range(m.up_w.shape[2] // CHUNK):
        piece = m.hidden_delta[begin:end, j * CHUNK : (j + 1) * CHUNK].astype(jnp.float32)
        m.sums[9 + 3 * slot + j : 10 + 3 * slot + j] += jnp.sum(piece, 0, keepdims=True)


def back_expert(m, g_ref, slot, begin, end):
    m.sums[slot : slot + 1, : g_ref.shape[1]] += jnp.sum(g_ref[begin:end].astype(jnp.float32), 0, keepdims=True)
    active_delta = matmul_turned(g_ref[begin:end], m.down_w[slot])
    m.hidden_delta[begin:end] = (active_delta * m.slope[begin:end].astype(jnp.float32)).astype(jnp.bfloat16)
    m.total[begin:end] = matmul_turned(m.hidden_delta[begin:end], m.up_w[slot])
    add_up_sums(m, slot, begin, end)


def both_expert(m, g_ref):
    m.sums[0:1, : g_ref.shape[1]] += jnp.sum(g_ref[...].astype(jnp.float32), 0, keepdims=True)

    def columns(j):
        return slice(j * PIECE, (j + 1) * PIECE)

    def widen(j):
        m.hidden[j % 2] = matmul(m.n2[...], m.up_w[0, :, columns(j)]) + m.up_b[2:3, columns(j)]
        m.active_delta[j % 2] = matmul_turned(g_ref[...], m.down_w[0, columns(j), :])

    def bend(j):
        hidden = m.hidden[j % 2]
        below, bell = normal_parts(hidden)
        m.active[:, columns(j)] = (hidden * below).astype(jnp.bfloat16)
        slope = below + hidden * bell
        m.hidden_delta[:, columns(j)] = (m.active_delta[j % 2] * slope).astype(jnp.bfloat16)

    in_turn(m.up_w.shape[2] // PIECE, widen, bend)
    m.total[...] = matmul_turned(m.hidden_delta[...], m.up_w[0])
    add_up_sums(m, 0, 0, ROWS)


def layers_kernel(names, *refs):
    m = Refs()
    for name, ref in zip(names, refs):
        setattr(m, name, ref)
    items, length = m.in_tokens.shape[:2]
    half = m.total.shape[1] // 2
    section = lax.axis_index("section")
    across = (1 - section, lax.axis_index("dp"))

    def send(i, part):
        rows = (slice(0, TEXT), slice(TEXT, ROWS))[part]
        return pltpu.make_async_remote_copy(
            src_ref=m.leaving.at[i, rows], dst_ref=m.landed.at[i, rows], send_sem=m.send_sem.at[i, part],
            recv_sem=m.recv_sem.at[i, part], device_id=across, device_id_type=MESH,
        )

    def side_copies(i):
        return (
            pltpu.make_async_copy(m.low.at[i], m.out_low.at[i], m.side_sem.at[0, i]),
            pltpu.make_async_copy(m.high.at[i], m.out_high.at[i], m.side_sem.at[1, i]),
        )

    def local(source, target, number):
        return pltpu.make_async_copy(source, target, m.copy_sem.at[number])

    def branch_copy(source, i):
        return pltpu.make_async_copy(source.at[i], m.branch.at[i], m.branch_sem.at[i])

    def weights(experts):
        found = [
            (m.qkv_w, [local(m.in_qkv.at[0], m.qkv_w, 0)]),
            (m.out_w, [local(m.in_out.at[0], m.out_w, 1)]),
            (m.up_w, []),
            (m.down_w, []),
        ]
        for slot, expert in enumerate(experts):
            found[2][1].append(local(m.in_up.at[expert], m.up_w.at[slot], 2 + slot))
            found[3][1].append(local(m.in_down.at[expert], m.down_w.at[slot], 4 + slot))
        return found

    def start_weights(found):
        copies = found[0][1] + found[1][1]
        for pair in zip(found[2][1], found[3][1]):
            copies += pair
        for copy in copies:
            copy.start()

    def needs(found, i):
        def need(ref):
            for here, copies in found:
                if here is ref:

                    @pl.when(i == 0)
                    def _():
                        for copy in copies:
                            copy.wait()

        return need

    leaving = (
        (m.n1, m.out_n1), (m.att, m.out_att), (m.n2, m.out_n2), (m.active, m.out_active), (m.qkv, m.kept_qkv),
        (m.probs, m.kept_probs), (m.att_turned, m.kept_turned), (m.middle, m.kept_middle), (m.slope, m.kept_slope),
        (m.mixed, m.out_mixed), (m.proj_delta, m.out_proj), (m.hidden_delta, m.out_hidden),
    )
    n1, att, n2, active, qkv, probs, turned, middle, slope, mixed, proj, hidden = range(len(leaving))

    def puts(i):
        return lambda number: local(leaving[number][0], leaving[number][1].at[i], 6 + number)

    def gets(i):
        return lambda number: local(leaving[number][1].at[i], leaving[number][0], 14 + number)

    def start(copies, *which):
        for number in which:
            copies(number).start()

    def wait(copies, *which):
        for number in which:
            copies(number).wait()

    def settle(i, *which):
        @pl.when(i > 0)
        def _():
            wait(puts(i), *which)

    def text_first(target, source, i):
        value = source[i].astype(jnp.float32)
        pad = jnp.zeros((ROWS - length, value.shape[1]), jnp.float32)
        target[i, :TEXT] = value[PATCHES:].astype(jnp.bfloat16)
        target[i, TEXT:] = jnp.concatenate([value[:PATCHES], pad], axis=0).astype(jnp.bfloat16)

    def mask_targets(i):
        row = lax.broadcasted_iota(jnp.int32, (ROWS, 1), 0)
        position = jnp.where(row < TEXT, row + PATCHES, jnp.where(row < length, row - TEXT, length))
        chosen = jnp.zeros((ROWS, 1), jnp.float32)
        for mask in (m.patch_mask, m.text_mask):
            same = jnp.where(position == mask[i : i + 1, :], 1.0, 0.0)
            chosen = jnp.maximum(chosen, jnp.max(same, 1, keepdims=True))
        m.targets[i] = (m.targets[i].astype(jnp.float32) * chosen).astype(jnp.bfloat16)

    def first_front(found, i, carry):
        m.need = needs(found, i)
        text_first(m.tokens, m.in_tokens, i)
        settle(i, n1, att, n2, qkv, probs, turned, middle)
        forward_front(m, m.tokens.at[i], length)
        start(puts(i), n1, att, n2, qkv, probs, turned, middle)
        settle(i, active, slope)
        m.need(m.up_w)
        m.need(m.down_w)
        forward_expert(m, 1, 0, TEXT)
        m.leaving[i, :TEXT] = m.total[:TEXT].astype(jnp.bfloat16)
        send(i, 0).start()
        forward_expert(m, 0, TEXT, ROWS)
        m.leaving[i, TEXT:] = m.total[TEXT:].astype(jnp.bfloat16)
        send(i, 1).start()
        start(puts(i), active, slope)
        return carry

    def first_back(i, carry):
        start(gets(i), slope, middle, turned, qkv, probs)

        @pl.when(i > 0)
        def _():
            send(i - 1, 0).wait_send()
            send(i - 1, 1).wait_send()

        settle(i, hidden)
        wait(gets(i), slope)
        gradient = m.landed.at[i]
        send(i, 0).wait_recv()
        back_expert(m, gradient, 1, 0, TEXT)
        send(i, 1).wait_recv()
        branch_copy(m.landed, i).start()
        back_expert(m, gradient, 0, TEXT, ROWS)
        start(puts(i), hidden)
        wait(gets(i), middle, turned, qkv, probs)
        settle(i, mixed, proj)

        def keep(value):
            m.low[i] = value[:, :half]
            m.high[i] = value[:, half:].astype(jnp.bfloat16)

        back_tail(m, m.tokens.at[i], gradient, m.total[...], keep)
        for copy in side_copies(i):
            copy.start()
        start(puts(i), mixed, proj)
        branch_copy(m.landed, i).wait()
        return carry

    def second_both(found, i, carry):
        m.need = needs(found, i)
        branch_copy(m.targets, i).start()
        send(i, 0).wait_recv()
        send(i, 1).wait_recv()
        settle(i, n1, att, n2)
        arrived = m.landed.at[i]
        forward_front(m, arrived, length)
        start(puts(i), n1, att, n2)
        settle(i, active, hidden)
        m.need(m.up_w)
        m.need(m.down_w)
        gradient = m.targets.at[i]
        both_expert(m, gradient)
        start(puts(i), active, hidden)
        settle(i, mixed, proj)

        def keep(value):
            m.leaving[i] = value.astype(jnp.bfloat16)

        back_tail(m, arrived, gradient, m.total[...], keep)
        send(i, 0).start()
        send(i, 1).start()
        start(puts(i), mixed, proj)
        branch_copy(m.targets, i).wait()
        return carry

    m.sums[...] = jnp.zeros(m.sums.shape, jnp.float32)
    barrier = pltpu.get_barrier_semaphore()
    pl.semaphore_signal(barrier, inc=1, device_id=across, device_id_type=MESH)

    @pl.when(section == 0)
    def _():
        found = weights((0, 1))
        start_weights(found)
        pl.semaphore_wait(barrier, 1)
        lax.fori_loop(0, items, functools.partial(first_front, found), 0)
        wait(puts(0), n1, att, n2, active, qkv, probs, turned, middle, slope)
        lax.fori_loop(0, items, first_back, 0)
        wait(puts(0), mixed, proj, hidden)
        send(items - 1, 0).wait_send()
        send(items - 1, 1).wait_send()
        for i in range(items):
            for copy in side_copies(i):
                copy.wait()

    @pl.when(section == 1)
    def _():
        found = weights((2,))
        start_weights(found)
        for i in range(items):
            text_first(m.targets, m.cotangent, i)
            mask_targets(i)
        pl.semaphore_wait(barrier, 1)
        lax.fori_loop(0, items, functools.partial(second_both, found), 0)
        wait(puts(0), n1, att, n2, active, mixed, proj, hidden)
        for i in range(items):
            send(i, 0).wait_send()
            send(i, 1).wait_send()


def both_layers(
    tokens, cotangent, patch_mask, text_mask, qkv_weight, out_weight, up_table, down_table, qv, proj, gain, shift, up_b, down_b
):
    items, length, width = tokens.shape
    rows = ROWS
    ff = up_b.shape[1]
    heads = width // HEAD_DIM
    bf16, f32 = jnp.bfloat16, jnp.float32
    dma = pltpu.SemaphoreType.DMA
    vmem, anywhere = pl.BlockSpec(memory_space=pltpu.VMEM), pl.BlockSpec(memory_space=pl.ANY)
    ins = dict(
        in_tokens=(tokens, vmem), cotangent=(cotangent, vmem), patch_mask=(patch_mask, vmem), text_mask=(text_mask, vmem), in_qkv=(qkv_weight, anywhere), in_out=(out_weight, anywhere),
        in_up=(up_table, anywhere), in_down=(down_table, anywhere), qv=(qv, vmem), proj=(proj, vmem), gain=(gain, vmem),
        shift=(shift, vmem), up_b=(up_b, vmem), down_b=(down_b, vmem),
    )

    def made(*shape, kind=bf16, spec=anywhere):
        return jax.ShapeDtypeStruct((items,) + shape, kind), spec

    outs = dict(
        out_n1=made(rows, width), out_att=made(rows, width), out_n2=made(rows, width), out_active=made(rows, ff),
        out_mixed=made(rows, 3 * width), out_proj=made(rows, width), out_hidden=made(rows, ff), branch=made(rows, width),
        kept_qkv=made(rows, 3 * width), kept_probs=made(heads, rows, rows), kept_turned=made(width, rows),
        kept_middle=made(rows, width, kind=f32), kept_slope=made(rows, ff),
        out_low=made(rows, width // 2, kind=f32), out_high=made(rows, width // 2),
        sums=(jax.ShapeDtypeStruct((16, CHUNK), f32), vmem),
    )
    low_row, wide_row = ((rows, width), bf16), ((rows, ff), bf16)
    buffers = dict(
        qkv_w=((width, 3 * width), bf16), out_w=((width, width), bf16), up_w=((2, width, ff), bf16),
        down_w=((2, ff, width), bf16), n1=low_row, att=low_row, n2=low_row, active=wide_row,
        qkv=((rows, 3 * width), bf16), probs=((heads, rows, rows), bf16), att_turned=((width, rows), bf16),
        middle=((rows, width), f32), slope=wide_row, total=((rows, width), f32), mixed=((rows, 3 * width), bf16),
        proj_delta=low_row, scores=((2, 2, rows, rows), f32),
        score_delta=((2, 2, rows, rows), bf16), inner=((2, 2, 1, rows), f32), hidden=((2, rows, PIECE), f32),
        active_delta=((2, rows, PIECE), f32), hidden_delta=wide_row, att_delta=low_row, middle_delta=((rows, width), f32),
        leaving=((items, rows, width), bf16), landed=((items, rows, width), bf16),
        low=((items, rows, width // 2), f32), high=((items, rows, width // 2), bf16),
        tokens=((items, rows, width), bf16), targets=((items, rows, width), bf16),
    )
    semaphores = dict(
        copy_sem=dma((23,)), branch_sem=dma((items,)), side_sem=dma((2, items)), send_sem=dma((items, 2)), recv_sem=dma((items, 2)),
    )
    names = list(ins) + list(outs) + list(buffers) + list(semaphores)
    results = pl.pallas_call(
        functools.partial(layers_kernel, names),
        out_shape=[shape for shape, spec in outs.values()],
        in_specs=[spec for value, spec in ins.values()],
        out_specs=[spec for shape, spec in outs.values()],
        scratch_shapes=[pltpu.VMEM(*kind) for kind in buffers.values()] + list(semaphores.values()),
        compiler_params=pltpu.CompilerParams(
            collective_id=1, has_side_effects=True, vmem_limit_bytes=60 * 1024 * 1024
        ),
        cost_estimate=pl.CostEstimate(flops=40_000_000_000, bytes_accessed=100_000_000, transcendentals=0),
    )(*[value for value, spec in ins.values()])
    m = Refs()
    for name, result in zip(outs, results):
        setattr(m, name, result)
    return m


def small_outs(own, other, is_first, width):
    first = jnp.where(is_first, own, other)
    second = jnp.where(is_first, other, own)
    me = lax.axis_index("dp")

    def columns(rows):
        wide = rows.shape[-1] // lax.axis_size("dp")
        return lax.dynamic_slice_in_dim(rows, me * wide, wide, rows.ndim - 1)

    down = columns(jnp.concatenate([first[:2], second[:1]])[:, :width])
    up = columns(jnp.concatenate([first[9:15].reshape(2, -1), second[9:12].reshape(1, -1)]))
    own = columns(own[2:9, :width])
    return own[0:2], own[2:3], own[3:5], own[5:7], up, down


def flat(value):
    return value.reshape((-1, value.shape[-1]))


def left_parts(m, is_first):
    n1, att, n2, branch_delta = (flat(part) for part in (m.out_n1, m.out_att, m.out_n2, m.branch))
    text = (jnp.arange(n1.shape[0]) % ROWS < TEXT)[:, None]
    vision = jnp.logical_not(text & is_first).astype(jnp.bfloat16)
    text = text.astype(jnp.bfloat16)
    return [
        piece.T for piece in (n2 * vision, branch_delta * vision, n2 * text, branch_delta * text, n1, att)
    ]


def all_grads(m, length):
    up, down, qkv, out, input_grad, *small = finished(
        length,
        *summed_grads(m.out_n1, m.out_att, m.out_n2, m.branch, m.out_hidden, m.out_active, m.out_mixed, m.out_proj, m.out_high, m.sums),
        m.out_low,
    )
    return qkv.T, out.T, up.transpose(0, 2, 1), down, small, input_grad


def large_grads_plain(m, is_first):
    lefts = left_parts(m, is_first)
    hidden_delta, active = flat(m.out_hidden), flat(m.out_active)

    def total_of(left, right):
        product = jnp.dot(left, right, preferred_element_type=jnp.float32).astype(jnp.bfloat16)
        return lax.psum_scatter(product, "dp", scatter_dimension=1, tiled=True)

    def table(vision_part, text_part):
        def swapped(part):
            return lax.psum(part, "section").astype(jnp.float32)

        return jnp.stack(
            [
                swapped(jnp.where(is_first, vision_part, 0)),
                swapped(jnp.where(is_first, text_part, 0)),
                swapped(jnp.where(is_first, 0, vision_part)),
            ]
        )

    up = table(total_of(lefts[0], hidden_delta), total_of(lefts[2], hidden_delta))
    down = table(total_of(lefts[1], active), total_of(lefts[3], active))
    small = lax.psum(m.sums, "dp")
    mixed, proj = flat(m.out_mixed), flat(m.out_proj)
    return (
        total_of(lefts[4], mixed).astype(jnp.float32),
        total_of(lefts[5], proj).astype(jnp.float32),
        up,
        down.transpose(0, 2, 1),
        small,
        lax.ppermute(small, "section", [(0, 1), (1, 0)]),
    )


def shards(
    tokens, cotangent, patch_mask, text_mask, qkv_weight, qv_bias, out_weight, out_bias, norm_gain, norm_bias,
    up_table, up_bias, down_table, down_bias,
):
    is_first = lax.axis_index("section") == 0
    m = both_layers(
        tokens, cotangent, patch_mask, text_mask, qkv_weight, out_weight, up_table, down_table, qv_bias[0], out_bias,
        norm_gain[0], norm_bias[0], up_bias, down_bias,
    )
    if lax.axis_size("dp") == 16:
        qkv, out, up, down, small, input_grad = all_grads(m, tokens.shape[1])
    else:
        qkv, out, up, down, own, other = large_grads_plain(m, is_first)
        small = small_outs(own, other, is_first, tokens.shape[2])
        high = lax.ppermute(m.out_high, "section", [(0, 1)])
        value = jnp.where(is_first, m.out_low, high.astype(jnp.float32))
        input_grad = jnp.concatenate([value[:, TEXT : tokens.shape[1]], value[:, :TEXT]], axis=1)
    qv_part, proj_part, gain_part, shift_part, up_part, down_part = small
    return (
        input_grad, qkv[None], qv_part[None], out[None], proj_part, gain_part[None], shift_part[None],
        up, up_part, down, down_part,
    )


def solution(mesh):
    items, layers = P("dp"), P("section")
    return jax.shard_map(
        shards,
        mesh=mesh,
        in_specs=(items,) * 4 + (layers,) * 6 + (P(),) * 4,
        out_specs=(
            P("dp", None, "section"), P("section", None, "dp"), P("section", None, "dp"), P("section", None, "dp"),
            P("section", "dp"), P("section", None, "dp"), P("section", None, "dp"),
            P(None, None, "dp"), P(None, "dp"), P(None, "dp", None), P(None, "dp"),
        ),
        check_vma=False,
    )
```

```python
import functools

import jax
import jax.numpy as jnp
from jax import lax
from jax.experimental import pallas as pl
from jax.experimental.pallas import tpu as pltpu
from jax.sharding import PartitionSpec as P

HEAD_DIM = 64
PATCHES = 197
EPSILON = 1e-05
BLOCK = 384
WINDOW = 640
RING = 3
TEXT = 64
ROWS = 272
MESH = pl.DeviceIdType.MESH


UNITS = (
    (
        (3, 3, 0), (2, 2, 0), (3, 0, 0), (0, 1, 0), (2, 3, 0), (1, 1, 0), (3, 1, 0), (1, 2, 0), (3,
        2, 0), (0, 0, 0), (2, 1, 0), (1, 0, 1), (2, 0, 0), (1, 3, 0), (0, 3, 0), (4, 0, 1), (4, 3,
        0), (0, 2, 0), (4, 1, 0), (4, 2, 0),
    ),
    (
        (1, 0, 0), (0, 1, 0), (1, 1, 0), (4, 3, 0), (0, 2, 0), (0, 3, 1), (3, 3, 0), (0, 0, 0), (1,
        2, 0), (4, 1, 0), (4, 0, 1), (1, 3, 0), (2, 3, 0), (3, 0, 0), (3, 1, 0), (3, 2, 0), (4, 2,
        0),
    ),
)
WAIT = 4
HOP = 2
MEET = WAIT + 3 * HOP + 1
MEET_LATE = MEET + 2
LEFT_OF = ((0,), (1,), (0,), (1,), (2, 3))
MOVED = [unit[:2] for unit in UNITS[1] if unit[0] in (2, 3)]
MOVED_BITS = sum(1 << (4 * kind + plane) for kind, plane in MOVED)
FIRST_MOVED = min(u for u, unit in enumerate(UNITS[1]) if unit[:2] in MOVED)


def packed(units, handed_on):
    counts = [0, 0]
    codes = []
    for kind, plane, z_first in units:
        slot = 0
        if not (handed_on and (kind, plane) in MOVED):
            slot = counts[z_first]
            counts[z_first] += 1
        codes.append(kind | plane << 3 | z_first << 5 | slot << 6)
    codes += [0] * (-len(codes) % 3)
    return [codes[i] | codes[i + 1] << 10 | codes[i + 2] << 20 for i in range(0, len(codes), 3)], counts


PACKED, COUNTS = zip(*(packed(units, side == 0) for side, units in enumerate(UNITS)))
Y_UNITS, Z_UNITS = (max(COUNTS[0][way], COUNTS[1][way], 1) for way in range(2))


def look_up(words, u):
    word = words[0]
    for n in range(1, len(words)):
        word = jnp.where(u // 3 == n, words[n], word)
    return word >> (10 * (u % 3))


class Refs:
    pass


def sum_kernel(names, *refs):
    m = Refs()
    for name, ref in zip(names, refs):
        setattr(m, name, ref)
    section = lax.axis_index("section")
    me = lax.axis_index("dp")
    z, y, core = me // 4, (me // 2) % 2, me % 2
    peer = (section, me + 1 - 2 * core)
    beside = (section, me + 2 - 4 * y)
    right = (section, me + 4)
    left = (section, me - 4)
    aslant = (1 - section, me + 1 - 2 * core)
    across = (1 - section, me)
    on_first = section == 0
    units = jnp.where(on_first, len(UNITS[0]), len(UNITS[1]))
    computed = jnp.where(on_first, len(UNITS[0]), len(UNITS[1]) - len(MOVED))

    arrivals = [u for u, unit in enumerate(UNITS[1]) if unit[:2] in MOVED]

    def is_moved(kind, plane):
        return ((MOVED_BITS >> (4 * kind + plane)) & 1) == 1

    class Unit:
        def __init__(self, u):
            self.u = u
            code = jnp.where(on_first, look_up(PACKED[0], u), look_up(PACKED[1], u))
            self.kind = code & 7
            self.plane = (code >> 3) & 3
            self.z_first = ((code >> 5) & 1) == 1
            self.slot = (code >> 6) & 15
            moved = is_moved(self.kind, self.plane)
            self.handed_on = on_first & moved
            self.handed_in = jnp.logical_not(on_first) & moved
            self.y_first = jnp.logical_not(self.z_first | self.handed_on)
            self.y_slot = self.slot + jnp.where(self.z_first, Y_UNITS, 0)
            self.uses_text = jnp.logical_not(on_first) | (self.kind > 1)
            self.uses_patches = jnp.logical_not(on_first) | (self.kind < 2) | (self.kind == 4)
            self.order = u
            for at in arrivals:
                self.order = self.order - jnp.where((section == 1) & (u > at), 1, 0)

    def following(u):
        u = u + 1
        for at in arrivals:
            u = u + jnp.where((section == 1) & (u == at), 1, 0)
        return u

    def remote(src, dst, send, recv, device):
        return pltpu.make_async_remote_copy(
            src_ref=src, dst_ref=dst, send_sem=send, recv_sem=recv, device_id=device, device_id_type=MESH
        )

    def core_copy(order, b):
        slot = order % RING
        return remote(m.made.at[slot, 1 - core, b], m.xr.at[slot, b], m.core_send.at[order, b], m.core_recv.at[order, b], peer)

    def y_copy(n):
        return remote(m.part.at[n.u, 0], m.yr.at[n.y_slot], m.y_send.at[n.y_slot], m.y_recv.at[n.y_slot], beside)

    def right_copy(n):
        return remote(m.part.at[n.u, 1], m.zr.at[n.slot], m.right_send.at[n.slot], m.right_recv.at[n.slot], right)

    def left_copy(n):
        return remote(m.part.at[n.u, 1], m.zl.at[n.slot], m.left_send.at[n.slot], m.left_recv.at[n.slot], left)

    def right_pair(n):
        g = n.slot
        return remote(m.part.at[n.u], m.wr.at[g], m.right_send.at[Y_UNITS + g], m.right_recv.at[Y_UNITS + g], right)

    def left_pair(n):
        g = n.slot
        return remote(m.part.at[n.u], m.wl.at[g], m.left_send.at[Y_UNITS + g], m.left_recv.at[Y_UNITS + g], left)

    def over_copy(n, source, target):
        number = 4 * (n.kind - 2) + n.plane
        return remote(m.part.at[source], m.part.at[target], m.over_send.at[number], m.over_recv.at[number], across)

    def over_target(n):
        target = 0
        for at in arrivals:
            kind, plane, unused = UNITS[1][at]
            target = target + jnp.where((n.kind == kind) & (n.plane == plane), at, 0)
        return target

    def half_copy():
        return remote(m.half, m.half_out, m.half_send.at[0], m.half_recv.at[0], across)

    def own_half():
        return pl.ds(pl.multiple_of(core * BLOCK, 128), BLOCK)

    def mine(size):
        return pl.ds(pl.multiple_of(core * size, 16), size)

    def theirs(size):
        return pl.ds(pl.multiple_of((1 - core) * size, 16), size)

    def table_of(k, by_second):
        return jnp.where((k < 2) & by_second, 2, k // 2) + jnp.where(k % 2 == 1, 3, 0)

    def table_rows(k, by_second):
        return m.tables_out.at[table_of(k, by_second), :, own_half()]

    def peer_copy(k):
        return remote(m.turned.at[k, theirs(192)], table_rows(k, section == 1), m.peer_send.at[k], m.peer_recv.at[k], peer)

    def cross_copy(k, by_second, other_core):
        source = theirs(192) if other_core else mine(192)
        device = aslant if other_core else across
        number = 1 if other_core else 0
        return remote(
            m.turned.at[k, source], table_rows(k, by_second), m.cross_send.at[number, k], m.cross_recv.at[number, k], device
        )

    def attention_copies():
        rows = pl.ds(pl.multiple_of(288 + (1 - core) * 48, 16), 48)
        return (
            remote(m.turned.at[4, theirs(144)], m.qkv_out.at[:, own_half()], m.peer_send.at[4], m.peer_recv.at[4], peer),
            remote(m.turned.at[4, rows], m.out_out.at[:, own_half()], m.peer_send.at[5], m.peer_recv.at[5], peer),
        )

    def start_cross(k):
        cross_copy(k, section == 1, False).start()
        cross_copy(k, section == 1, True).start()

    def mixed_start(plane):
        return pl.multiple_of((9 * plane // 2) * 128, 128)

    def proj_start(plane):
        return pl.multiple_of((3 * plane // 2) * 128, 128)

    def tile_copies(n):
        k = n.kind
        slot = n.order % 2
        wide = pl.ds(pl.multiple_of(n.plane * 2 * BLOCK, 128), 2 * BLOCK)
        cases = []
        for ref, number, here, source, target in (
            (m.hidden, 0, (k == 0) | (k == 2), wide, slice(0, 2 * BLOCK)),
            (m.active, 0, (k == 1) | (k == 3), wide, slice(0, 2 * BLOCK)),
            (m.mixed, 0, k == 4, pl.ds(mixed_start(n.plane), WINDOW), slice(0, WINDOW)),
            (m.proj, 1, k == 4, pl.ds(proj_start(n.plane), 256), slice(WINDOW, WINDOW + 256)),
        ):
            copy = pltpu.make_async_copy(
                ref.at[:, :TEXT, source], m.text_tile.at[slot, :, :, target], m.text_sem.at[slot, number]
            )
            cases.append((here & n.uses_text, copy))
            copy = pltpu.make_async_copy(
                ref.at[:, TEXT:, source], m.patch_tile.at[slot, :, :, target], m.patch_sem.at[slot, number]
            )
            cases.append((here & n.uses_patches, copy))
        return cases

    def join_columns(slot, begin):
        for tile, joint in ((m.text_tile, m.text_joint), (m.patch_tile, m.patch_joint)):
            for side in range(2):
                at, mixed, proj = side * BLOCK, begin + side * 288, WINDOW + begin + side * 96
                joint[:, :, at : at + 288] = tile[slot, :, :, mixed : mixed + 288]
                joint[:, :, at + 288 : at + BLOCK] = tile[slot, :, :, proj : proj + 96]

    def start_tile(n):
        for here, copy in tile_copies(n):
            pl.when(here)(copy.start)

    def wait_tile(n):
        for here, copy in tile_copies(n):
            pl.when(here)(copy.wait)

    def add_into(target, source):
        target[...] = target[...] + source[...]

    def rows_dot(left, tile, *columns):
        tile = jnp.concatenate([tile[:, :, at] for at in columns], axis=2)
        return matmul(left, tile.reshape(-1, tile.shape[2]))

    def text_dot(index, slot, *columns):
        return rows_dot(m.text_left[index], m.text_tile.at[slot], *columns)

    def patch_dot(index, slot, *columns):
        return rows_dot(m.patch_left[index], m.patch_tile.at[slot], *columns)

    def joint_dot(index, *columns):
        text = rows_dot(m.text_left[index], m.text_joint, *columns)
        return rows_dot(m.patch_left[index], m.patch_joint, *columns) + text

    def compute(n):
        k = n.kind
        slot = n.order % RING

        @pl.when(n.order >= RING)
        def _():
            core_copy(n.order - RING, 0).wait_send()
            core_copy(n.order - RING, 1).wait_send()
            pl.semaphore_wait(m.credit, 1)

        @pl.when(n.order + 1 < computed)
        def _():
            start_tile(Unit(following(n.u)))

        wait_tile(n)
        tile = n.order % 2
        everything = slice(0, 2 * BLOCK)

        def put(value, columns, begin):
            for half in range(2):
                for side in range(2):
                    piece = value[half * BLOCK : (half + 1) * BLOCK, columns[side]]
                    at = slice(begin, begin + piece.shape[1])
                    m.made[slot, half, jnp.where(y == side, 1, 0), :, at] = piece.astype(jnp.bfloat16)

        sides = (slice(0, BLOCK), slice(BLOCK, 2 * BLOCK))

        @pl.when((k < 4) & jnp.logical_not(n.uses_text))
        def _():
            put(patch_dot(k % 2, tile, everything), sides, 0)

        @pl.when((k < 4) & jnp.logical_not(n.uses_patches))
        def _():
            put(text_dot(k % 2, tile, everything), sides, 0)

        @pl.when((k < 4) & n.uses_text & n.uses_patches)
        def _():
            put(patch_dot(k % 2, tile, everything) + text_dot(k % 2, tile, everything), sides, 0)

        @pl.when(k == 4)
        def _():
            ends = (slice(256, BLOCK), slice(BLOCK + 256, 2 * BLOCK))
            for odd in range(2):
                pl.when(n.plane % 2 == odd)(functools.partial(join_columns, tile, 64 * odd))
            mixed = joint_dot(2, everything)
            proj = joint_dot(3, *ends)
            put(mixed, (slice(0, 256), slice(BLOCK, BLOCK + 256)), 0)
            lanes = lax.broadcasted_iota(jnp.int32, (1, 128), 1)
            last = [jnp.where(lanes < 32, mixed[:, ends[side]], proj[:, 128 * side : 128 * side + 128]) for side in range(2)]
            put(jnp.concatenate(last, axis=1), (slice(0, 128), slice(128, 256)), 256)

        core_copy(n.order, 0).start()
        core_copy(n.order, 1).start()

    def join_core(n):
        slot = n.order % RING

        @pl.when(n.handed_in)
        def _():
            over_copy(n, 0, n.u).wait_recv()

        @pl.when(jnp.logical_not(n.handed_in))
        def _():
            core_copy(n.order, 0).wait_recv()
            m.part[n.u, 0] = m.made[slot, core, 0] + m.xr[slot, 0]

        pl.when(n.y_first)(lambda: y_copy(n).start())

        @pl.when(jnp.logical_not(n.handed_in))
        def _():
            core_copy(n.order, 1).wait_recv()
            m.part[n.u, 1] = m.made[slot, core, 1] + m.xr[slot, 1]

            @pl.when(n.order + RING < computed)
            def _():
                pl.semaphore_signal(m.credit, inc=1, device_id=peer, device_id_type=MESH)

        pl.when(n.handed_on)(lambda: over_copy(n, n.u, over_target(n)).start())

    def join_y(n):
        y_copy(n).wait_recv()
        add_into(m.part.at[n.u, 1], m.yr.at[n.y_slot])

    def take(n, one, pair, single_from, pair_from):
        @pl.when(n.y_first)
        def _():
            one(n).wait_recv()
            add_into(m.part.at[n.u, 1], single_from.at[n.slot])

        @pl.when(n.z_first)
        def _():
            pair(n).wait_recv()
            add_into(m.part.at[n.u], pair_from.at[n.slot])

    def take_right(n):
        take(n, right_copy, right_pair, m.zr, m.wr)

    def take_left(n):
        take(n, left_copy, left_pair, m.zl, m.wl)

    def pass_right(n):
        pl.when(z > 0)(lambda: take_right(n))
        pl.when(n.y_first)(lambda: right_copy(n).start())
        pl.when(n.z_first)(lambda: right_pair(n).start())

    def pass_left(n):
        pl.when(z < 3)(lambda: take_left(n))
        pl.when(n.y_first)(lambda: left_copy(n).start())
        pl.when(n.z_first)(lambda: left_pair(n).start())

    def give(n, i):
        k = n.kind
        m.turned[k] = m.part[n.u, 1].T

        @pl.when(k < 4)
        def _():
            m.tables_out[table_of(k, section == 1), :, own_half()] = m.turned[k, mine(192), :]
            peer_copy(k).start()
            pl.when(on_first | (i > FIRST_MOVED))(lambda: start_cross(k))

        @pl.when(k == 4)
        def _():
            m.qkv_out[:, own_half()] = m.turned[4, mine(144), :]
            m.out_out[:, own_half()] = m.turned[4, pl.ds(pl.multiple_of(288 + core * 48, 16), 48), :]
            for copy in attention_copies():
                copy.start()

    def greet_first(u, carry):
        n = Unit(u)
        ended = jnp.where(n.z_first, MEET_LATE, MEET) + u <= FIRST_MOVED
        pl.when(ended & (n.kind < 4) & (n.plane == z))(lambda: start_cross(n.kind))
        return carry

    def meet(n, i):
        pl.when(z > 0)(lambda: take_right(n))
        pl.when(z < 3)(lambda: take_left(n))
        pl.when(n.z_first)(lambda: y_copy(n).start())
        pl.when(n.y_first)(lambda: give(n, i))

    def meet_late(n, i):
        join_y(n)
        give(n, i)

    flips = (peer, beside, (section, me + 4 - 8 * (z % 2)), (section, me + 8 - 16 * (z // 2)), across)

    def small_copy(j):
        return remote(m.small_sum.at[j], m.small_in.at[j], m.small_send.at[j], m.small_recv.at[j], flips[j])

    def small_step(j):
        if j == 0:
            m.small_sum[0] = m.small[...]
        else:
            small_copy(j - 1).wait_recv()
            if j == 5:
                m.small_out[0] = m.small_sum[4]
                m.small_out[1] = m.small_in[4]
            else:
                m.small_sum[j] = m.small_sum[j - 1] + m.small_in[j - 1]
        if j < 5:
            small_copy(j).start()

    lefts = (m.n2, m.branch, m.n1, m.att)
    turns = [[], []]
    for side in range(2):
        for kind, plane, z_first in UNITS[side]:
            for index in () if side == 1 and (kind, plane) in MOVED else LEFT_OF[kind]:
                if index not in turns[side]:
                    turns[side].append(index)

    def stage_copy(index):
        return pltpu.make_async_copy(lefts[index], m.stage, m.stage_sem.at[0])

    def start_stage(turn):
        for side in range(2):
            pl.when(section == side)(stage_copy(turns[side][turn]).start)

    def prepare(turn):
        stage_copy(0).wait()
        number = jnp.where(on_first, turns[0][turn], turns[1][turn])

        def part(c, carry):
            at = pl.ds(pl.multiple_of(c * 128, 128), 128)
            m.text_left[number, at, :] = m.stage[:, :TEXT, at].reshape(-1, 128).T
            m.patch_left[number, at, :] = m.stage[:, TEXT:, at].reshape(-1, 128).T
            return carry

        lax.fori_loop(0, m.stage.shape[2] // 128, part, 0)
        if turn < 3:
            start_stage(turn + 1)

    barrier = pltpu.get_barrier_semaphore()
    for device in (peer, beside, flips[3]):
        pl.semaphore_signal(barrier, inc=1, device_id=device, device_id_type=MESH)

    @pl.when(section == 1)
    def _():
        for device in (across, aslant):
            pl.semaphore_signal(barrier, inc=1, device_id=device, device_id_type=MESH)

    @pl.when(z < 3)
    def _():
        pl.semaphore_signal(barrier, inc=1, device_id=right, device_id_type=MESH)

    @pl.when(z > 0)
    def _():
        pl.semaphore_signal(barrier, inc=1, device_id=left, device_id_type=MESH)

    start_stage(0)
    start_tile(Unit(jnp.int32(0)))
    prepare(0)
    pl.semaphore_wait(barrier, 3 + jnp.where(on_first, 2, 0) + jnp.where(z < 3, 1, 0) + jnp.where(z > 0, 1, 0))

    @pl.when(on_first)
    def _():
        for device in (across, aslant):
            pl.semaphore_signal(m.ready, inc=1, device_id=device, device_id_type=MESH)
        half_copy().start()


    def at_unit(u, condition, action, *more):
        n = Unit(jnp.maximum(u, 0))

        @pl.when((u >= 0) & (u < units) & condition(n))
        def _():
            action(n, *more)

    def in_flow(n):
        return jnp.logical_not(n.handed_on)

    def step(i, carry):
        @pl.when((i == FIRST_MOVED + 1) & (section == 1))
        def _():
            pl.semaphore_wait(m.ready, 2)
            lax.fori_loop(0, units, greet_first, 0)

        at_unit(i, lambda n: jnp.logical_not(n.handed_in), compute)
        for number in range(3):
            pl.when(i == number)(functools.partial(prepare, number + 1))
        at_unit(i - 1, lambda n: n.kind >= 0, join_core)
        at_unit(i - WAIT, lambda n: n.y_first, join_y)
        at_unit(i - WAIT - HOP * z, lambda n: in_flow(n) & (n.plane > z), pass_right)
        at_unit(i - WAIT - HOP * (3 - z), lambda n: in_flow(n) & (n.plane < z), pass_left)
        at_unit(i - MEET, lambda n: in_flow(n) & (n.plane == z), meet, i)
        at_unit(i - MEET_LATE, lambda n: n.z_first & (n.plane == z), meet_late, i)
        for j in range(4):
            pl.when(i == 3 + j)(functools.partial(small_step, j))
        return carry

    lax.fori_loop(0, units + MEET_LATE, step, 0)
    small_step(4)

    def ours(k):
        return True if k in (0, 1, 4) else is_moved(k, z) == (section == 1)

    def when_ours(k, wanted, action):
        pl.when(jnp.logical_not(ours(k) ^ wanted) if k in (2, 3) else True)(action)

    small_step(5)

    def settle(u, carry):
        n = Unit(u)

        @pl.when(jnp.logical_not(n.handed_in) & (n.order >= computed - RING))
        def _():
            core_copy(n.order, 0).wait_send()
            core_copy(n.order, 1).wait_send()

        pl.when(n.handed_on)(lambda: over_copy(n, n.u, over_target(n)).wait_send())
        pl.when(n.y_first | (n.z_first & (n.plane == z)))(lambda: y_copy(n).wait_send())
        pl.when(n.y_first & (n.plane > z))(lambda: right_copy(n).wait_send())
        pl.when(n.z_first & (n.plane > z))(lambda: right_pair(n).wait_send())
        pl.when(n.y_first & (n.plane < z))(lambda: left_copy(n).wait_send())
        pl.when(n.z_first & (n.plane < z))(lambda: left_pair(n).wait_send())
        return carry

    lax.fori_loop(0, units, settle, 0)
    for j in range(5):
        small_copy(j).wait_send()
    for k in range(4):

        def arrived(k=k):
            for other_core in (False, True):
                cross_copy(k, section == 0, other_core).wait_recv()

        def sent(k=k):
            peer_copy(k).wait()
            for other_core in (False, True):
                cross_copy(k, section == 1, other_core).wait_send()

        when_ours(k, True, sent)
        when_ours(k, False, arrived)
    for copy in attention_copies():
        copy.wait()

    @pl.when(on_first)
    def _():
        half_copy().wait_send()

    @pl.when(section == 1)
    def _():
        half_copy().wait_recv()

def summed_grads(n1, att, n2, branch, hidden, active, mixed, proj, half, small):
    dma = pltpu.SemaphoreType.DMA
    items, depth, width = n1.shape
    bf16, f32 = jnp.bfloat16, jnp.float32
    tile = (BLOCK, BLOCK)
    vmem, anywhere = pl.BlockSpec(memory_space=pltpu.VMEM), pl.BlockSpec(memory_space=pl.ANY)
    ins = dict(n1=n1, att=att, n2=n2, branch=branch, hidden=hidden, active=active, mixed=mixed, proj=proj, half=half,
        small=small)
    outs = dict(
        tables_out=((6, 192, width), bf16), qkv_out=((144, width), bf16),
        out_out=((48, width), bf16), small_out=((2,) + small.shape, f32), half_out=(half.shape, bf16),
    )
    buffers = dict(
        text_tile=((2, items, TEXT, WINDOW + 256), bf16),
        patch_tile=((2, items, depth - TEXT, WINDOW + 256), bf16), text_joint=((items, TEXT, 2 * BLOCK), bf16),
        patch_joint=((items, depth - TEXT, 2 * BLOCK), bf16), part=((20, 2) + tile, bf16), made=((RING, 2, 2) + tile, bf16),
        xr=((RING, 2) + tile, bf16), yr=((Y_UNITS + Z_UNITS,) + tile, bf16), zr=((Y_UNITS,) + tile, bf16), zl=((Y_UNITS,) + tile, bf16),
        wr=((Z_UNITS, 2) + tile, bf16), wl=((Z_UNITS, 2) + tile, bf16), turned=((5,) + tile, bf16),
        text_left=((4, width, items * TEXT), bf16), patch_left=((4, width, items * (depth - TEXT)), bf16), stage=((items, depth, width), bf16), small_sum=((5,) + small.shape, f32),
        small_in=((5,) + small.shape, f32),
    )
    semaphores = dict(
        small_send=dma((5,)), small_recv=dma((5,)), text_sem=dma((2, 2)), patch_sem=dma((2, 2)), stage_sem=dma((1,)), core_send=dma((20, 2)),
        core_recv=dma((20, 2)), y_send=dma((Y_UNITS + Z_UNITS,)), y_recv=dma((Y_UNITS + Z_UNITS,)), right_send=dma((Y_UNITS + Z_UNITS,)), right_recv=dma((Y_UNITS + Z_UNITS,)),
        left_send=dma((Y_UNITS + Z_UNITS,)), left_recv=dma((Y_UNITS + Z_UNITS,)), over_send=dma((8,)), over_recv=dma((8,)), half_send=dma((1,)), half_recv=dma((1,)), peer_send=dma((6,)),
        peer_recv=dma((6,)), cross_send=dma((2, 4)), cross_recv=dma((2, 4)),
        credit=pltpu.SemaphoreType.REGULAR, ready=pltpu.SemaphoreType.REGULAR,
    )
    names = list(ins) + list(outs) + list(buffers) + list(semaphores)
    return pl.pallas_call(
        functools.partial(sum_kernel, names),
        out_shape=[jax.ShapeDtypeStruct(*kind) for kind in outs.values()],
        in_specs=[anywhere] * 9 + [vmem],
        out_specs=[vmem] * (len(outs) - 1) + [anywhere],
        scratch_shapes=[pltpu.VMEM(*kind) for kind in buffers.values()] + list(semaphores.values()),
        compiler_params=pltpu.CompilerParams(
            collective_id=0, has_side_effects=True, vmem_limit_bytes=60 * 1024 * 1024
        ),
        cost_estimate=pl.CostEstimate(flops=48 * 2 * 768 * 384 * items * depth, bytes_accessed=40_000_000, transcendentals=0),
    )(*ins.values())


def finish_kernel(count, *refs):
    sources, targets = refs[:count], refs[count : count + 11]
    held, made, (load_sem, store_sem) = refs[count + 11 : -7], refs[-7:-2], refs[-2:]
    loads = [pltpu.make_async_copy(*pair, load_sem.at[n]) for n, pair in enumerate(zip(sources, held))]
    stores = [pltpu.make_async_copy(*pair, store_sem.at[n]) for n, pair in enumerate(zip(made, targets[:5]))]
    for load in loads:
        load.start()
    tables, qkv, out, small, half, grad = held
    small_outs = targets[5:]
    loads[0].wait()
    for number, source in enumerate((tables.at[:3], tables.at[3:], qkv, out)):
        if number > 1:
            loads[number - 1].wait()
        made[number][...] = source[...].astype(jnp.float32)
        stores[number].start()
    for load in loads[3:]:
        load.wait()
    section, me = lax.axis_index("section"), lax.axis_index("dp")
    width, wide = tables.shape[2], tables.shape[2] // 16
    ff = width * 4

    def columns(row, size):
        return pltpu.roll(row, (row.shape[1] - size * me) % row.shape[1], 1)[:, :size]

    def up_bias(side, slot):
        return columns(jnp.concatenate([small[side, 9 + 3 * slot + j : 10 + 3 * slot + j] for j in range(3)], axis=1), ff // 16)

    own = columns(small[0, :9, :width], wide)
    other = columns(small[1, :9, :width], wide)
    qv_out, proj_out, gain_out, shift_out, up_bias_out, down_bias_out = small_outs
    qv_out[...] = own[2:4]
    proj_out[...] = own[4:5]
    gain_out[...] = own[5:7]
    shift_out[...] = own[7:9]
    for side in range(2):
        mine, theirs = (own, other) if side == 0 else (other, own)

        @pl.when(section == side)
        def _():
            for i in range(grad.shape[0]):
                place(made[4], i, grad[i] if side == 0 else half[i].astype(jnp.float32))
            stores[4].start()
            down_bias_out[0:2] = mine[0:2]
            down_bias_out[2:3] = theirs[0:1]
            up_bias_out[0:1] = up_bias(side, 0)
            up_bias_out[1:2] = up_bias(side, 1)
            up_bias_out[2:3] = up_bias(1 - side, 0)

    for store in stores:
        store.wait()


def place(target, i, value):
    target[i, :PATCHES] = value[TEXT : target.shape[1]]
    target[i, PATCHES:] = value[:TEXT]


def finished(length, *sources):
    tables, qkv, out, small, half, grad = sources
    width = tables.shape[2]
    shapes = [(3,) + tables.shape[1:]] * 2 + [qkv.shape, out.shape, (grad.shape[0], length, grad.shape[2])]
    shapes += [(rows, width // 16) for rows in (2, 1, 2, 2)] + [(3, width // 4), (3, width // 16)]
    return pl.pallas_call(
        functools.partial(finish_kernel, len(sources)),
        out_shape=[jax.ShapeDtypeStruct(shape, jnp.float32) for shape in shapes],
        in_specs=[pl.BlockSpec(memory_space=pltpu.HBM)] * len(sources),
        out_specs=[pl.BlockSpec(memory_space=pl.ANY)] * 5 + [pl.BlockSpec(memory_space=pltpu.VMEM)] * 6,
        scratch_shapes=[pltpu.VMEM(value.shape, value.dtype) for value in sources]
        + [pltpu.VMEM(shape, jnp.float32) for shape in shapes[:5]]
        + [pltpu.SemaphoreType.DMA((len(sources),)), pltpu.SemaphoreType.DMA((5,))],
        compiler_params=pltpu.CompilerParams(vmem_limit_bytes=60 * 1024 * 1024),
    )(*sources)


CHUNK = 1024
PIECE = 768
KEY_SPLIT = 256
TAIL = (0.319381530, -0.356563782, 1.781477937, -1.821255978, 1.330274429)
PEAK = 0.3989422804014327


def normal_parts(z):
    size = jnp.abs(z)
    scale = 1.0 + 0.2316419 * size
    t = pl.reciprocal(scale, approx=True)
    t = t * (2.0 - scale * t)
    bell = jnp.exp(-0.5 * z * z) * PEAK
    series = TAIL[4]
    for factor in TAIL[3::-1]:
        series = series * t + factor
    upper = bell * (series * t)
    return jnp.where(z >= 0, 1.0 - upper, upper), bell


def matmul(left, right):
    return jnp.dot(left, right, preferred_element_type=jnp.float32)


def matmul_turned(left, right):
    return lax.dot_general(left, right, (((1,), (1,)), ((), ())), preferred_element_type=jnp.float32)


def standardized(values):
    centre = values - jnp.mean(values, -1, keepdims=True)
    inverse = lax.rsqrt(jnp.mean(centre * centre, -1, keepdims=True) + EPSILON)
    return centre * inverse, inverse


def norm_step_back(delta, standard, inverse, gain_row):
    scaled = delta * gain_row
    moved = inverse * (
        scaled - jnp.mean(scaled, -1, keepdims=True) - standard * jnp.mean(scaled * standard, -1, keepdims=True)
    )
    return moved, jnp.sum(delta * standard, 0, keepdims=True), jnp.sum(delta, 0, keepdims=True)


def half_mask(half):
    lanes = lax.broadcasted_iota(jnp.int32, (1, 128), 1)
    return (lanes < 64) if half == 0 else (lanes >= 64)


def pair_columns(p, part, width):
    return slice(part * width + p * 128, part * width + p * 128 + 128)


def both_halves(pair):
    return jnp.concatenate([jnp.where(half_mask(half), pair, jnp.zeros_like(pair)) for half in range(2)], axis=0)


def in_turn(count, *stages):
    for turn in range(count + len(stages) - 1):
        for number, stage in enumerate(stages):
            if 0 <= turn - number < count:
                stage(turn - number)


def attention_forward(m, length):
    rows, width = m.att.shape

    def scores(p):
        q2 = m.qkv[:, pair_columns(p, 0, width)]
        k2 = m.qkv[:, pair_columns(p, 1, width)]
        m.scores[p % 2] = matmul_turned(both_halves(k2), q2).reshape(2, rows, rows)

    def soften(p):
        for half in range(2):
            top = m.scores[p % 2, half, :KEY_SPLIT]
            low = m.scores[p % 2, half, KEY_SPLIT:]
            key_row = KEY_SPLIT + lax.broadcasted_iota(jnp.int32, low.shape, 0)
            low = jnp.where(key_row < length, low, -1e30)
            peak = jnp.maximum(jnp.max(top, 0, keepdims=True), jnp.max(low, 0, keepdims=True))
            top = jnp.exp(top - peak)
            low = jnp.exp(low - peak)
            over = 1.0 / (jnp.sum(top, 0, keepdims=True) + jnp.sum(low, 0, keepdims=True))
            m.probs[2 * p + half, :KEY_SPLIT] = (top * over).astype(jnp.bfloat16)
            m.probs[2 * p + half, KEY_SPLIT:] = (low * over).astype(jnp.bfloat16)

    def blend(p):
        v_turned = m.qkv[:, pair_columns(p, 2, width)].T
        parts = [matmul(v_turned[64 * half : 64 * half + 64], m.probs[2 * p + half]) for half in range(2)]
        turned = jnp.concatenate(parts, axis=0)
        m.att_turned[p * 128 : p * 128 + 128, :] = turned.astype(jnp.bfloat16)
        m.att[:, p * 128 : p * 128 + 128] = turned.T.astype(jnp.bfloat16)

    in_turn(width // 128, scores, soften, blend)


def attention_back(m):
    rows, width = m.att.shape

    def probs_back(p):
        v2 = m.qkv[:, pair_columns(p, 2, width)]
        d_turned = m.att_delta[:, pair_columns(p, 0, width)].T
        m.scores[p % 2] = matmul(both_halves(v2), d_turned).reshape(2, rows, rows)
        product = d_turned.astype(jnp.float32) * m.att_turned[p * 128 : p * 128 + 128, :].astype(jnp.float32)
        for half in range(2):
            m.inner[p % 2, half] = jnp.sum(product[64 * half : 64 * half + 64], 0, keepdims=True)

    def scores_back(p):
        for half in range(2):
            probs = m.probs[2 * p + half].astype(jnp.float32)
            m.score_delta[p % 2, half] = (probs * (m.scores[p % 2, half] - m.inner[p % 2, half])).astype(jnp.bfloat16)

    def heads_back(p):
        q_at, k_at, v_at = (pair_columns(p, part, width) for part in range(3))
        score = m.score_delta[p % 2]
        probs = m.probs[2 * p : 2 * p + 2].reshape(2 * rows, rows)
        k_turned = m.qkv[:, k_at].T
        value = matmul(probs, m.att_delta[:, q_at])
        key = matmul(score.reshape(2 * rows, rows), m.qkv[:, q_at])
        query = jnp.concatenate(
            [matmul(k_turned[64 * half : 64 * half + 64], score[half]) for half in range(2)], axis=0
        )
        dq = (query.T * HEAD_DIM ** (-0.5)).astype(jnp.bfloat16)
        dk = jnp.where(half_mask(0), key[:rows], key[rows:]).astype(jnp.bfloat16)
        dv = jnp.where(half_mask(0), value[:rows], value[rows:]).astype(jnp.bfloat16)
        m.mixed[:, q_at] = dq
        m.mixed[:, k_at] = dk
        m.mixed[:, v_at] = dv
        m.sums[2:3, q_at] += jnp.sum(dq.astype(jnp.float32), 0, keepdims=True)
        m.sums[3:4, q_at] += jnp.sum(dv.astype(jnp.float32), 0, keepdims=True)

    in_turn(width // 128, probs_back, scores_back, heads_back)


def forward_front(m, x_ref, length, hold):
    x = x_ref[...].astype(jnp.float32)
    standard, inverse = standardized(x)
    if hold:
        m.standard[...] = standard
        m.inverse[0] = inverse
    m.n1[...] = (standard * m.gain[0:1] + m.shift[0:1]).astype(jnp.bfloat16)
    width = x.shape[1]
    m.need(m.qkv_w)
    value = matmul(m.n1[...], m.qkv_w[...])
    query = (value[:, :width] + m.qv[0:1]).astype(jnp.bfloat16)
    m.qkv[:, :width] = query * jnp.bfloat16(HEAD_DIM ** (-0.5))
    m.qkv[:, width : 2 * width] = value[:, width : 2 * width].astype(jnp.bfloat16)
    m.qkv[:, 2 * width :] = (value[:, 2 * width :] + m.qv[1:2]).astype(jnp.bfloat16)
    attention_forward(m, length)
    m.need(m.out_w)
    middle = x_ref[...].astype(jnp.float32) + matmul(m.att[...], m.out_w[...]) + m.proj[0:1]
    standard, inverse = standardized(middle)
    m.middle[...] = standard if hold else middle
    if hold:
        m.inverse[1] = inverse
    m.n2[...] = (standard * m.gain[1:2] + m.shift[1:2]).astype(jnp.bfloat16)


def back_tail(m, x_ref, g_ref, n2_delta, keep, held):
    standard, inverse = (m.middle[...], m.inverse[1]) if held else standardized(m.middle[...])
    middle_part, gain, shift = norm_step_back(n2_delta, standard, inverse, m.gain[1:2])
    m.sums[6:7, :gain.shape[1]] += gain
    m.sums[8:9, :gain.shape[1]] += shift
    middle_delta = g_ref[...].astype(jnp.float32) + middle_part
    proj_delta = middle_delta.astype(jnp.bfloat16)
    m.sums[4:5, :gain.shape[1]] += jnp.sum(proj_delta.astype(jnp.float32), 0, keepdims=True)
    m.proj_delta[...] = proj_delta
    m.middle_delta[...] = middle_delta
    m.att_delta[...] = matmul_turned(proj_delta, m.out_w[...]).astype(jnp.bfloat16)
    attention_back(m)
    total = matmul_turned(m.mixed[...], m.qkv_w[...])
    standard, inverse = (m.standard[...], m.inverse[0]) if held else standardized(x_ref[...].astype(jnp.float32))
    input_part, gain, shift = norm_step_back(total, standard, inverse, m.gain[0:1])
    m.sums[5:6, :gain.shape[1]] += gain
    m.sums[7:8, :gain.shape[1]] += shift
    keep(m.middle_delta[...] + input_part)


def forward_expert(m, slot, begin, end):
    def columns(j):
        return slice(j * PIECE, (j + 1) * PIECE)

    def widen(j):
        hidden = matmul(m.n2[begin:end], m.up_w[slot, :, columns(j)])
        m.hidden[j % 2, begin:end] = hidden + m.up_b[slot : slot + 1, columns(j)]

    def bend(j):
        hidden = m.hidden[j % 2, begin:end]
        below, bell = normal_parts(hidden)
        m.active[begin:end, columns(j)] = (hidden * below).astype(jnp.bfloat16)
        m.slope[begin:end, columns(j)] = (below + hidden * bell).astype(jnp.bfloat16)

    in_turn(m.up_w.shape[2] // PIECE, widen, bend)
    result = matmul(m.active[begin:end], m.down_w[slot])
    m.total[begin:end] = m.middle[begin:end] + result + m.down_b[slot : slot + 1]


def add_up_sums(m, slot, begin, end):
    for j in range(m.up_w.shape[2] // CHUNK):
        piece = m.hidden_delta[begin:end, j * CHUNK : (j + 1) * CHUNK].astype(jnp.float32)
        m.sums[9 + 3 * slot + j : 10 + 3 * slot + j] += jnp.sum(piece, 0, keepdims=True)


def back_expert(m, g_ref, slot, begin, end):
    m.sums[slot : slot + 1, : g_ref.shape[1]] += jnp.sum(g_ref[begin:end].astype(jnp.float32), 0, keepdims=True)
    active_delta = matmul_turned(g_ref[begin:end], m.down_w[slot])
    m.hidden_delta[begin:end] = (active_delta * m.slope[begin:end].astype(jnp.float32)).astype(jnp.bfloat16)
    m.total[begin:end] = matmul_turned(m.hidden_delta[begin:end], m.up_w[slot])
    add_up_sums(m, slot, begin, end)


def both_expert(m, g_ref):
    def columns(j):
        return slice(j * PIECE, (j + 1) * PIECE)

    def widen(j):
        m.hidden[j % 2] = matmul(m.n2[...], m.up_w[0, :, columns(j)]) + m.up_b[2:3, columns(j)]
        m.active_delta[j % 2] = matmul_turned(g_ref[...], m.down_w[0, columns(j), :])

    def bend(j):
        hidden = m.hidden[j % 2]
        below, bell = normal_parts(hidden)
        m.active[:, columns(j)] = (hidden * below).astype(jnp.bfloat16)
        slope = below + hidden * bell
        m.hidden_delta[:, columns(j)] = (m.active_delta[j % 2] * slope).astype(jnp.bfloat16)

    in_turn(m.up_w.shape[2] // PIECE, widen, bend)
    m.total[...] = matmul_turned(m.hidden_delta[...], m.up_w[0])
    add_up_sums(m, 0, 0, ROWS)


def layers_kernel(names, *refs):
    m = Refs()
    for name, ref in zip(names, refs):
        setattr(m, name, ref)
    items, length = m.in_tokens.shape[:2]
    half = m.total.shape[1] // 2
    section = lax.axis_index("section")
    across = (1 - section, lax.axis_index("dp"))

    def send(i, part):
        rows = (slice(0, TEXT), slice(TEXT, ROWS))[part]
        return pltpu.make_async_remote_copy(
            src_ref=m.leaving.at[i, rows], dst_ref=m.landed.at[i, rows], send_sem=m.send_sem.at[i, part],
            recv_sem=m.recv_sem.at[i, part], device_id=across, device_id_type=MESH,
        )

    def side_copies(i):
        return (
            pltpu.make_async_copy(m.low.at[i], m.out_low.at[i], m.side_sem.at[0, i]),
            pltpu.make_async_copy(m.high.at[i], m.out_high.at[i], m.side_sem.at[1, i]),
        )

    def local(source, target, number):
        return pltpu.make_async_copy(source, target, m.copy_sem.at[number])

    def branch_copy(source, i):
        return pltpu.make_async_copy(source.at[i], m.branch.at[i], m.branch_sem.at[i])

    def weights(experts):
        found = [
            (m.qkv_w, [local(m.in_qkv.at[0], m.qkv_w, 0)]),
            (m.out_w, [local(m.in_out.at[0], m.out_w, 1)]),
            (m.up_w, []),
            (m.down_w, []),
        ]
        for slot, expert in enumerate(experts):
            found[2][1].append(local(m.in_up.at[expert], m.up_w.at[slot], 2 + slot))
            found[3][1].append(local(m.in_down.at[expert], m.down_w.at[slot], 4 + slot))
        return found

    def start_weights(found):
        copies = found[0][1] + found[1][1]
        for pair in zip(found[2][1], found[3][1]):
            copies += pair
        for copy in copies:
            copy.start()

    def needs(found, i):
        def need(ref):
            for here, copies in found:
                if here is ref:

                    @pl.when(i == 0)
                    def _():
                        for copy in copies:
                            copy.wait()

        return need

    leaving = (
        (m.n1, m.out_n1), (m.att, m.out_att), (m.n2, m.out_n2), (m.active, m.out_active), (m.qkv, m.kept_qkv),
        (m.probs, m.kept_probs), (m.att_turned, m.kept_turned), (m.middle, m.kept_middle), (m.slope, m.kept_slope),
        (m.mixed, m.out_mixed), (m.proj_delta, m.out_proj), (m.hidden_delta, m.out_hidden),
    )
    n1, att, n2, active, qkv, probs, turned, middle, slope, mixed, proj, hidden = range(len(leaving))

    def puts(i):
        return lambda number: local(leaving[number][0], leaving[number][1].at[i], 6 + number)

    def gets(i):
        return lambda number: local(leaving[number][1].at[i], leaving[number][0], 14 + number)

    def start(copies, *which):
        for number in which:
            copies(number).start()

    def wait(copies, *which):
        for number in which:
            copies(number).wait()

    def settle(i, *which):
        @pl.when(i > 0)
        def _():
            wait(puts(i), *which)

    def text_first(target, source, i):
        value = source[i].astype(jnp.float32)
        pad = jnp.zeros((ROWS - length, value.shape[1]), jnp.float32)
        target[i, :TEXT] = value[PATCHES:].astype(jnp.bfloat16)
        target[i, TEXT:] = jnp.concatenate([value[:PATCHES], pad], axis=0).astype(jnp.bfloat16)

    def mask_targets(i):
        row = lax.broadcasted_iota(jnp.int32, (ROWS, 1), 0)
        position = jnp.where(row < TEXT, row + PATCHES, jnp.where(row < length, row - TEXT, length))
        chosen = jnp.zeros((ROWS, 1), jnp.float32)
        for mask in (m.patch_mask, m.text_mask):
            same = jnp.where(position == mask[i : i + 1, :], 1.0, 0.0)
            chosen = jnp.maximum(chosen, jnp.max(same, 1, keepdims=True))
        target = m.targets[i].astype(jnp.float32) * chosen
        m.targets[i] = target.astype(jnp.bfloat16)
        m.sums[0:1, : target.shape[1]] += jnp.sum(target, 0, keepdims=True)

    def first_front(found, i, carry):
        m.need = needs(found, i)
        text_first(m.tokens, m.in_tokens, i)
        settle(i, n1, att, n2, qkv, probs, turned, middle)
        forward_front(m, m.tokens.at[i], length, False)
        start(puts(i), n1, att, n2, qkv, probs, turned, middle)
        settle(i, active, slope)
        m.need(m.up_w)
        m.need(m.down_w)
        forward_expert(m, 1, 0, TEXT)
        m.leaving[i, :TEXT] = m.total[:TEXT].astype(jnp.bfloat16)
        send(i, 0).start()
        forward_expert(m, 0, TEXT, ROWS)
        m.leaving[i, TEXT:] = m.total[TEXT:].astype(jnp.bfloat16)
        send(i, 1).start()
        start(puts(i), active, slope)
        return carry

    def first_back(i, carry):
        start(gets(i), slope, middle, turned, qkv, probs)

        @pl.when(i > 0)
        def _():
            send(i - 1, 0).wait_send()
            send(i - 1, 1).wait_send()

        settle(i, hidden)
        wait(gets(i), slope)
        gradient = m.landed.at[i]
        send(i, 0).wait_recv()
        back_expert(m, gradient, 1, 0, TEXT)
        send(i, 1).wait_recv()
        branch_copy(m.landed, i).start()
        back_expert(m, gradient, 0, TEXT, ROWS)
        start(puts(i), hidden)
        wait(gets(i), middle, turned, qkv, probs)
        settle(i, mixed, proj)

        def keep(value):
            m.low[i] = value[:, :half]
            m.high[i] = value[:, half:].astype(jnp.bfloat16)

        back_tail(m, m.tokens.at[i], gradient, m.total[...], keep, False)
        for copy in side_copies(i):
            copy.start()
        start(puts(i), mixed, proj)
        branch_copy(m.landed, i).wait()
        return carry

    def second_both(found, i, carry):
        m.need = needs(found, i)
        branch_copy(m.targets, i).start()
        send(i, 0).wait_recv()
        send(i, 1).wait_recv()
        settle(i, n1, att, n2)
        arrived = m.landed.at[i]
        forward_front(m, arrived, length, True)
        start(puts(i), n1, att, n2)
        settle(i, active, hidden)
        m.need(m.up_w)
        m.need(m.down_w)
        gradient = m.targets.at[i]
        both_expert(m, gradient)
        start(puts(i), active, hidden)
        settle(i, mixed, proj)

        def keep(value):
            m.leaving[i] = value.astype(jnp.bfloat16)

        back_tail(m, arrived, gradient, m.total[...], keep, True)
        send(i, 0).start()
        send(i, 1).start()
        start(puts(i), mixed, proj)
        branch_copy(m.targets, i).wait()
        return carry

    m.sums[...] = jnp.zeros(m.sums.shape, jnp.float32)
    barrier = pltpu.get_barrier_semaphore()
    pl.semaphore_signal(barrier, inc=1, device_id=across, device_id_type=MESH)

    @pl.when(section == 0)
    def _():
        found = weights((0, 1))
        start_weights(found)
        pl.semaphore_wait(barrier, 1)
        lax.fori_loop(0, items, functools.partial(first_front, found), 0)
        wait(puts(0), n1, att, n2, active, qkv, probs, turned, middle, slope)
        lax.fori_loop(0, items, first_back, 0)
        wait(puts(0), mixed, proj, hidden)
        send(items - 1, 0).wait_send()
        send(items - 1, 1).wait_send()
        for i in range(items):
            for copy in side_copies(i):
                copy.wait()

    @pl.when(section == 1)
    def _():
        found = weights((2,))
        start_weights(found)
        for i in range(items):
            text_first(m.targets, m.cotangent, i)
            mask_targets(i)
        pl.semaphore_wait(barrier, 1)
        lax.fori_loop(0, items, functools.partial(second_both, found), 0)
        wait(puts(0), n1, att, n2, active, mixed, proj, hidden)
        for i in range(items):
            send(i, 0).wait_send()
            send(i, 1).wait_send()


def both_layers(
    tokens, cotangent, patch_mask, text_mask, qkv_weight, out_weight, up_table, down_table, qv, proj, gain, shift, up_b, down_b
):
    items, length, width = tokens.shape
    rows = ROWS
    ff = up_b.shape[1]
    heads = width // HEAD_DIM
    bf16, f32 = jnp.bfloat16, jnp.float32
    dma = pltpu.SemaphoreType.DMA
    vmem, anywhere = pl.BlockSpec(memory_space=pltpu.VMEM), pl.BlockSpec(memory_space=pl.ANY)
    ins = dict(
        in_tokens=(tokens, vmem), cotangent=(cotangent, vmem), patch_mask=(patch_mask, vmem), text_mask=(text_mask, vmem), in_qkv=(qkv_weight, anywhere), in_out=(out_weight, anywhere),
        in_up=(up_table, anywhere), in_down=(down_table, anywhere), qv=(qv, vmem), proj=(proj, vmem), gain=(gain, vmem),
        shift=(shift, vmem), up_b=(up_b, vmem), down_b=(down_b, vmem),
    )

    def made(*shape, kind=bf16, spec=anywhere):
        return jax.ShapeDtypeStruct((items,) + shape, kind), spec

    outs = dict(
        out_n1=made(rows, width), out_att=made(rows, width), out_n2=made(rows, width), out_active=made(rows, ff),
        out_mixed=made(rows, 3 * width), out_proj=made(rows, width), out_hidden=made(rows, ff), branch=made(rows, width),
        kept_qkv=made(rows, 3 * width), kept_probs=made(heads, rows, rows), kept_turned=made(width, rows),
        kept_middle=made(rows, width, kind=f32), kept_slope=made(rows, ff),
        out_low=made(rows, width // 2, kind=f32), out_high=made(rows, width // 2),
        sums=(jax.ShapeDtypeStruct((16, CHUNK), f32), vmem),
    )
    low_row, wide_row = ((rows, width), bf16), ((rows, ff), bf16)
    buffers = dict(
        qkv_w=((width, 3 * width), bf16), out_w=((width, width), bf16), up_w=((2, width, ff), bf16),
        down_w=((2, ff, width), bf16), n1=low_row, att=low_row, n2=low_row, active=wide_row,
        qkv=((rows, 3 * width), bf16), probs=((heads, rows, rows), bf16), att_turned=((width, rows), bf16),
        middle=((rows, width), f32), slope=wide_row, total=((rows, width), f32), mixed=((rows, 3 * width), bf16),
        standard=((rows, width), f32), inverse=((2, rows, 1), f32), proj_delta=low_row, scores=((2, 2, rows, rows), f32),
        score_delta=((2, 2, rows, rows), bf16), inner=((2, 2, 1, rows), f32), hidden=((2, rows, PIECE), f32),
        active_delta=((2, rows, PIECE), f32), hidden_delta=wide_row, att_delta=low_row, middle_delta=((rows, width), f32),
        leaving=((items, rows, width), bf16), landed=((items, rows, width), bf16),
        low=((items, rows, width // 2), f32), high=((items, rows, width // 2), bf16),
        tokens=((items, rows, width), bf16), targets=((items, rows, width), bf16),
    )
    semaphores = dict(
        copy_sem=dma((23,)), branch_sem=dma((items,)), side_sem=dma((2, items)), send_sem=dma((items, 2)), recv_sem=dma((items, 2)),
    )
    names = list(ins) + list(outs) + list(buffers) + list(semaphores)
    results = pl.pallas_call(
        functools.partial(layers_kernel, names),
        out_shape=[shape for shape, spec in outs.values()],
        in_specs=[spec for value, spec in ins.values()],
        out_specs=[spec for shape, spec in outs.values()],
        scratch_shapes=[pltpu.VMEM(*kind) for kind in buffers.values()] + list(semaphores.values()),
        compiler_params=pltpu.CompilerParams(
            collective_id=1, has_side_effects=True, vmem_limit_bytes=60 * 1024 * 1024
        ),
        cost_estimate=pl.CostEstimate(flops=40_000_000_000, bytes_accessed=100_000_000, transcendentals=0),
    )(*[value for value, spec in ins.values()])
    m = Refs()
    for name, result in zip(outs, results):
        setattr(m, name, result)
    return m


def small_outs(own, other, is_first, width):
    first = jnp.where(is_first, own, other)
    second = jnp.where(is_first, other, own)
    me = lax.axis_index("dp")

    def columns(rows):
        wide = rows.shape[-1] // lax.axis_size("dp")
        return lax.dynamic_slice_in_dim(rows, me * wide, wide, rows.ndim - 1)

    down = columns(jnp.concatenate([first[:2], second[:1]])[:, :width])
    up = columns(jnp.concatenate([first[9:15].reshape(2, -1), second[9:12].reshape(1, -1)]))
    own = columns(own[2:9, :width])
    return own[0:2], own[2:3], own[3:5], own[5:7], up, down


def flat(value):
    return value.reshape((-1, value.shape[-1]))


def left_parts(m, is_first):
    n1, att, n2, branch_delta = (flat(part) for part in (m.out_n1, m.out_att, m.out_n2, m.branch))
    text = (jnp.arange(n1.shape[0]) % ROWS < TEXT)[:, None]
    vision = jnp.logical_not(text & is_first).astype(jnp.bfloat16)
    text = text.astype(jnp.bfloat16)
    return [
        piece.T for piece in (n2 * vision, branch_delta * vision, n2 * text, branch_delta * text, n1, att)
    ]


def all_grads(m, length):
    up, down, qkv, out, input_grad, *small = finished(
        length,
        *summed_grads(m.out_n1, m.out_att, m.out_n2, m.branch, m.out_hidden, m.out_active, m.out_mixed, m.out_proj, m.out_high, m.sums),
        m.out_low,
    )
    return qkv.T, out.T, up.transpose(0, 2, 1), down, small, input_grad


def large_grads_plain(m, is_first):
    lefts = left_parts(m, is_first)
    hidden_delta, active = flat(m.out_hidden), flat(m.out_active)

    def total_of(left, right):
        product = jnp.dot(left, right, preferred_element_type=jnp.float32).astype(jnp.bfloat16)
        return lax.psum_scatter(product, "dp", scatter_dimension=1, tiled=True)

    def table(vision_part, text_part):
        def swapped(part):
            return lax.psum(part, "section").astype(jnp.float32)

        return jnp.stack(
            [
                swapped(jnp.where(is_first, vision_part, 0)),
                swapped(jnp.where(is_first, text_part, 0)),
                swapped(jnp.where(is_first, 0, vision_part)),
            ]
        )

    up = table(total_of(lefts[0], hidden_delta), total_of(lefts[2], hidden_delta))
    down = table(total_of(lefts[1], active), total_of(lefts[3], active))
    small = lax.psum(m.sums, "dp")
    mixed, proj = flat(m.out_mixed), flat(m.out_proj)
    return (
        total_of(lefts[4], mixed).astype(jnp.float32),
        total_of(lefts[5], proj).astype(jnp.float32),
        up,
        down.transpose(0, 2, 1),
        small,
        lax.ppermute(small, "section", [(0, 1), (1, 0)]),
    )


def shards(
    tokens, cotangent, patch_mask, text_mask, qkv_weight, qv_bias, out_weight, out_bias, norm_gain, norm_bias,
    up_table, up_bias, down_table, down_bias,
):
    is_first = lax.axis_index("section") == 0
    m = both_layers(
        tokens, cotangent, patch_mask, text_mask, qkv_weight, out_weight, up_table, down_table, qv_bias[0], out_bias,
        norm_gain[0], norm_bias[0], up_bias, down_bias,
    )
    if lax.axis_size("dp") == 16:
        qkv, out, up, down, small, input_grad = all_grads(m, tokens.shape[1])
    else:
        qkv, out, up, down, own, other = large_grads_plain(m, is_first)
        small = small_outs(own, other, is_first, tokens.shape[2])
        high = lax.ppermute(m.out_high, "section", [(0, 1)])
        value = jnp.where(is_first, m.out_low, high.astype(jnp.float32))
        input_grad = jnp.concatenate([value[:, TEXT : tokens.shape[1]], value[:, :TEXT]], axis=1)
    qv_part, proj_part, gain_part, shift_part, up_part, down_part = small
    return (
        input_grad, qkv[None], qv_part[None], out[None], proj_part, gain_part[None], shift_part[None],
        up, up_part, down, down_part,
    )


def solution(mesh):
    items, layers = P("dp"), P("section")
    return jax.shard_map(
        shards,
        mesh=mesh,
        in_specs=(items,) * 4 + (layers,) * 6 + (P(),) * 4,
        out_specs=(
            P("dp", None, "section"), P("section", None, "dp"), P("section", None, "dp"), P("section", None, "dp"),
            P("section", "dp"), P("section", None, "dp"), P("section", None, "dp"),
            P(None, None, "dp"), P(None, "dp"), P(None, "dp", None), P(None, "dp"),
        ),
        check_vma=False,
    )
```

```python
import functools

import jax
import jax.numpy as jnp
from jax import lax
from jax.experimental import pallas as pl
from jax.experimental.pallas import tpu as pltpu
from jax.sharding import PartitionSpec as P

HEAD_DIM = 64
PATCHES = 197
EPSILON = 1e-05
BLOCK = 384
WINDOW = 640
RING = 3
TEXT = 64
ROWS = 272
MESH = pl.DeviceIdType.MESH


UNITS = (
    (
        (3, 3, 0), (2, 2, 0), (3, 0, 0), (0, 1, 0), (2, 3, 0), (1, 1, 0), (3, 1, 0), (1, 2, 0), (3,
        2, 0), (0, 0, 0), (2, 1, 0), (1, 0, 1), (2, 0, 0), (1, 3, 0), (0, 3, 0), (4, 0, 1), (4, 3,
        0), (0, 2, 0), (4, 1, 0), (4, 2, 0),
    ),
    (
        (1, 0, 0), (0, 1, 0), (1, 1, 0), (4, 3, 0), (0, 2, 0), (0, 3, 1), (3, 3, 0), (0, 0, 0), (1,
        2, 0), (4, 1, 0), (4, 0, 1), (1, 3, 0), (2, 3, 0), (3, 0, 0), (3, 1, 0), (3, 2, 0), (4, 2,
        0),
    ),
)
WAIT = 4
HOP = 2
MEET = WAIT + 3 * HOP + 1
MEET_LATE = MEET + 2
LEFT_OF = ((0,), (1,), (0,), (1,), (2, 3))
MOVED = [unit[:2] for unit in UNITS[1] if unit[0] in (2, 3)]
MOVED_BITS = sum(1 << (4 * kind + plane) for kind, plane in MOVED)
FIRST_MOVED = min(u for u, unit in enumerate(UNITS[1]) if unit[:2] in MOVED)


def packed(units, handed_on):
    counts = [0, 0]
    codes = []
    for kind, plane, z_first in units:
        slot = 0
        if not (handed_on and (kind, plane) in MOVED):
            slot = counts[z_first]
            counts[z_first] += 1
        codes.append(kind | plane << 3 | z_first << 5 | slot << 6)
    codes += [0] * (-len(codes) % 3)
    return [codes[i] | codes[i + 1] << 10 | codes[i + 2] << 20 for i in range(0, len(codes), 3)], counts


PACKED, COUNTS = zip(*(packed(units, side == 0) for side, units in enumerate(UNITS)))
Y_UNITS, Z_UNITS = (max(COUNTS[0][way], COUNTS[1][way], 1) for way in range(2))


def look_up(words, u):
    word = words[0]
    for n in range(1, len(words)):
        word = jnp.where(u // 3 == n, words[n], word)
    return word >> (10 * (u % 3))


class Refs:
    pass


def sum_kernel(names, *refs):
    m = Refs()
    for name, ref in zip(names, refs):
        setattr(m, name, ref)
    section = lax.axis_index("section")
    me = lax.axis_index("dp")
    z, y, core = me // 4, (me // 2) % 2, me % 2
    peer = (section, me + 1 - 2 * core)
    beside = (section, me + 2 - 4 * y)
    right = (section, me + 4)
    left = (section, me - 4)
    aslant = (1 - section, me + 1 - 2 * core)
    across = (1 - section, me)
    on_first = section == 0
    units = jnp.where(on_first, len(UNITS[0]), len(UNITS[1]))
    computed = jnp.where(on_first, len(UNITS[0]), len(UNITS[1]) - len(MOVED))

    arrivals = [u for u, unit in enumerate(UNITS[1]) if unit[:2] in MOVED]

    def is_moved(kind, plane):
        return ((MOVED_BITS >> (4 * kind + plane)) & 1) == 1

    class Unit:
        def __init__(self, u):
            self.u = u
            code = jnp.where(on_first, look_up(PACKED[0], u), look_up(PACKED[1], u))
            self.kind = code & 7
            self.plane = (code >> 3) & 3
            self.z_first = ((code >> 5) & 1) == 1
            self.slot = (code >> 6) & 15
            moved = is_moved(self.kind, self.plane)
            self.handed_on = on_first & moved
            self.handed_in = jnp.logical_not(on_first) & moved
            self.y_first = jnp.logical_not(self.z_first | self.handed_on)
            self.y_slot = self.slot + jnp.where(self.z_first, Y_UNITS, 0)
            self.uses_text = jnp.logical_not(on_first) | (self.kind > 1)
            self.uses_patches = jnp.logical_not(on_first) | (self.kind < 2) | (self.kind == 4)
            self.order = u
            for at in arrivals:
                self.order = self.order - jnp.where((section == 1) & (u > at), 1, 0)

    def following(u):
        u = u + 1
        for at in arrivals:
            u = u + jnp.where((section == 1) & (u == at), 1, 0)
        return u

    def remote(src, dst, send, recv, device):
        return pltpu.make_async_remote_copy(
            src_ref=src, dst_ref=dst, send_sem=send, recv_sem=recv, device_id=device, device_id_type=MESH
        )

    def core_copy(order, b):
        slot = order % RING
        return remote(m.made.at[slot, 1 - core, b], m.xr.at[slot, b], m.core_send.at[order, b], m.core_recv.at[order, b], peer)

    def y_copy(n):
        return remote(m.part.at[n.u, 0], m.yr.at[n.y_slot], m.y_send.at[n.y_slot], m.y_recv.at[n.y_slot], beside)

    def right_copy(n):
        return remote(m.part.at[n.u, 1], m.zr.at[n.slot], m.right_send.at[n.slot], m.right_recv.at[n.slot], right)

    def left_copy(n):
        return remote(m.part.at[n.u, 1], m.zl.at[n.slot], m.left_send.at[n.slot], m.left_recv.at[n.slot], left)

    def right_pair(n):
        g = n.slot
        return remote(m.part.at[n.u], m.wr.at[g], m.right_send.at[Y_UNITS + g], m.right_recv.at[Y_UNITS + g], right)

    def left_pair(n):
        g = n.slot
        return remote(m.part.at[n.u], m.wl.at[g], m.left_send.at[Y_UNITS + g], m.left_recv.at[Y_UNITS + g], left)

    def over_copy(n, source, target):
        number = 4 * (n.kind - 2) + n.plane
        return remote(m.part.at[source], m.part.at[target], m.over_send.at[number], m.over_recv.at[number], across)

    def over_target(n):
        target = 0
        for at in arrivals:
            kind, plane, unused = UNITS[1][at]
            target = target + jnp.where((n.kind == kind) & (n.plane == plane), at, 0)
        return target

    def half_copy():
        return remote(m.half, m.half_out, m.half_send.at[0], m.half_recv.at[0], across)

    def own_half():
        return pl.ds(pl.multiple_of(core * BLOCK, 128), BLOCK)

    def mine(size):
        return pl.ds(pl.multiple_of(core * size, 16), size)

    def theirs(size):
        return pl.ds(pl.multiple_of((1 - core) * size, 16), size)

    def table_of(k, by_second):
        return jnp.where((k < 2) & by_second, 2, k // 2) + jnp.where(k % 2 == 1, 3, 0)

    def table_rows(k, by_second):
        return m.tables_out.at[table_of(k, by_second), :, own_half()]

    def peer_copy(k):
        return remote(m.turned.at[k, theirs(192)], table_rows(k, section == 1), m.peer_send.at[k], m.peer_recv.at[k], peer)

    def cross_copy(k, by_second, other_core):
        source = theirs(192) if other_core else mine(192)
        device = aslant if other_core else across
        number = 1 if other_core else 0
        return remote(
            m.turned.at[k, source], table_rows(k, by_second), m.cross_send.at[number, k], m.cross_recv.at[number, k], device
        )

    def attention_copies():
        rows = pl.ds(pl.multiple_of(288 + (1 - core) * 48, 16), 48)
        return (
            remote(m.turned.at[4, theirs(144)], m.qkv_out.at[:, own_half()], m.peer_send.at[4], m.peer_recv.at[4], peer),
            remote(m.turned.at[4, rows], m.out_out.at[:, own_half()], m.peer_send.at[5], m.peer_recv.at[5], peer),
        )

    def start_cross(k):
        cross_copy(k, section == 1, False).start()
        cross_copy(k, section == 1, True).start()

    def mixed_start(plane):
        return pl.multiple_of((9 * plane // 2) * 128, 128)

    def proj_start(plane):
        return pl.multiple_of((3 * plane // 2) * 128, 128)

    def tile_copies(n):
        k = n.kind
        slot = n.order % 2
        wide = pl.ds(pl.multiple_of(n.plane * 2 * BLOCK, 128), 2 * BLOCK)
        cases = []
        for ref, number, here, source, target in (
            (m.hidden, 0, (k == 0) | (k == 2), wide, slice(0, 2 * BLOCK)),
            (m.active, 0, (k == 1) | (k == 3), wide, slice(0, 2 * BLOCK)),
            (m.mixed, 0, k == 4, pl.ds(mixed_start(n.plane), WINDOW), slice(0, WINDOW)),
            (m.proj, 1, k == 4, pl.ds(proj_start(n.plane), 256), slice(WINDOW, WINDOW + 256)),
        ):
            copy = pltpu.make_async_copy(
                ref.at[:, :TEXT, source], m.text_tile.at[slot, :, :, target], m.text_sem.at[slot, number]
            )
            cases.append((here & n.uses_text, copy))
            copy = pltpu.make_async_copy(
                ref.at[:, TEXT:, source], m.patch_tile.at[slot, :, :, target], m.patch_sem.at[slot, number]
            )
            cases.append((here & n.uses_patches, copy))
        return cases

    def join_columns(slot, begin):
        for tile, joint in ((m.text_tile, m.text_joint), (m.patch_tile, m.patch_joint)):
            for side in range(2):
                at, mixed, proj = side * BLOCK, begin + side * 288, WINDOW + begin + side * 96
                joint[:, :, at : at + 288] = tile[slot, :, :, mixed : mixed + 288]
                joint[:, :, at + 288 : at + BLOCK] = tile[slot, :, :, proj : proj + 96]

    def start_tile(n):
        for here, copy in tile_copies(n):
            pl.when(here)(copy.start)

    def wait_tile(n):
        for here, copy in tile_copies(n):
            pl.when(here)(copy.wait)

    def add_into(target, source):
        target[...] = target[...] + source[...]

    def rows_dot(left, tile, *columns):
        tile = jnp.concatenate([tile[:, :, at] for at in columns], axis=2)
        return matmul(left, tile.reshape(-1, tile.shape[2]))

    def text_dot(index, slot, *columns):
        return rows_dot(m.text_left[index], m.text_tile.at[slot], *columns)

    def patch_dot(index, slot, *columns):
        return rows_dot(m.patch_left[index], m.patch_tile.at[slot], *columns)

    def joint_dot(index, *columns):
        text = rows_dot(m.text_left[index], m.text_joint, *columns)
        return rows_dot(m.patch_left[index], m.patch_joint, *columns) + text

    def compute(n):
        k = n.kind
        slot = n.order % RING

        @pl.when(n.order >= RING)
        def _():
            core_copy(n.order - RING, 0).wait_send()
            core_copy(n.order - RING, 1).wait_send()
            pl.semaphore_wait(m.credit, 1)

        @pl.when(n.order + 1 < computed)
        def _():
            start_tile(Unit(following(n.u)))

        wait_tile(n)
        tile = n.order % 2
        everything = slice(0, 2 * BLOCK)

        def put(value, columns, begin):
            for half in range(2):
                for side in range(2):
                    piece = value[half * BLOCK : (half + 1) * BLOCK, columns[side]]
                    at = slice(begin, begin + piece.shape[1])
                    m.made[slot, half, jnp.where(y == side, 1, 0), :, at] = piece.astype(jnp.bfloat16)

        sides = (slice(0, BLOCK), slice(BLOCK, 2 * BLOCK))

        @pl.when((k < 4) & jnp.logical_not(n.uses_text))
        def _():
            put(patch_dot(k % 2, tile, everything), sides, 0)

        @pl.when((k < 4) & jnp.logical_not(n.uses_patches))
        def _():
            put(text_dot(k % 2, tile, everything), sides, 0)

        @pl.when((k < 4) & n.uses_text & n.uses_patches)
        def _():
            put(patch_dot(k % 2, tile, everything) + text_dot(k % 2, tile, everything), sides, 0)

        @pl.when(k == 4)
        def _():
            ends = (slice(256, BLOCK), slice(BLOCK + 256, 2 * BLOCK))
            for odd in range(2):
                pl.when(n.plane % 2 == odd)(functools.partial(join_columns, tile, 64 * odd))
            mixed = joint_dot(2, everything)
            proj = joint_dot(3, *ends)
            put(mixed, (slice(0, 256), slice(BLOCK, BLOCK + 256)), 0)
            lanes = lax.broadcasted_iota(jnp.int32, (1, 128), 1)
            last = [jnp.where(lanes < 32, mixed[:, ends[side]], proj[:, 128 * side : 128 * side + 128]) for side in range(2)]
            put(jnp.concatenate(last, axis=1), (slice(0, 128), slice(128, 256)), 256)

        core_copy(n.order, 0).start()
        core_copy(n.order, 1).start()

    def join_core(n):
        slot = n.order % RING

        @pl.when(n.handed_in)
        def _():
            over_copy(n, 0, n.u).wait_recv()

        @pl.when(jnp.logical_not(n.handed_in))
        def _():
            core_copy(n.order, 0).wait_recv()
            m.part[n.u, 0] = m.made[slot, core, 0] + m.xr[slot, 0]

        pl.when(n.y_first)(lambda: y_copy(n).start())

        @pl.when(jnp.logical_not(n.handed_in))
        def _():
            core_copy(n.order, 1).wait_recv()
            m.part[n.u, 1] = m.made[slot, core, 1] + m.xr[slot, 1]

            @pl.when(n.order + RING < computed)
            def _():
                pl.semaphore_signal(m.credit, inc=1, device_id=peer, device_id_type=MESH)

        pl.when(n.handed_on)(lambda: over_copy(n, n.u, over_target(n)).start())

    def join_y(n):
        y_copy(n).wait_recv()
        add_into(m.part.at[n.u, 1], m.yr.at[n.y_slot])

    def take(n, one, pair, single_from, pair_from):
        @pl.when(n.y_first)
        def _():
            one(n).wait_recv()
            add_into(m.part.at[n.u, 1], single_from.at[n.slot])

        @pl.when(n.z_first)
        def _():
            pair(n).wait_recv()
            add_into(m.part.at[n.u], pair_from.at[n.slot])

    def take_right(n):
        take(n, right_copy, right_pair, m.zr, m.wr)

    def take_left(n):
        take(n, left_copy, left_pair, m.zl, m.wl)

    def pass_right(n):
        pl.when(z > 0)(lambda: take_right(n))
        pl.when(n.y_first)(lambda: right_copy(n).start())
        pl.when(n.z_first)(lambda: right_pair(n).start())

    def pass_left(n):
        pl.when(z < 3)(lambda: take_left(n))
        pl.when(n.y_first)(lambda: left_copy(n).start())
        pl.when(n.z_first)(lambda: left_pair(n).start())

    def give(n, i):
        k = n.kind
        m.turned[k] = m.part[n.u, 1].T

        @pl.when(k < 4)
        def _():
            m.tables_out[table_of(k, section == 1), :, own_half()] = m.turned[k, mine(192), :]
            peer_copy(k).start()
            pl.when(on_first | (i > FIRST_MOVED))(lambda: start_cross(k))

        @pl.when(k == 4)
        def _():
            m.qkv_out[:, own_half()] = m.turned[4, mine(144), :]
            m.out_out[:, own_half()] = m.turned[4, pl.ds(pl.multiple_of(288 + core * 48, 16), 48), :]
            for copy in attention_copies():
                copy.start()

    def greet_first(u, carry):
        n = Unit(u)
        ended = jnp.where(n.z_first, MEET_LATE, MEET) + u <= FIRST_MOVED
        pl.when(ended & (n.kind < 4) & (n.plane == z))(lambda: start_cross(n.kind))
        return carry

    def meet(n, i):
        pl.when(z > 0)(lambda: take_right(n))
        pl.when(z < 3)(lambda: take_left(n))
        pl.when(n.z_first)(lambda: y_copy(n).start())
        pl.when(n.y_first)(lambda: give(n, i))

    def meet_late(n, i):
        join_y(n)
        give(n, i)

    flips = (peer, beside, (section, me + 4 - 8 * (z % 2)), (section, me + 8 - 16 * (z // 2)), across)

    def small_copy(j):
        return remote(m.small_sum.at[j], m.small_in.at[j], m.small_send.at[j], m.small_recv.at[j], flips[j])

    def small_step(j):
        if j == 0:
            m.small_sum[0] = m.small[...]
        else:
            small_copy(j - 1).wait_recv()
            if j == 5:
                m.small_out[0] = m.small_sum[4]
                m.small_out[1] = m.small_in[4]
            else:
                m.small_sum[j] = m.small_sum[j - 1] + m.small_in[j - 1]
        if j < 5:
            small_copy(j).start()

    lefts = (m.n2, m.branch, m.n1, m.att)
    turns = [[], []]
    for side in range(2):
        for kind, plane, z_first in UNITS[side]:
            for index in () if side == 1 and (kind, plane) in MOVED else LEFT_OF[kind]:
                if index not in turns[side]:
                    turns[side].append(index)

    def stage_copy(index):
        return pltpu.make_async_copy(lefts[index], m.stage, m.stage_sem.at[0])

    def start_stage(turn):
        for side in range(2):
            pl.when(section == side)(stage_copy(turns[side][turn]).start)

    def prepare(turn):
        stage_copy(0).wait()
        number = jnp.where(on_first, turns[0][turn], turns[1][turn])

        def part(c, carry):
            at = pl.ds(pl.multiple_of(c * 128, 128), 128)
            m.text_left[number, at, :] = m.stage[:, :TEXT, at].reshape(-1, 128).T
            m.patch_left[number, at, :] = m.stage[:, TEXT:, at].reshape(-1, 128).T
            return carry

        lax.fori_loop(0, m.stage.shape[2] // 128, part, 0)
        if turn < 3:
            start_stage(turn + 1)

    barrier = pltpu.get_barrier_semaphore()
    for device in (peer, beside, flips[3]):
        pl.semaphore_signal(barrier, inc=1, device_id=device, device_id_type=MESH)

    @pl.when(section == 1)
    def _():
        for device in (across, aslant):
            pl.semaphore_signal(barrier, inc=1, device_id=device, device_id_type=MESH)

    @pl.when(z < 3)
    def _():
        pl.semaphore_signal(barrier, inc=1, device_id=right, device_id_type=MESH)

    @pl.when(z > 0)
    def _():
        pl.semaphore_signal(barrier, inc=1, device_id=left, device_id_type=MESH)

    start_stage(0)
    start_tile(Unit(jnp.int32(0)))
    prepare(0)
    pl.semaphore_wait(barrier, 3 + jnp.where(on_first, 2, 0) + jnp.where(z < 3, 1, 0) + jnp.where(z > 0, 1, 0))

    @pl.when(on_first)
    def _():
        for device in (across, aslant):
            pl.semaphore_signal(m.ready, inc=1, device_id=device, device_id_type=MESH)
        half_copy().start()


    def at_unit(u, condition, action, *more):
        n = Unit(jnp.maximum(u, 0))

        @pl.when((u >= 0) & (u < units) & condition(n))
        def _():
            action(n, *more)

    def in_flow(n):
        return jnp.logical_not(n.handed_on)

    def step(i, carry):
        @pl.when((i == FIRST_MOVED + 1) & (section == 1))
        def _():
            pl.semaphore_wait(m.ready, 2)
            lax.fori_loop(0, units, greet_first, 0)

        at_unit(i, lambda n: jnp.logical_not(n.handed_in), compute)
        for number in range(3):
            pl.when(i == number)(functools.partial(prepare, number + 1))
        at_unit(i - 1, lambda n: n.kind >= 0, join_core)
        at_unit(i - WAIT, lambda n: n.y_first, join_y)
        at_unit(i - WAIT - HOP * z, lambda n: in_flow(n) & (n.plane > z), pass_right)
        at_unit(i - WAIT - HOP * (3 - z), lambda n: in_flow(n) & (n.plane < z), pass_left)
        at_unit(i - MEET, lambda n: in_flow(n) & (n.plane == z), meet, i)
        at_unit(i - MEET_LATE, lambda n: n.z_first & (n.plane == z), meet_late, i)
        for j in range(4):
            pl.when(i == 3 + j)(functools.partial(small_step, j))
        return carry

    lax.fori_loop(0, units + MEET_LATE, step, 0)
    small_step(4)

    def ours(k):
        return True if k in (0, 1, 4) else is_moved(k, z) == (section == 1)

    def when_ours(k, wanted, action):
        pl.when(jnp.logical_not(ours(k) ^ wanted) if k in (2, 3) else True)(action)

    small_step(5)

    def settle(u, carry):
        n = Unit(u)

        @pl.when(jnp.logical_not(n.handed_in) & (n.order >= computed - RING))
        def _():
            core_copy(n.order, 0).wait_send()
            core_copy(n.order, 1).wait_send()

        pl.when(n.handed_on)(lambda: over_copy(n, n.u, over_target(n)).wait_send())
        pl.when(n.y_first | (n.z_first & (n.plane == z)))(lambda: y_copy(n).wait_send())
        pl.when(n.y_first & (n.plane > z))(lambda: right_copy(n).wait_send())
        pl.when(n.z_first & (n.plane > z))(lambda: right_pair(n).wait_send())
        pl.when(n.y_first & (n.plane < z))(lambda: left_copy(n).wait_send())
        pl.when(n.z_first & (n.plane < z))(lambda: left_pair(n).wait_send())
        return carry

    lax.fori_loop(0, units, settle, 0)
    for j in range(5):
        small_copy(j).wait_send()
    for k in range(4):

        def arrived(k=k):
            for other_core in (False, True):
                cross_copy(k, section == 0, other_core).wait_recv()

        def sent(k=k):
            peer_copy(k).wait()
            for other_core in (False, True):
                cross_copy(k, section == 1, other_core).wait_send()

        when_ours(k, True, sent)
        when_ours(k, False, arrived)
    for copy in attention_copies():
        copy.wait()

    @pl.when(on_first)
    def _():
        half_copy().wait_send()

    @pl.when(section == 1)
    def _():
        half_copy().wait_recv()

def summed_grads(n1, att, n2, branch, hidden, active, mixed, proj, half, small):
    dma = pltpu.SemaphoreType.DMA
    items, depth, width = n1.shape
    bf16, f32 = jnp.bfloat16, jnp.float32
    tile = (BLOCK, BLOCK)
    vmem, anywhere = pl.BlockSpec(memory_space=pltpu.VMEM), pl.BlockSpec(memory_space=pl.ANY)
    ins = dict(n1=n1, att=att, n2=n2, branch=branch, hidden=hidden, active=active, mixed=mixed, proj=proj, half=half,
        small=small)
    outs = dict(
        tables_out=((6, 192, width), bf16), qkv_out=((144, width), bf16),
        out_out=((48, width), bf16), small_out=((2,) + small.shape, f32), half_out=(half.shape, bf16),
    )
    buffers = dict(
        text_tile=((2, items, TEXT, WINDOW + 256), bf16),
        patch_tile=((2, items, depth - TEXT, WINDOW + 256), bf16), text_joint=((items, TEXT, 2 * BLOCK), bf16),
        patch_joint=((items, depth - TEXT, 2 * BLOCK), bf16), part=((20, 2) + tile, bf16), made=((RING, 2, 2) + tile, bf16),
        xr=((RING, 2) + tile, bf16), yr=((Y_UNITS + Z_UNITS,) + tile, bf16), zr=((Y_UNITS,) + tile, bf16), zl=((Y_UNITS,) + tile, bf16),
        wr=((Z_UNITS, 2) + tile, bf16), wl=((Z_UNITS, 2) + tile, bf16), turned=((5,) + tile, bf16),
        text_left=((4, width, items * TEXT), bf16), patch_left=((4, width, items * (depth - TEXT)), bf16), stage=((items, depth, width), bf16), small_sum=((5,) + small.shape, f32),
        small_in=((5,) + small.shape, f32),
    )
    semaphores = dict(
        small_send=dma((5,)), small_recv=dma((5,)), text_sem=dma((2, 2)), patch_sem=dma((2, 2)), stage_sem=dma((1,)), core_send=dma((20, 2)),
        core_recv=dma((20, 2)), y_send=dma((Y_UNITS + Z_UNITS,)), y_recv=dma((Y_UNITS + Z_UNITS,)), right_send=dma((Y_UNITS + Z_UNITS,)), right_recv=dma((Y_UNITS + Z_UNITS,)),
        left_send=dma((Y_UNITS + Z_UNITS,)), left_recv=dma((Y_UNITS + Z_UNITS,)), over_send=dma((8,)), over_recv=dma((8,)), half_send=dma((1,)), half_recv=dma((1,)), peer_send=dma((6,)),
        peer_recv=dma((6,)), cross_send=dma((2, 4)), cross_recv=dma((2, 4)),
        credit=pltpu.SemaphoreType.REGULAR, ready=pltpu.SemaphoreType.REGULAR,
    )
    names = list(ins) + list(outs) + list(buffers) + list(semaphores)
    return pl.pallas_call(
        functools.partial(sum_kernel, names),
        out_shape=[jax.ShapeDtypeStruct(*kind) for kind in outs.values()],
        in_specs=[anywhere] * 9 + [vmem],
        out_specs=[vmem] * (len(outs) - 1) + [anywhere],
        scratch_shapes=[pltpu.VMEM(*kind) for kind in buffers.values()] + list(semaphores.values()),
        compiler_params=pltpu.CompilerParams(
            collective_id=0, has_side_effects=True, vmem_limit_bytes=60 * 1024 * 1024
        ),
        cost_estimate=pl.CostEstimate(flops=48 * 2 * 768 * 384 * items * depth, bytes_accessed=40_000_000, transcendentals=0),
    )(*ins.values())


def finish_kernel(count, *refs):
    sources, targets = refs[:count], refs[count : count + 11]
    held, made, (load_sem, store_sem) = refs[count + 11 : -7], refs[-7:-2], refs[-2:]
    loads = [pltpu.make_async_copy(*pair, load_sem.at[n]) for n, pair in enumerate(zip(sources, held))]
    stores = [pltpu.make_async_copy(*pair, store_sem.at[n]) for n, pair in enumerate(zip(made, targets[:5]))]
    for load in loads:
        load.start()
    tables, qkv, out, small, half, grad = held
    small_outs = targets[5:]
    loads[0].wait()
    for number, source in enumerate((tables.at[:3], tables.at[3:], qkv, out)):
        if number > 1:
            loads[number - 1].wait()
        made[number][...] = source[...].astype(jnp.float32)
        stores[number].start()
    for load in loads[3:]:
        load.wait()
    section, me = lax.axis_index("section"), lax.axis_index("dp")
    width, wide = tables.shape[2], tables.shape[2] // 16
    ff = width * 4

    def columns(row, size):
        return pltpu.roll(row, (row.shape[1] - size * me) % row.shape[1], 1)[:, :size]

    def up_bias(side, slot):
        return columns(jnp.concatenate([small[side, 9 + 3 * slot + j : 10 + 3 * slot + j] for j in range(3)], axis=1), ff // 16)

    own = columns(small[0, :9, :width], wide)
    other = columns(small[1, :9, :width], wide)
    qv_out, proj_out, gain_out, shift_out, up_bias_out, down_bias_out = small_outs
    qv_out[...] = own[2:4]
    proj_out[...] = own[4:5]
    gain_out[...] = own[5:7]
    shift_out[...] = own[7:9]
    for side in range(2):
        mine, theirs = (own, other) if side == 0 else (other, own)

        @pl.when(section == side)
        def _():
            for i in range(grad.shape[0]):
                place(made[4], i, grad[i] if side == 0 else half[i].astype(jnp.float32))
            stores[4].start()
            down_bias_out[0:2] = mine[0:2]
            down_bias_out[2:3] = theirs[0:1]
            up_bias_out[0:1] = up_bias(side, 0)
            up_bias_out[1:2] = up_bias(side, 1)
            up_bias_out[2:3] = up_bias(1 - side, 0)

    for store in stores:
        store.wait()


def place(target, i, value):
    target[i, :PATCHES] = value[TEXT : target.shape[1]]
    target[i, PATCHES:] = value[:TEXT]


def finished(length, *sources):
    tables, qkv, out, small, half, grad = sources
    width = tables.shape[2]
    shapes = [(3,) + tables.shape[1:]] * 2 + [qkv.shape, out.shape, (grad.shape[0], length, grad.shape[2])]
    shapes += [(rows, width // 16) for rows in (2, 1, 2, 2)] + [(3, width // 4), (3, width // 16)]
    return pl.pallas_call(
        functools.partial(finish_kernel, len(sources)),
        out_shape=[jax.ShapeDtypeStruct(shape, jnp.float32) for shape in shapes],
        in_specs=[pl.BlockSpec(memory_space=pltpu.HBM)] * len(sources),
        out_specs=[pl.BlockSpec(memory_space=pl.ANY)] * 5 + [pl.BlockSpec(memory_space=pltpu.VMEM)] * 6,
        scratch_shapes=[pltpu.VMEM(value.shape, value.dtype) for value in sources]
        + [pltpu.VMEM(shape, jnp.float32) for shape in shapes[:5]]
        + [pltpu.SemaphoreType.DMA((len(sources),)), pltpu.SemaphoreType.DMA((5,))],
        compiler_params=pltpu.CompilerParams(vmem_limit_bytes=60 * 1024 * 1024),
    )(*sources)


CHUNK = 1024
PIECE = 768
KEY_SPLIT = 256
TAIL = (0.319381530, -0.356563782, 1.781477937, -1.821255978, 1.330274429)
LOG2_E = 1.4426950408889634
LOG2_PEAK = -1.3257480647361593


def normal_parts(z):
    size = jnp.abs(z)
    scale = 1.0 + 0.2316419 * size
    t = pl.reciprocal(scale, approx=True)
    t = t * (2.0 - scale * t)
    bell = jnp.exp2(z * z * (-0.5 * LOG2_E) + LOG2_PEAK)
    series = TAIL[4]
    for factor in TAIL[3::-1]:
        series = series * t + factor
    upper = bell * (series * t)
    return jnp.where(z >= 0, 1.0 - upper, upper), bell


def matmul(left, right):
    return jnp.dot(left, right, preferred_element_type=jnp.float32)


def matmul_turned(left, right):
    return lax.dot_general(left, right, (((1,), (1,)), ((), ())), preferred_element_type=jnp.float32)


def standardized(values):
    centre = values - jnp.mean(values, -1, keepdims=True)
    inverse = lax.rsqrt(jnp.mean(centre * centre, -1, keepdims=True) + EPSILON)
    return centre * inverse, inverse


def norm_step_back(delta, standard, inverse, gain_row):
    scaled = delta * gain_row
    moved = inverse * (
        scaled - jnp.mean(scaled, -1, keepdims=True) - standard * jnp.mean(scaled * standard, -1, keepdims=True)
    )
    return moved, jnp.sum(delta * standard, 0, keepdims=True), jnp.sum(delta, 0, keepdims=True)


def half_mask(half):
    lanes = lax.broadcasted_iota(jnp.int32, (1, 128), 1)
    return (lanes < 64) if half == 0 else (lanes >= 64)


def pair_columns(p, part, width):
    return slice(part * width + p * 128, part * width + p * 128 + 128)


def both_halves(pair):
    return jnp.concatenate([jnp.where(half_mask(half), pair, jnp.zeros_like(pair)) for half in range(2)], axis=0)


def in_turn(count, *stages):
    for turn in range(count + len(stages) - 1):
        for number, stage in enumerate(stages):
            if 0 <= turn - number < count:
                stage(turn - number)


def attention_forward(m, length):
    rows, width = m.att.shape

    def scores(p):
        q2 = m.qkv[:, pair_columns(p, 0, width)]
        k2 = m.qkv[:, pair_columns(p, 1, width)]
        m.scores[p % 2] = matmul_turned(both_halves(k2), q2).reshape(2, rows, rows)

    def soften(p):
        for half in range(2):
            top = m.scores[p % 2, half, :KEY_SPLIT]
            low = m.scores[p % 2, half, KEY_SPLIT:]
            key_row = KEY_SPLIT + lax.broadcasted_iota(jnp.int32, low.shape, 0)
            low = jnp.where(key_row < length, low, -1e30)
            peak = jnp.maximum(jnp.max(top, 0, keepdims=True), jnp.max(low, 0, keepdims=True))
            top = jnp.exp(top - peak)
            low = jnp.exp(low - peak)
            over = 1.0 / (jnp.sum(top, 0, keepdims=True) + jnp.sum(low, 0, keepdims=True))
            m.probs[2 * p + half, :KEY_SPLIT] = (top * over).astype(jnp.bfloat16)
            m.probs[2 * p + half, KEY_SPLIT:] = (low * over).astype(jnp.bfloat16)

    def blend(p):
        v_turned = m.qkv[:, pair_columns(p, 2, width)].T
        parts = [matmul(v_turned[64 * half : 64 * half + 64], m.probs[2 * p + half]) for half in range(2)]
        turned = jnp.concatenate(parts, axis=0)
        m.att_turned[p * 128 : p * 128 + 128, :] = turned.astype(jnp.bfloat16)
        m.att[:, p * 128 : p * 128 + 128] = turned.T.astype(jnp.bfloat16)

    in_turn(width // 128, scores, soften, blend)


def attention_back(m):
    rows, width = m.att.shape

    def probs_back(p):
        v2 = m.qkv[:, pair_columns(p, 2, width)]
        d_turned = m.att_delta[:, pair_columns(p, 0, width)].T
        m.scores[p % 2] = matmul(both_halves(v2), d_turned).reshape(2, rows, rows)
        product = d_turned.astype(jnp.float32) * m.att_turned[p * 128 : p * 128 + 128, :].astype(jnp.float32)
        for half in range(2):
            m.inner[p % 2, half] = jnp.sum(product[64 * half : 64 * half + 64], 0, keepdims=True)

    def scores_back(p):
        for half in range(2):
            probs = m.probs[2 * p + half].astype(jnp.float32)
            m.score_delta[p % 2, half] = (probs * (m.scores[p % 2, half] - m.inner[p % 2, half])).astype(jnp.bfloat16)

    def heads_back(p):
        q_at, k_at, v_at = (pair_columns(p, part, width) for part in range(3))
        score = m.score_delta[p % 2]
        probs = m.probs[2 * p : 2 * p + 2].reshape(2 * rows, rows)
        k_turned = m.qkv[:, k_at].T
        value = matmul(probs, m.att_delta[:, q_at])
        key = matmul(score.reshape(2 * rows, rows), m.qkv[:, q_at])
        query = jnp.concatenate(
            [matmul(k_turned[64 * half : 64 * half + 64], score[half]) for half in range(2)], axis=0
        )
        dq = (query.T * HEAD_DIM ** (-0.5)).astype(jnp.bfloat16)
        dk = jnp.where(half_mask(0), key[:rows], key[rows:]).astype(jnp.bfloat16)
        dv = jnp.where(half_mask(0), value[:rows], value[rows:]).astype(jnp.bfloat16)
        m.mixed[:, q_at] = dq
        m.mixed[:, k_at] = dk
        m.mixed[:, v_at] = dv
        m.sums[2:3, q_at] += jnp.sum(dq.astype(jnp.float32), 0, keepdims=True)
        m.sums[3:4, q_at] += jnp.sum(dv.astype(jnp.float32), 0, keepdims=True)

    in_turn(width // 128, probs_back, scores_back, heads_back)


def forward_front(m, x_ref, length, hold):
    x = x_ref[...].astype(jnp.float32)
    standard, inverse = standardized(x)
    if hold:
        m.standard[...] = standard
        m.inverse[0] = inverse
    m.n1[...] = (standard * m.gain[0:1] + m.shift[0:1]).astype(jnp.bfloat16)
    width = x.shape[1]
    m.need(m.qkv_w)
    value = matmul(m.n1[...], m.qkv_w[...])
    query = (value[:, :width] + m.qv[0:1]).astype(jnp.bfloat16)
    m.qkv[:, :width] = query * jnp.bfloat16(HEAD_DIM ** (-0.5))
    m.qkv[:, width : 2 * width] = value[:, width : 2 * width].astype(jnp.bfloat16)
    m.qkv[:, 2 * width :] = (value[:, 2 * width :] + m.qv[1:2]).astype(jnp.bfloat16)
    attention_forward(m, length)
    m.need(m.out_w)
    middle = x_ref[...].astype(jnp.float32) + matmul(m.att[...], m.out_w[...]) + m.proj[0:1]
    standard, inverse = standardized(middle)
    m.middle[...] = standard if hold else middle
    if hold:
        m.inverse[1] = inverse
    m.n2[...] = (standard * m.gain[1:2] + m.shift[1:2]).astype(jnp.bfloat16)


def back_tail(m, x_ref, g_ref, n2_delta, keep, held):
    standard, inverse = (m.middle[...], m.inverse[1]) if held else standardized(m.middle[...])
    middle_part, gain, shift = norm_step_back(n2_delta, standard, inverse, m.gain[1:2])
    m.sums[6:7, :gain.shape[1]] += gain
    m.sums[8:9, :gain.shape[1]] += shift
    middle_delta = g_ref[...].astype(jnp.float32) + middle_part
    proj_delta = middle_delta.astype(jnp.bfloat16)
    m.sums[4:5, :gain.shape[1]] += jnp.sum(proj_delta.astype(jnp.float32), 0, keepdims=True)
    m.proj_delta[...] = proj_delta
    m.middle_delta[...] = middle_delta
    m.att_delta[...] = matmul_turned(proj_delta, m.out_w[...]).astype(jnp.bfloat16)
    attention_back(m)
    total = matmul_turned(m.mixed[...], m.qkv_w[...])
    standard, inverse = (m.standard[...], m.inverse[0]) if held else standardized(x_ref[...].astype(jnp.float32))
    input_part, gain, shift = norm_step_back(total, standard, inverse, m.gain[0:1])
    m.sums[5:6, :gain.shape[1]] += gain
    m.sums[7:8, :gain.shape[1]] += shift
    keep(m.middle_delta[...] + input_part)


def forward_expert(m, slot, begin, end):
    def columns(j):
        return slice(j * PIECE, (j + 1) * PIECE)

    def widen(j):
        hidden = matmul(m.n2[begin:end], m.up_w[slot, :, columns(j)])
        m.hidden[j % 2, begin:end] = hidden + m.up_b[slot : slot + 1, columns(j)]

    def bend(j):
        hidden = m.hidden[j % 2, begin:end]
        below, bell = normal_parts(hidden)
        m.active[begin:end, columns(j)] = (hidden * below).astype(jnp.bfloat16)
        m.slope[begin:end, columns(j)] = (below + hidden * bell).astype(jnp.bfloat16)

    in_turn(m.up_w.shape[2] // PIECE, widen, bend)
    result = matmul(m.active[begin:end], m.down_w[slot])
    m.total[begin:end] = m.middle[begin:end] + result + m.down_b[slot : slot + 1]


def add_up_sums(m, slot, begin, end):
    for j in range(m.up_w.shape[2] // CHUNK):
        piece = m.hidden_delta[begin:end, j * CHUNK : (j + 1) * CHUNK].astype(jnp.float32)
        m.sums[9 + 3 * slot + j : 10 + 3 * slot + j] += jnp.sum(piece, 0, keepdims=True)


def back_expert(m, g_ref, slot, begin, end):
    m.sums[slot : slot + 1, : g_ref.shape[1]] += jnp.sum(g_ref[begin:end].astype(jnp.float32), 0, keepdims=True)
    active_delta = matmul_turned(g_ref[begin:end], m.down_w[slot])
    m.hidden_delta[begin:end] = (active_delta * m.slope[begin:end].astype(jnp.float32)).astype(jnp.bfloat16)
    m.total[begin:end] = matmul_turned(m.hidden_delta[begin:end], m.up_w[slot])
    add_up_sums(m, slot, begin, end)


def both_expert(m, g_ref):
    def columns(j):
        return slice(j * PIECE, (j + 1) * PIECE)

    def widen(j):
        m.hidden[j % 2] = matmul(m.n2[...], m.up_w[0, :, columns(j)]) + m.up_b[2:3, columns(j)]
        m.active_delta[j % 2] = matmul_turned(g_ref[...], m.down_w[0, columns(j), :])

    def bend(j):
        hidden = m.hidden[j % 2]
        below, bell = normal_parts(hidden)
        m.active[:, columns(j)] = (hidden * below).astype(jnp.bfloat16)
        slope = below + hidden * bell
        m.hidden_delta[:, columns(j)] = (m.active_delta[j % 2] * slope).astype(jnp.bfloat16)

    def narrow(j):
        piece = matmul_turned(m.hidden_delta[:, columns(j)], m.up_w[0, :, columns(j)])
        m.total[...] = piece if j == 0 else m.total[...] + piece

    in_turn(m.up_w.shape[2] // PIECE, widen, bend, narrow)
    add_up_sums(m, 0, 0, ROWS)


def layers_kernel(names, *refs):
    m = Refs()
    for name, ref in zip(names, refs):
        setattr(m, name, ref)
    items, length = m.in_tokens.shape[:2]
    half = m.total.shape[1] // 2
    section = lax.axis_index("section")
    across = (1 - section, lax.axis_index("dp"))

    def send(i, part):
        rows = (slice(0, TEXT), slice(TEXT, ROWS))[part]
        return pltpu.make_async_remote_copy(
            src_ref=m.leaving.at[i, rows], dst_ref=m.landed.at[i, rows], send_sem=m.send_sem.at[i, part],
            recv_sem=m.recv_sem.at[i, part], device_id=across, device_id_type=MESH,
        )

    def side_copies(i):
        return (
            pltpu.make_async_copy(m.low.at[i], m.out_low.at[i], m.side_sem.at[0, i]),
            pltpu.make_async_copy(m.high.at[i], m.out_high.at[i], m.side_sem.at[1, i]),
        )

    def local(source, target, number):
        return pltpu.make_async_copy(source, target, m.copy_sem.at[number])

    def branch_copy(source, i):
        return pltpu.make_async_copy(source.at[i], m.branch.at[i], m.branch_sem.at[i])

    def weights(experts):
        found = [
            (m.qkv_w, [local(m.in_qkv.at[0], m.qkv_w, 0)]),
            (m.out_w, [local(m.in_out.at[0], m.out_w, 1)]),
            (m.up_w, []),
            (m.down_w, []),
        ]
        for slot, expert in enumerate(experts):
            found[2][1].append(local(m.in_up.at[expert], m.up_w.at[slot], 2 + slot))
            found[3][1].append(local(m.in_down.at[expert], m.down_w.at[slot], 4 + slot))
        return found

    def start_weights(found):
        copies = found[0][1] + found[1][1]
        for pair in zip(found[2][1], found[3][1]):
            copies += pair
        for copy in copies:
            copy.start()

    def needs(found, i):
        def need(ref, slot=0):
            for here, copies in found:
                if here is ref:
                    pl.when(i == 0)(copies[slot].wait)

        return need

    leaving = (
        (m.n1, m.out_n1), (m.att, m.out_att), (m.n2, m.out_n2), (m.active, m.out_active), (m.qkv, m.kept_qkv),
        (m.probs, m.kept_probs), (m.att_turned, m.kept_turned), (m.middle, m.kept_middle), (m.slope, m.kept_slope),
        (m.mixed, m.out_mixed), (m.proj_delta, m.out_proj), (m.hidden_delta, m.out_hidden),
    )
    n1, att, n2, active, qkv, probs, turned, middle, slope, mixed, proj, hidden = range(len(leaving))

    def puts(i):
        return lambda number: local(leaving[number][0], leaving[number][1].at[i], 6 + number)

    def gets(i):
        return lambda number: local(leaving[number][1].at[i], leaving[number][0], 14 + number)

    def start(copies, *which):
        for number in which:
            copies(number).start()

    def wait(copies, *which):
        for number in which:
            copies(number).wait()

    def settle(i, *which):
        @pl.when(i > 0)
        def _():
            wait(puts(i), *which)

    def text_first(target, source, i):
        value = source[i].astype(jnp.float32)
        pad = jnp.zeros((ROWS - length, value.shape[1]), jnp.float32)
        target[i, :TEXT] = value[PATCHES:].astype(jnp.bfloat16)
        target[i, TEXT:] = jnp.concatenate([value[:PATCHES], pad], axis=0).astype(jnp.bfloat16)

    def mask_targets(i):
        row = lax.broadcasted_iota(jnp.int32, (ROWS, 1), 0)
        position = jnp.where(row < TEXT, row + PATCHES, jnp.where(row < length, row - TEXT, length))
        chosen = jnp.zeros((ROWS, 1), jnp.float32)
        for mask in (m.patch_mask, m.text_mask):
            same = jnp.where(position == mask[i : i + 1, :], 1.0, 0.0)
            chosen = jnp.maximum(chosen, jnp.max(same, 1, keepdims=True))
        target = m.targets[i].astype(jnp.float32) * chosen
        m.targets[i] = target.astype(jnp.bfloat16)
        m.sums[0:1, : target.shape[1]] += jnp.sum(target, 0, keepdims=True)

    def first_front(found, i, carry):
        m.need = needs(found, i)
        text_first(m.tokens, m.in_tokens, i)
        settle(i, n1, att, n2, qkv, probs, turned, middle)
        forward_front(m, m.tokens.at[i], length, False)
        start(puts(i), n1, att, n2, qkv, probs, turned, middle)
        settle(i, active, slope)
        m.need(m.up_w)
        m.need(m.down_w)
        forward_expert(m, 0, TEXT, ROWS)
        m.leaving[i, TEXT:] = m.total[TEXT:].astype(jnp.bfloat16)
        send(i, 1).start()
        m.need(m.up_w, 1)
        m.need(m.down_w, 1)
        forward_expert(m, 1, 0, TEXT)
        m.leaving[i, :TEXT] = m.total[:TEXT].astype(jnp.bfloat16)
        send(i, 0).start()
        start(puts(i), active, slope)
        return carry

    def first_back(i, carry):
        start(gets(i), slope, middle, turned, qkv, probs)

        @pl.when(i > 0)
        def _():
            send(i - 1, 0).wait_send()
            send(i - 1, 1).wait_send()

        settle(i, hidden)
        wait(gets(i), slope)
        gradient = m.landed.at[i]
        send(i, 0).wait_recv()
        back_expert(m, gradient, 1, 0, TEXT)
        send(i, 1).wait_recv()
        branch_copy(m.landed, i).start()
        back_expert(m, gradient, 0, TEXT, ROWS)
        start(puts(i), hidden)
        wait(gets(i), middle, turned, qkv, probs)
        settle(i, mixed, proj)

        def keep(value):
            m.low[i] = value[:, :half]
            m.high[i] = value[:, half:].astype(jnp.bfloat16)

        back_tail(m, m.tokens.at[i], gradient, m.total[...], keep, False)
        for copy in side_copies(i):
            copy.start()
        start(puts(i), mixed, proj)
        branch_copy(m.landed, i).wait()
        return carry

    def second_both(found, i, carry):
        m.need = needs(found, i)
        branch_copy(m.targets, i).start()
        send(i, 0).wait_recv()
        send(i, 1).wait_recv()
        settle(i, n1, att, n2)
        arrived = m.landed.at[i]
        forward_front(m, arrived, length, True)
        start(puts(i), n1, att, n2)
        settle(i, active, hidden)
        m.need(m.up_w)
        m.need(m.down_w)
        gradient = m.targets.at[i]
        both_expert(m, gradient)
        start(puts(i), active, hidden)
        settle(i, mixed, proj)

        def keep(value):
            m.leaving[i] = value.astype(jnp.bfloat16)

        back_tail(m, arrived, gradient, m.total[...], keep, True)
        send(i, 0).start()
        send(i, 1).start()
        start(puts(i), mixed, proj)
        branch_copy(m.targets, i).wait()
        return carry

    m.sums[...] = jnp.zeros(m.sums.shape, jnp.float32)
    barrier = pltpu.get_barrier_semaphore()
    pl.semaphore_signal(barrier, inc=1, device_id=across, device_id_type=MESH)

    @pl.when(section == 0)
    def _():
        found = weights((0, 1))
        start_weights(found)
        pl.semaphore_wait(barrier, 1)
        lax.fori_loop(0, items, functools.partial(first_front, found), 0)
        wait(puts(0), n1, att, n2, active, qkv, probs, turned, middle, slope)
        lax.fori_loop(0, items, first_back, 0)
        wait(puts(0), mixed, proj, hidden)
        send(items - 1, 0).wait_send()
        send(items - 1, 1).wait_send()
        for i in range(items):
            for copy in side_copies(i):
                copy.wait()

    @pl.when(section == 1)
    def _():
        found = weights((2,))
        start_weights(found)
        for i in range(items):
            text_first(m.targets, m.cotangent, i)
            mask_targets(i)
        pl.semaphore_wait(barrier, 1)
        lax.fori_loop(0, items, functools.partial(second_both, found), 0)
        wait(puts(0), n1, att, n2, active, mixed, proj, hidden)
        for i in range(items):
            send(i, 0).wait_send()
            send(i, 1).wait_send()


def both_layers(
    tokens, cotangent, patch_mask, text_mask, qkv_weight, out_weight, up_table, down_table, qv, proj, gain, shift, up_b, down_b
):
    items, length, width = tokens.shape
    rows = ROWS
    ff = up_b.shape[1]
    heads = width // HEAD_DIM
    bf16, f32 = jnp.bfloat16, jnp.float32
    dma = pltpu.SemaphoreType.DMA
    vmem, anywhere = pl.BlockSpec(memory_space=pltpu.VMEM), pl.BlockSpec(memory_space=pl.ANY)
    ins = dict(
        in_tokens=(tokens, vmem), cotangent=(cotangent, vmem), patch_mask=(patch_mask, vmem), text_mask=(text_mask, vmem), in_qkv=(qkv_weight, anywhere), in_out=(out_weight, anywhere),
        in_up=(up_table, anywhere), in_down=(down_table, anywhere), qv=(qv, vmem), proj=(proj, vmem), gain=(gain, vmem),
        shift=(shift, vmem), up_b=(up_b, vmem), down_b=(down_b, vmem),
    )

    def made(*shape, kind=bf16, spec=anywhere):
        return jax.ShapeDtypeStruct((items,) + shape, kind), spec

    outs = dict(
        out_n1=made(rows, width), out_att=made(rows, width), out_n2=made(rows, width), out_active=made(rows, ff),
        out_mixed=made(rows, 3 * width), out_proj=made(rows, width), out_hidden=made(rows, ff), branch=made(rows, width),
        kept_qkv=made(rows, 3 * width), kept_probs=made(heads, rows, rows), kept_turned=made(width, rows),
        kept_middle=made(rows, width, kind=f32), kept_slope=made(rows, ff),
        out_low=made(rows, width // 2, kind=f32), out_high=made(rows, width // 2),
        sums=(jax.ShapeDtypeStruct((16, CHUNK), f32), vmem),
    )
    low_row, wide_row = ((rows, width), bf16), ((rows, ff), bf16)
    buffers = dict(
        qkv_w=((width, 3 * width), bf16), out_w=((width, width), bf16), up_w=((2, width, ff), bf16),
        down_w=((2, ff, width), bf16), n1=low_row, att=low_row, n2=low_row, active=wide_row,
        qkv=((rows, 3 * width), bf16), probs=((heads, rows, rows), bf16), att_turned=((width, rows), bf16),
        middle=((rows, width), f32), slope=wide_row, total=((rows, width), f32), mixed=((rows, 3 * width), bf16),
        standard=((rows, width), f32), inverse=((2, rows, 1), f32), proj_delta=low_row, scores=((2, 2, rows, rows), f32),
        score_delta=((2, 2, rows, rows), bf16), inner=((2, 2, 1, rows), f32), hidden=((2, rows, PIECE), f32),
        active_delta=((2, rows, PIECE), f32), hidden_delta=wide_row, att_delta=low_row, middle_delta=((rows, width), f32),
        leaving=((items, rows, width), bf16), landed=((items, rows, width), bf16),
        low=((items, rows, width // 2), f32), high=((items, rows, width // 2), bf16),
        tokens=((items, rows, width), bf16), targets=((items, rows, width), bf16),
    )
    semaphores = dict(
        copy_sem=dma((23,)), branch_sem=dma((items,)), side_sem=dma((2, items)), send_sem=dma((items, 2)), recv_sem=dma((items, 2)),
    )
    names = list(ins) + list(outs) + list(buffers) + list(semaphores)
    results = pl.pallas_call(
        functools.partial(layers_kernel, names),
        out_shape=[shape for shape, spec in outs.values()],
        in_specs=[spec for value, spec in ins.values()],
        out_specs=[spec for shape, spec in outs.values()],
        scratch_shapes=[pltpu.VMEM(*kind) for kind in buffers.values()] + list(semaphores.values()),
        compiler_params=pltpu.CompilerParams(
            collective_id=1, has_side_effects=True, vmem_limit_bytes=60 * 1024 * 1024
        ),
        cost_estimate=pl.CostEstimate(flops=40_000_000_000, bytes_accessed=100_000_000, transcendentals=0),
    )(*[value for value, spec in ins.values()])
    m = Refs()
    for name, result in zip(outs, results):
        setattr(m, name, result)
    return m


def small_outs(own, other, is_first, width):
    first = jnp.where(is_first, own, other)
    second = jnp.where(is_first, other, own)
    me = lax.axis_index("dp")

    def columns(rows):
        wide = rows.shape[-1] // lax.axis_size("dp")
        return lax.dynamic_slice_in_dim(rows, me * wide, wide, rows.ndim - 1)

    down = columns(jnp.concatenate([first[:2], second[:1]])[:, :width])
    up = columns(jnp.concatenate([first[9:15].reshape(2, -1), second[9:12].reshape(1, -1)]))
    own = columns(own[2:9, :width])
    return own[0:2], own[2:3], own[3:5], own[5:7], up, down


def flat(value):
    return value.reshape((-1, value.shape[-1]))


def left_parts(m, is_first):
    n1, att, n2, branch_delta = (flat(part) for part in (m.out_n1, m.out_att, m.out_n2, m.branch))
    text = (jnp.arange(n1.shape[0]) % ROWS < TEXT)[:, None]
    vision = jnp.logical_not(text & is_first).astype(jnp.bfloat16)
    text = text.astype(jnp.bfloat16)
    return [
        piece.T for piece in (n2 * vision, branch_delta * vision, n2 * text, branch_delta * text, n1, att)
    ]


def all_grads(m, length):
    up, down, qkv, out, input_grad, *small = finished(
        length,
        *summed_grads(m.out_n1, m.out_att, m.out_n2, m.branch, m.out_hidden, m.out_active, m.out_mixed, m.out_proj, m.out_high, m.sums),
        m.out_low,
    )
    return qkv.T, out.T, up.transpose(0, 2, 1), down, small, input_grad


def large_grads_plain(m, is_first):
    lefts = left_parts(m, is_first)
    hidden_delta, active = flat(m.out_hidden), flat(m.out_active)

    def total_of(left, right):
        product = jnp.dot(left, right, preferred_element_type=jnp.float32).astype(jnp.bfloat16)
        return lax.psum_scatter(product, "dp", scatter_dimension=1, tiled=True)

    def table(vision_part, text_part):
        def swapped(part):
            return lax.psum(part, "section").astype(jnp.float32)

        return jnp.stack(
            [
                swapped(jnp.where(is_first, vision_part, 0)),
                swapped(jnp.where(is_first, text_part, 0)),
                swapped(jnp.where(is_first, 0, vision_part)),
            ]
        )

    up = table(total_of(lefts[0], hidden_delta), total_of(lefts[2], hidden_delta))
    down = table(total_of(lefts[1], active), total_of(lefts[3], active))
    small = lax.psum(m.sums, "dp")
    mixed, proj = flat(m.out_mixed), flat(m.out_proj)
    return (
        total_of(lefts[4], mixed).astype(jnp.float32),
        total_of(lefts[5], proj).astype(jnp.float32),
        up,
        down.transpose(0, 2, 1),
        small,
        lax.ppermute(small, "section", [(0, 1), (1, 0)]),
    )


def shards(
    tokens, cotangent, patch_mask, text_mask, qkv_weight, qv_bias, out_weight, out_bias, norm_gain, norm_bias,
    up_table, up_bias, down_table, down_bias,
):
    is_first = lax.axis_index("section") == 0
    m = both_layers(
        tokens, cotangent, patch_mask, text_mask, qkv_weight, out_weight, up_table, down_table, qv_bias[0], out_bias,
        norm_gain[0], norm_bias[0], up_bias, down_bias,
    )
    if lax.axis_size("dp") == 16:
        qkv, out, up, down, small, input_grad = all_grads(m, tokens.shape[1])
    else:
        qkv, out, up, down, own, other = large_grads_plain(m, is_first)
        small = small_outs(own, other, is_first, tokens.shape[2])
        high = lax.ppermute(m.out_high, "section", [(0, 1)])
        value = jnp.where(is_first, m.out_low, high.astype(jnp.float32))
        input_grad = jnp.concatenate([value[:, TEXT : tokens.shape[1]], value[:, :TEXT]], axis=1)
    qv_part, proj_part, gain_part, shift_part, up_part, down_part = small
    return (
        input_grad, qkv[None], qv_part[None], out[None], proj_part, gain_part[None], shift_part[None],
        up, up_part, down, down_part,
    )


def solution(mesh):
    items, layers = P("dp"), P("section")
    return jax.shard_map(
        shards,
        mesh=mesh,
        in_specs=(items,) * 4 + (layers,) * 6 + (P(),) * 4,
        out_specs=(
            P("dp", None, "section"), P("section", None, "dp"), P("section", None, "dp"), P("section", None, "dp"),
            P("section", "dp"), P("section", None, "dp"), P("section", None, "dp"),
            P(None, None, "dp"), P(None, "dp"), P(None, "dp", None), P(None, "dp"),
        ),
        check_vma=False,
    )
```

```python
import functools

import jax
import jax.numpy as jnp
from jax import lax
from jax.experimental import pallas as pl
from jax.experimental.pallas import tpu as pltpu
from jax.sharding import PartitionSpec as P

HEAD_DIM = 64
PATCHES = 197
EPSILON = 1e-05
BLOCK = 384
WINDOW = 640
RING = 3
TEXT = 64
ROWS = 272
MESH = pl.DeviceIdType.MESH


UNITS = (
    (
        (2, 2, 0), (3, 2, 0), (2, 3, 0), (3, 0, 0), (0, 1, 0), (3, 3, 0), (0, 2, 0), (3, 1, 0), (2,
        0, 0), (4, 3, 1), (1, 0, 0), (0, 3, 0), (0, 0, 1), (2, 1, 0), (1, 3, 0), (1, 1, 0), (4, 0,
        0), (4, 1, 0), (1, 2, 0), (4, 2, 0),
    ),
    (
        (0, 2, 0), (1, 0, 0), (1, 2, 0), (1, 1, 0), (0, 1, 0), (0, 3, 1), (4, 1, 1), (4, 2, 0), (1,
        3, 0), (0, 0, 0), (3, 0, 0), (4, 0, 0), (3, 2, 0), (3, 3, 0), (4, 3, 0), (3, 1, 0), (2, 1,
        0),
    ),
)
WAIT = 4
HOP = 3
MEET = WAIT + 3 * HOP + 1
MEET_LATE = MEET + 2
LEFT_OF = ((0,), (1,), (0,), (1,), (2, 3))
MOVED = [unit[:2] for unit in UNITS[1] if unit[0] in (2, 3)]
MOVED_BITS = sum(1 << (4 * kind + plane) for kind, plane in MOVED)
FIRST_MOVED = min(u for u, unit in enumerate(UNITS[1]) if unit[:2] in MOVED)


def packed(units, handed_on):
    counts = [0, 0]
    codes = []
    for kind, plane, z_first in units:
        slot = 0
        if not (handed_on and (kind, plane) in MOVED):
            slot = counts[z_first]
            counts[z_first] += 1
        codes.append(kind | plane << 3 | z_first << 5 | slot << 6)
    codes += [0] * (-len(codes) % 3)
    return [codes[i] | codes[i + 1] << 10 | codes[i + 2] << 20 for i in range(0, len(codes), 3)], counts


PACKED, COUNTS = zip(*(packed(units, side == 0) for side, units in enumerate(UNITS)))
Y_UNITS, Z_UNITS = (max(COUNTS[0][way], COUNTS[1][way], 1) for way in range(2))


def look_up(words, u):
    word = words[0]
    for n in range(1, len(words)):
        word = jnp.where(u // 3 == n, words[n], word)
    return word >> (10 * (u % 3))


class Refs:
    pass


def sum_kernel(names, *refs):
    m = Refs()
    for name, ref in zip(names, refs):
        setattr(m, name, ref)
    section = lax.axis_index("section")
    me = lax.axis_index("dp")
    z, y, core = me // 4, (me // 2) % 2, me % 2
    peer = (section, me + 1 - 2 * core)
    beside = (section, me + 2 - 4 * y)
    right = (section, me + 4)
    left = (section, me - 4)
    aslant = (1 - section, me + 1 - 2 * core)
    across = (1 - section, me)
    on_first = section == 0
    units = jnp.where(on_first, len(UNITS[0]), len(UNITS[1]))
    computed = jnp.where(on_first, len(UNITS[0]), len(UNITS[1]) - len(MOVED))

    arrivals = [u for u, unit in enumerate(UNITS[1]) if unit[:2] in MOVED]

    def is_moved(kind, plane):
        return ((MOVED_BITS >> (4 * kind + plane)) & 1) == 1

    class Unit:
        def __init__(self, u):
            self.u = u
            code = jnp.where(on_first, look_up(PACKED[0], u), look_up(PACKED[1], u))
            self.kind = code & 7
            self.plane = (code >> 3) & 3
            self.z_first = ((code >> 5) & 1) == 1
            self.slot = (code >> 6) & 15
            moved = is_moved(self.kind, self.plane)
            self.handed_on = on_first & moved
            self.handed_in = jnp.logical_not(on_first) & moved
            self.y_first = jnp.logical_not(self.z_first | self.handed_on)
            self.y_slot = self.slot + jnp.where(self.z_first, Y_UNITS, 0)
            self.uses_text = jnp.logical_not(on_first) | (self.kind > 1)
            self.uses_patches = jnp.logical_not(on_first) | (self.kind < 2) | (self.kind == 4)
            self.order = u
            for at in arrivals:
                self.order = self.order - jnp.where((section == 1) & (u > at), 1, 0)

    def following(u):
        u = u + 1
        for at in arrivals:
            u = u + jnp.where((section == 1) & (u == at), 1, 0)
        return u

    def remote(src, dst, send, recv, device):
        return pltpu.make_async_remote_copy(
            src_ref=src, dst_ref=dst, send_sem=send, recv_sem=recv, device_id=device, device_id_type=MESH
        )

    def core_copy(order, b):
        slot = order % RING
        return remote(m.made.at[slot, 1 - core, b], m.xr.at[slot, b], m.core_send.at[order, b], m.core_recv.at[order, b], peer)

    def y_copy(n):
        return remote(m.part.at[n.u, 0], m.yr.at[n.y_slot], m.y_send.at[n.y_slot], m.y_recv.at[n.y_slot], beside)

    def right_copy(n):
        return remote(m.part.at[n.u, 1], m.zr.at[n.slot], m.right_send.at[n.slot], m.right_recv.at[n.slot], right)

    def left_copy(n):
        return remote(m.part.at[n.u, 1], m.zl.at[n.slot], m.left_send.at[n.slot], m.left_recv.at[n.slot], left)

    def right_pair(n):
        g = n.slot
        return remote(m.part.at[n.u], m.wr.at[g], m.right_send.at[Y_UNITS + g], m.right_recv.at[Y_UNITS + g], right)

    def left_pair(n):
        g = n.slot
        return remote(m.part.at[n.u], m.wl.at[g], m.left_send.at[Y_UNITS + g], m.left_recv.at[Y_UNITS + g], left)

    def over_copy(n, source, target):
        number = 4 * (n.kind - 2) + n.plane
        return remote(m.part.at[source], m.part.at[target], m.over_send.at[number], m.over_recv.at[number], across)

    def over_target(n):
        target = 0
        for at in arrivals:
            kind, plane, unused = UNITS[1][at]
            target = target + jnp.where((n.kind == kind) & (n.plane == plane), at, 0)
        return target

    def half_copy():
        return remote(m.half, m.half_out, m.half_send.at[0], m.half_recv.at[0], across)

    def own_half():
        return pl.ds(pl.multiple_of(core * BLOCK, 128), BLOCK)

    def mine(size):
        return pl.ds(pl.multiple_of(core * size, 16), size)

    def theirs(size):
        return pl.ds(pl.multiple_of((1 - core) * size, 16), size)

    def table_of(k, by_second):
        return jnp.where((k < 2) & by_second, 2, k // 2) + jnp.where(k % 2 == 1, 3, 0)

    def table_rows(k, by_second):
        return m.tables_out.at[table_of(k, by_second), :, own_half()]

    def peer_copy(k):
        return remote(m.turned.at[k, theirs(192)], table_rows(k, section == 1), m.peer_send.at[k], m.peer_recv.at[k], peer)

    def cross_copy(k, by_second, other_core):
        source = theirs(192) if other_core else mine(192)
        device = aslant if other_core else across
        number = 1 if other_core else 0
        return remote(
            m.turned.at[k, source], table_rows(k, by_second), m.cross_send.at[number, k], m.cross_recv.at[number, k], device
        )

    def attention_copies():
        rows = pl.ds(pl.multiple_of(288 + (1 - core) * 48, 16), 48)
        return (
            remote(m.turned.at[4, theirs(144)], m.qkv_out.at[:, own_half()], m.peer_send.at[4], m.peer_recv.at[4], peer),
            remote(m.turned.at[4, rows], m.out_out.at[:, own_half()], m.peer_send.at[5], m.peer_recv.at[5], peer),
        )

    def start_cross(k):
        cross_copy(k, section == 1, False).start()
        cross_copy(k, section == 1, True).start()

    def mixed_start(plane):
        return pl.multiple_of((9 * plane // 2) * 128, 128)

    def proj_start(plane):
        return pl.multiple_of((3 * plane // 2) * 128, 128)

    def tile_copies(n):
        k = n.kind
        slot = n.order % 2
        wide = pl.ds(pl.multiple_of(n.plane * 2 * BLOCK, 128), 2 * BLOCK)
        cases = []
        for ref, number, here, source, target in (
            (m.hidden, 0, (k == 0) | (k == 2), wide, slice(0, 2 * BLOCK)),
            (m.active, 0, (k == 1) | (k == 3), wide, slice(0, 2 * BLOCK)),
            (m.mixed, 0, k == 4, pl.ds(mixed_start(n.plane), WINDOW), slice(0, WINDOW)),
            (m.proj, 1, k == 4, pl.ds(proj_start(n.plane), 256), slice(WINDOW, WINDOW + 256)),
        ):
            copy = pltpu.make_async_copy(
                ref.at[:, :TEXT, source], m.text_tile.at[slot, :, :, target], m.text_sem.at[slot, number]
            )
            cases.append((here & n.uses_text, copy))
            copy = pltpu.make_async_copy(
                ref.at[:, TEXT:, source], m.patch_tile.at[slot, :, :, target], m.patch_sem.at[slot, number]
            )
            cases.append((here & n.uses_patches, copy))
        return cases

    def join_columns(slot, begin):
        for tile, joint in ((m.text_tile, m.text_joint), (m.patch_tile, m.patch_joint)):
            for side in range(2):
                at, mixed, proj = side * BLOCK, begin + side * 288, WINDOW + begin + side * 96
                joint[:, :, at : at + 288] = tile[slot, :, :, mixed : mixed + 288]
                joint[:, :, at + 288 : at + BLOCK] = tile[slot, :, :, proj : proj + 96]

    def start_tile(n):
        for here, copy in tile_copies(n):
            pl.when(here)(copy.start)

    def wait_tile(n):
        for here, copy in tile_copies(n):
            pl.when(here)(copy.wait)

    def add_into(target, source):
        target[...] = target[...] + source[...]

    def rows_dot(left, tile, *columns):
        tile = jnp.concatenate([tile[:, :, at] for at in columns], axis=2)
        return matmul(left, tile.reshape(-1, tile.shape[2]))

    def text_dot(index, slot, *columns):
        return rows_dot(m.text_left[index], m.text_tile.at[slot], *columns)

    def patch_dot(index, slot, *columns):
        return rows_dot(m.patch_left[index], m.patch_tile.at[slot], *columns)

    def joint_dot(index, *columns):
        text = rows_dot(m.text_left[index], m.text_joint, *columns)
        return rows_dot(m.patch_left[index], m.patch_joint, *columns) + text

    def compute(n):
        k = n.kind
        slot = n.order % RING

        @pl.when(n.order >= RING)
        def _():
            core_copy(n.order - RING, 0).wait_send()
            core_copy(n.order - RING, 1).wait_send()
            pl.semaphore_wait(m.credit, 1)

        @pl.when(n.order + 1 < computed)
        def _():
            start_tile(Unit(following(n.u)))

        wait_tile(n)
        tile = n.order % 2
        everything = slice(0, 2 * BLOCK)

        def put(value, columns, begin):
            for half in range(2):
                for side in range(2):
                    piece = value[half * BLOCK : (half + 1) * BLOCK, columns[side]]
                    at = slice(begin, begin + piece.shape[1])
                    m.made[slot, half, jnp.where(y == side, 1, 0), :, at] = piece.astype(jnp.bfloat16)

        sides = (slice(0, BLOCK), slice(BLOCK, 2 * BLOCK))

        @pl.when((k < 4) & jnp.logical_not(n.uses_text))
        def _():
            put(patch_dot(k % 2, tile, everything), sides, 0)

        @pl.when((k < 4) & jnp.logical_not(n.uses_patches))
        def _():
            put(text_dot(k % 2, tile, everything), sides, 0)

        @pl.when((k < 4) & n.uses_text & n.uses_patches)
        def _():
            put(patch_dot(k % 2, tile, everything) + text_dot(k % 2, tile, everything), sides, 0)

        @pl.when(k == 4)
        def _():
            ends = (slice(256, BLOCK), slice(BLOCK + 256, 2 * BLOCK))
            for odd in range(2):
                pl.when(n.plane % 2 == odd)(functools.partial(join_columns, tile, 64 * odd))
            mixed = joint_dot(2, everything)
            proj = joint_dot(3, *ends)
            put(mixed, (slice(0, 256), slice(BLOCK, BLOCK + 256)), 0)
            lanes = lax.broadcasted_iota(jnp.int32, (1, 128), 1)
            last = [jnp.where(lanes < 32, mixed[:, ends[side]], proj[:, 128 * side : 128 * side + 128]) for side in range(2)]
            put(jnp.concatenate(last, axis=1), (slice(0, 128), slice(128, 256)), 256)

        core_copy(n.order, 0).start()
        core_copy(n.order, 1).start()

    def join_core(n):
        slot = n.order % RING

        @pl.when(n.handed_in)
        def _():
            over_copy(n, 0, n.u).wait_recv()

        @pl.when(jnp.logical_not(n.handed_in))
        def _():
            core_copy(n.order, 0).wait_recv()
            m.part[n.u, 0] = m.made[slot, core, 0] + m.xr[slot, 0]

        pl.when(n.y_first)(lambda: y_copy(n).start())

        @pl.when(jnp.logical_not(n.handed_in))
        def _():
            core_copy(n.order, 1).wait_recv()
            m.part[n.u, 1] = m.made[slot, core, 1] + m.xr[slot, 1]

            @pl.when(n.order + RING < computed)
            def _():
                pl.semaphore_signal(m.credit, inc=1, device_id=peer, device_id_type=MESH)

        pl.when(n.handed_on)(lambda: over_copy(n, n.u, over_target(n)).start())

    def join_y(n):
        y_copy(n).wait_recv()
        add_into(m.part.at[n.u, 1], m.yr.at[n.y_slot])

    def take(n, one, pair, single_from, pair_from):
        @pl.when(n.y_first)
        def _():
            one(n).wait_recv()
            add_into(m.part.at[n.u, 1], single_from.at[n.slot])

        @pl.when(n.z_first)
        def _():
            pair(n).wait_recv()
            add_into(m.part.at[n.u], pair_from.at[n.slot])

    def take_right(n):
        take(n, right_copy, right_pair, m.zr, m.wr)

    def take_left(n):
        take(n, left_copy, left_pair, m.zl, m.wl)

    def pass_right(n):
        pl.when(z > 0)(lambda: take_right(n))
        pl.when(n.y_first)(lambda: right_copy(n).start())
        pl.when(n.z_first)(lambda: right_pair(n).start())

    def pass_left(n):
        pl.when(z < 3)(lambda: take_left(n))
        pl.when(n.y_first)(lambda: left_copy(n).start())
        pl.when(n.z_first)(lambda: left_pair(n).start())

    def give(n, i):
        k = n.kind
        m.turned[k] = m.part[n.u, 1].T

        @pl.when(k < 4)
        def _():
            m.tables_out[table_of(k, section == 1), :, own_half()] = m.turned[k, mine(192), :]
            peer_copy(k).start()
            pl.when(on_first | (i > FIRST_MOVED))(lambda: start_cross(k))

        @pl.when(k == 4)
        def _():
            m.qkv_out[:, own_half()] = m.turned[4, mine(144), :]
            m.out_out[:, own_half()] = m.turned[4, pl.ds(pl.multiple_of(288 + core * 48, 16), 48), :]
            for copy in attention_copies():
                copy.start()

    def greet_first(u, carry):
        n = Unit(u)
        ended = jnp.where(n.z_first, MEET_LATE, MEET) + u <= FIRST_MOVED
        pl.when(ended & (n.kind < 4) & (n.plane == z))(lambda: start_cross(n.kind))
        return carry

    def meet(n, i):
        pl.when(z > 0)(lambda: take_right(n))
        pl.when(z < 3)(lambda: take_left(n))
        pl.when(n.z_first)(lambda: y_copy(n).start())
        pl.when(n.y_first)(lambda: give(n, i))

    def meet_late(n, i):
        join_y(n)
        give(n, i)

    flips = (peer, beside, (section, me + 4 - 8 * (z % 2)), (section, me + 8 - 16 * (z // 2)), across)

    def small_copy(j):
        return remote(m.small_sum.at[j], m.small_in.at[j], m.small_send.at[j], m.small_recv.at[j], flips[j])

    def small_step(j):
        if j == 0:
            m.small_sum[0] = m.small[...]
        else:
            small_copy(j - 1).wait_recv()
            if j == 5:
                m.small_out[0] = m.small_sum[4]
                m.small_out[1] = m.small_in[4]
            else:
                m.small_sum[j] = m.small_sum[j - 1] + m.small_in[j - 1]
        if j < 5:
            small_copy(j).start()

    lefts = (m.n2, m.branch, m.n1, m.att)
    turns = [[], []]
    for side in range(2):
        for kind, plane, z_first in UNITS[side]:
            for index in () if side == 1 and (kind, plane) in MOVED else LEFT_OF[kind]:
                if index not in turns[side]:
                    turns[side].append(index)

    def stage_copy(index):
        return pltpu.make_async_copy(lefts[index], m.stage, m.stage_sem.at[0])

    def start_stage(turn):
        for side in range(2):
            pl.when(section == side)(stage_copy(turns[side][turn]).start)

    def prepare(turn):
        stage_copy(0).wait()
        number = jnp.where(on_first, turns[0][turn], turns[1][turn])

        def part(c, carry):
            at = pl.ds(pl.multiple_of(c * 128, 128), 128)
            m.text_left[number, at, :] = m.stage[:, :TEXT, at].reshape(-1, 128).T
            m.patch_left[number, at, :] = m.stage[:, TEXT:, at].reshape(-1, 128).T
            return carry

        lax.fori_loop(0, m.stage.shape[2] // 128, part, 0)
        if turn < 3:
            start_stage(turn + 1)

    barrier = pltpu.get_barrier_semaphore()
    for device in (peer, beside, flips[3]):
        pl.semaphore_signal(barrier, inc=1, device_id=device, device_id_type=MESH)

    @pl.when(section == 1)
    def _():
        for device in (across, aslant):
            pl.semaphore_signal(barrier, inc=1, device_id=device, device_id_type=MESH)

    @pl.when(z < 3)
    def _():
        pl.semaphore_signal(barrier, inc=1, device_id=right, device_id_type=MESH)

    @pl.when(z > 0)
    def _():
        pl.semaphore_signal(barrier, inc=1, device_id=left, device_id_type=MESH)

    start_stage(0)
    start_tile(Unit(jnp.int32(0)))
    prepare(0)
    pl.semaphore_wait(barrier, 3 + jnp.where(on_first, 2, 0) + jnp.where(z < 3, 1, 0) + jnp.where(z > 0, 1, 0))

    @pl.when(on_first)
    def _():
        for device in (across, aslant):
            pl.semaphore_signal(m.ready, inc=1, device_id=device, device_id_type=MESH)
        half_copy().start()


    def at_unit(u, condition, action, *more):
        n = Unit(jnp.maximum(u, 0))

        @pl.when((u >= 0) & (u < units) & condition(n))
        def _():
            action(n, *more)

    def in_flow(n):
        return jnp.logical_not(n.handed_on)

    def step(i, carry):
        @pl.when((i == FIRST_MOVED + 1) & (section == 1))
        def _():
            pl.semaphore_wait(m.ready, 2)
            lax.fori_loop(0, units, greet_first, 0)

        at_unit(i, lambda n: jnp.logical_not(n.handed_in), compute)
        for number in range(3):
            pl.when(i == number)(functools.partial(prepare, number + 1))
        at_unit(i - 1, lambda n: n.kind >= 0, join_core)
        at_unit(i - WAIT, lambda n: n.y_first, join_y)
        at_unit(i - WAIT - HOP * z, lambda n: in_flow(n) & (n.plane > z), pass_right)
        at_unit(i - WAIT - HOP * (3 - z), lambda n: in_flow(n) & (n.plane < z), pass_left)
        at_unit(i - MEET, lambda n: in_flow(n) & (n.plane == z), meet, i)
        at_unit(i - MEET_LATE, lambda n: n.z_first & (n.plane == z), meet_late, i)
        for j in range(4):
            pl.when(i == 3 + j)(functools.partial(small_step, j))
        return carry

    lax.fori_loop(0, units + MEET_LATE, step, 0)
    small_step(4)

    def ours(k):
        return True if k in (0, 1, 4) else is_moved(k, z) == (section == 1)

    def when_ours(k, wanted, action):
        pl.when(jnp.logical_not(ours(k) ^ wanted) if k in (2, 3) else True)(action)

    small_step(5)

    def settle(u, carry):
        n = Unit(u)

        @pl.when(jnp.logical_not(n.handed_in) & (n.order >= computed - RING))
        def _():
            core_copy(n.order, 0).wait_send()
            core_copy(n.order, 1).wait_send()

        pl.when(n.handed_on)(lambda: over_copy(n, n.u, over_target(n)).wait_send())
        pl.when(n.y_first | (n.z_first & (n.plane == z)))(lambda: y_copy(n).wait_send())
        pl.when(n.y_first & (n.plane > z))(lambda: right_copy(n).wait_send())
        pl.when(n.z_first & (n.plane > z))(lambda: right_pair(n).wait_send())
        pl.when(n.y_first & (n.plane < z))(lambda: left_copy(n).wait_send())
        pl.when(n.z_first & (n.plane < z))(lambda: left_pair(n).wait_send())
        return carry

    lax.fori_loop(0, units, settle, 0)
    for j in range(5):
        small_copy(j).wait_send()
    for k in range(4):

        def arrived(k=k):
            for other_core in (False, True):
                cross_copy(k, section == 0, other_core).wait_recv()

        def sent(k=k):
            peer_copy(k).wait()
            for other_core in (False, True):
                cross_copy(k, section == 1, other_core).wait_send()

        when_ours(k, True, sent)
        when_ours(k, False, arrived)
    for copy in attention_copies():
        copy.wait()

    @pl.when(on_first)
    def _():
        half_copy().wait_send()

    @pl.when(section == 1)
    def _():
        half_copy().wait_recv()

def summed_grads(n1, att, n2, branch, hidden, active, mixed, proj, half, small):
    dma = pltpu.SemaphoreType.DMA
    items, depth, width = n1.shape
    bf16, f32 = jnp.bfloat16, jnp.float32
    tile = (BLOCK, BLOCK)
    vmem, anywhere = pl.BlockSpec(memory_space=pltpu.VMEM), pl.BlockSpec(memory_space=pl.ANY)
    ins = dict(n1=n1, att=att, n2=n2, branch=branch, hidden=hidden, active=active, mixed=mixed, proj=proj, half=half,
        small=small)
    outs = dict(
        tables_out=((6, 192, width), bf16), qkv_out=((144, width), bf16),
        out_out=((48, width), bf16), small_out=((2,) + small.shape, f32), half_out=(half.shape, bf16),
    )
    buffers = dict(
        text_tile=((2, items, TEXT, WINDOW + 256), bf16),
        patch_tile=((2, items, depth - TEXT, WINDOW + 256), bf16), text_joint=((items, TEXT, 2 * BLOCK), bf16),
        patch_joint=((items, depth - TEXT, 2 * BLOCK), bf16), part=((20, 2) + tile, bf16), made=((RING, 2, 2) + tile, bf16),
        xr=((RING, 2) + tile, bf16), yr=((Y_UNITS + Z_UNITS,) + tile, bf16), zr=((Y_UNITS,) + tile, bf16), zl=((Y_UNITS,) + tile, bf16),
        wr=((Z_UNITS, 2) + tile, bf16), wl=((Z_UNITS, 2) + tile, bf16), turned=((5,) + tile, bf16),
        text_left=((4, width, items * TEXT), bf16), patch_left=((4, width, items * (depth - TEXT)), bf16), stage=((items, depth, width), bf16), small_sum=((5,) + small.shape, f32),
        small_in=((5,) + small.shape, f32),
    )
    semaphores = dict(
        small_send=dma((5,)), small_recv=dma((5,)), text_sem=dma((2, 2)), patch_sem=dma((2, 2)), stage_sem=dma((1,)), core_send=dma((20, 2)),
        core_recv=dma((20, 2)), y_send=dma((Y_UNITS + Z_UNITS,)), y_recv=dma((Y_UNITS + Z_UNITS,)), right_send=dma((Y_UNITS + Z_UNITS,)), right_recv=dma((Y_UNITS + Z_UNITS,)),
        left_send=dma((Y_UNITS + Z_UNITS,)), left_recv=dma((Y_UNITS + Z_UNITS,)), over_send=dma((8,)), over_recv=dma((8,)), half_send=dma((1,)), half_recv=dma((1,)), peer_send=dma((6,)),
        peer_recv=dma((6,)), cross_send=dma((2, 4)), cross_recv=dma((2, 4)),
        credit=pltpu.SemaphoreType.REGULAR, ready=pltpu.SemaphoreType.REGULAR,
    )
    names = list(ins) + list(outs) + list(buffers) + list(semaphores)
    return pl.pallas_call(
        functools.partial(sum_kernel, names),
        out_shape=[jax.ShapeDtypeStruct(*kind) for kind in outs.values()],
        in_specs=[anywhere] * 9 + [vmem],
        out_specs=[vmem] * (len(outs) - 1) + [anywhere],
        scratch_shapes=[pltpu.VMEM(*kind) for kind in buffers.values()] + list(semaphores.values()),
        compiler_params=pltpu.CompilerParams(
            collective_id=0, has_side_effects=True, vmem_limit_bytes=60 * 1024 * 1024
        ),
        cost_estimate=pl.CostEstimate(flops=48 * 2 * 768 * 384 * items * depth, bytes_accessed=40_000_000, transcendentals=0),
    )(*ins.values())


def finish_kernel(count, *refs):
    sources, targets = refs[:count], refs[count : count + 11]
    held, made, (load_sem, store_sem) = refs[count + 11 : -7], refs[-7:-2], refs[-2:]
    loads = [pltpu.make_async_copy(*pair, load_sem.at[n]) for n, pair in enumerate(zip(sources, held))]
    stores = [pltpu.make_async_copy(*pair, store_sem.at[n]) for n, pair in enumerate(zip(made, targets[:5]))]
    for load in loads:
        load.start()
    tables, qkv, out, small, half, grad = held
    small_outs = targets[5:]
    loads[0].wait()
    for number, source in enumerate((tables.at[:3], tables.at[3:], qkv, out)):
        if number > 1:
            loads[number - 1].wait()
        made[number][...] = source[...].astype(jnp.float32)
        stores[number].start()
    for load in loads[3:]:
        load.wait()
    section, me = lax.axis_index("section"), lax.axis_index("dp")
    width, wide = tables.shape[2], tables.shape[2] // 16
    ff = width * 4

    def columns(row, size):
        return pltpu.roll(row, (row.shape[1] - size * me) % row.shape[1], 1)[:, :size]

    def up_bias(side, slot):
        return columns(jnp.concatenate([small[side, 9 + 3 * slot + j : 10 + 3 * slot + j] for j in range(3)], axis=1), ff // 16)

    own = columns(small[0, :9, :width], wide)
    other = columns(small[1, :9, :width], wide)
    qv_out, proj_out, gain_out, shift_out, up_bias_out, down_bias_out = small_outs
    qv_out[...] = own[2:4]
    proj_out[...] = own[4:5]
    gain_out[...] = own[5:7]
    shift_out[...] = own[7:9]
    for side in range(2):
        mine, theirs = (own, other) if side == 0 else (other, own)

        @pl.when(section == side)
        def _():
            for i in range(grad.shape[0]):
                place(made[4], i, grad[i] if side == 0 else half[i].astype(jnp.float32))
            stores[4].start()
            down_bias_out[0:2] = mine[0:2]
            down_bias_out[2:3] = theirs[0:1]
            up_bias_out[0:1] = up_bias(side, 0)
            up_bias_out[1:2] = up_bias(side, 1)
            up_bias_out[2:3] = up_bias(1 - side, 0)

    for store in stores:
        store.wait()


def place(target, i, value):
    target[i, :PATCHES] = value[TEXT : target.shape[1]]
    target[i, PATCHES:] = value[:TEXT]


def finished(length, *sources):
    tables, qkv, out, small, half, grad = sources
    width = tables.shape[2]
    shapes = [(3,) + tables.shape[1:]] * 2 + [qkv.shape, out.shape, (grad.shape[0], length, grad.shape[2])]
    shapes += [(rows, width // 16) for rows in (2, 1, 2, 2)] + [(3, width // 4), (3, width // 16)]
    return pl.pallas_call(
        functools.partial(finish_kernel, len(sources)),
        out_shape=[jax.ShapeDtypeStruct(shape, jnp.float32) for shape in shapes],
        in_specs=[pl.BlockSpec(memory_space=pltpu.HBM)] * len(sources),
        out_specs=[pl.BlockSpec(memory_space=pl.ANY)] * 5 + [pl.BlockSpec(memory_space=pltpu.VMEM)] * 6,
        scratch_shapes=[pltpu.VMEM(value.shape, value.dtype) for value in sources]
        + [pltpu.VMEM(shape, jnp.float32) for shape in shapes[:5]]
        + [pltpu.SemaphoreType.DMA((len(sources),)), pltpu.SemaphoreType.DMA((5,))],
        compiler_params=pltpu.CompilerParams(vmem_limit_bytes=60 * 1024 * 1024),
    )(*sources)


CHUNK = 1024
PIECE = 768
KEY_SPLIT = 256
TAIL = (0.319381530, -0.356563782, 1.781477937, -1.821255978, 1.330274429)
LOG2_E = 1.4426950408889634
LOG2_PEAK = -1.3257480647361593


def normal_parts(z):
    size = jnp.abs(z)
    scale = 1.0 + 0.2316419 * size
    t = pl.reciprocal(scale, approx=True)
    t = t * (2.0 - scale * t)
    bell = jnp.exp2(z * z * (-0.5 * LOG2_E) + LOG2_PEAK)
    series = TAIL[4]
    for factor in TAIL[3::-1]:
        series = series * t + factor
    upper = bell * (series * t)
    return jnp.where(z >= 0, 1.0 - upper, upper), bell


def matmul(left, right):
    return jnp.dot(left, right, preferred_element_type=jnp.float32)


def matmul_turned(left, right):
    return lax.dot_general(left, right, (((1,), (1,)), ((), ())), preferred_element_type=jnp.float32)


def standardized(values):
    centre = values - jnp.mean(values, -1, keepdims=True)
    inverse = lax.rsqrt(jnp.mean(centre * centre, -1, keepdims=True) + EPSILON)
    return centre * inverse, inverse


def norm_step_back(delta, standard, inverse, gain_row):
    scaled = delta * gain_row
    moved = inverse * (
        scaled - jnp.mean(scaled, -1, keepdims=True) - standard * jnp.mean(scaled * standard, -1, keepdims=True)
    )
    return moved, jnp.sum(delta * standard, 0, keepdims=True), jnp.sum(delta, 0, keepdims=True)


def half_mask(half):
    lanes = lax.broadcasted_iota(jnp.int32, (1, 128), 1)
    return (lanes < 64) if half == 0 else (lanes >= 64)


def pair_columns(p, part, width):
    return slice(part * width + p * 128, part * width + p * 128 + 128)


def both_halves(pair):
    return jnp.concatenate([jnp.where(half_mask(half), pair, jnp.zeros_like(pair)) for half in range(2)], axis=0)


def in_turn(count, *stages):
    for turn in range(count + len(stages) - 1):
        for number, stage in enumerate(stages):
            if 0 <= turn - number < count:
                stage(turn - number)


def attention_forward(m, length, beside):
    rows, width = m.att.shape

    def scores(p):
        q2 = m.qkv[:, pair_columns(p, 0, width)]
        k2 = m.qkv[:, pair_columns(p, 1, width)]
        m.scores[p % 2] = matmul_turned(both_halves(k2), q2).reshape(2, rows, rows)

    def soften(p):
        for half in range(2):
            top = m.scores[p % 2, half, :KEY_SPLIT]
            low = m.scores[p % 2, half, KEY_SPLIT:]
            key_row = KEY_SPLIT + lax.broadcasted_iota(jnp.int32, low.shape, 0)
            low = jnp.where(key_row < length, low, -1e30)
            peak = jnp.maximum(jnp.max(top, 0, keepdims=True), jnp.max(low, 0, keepdims=True))
            top = jnp.exp(top - peak)
            low = jnp.exp(low - peak)
            over = 1.0 / (jnp.sum(top, 0, keepdims=True) + jnp.sum(low, 0, keepdims=True))
            m.probs[2 * p + half, :KEY_SPLIT] = (top * over).astype(jnp.bfloat16)
            m.probs[2 * p + half, KEY_SPLIT:] = (low * over).astype(jnp.bfloat16)

    def blend(p):
        v_turned = m.qkv[:, pair_columns(p, 2, width)].T
        parts = [matmul(v_turned[64 * half : 64 * half + 64], m.probs[2 * p + half]) for half in range(2)]
        turned = jnp.concatenate(parts, axis=0)
        m.att_turned[p * 128 : p * 128 + 128, :] = turned.astype(jnp.bfloat16)
        m.att[:, p * 128 : p * 128 + 128] = turned.T.astype(jnp.bfloat16)

    in_turn(width // 128, scores, soften, blend, *beside)


def attention_back(m):
    rows, width = m.att.shape

    def probs_back(p):
        v2 = m.qkv[:, pair_columns(p, 2, width)]
        d_turned = m.att_delta[:, pair_columns(p, 0, width)].T
        m.scores[p % 2] = matmul(both_halves(v2), d_turned).reshape(2, rows, rows)
        product = d_turned.astype(jnp.float32) * m.att_turned[p * 128 : p * 128 + 128, :].astype(jnp.float32)
        for half in range(2):
            m.inner[p % 2, half] = jnp.sum(product[64 * half : 64 * half + 64], 0, keepdims=True)

    def scores_back(p):
        for half in range(2):
            probs = m.probs[2 * p + half].astype(jnp.float32)
            m.score_delta[p % 2, half] = (probs * (m.scores[p % 2, half] - m.inner[p % 2, half])).astype(jnp.bfloat16)

    def heads_back(p):
        q_at, k_at, v_at = (pair_columns(p, part, width) for part in range(3))
        score = m.score_delta[p % 2]
        probs = m.probs[2 * p : 2 * p + 2].reshape(2 * rows, rows)
        k_turned = m.qkv[:, k_at].T
        value = matmul(probs, m.att_delta[:, q_at])
        key = matmul(score.reshape(2 * rows, rows), m.qkv[:, q_at])
        query = jnp.concatenate(
            [matmul(k_turned[64 * half : 64 * half + 64], score[half]) for half in range(2)], axis=0
        )
        dq = (query.T * HEAD_DIM ** (-0.5)).astype(jnp.bfloat16)
        dk = jnp.where(half_mask(0), key[:rows], key[rows:]).astype(jnp.bfloat16)
        dv = jnp.where(half_mask(0), value[:rows], value[rows:]).astype(jnp.bfloat16)
        m.mixed[:, q_at] = dq
        m.mixed[:, k_at] = dk
        m.mixed[:, v_at] = dv
        m.sums[2:3, q_at] += jnp.sum(dq.astype(jnp.float32), 0, keepdims=True)
        m.sums[3:4, q_at] += jnp.sum(dv.astype(jnp.float32), 0, keepdims=True)

    in_turn(width // 128, probs_back, scores_back, heads_back)


def forward_front(m, x_ref, length, hold, *beside):
    x = x_ref[...].astype(jnp.float32)
    standard, inverse = standardized(x)
    if hold:
        m.standard[...] = standard
        m.inverse[0] = inverse
    m.n1[...] = (standard * m.gain[0:1] + m.shift[0:1]).astype(jnp.bfloat16)
    width = x.shape[1]
    m.need(m.qkv_w)

    def part_columns(part):
        return slice(part * width, (part + 1) * width)

    def mix(part):
        m.hidden[part % 2] = matmul(m.n1[...], m.qkv_w[:, part_columns(part)])

    def split(part):
        value = m.hidden[part % 2]
        if part == 0:
            value = (value + m.qv[0:1]).astype(jnp.bfloat16) * jnp.bfloat16(HEAD_DIM ** (-0.5))
        elif part == 2:
            value = value + m.qv[1:2]
        m.qkv[:, part_columns(part)] = value.astype(jnp.bfloat16)

    in_turn(3, mix, split)
    attention_forward(m, length, beside)
    m.need(m.out_w)
    middle = x_ref[...].astype(jnp.float32) + matmul(m.att[...], m.out_w[...]) + m.proj[0:1]
    standard, inverse = standardized(middle)
    m.middle[...] = standard if hold else middle
    if hold:
        m.inverse[1] = inverse
    m.n2[...] = (standard * m.gain[1:2] + m.shift[1:2]).astype(jnp.bfloat16)


def back_tail(m, x_ref, g_ref, n2_delta, keep, held):
    standard, inverse = (m.middle[...], m.inverse[1]) if held else standardized(m.middle[...])
    middle_part, gain, shift = norm_step_back(n2_delta, standard, inverse, m.gain[1:2])
    m.sums[6:7, :gain.shape[1]] += gain
    m.sums[8:9, :gain.shape[1]] += shift
    middle_delta = g_ref[...].astype(jnp.float32) + middle_part
    proj_delta = middle_delta.astype(jnp.bfloat16)
    m.sums[4:5, :gain.shape[1]] += jnp.sum(proj_delta.astype(jnp.float32), 0, keepdims=True)
    m.proj_delta[...] = proj_delta
    m.middle_delta[...] = middle_delta
    m.att_delta[...] = matmul_turned(proj_delta, m.out_w[...]).astype(jnp.bfloat16)
    attention_back(m)
    total = matmul_turned(m.mixed[...], m.qkv_w[...])
    standard, inverse = (m.standard[...], m.inverse[0]) if held else standardized(x_ref[...].astype(jnp.float32))
    input_part, gain, shift = norm_step_back(total, standard, inverse, m.gain[0:1])
    m.sums[5:6, :gain.shape[1]] += gain
    m.sums[7:8, :gain.shape[1]] += shift
    keep(m.middle_delta[...] + input_part)


def forward_expert(m, slot, begin, end):
    def columns(j):
        return slice(j * PIECE, (j + 1) * PIECE)

    def widen(j):
        hidden = matmul(m.n2[begin:end], m.up_w[slot, :, columns(j)])
        m.hidden[j % 2, begin:end] = hidden + m.up_b[slot : slot + 1, columns(j)]

    def bend(j):
        hidden = m.hidden[j % 2, begin:end]
        below, bell = normal_parts(hidden)
        m.active[begin:end, columns(j)] = (hidden * below).astype(jnp.bfloat16)
        m.slope[begin:end, columns(j)] = (below + hidden * bell).astype(jnp.bfloat16)

    def narrow(j):
        piece = matmul(m.active[begin:end, columns(j)], m.down_w[slot, columns(j), :])
        m.total[begin:end] = piece + (m.middle[begin:end] + m.down_b[slot : slot + 1] if j == 0 else m.total[begin:end])

    in_turn(m.up_w.shape[2] // PIECE, widen, bend, narrow)


def add_up_sums(m, slot, begin, end):
    for j in range(m.up_w.shape[2] // CHUNK):
        piece = m.hidden_delta[begin:end, j * CHUNK : (j + 1) * CHUNK].astype(jnp.float32)
        m.sums[9 + 3 * slot + j : 10 + 3 * slot + j] += jnp.sum(piece, 0, keepdims=True)


def back_expert(m, g_ref, slot, begin, end):
    m.sums[slot : slot + 1, : g_ref.shape[1]] += jnp.sum(g_ref[begin:end].astype(jnp.float32), 0, keepdims=True)

    def columns(j):
        return slice(j * PIECE, (j + 1) * PIECE)

    def widen(j):
        m.hidden[j % 2, begin:end] = matmul_turned(g_ref[begin:end], m.down_w[slot, columns(j), :])

    def bend(j):
        slope = m.slope[begin:end, columns(j)].astype(jnp.float32)
        m.hidden_delta[begin:end, columns(j)] = (m.hidden[j % 2, begin:end] * slope).astype(jnp.bfloat16)

    def narrow(j):
        piece = matmul_turned(m.hidden_delta[begin:end, columns(j)], m.up_w[slot, :, columns(j)])
        m.total[begin:end] = piece if j == 0 else m.total[begin:end] + piece

    in_turn(m.up_w.shape[2] // PIECE, widen, bend, narrow)
    add_up_sums(m, slot, begin, end)


def early_delta(m, g_ref, pieces):
    size = m.active_delta.shape[1] // pieces

    def stage(p):
        columns = slice(p * size, (p + 1) * size)
        m.active_delta[:, columns] = matmul_turned(g_ref[...], m.down_w[0, columns, :])

    return stage


def both_expert(m):
    def columns(j):
        return slice(j * PIECE, (j + 1) * PIECE)

    def widen(j):
        m.hidden[j % 2] = matmul(m.n2[...], m.up_w[0, :, columns(j)]) + m.up_b[2:3, columns(j)]

    def bend(j):
        hidden = m.hidden[j % 2]
        below, bell = normal_parts(hidden)
        m.active[:, columns(j)] = (hidden * below).astype(jnp.bfloat16)
        slope = below + hidden * bell
        m.hidden_delta[:, columns(j)] = (m.active_delta[:, columns(j)] * slope).astype(jnp.bfloat16)

    def narrow(j):
        piece = matmul_turned(m.hidden_delta[:, columns(j)], m.up_w[0, :, columns(j)])
        m.total[...] = piece if j == 0 else m.total[...] + piece

    in_turn(m.up_w.shape[2] // PIECE, widen, bend, narrow)
    add_up_sums(m, 0, 0, ROWS)


def layers_kernel(names, *refs):
    m = Refs()
    for name, ref in zip(names, refs):
        setattr(m, name, ref)
    items, length = m.in_tokens.shape[:2]
    half = m.total.shape[1] // 2
    section = lax.axis_index("section")
    across = (1 - section, lax.axis_index("dp"))

    def send(i, part):
        rows = (slice(0, TEXT), slice(TEXT, ROWS))[part]
        return pltpu.make_async_remote_copy(
            src_ref=m.leaving.at[i, rows], dst_ref=m.landed.at[i, rows], send_sem=m.send_sem.at[i, part],
            recv_sem=m.recv_sem.at[i, part], device_id=across, device_id_type=MESH,
        )

    def side_copies(i):
        return (
            pltpu.make_async_copy(m.low.at[i], m.out_low.at[i], m.side_sem.at[0, i]),
            pltpu.make_async_copy(m.high.at[i], m.out_high.at[i], m.side_sem.at[1, i]),
        )

    def local(source, target, number):
        return pltpu.make_async_copy(source, target, m.copy_sem.at[number])

    def branch_copy(source, i):
        return pltpu.make_async_copy(source.at[i], m.branch.at[i], m.branch_sem.at[i])

    def weights(experts):
        found = [
            (m.qkv_w, [local(m.in_qkv.at[0], m.qkv_w, 0)]),
            (m.out_w, [local(m.in_out.at[0], m.out_w, 1)]),
            (m.up_w, []),
            (m.down_w, []),
        ]
        for slot, expert in enumerate(experts):
            found[2][1].append(local(m.in_up.at[expert], m.up_w.at[slot], 2 + slot))
            found[3][1].append(local(m.in_down.at[expert], m.down_w.at[slot], 4 + slot))
        return found

    def start_weights(found):
        copies = found[0][1] + found[1][1]
        for pair in zip(found[2][1], found[3][1]):
            copies += pair
        for copy in copies:
            copy.start()

    def needs(found, i):
        def need(ref, slot=0):
            for here, copies in found:
                if here is ref:
                    pl.when(i == 0)(copies[slot].wait)

        return need

    leaving = (
        (m.n1, m.out_n1), (m.att, m.out_att), (m.n2, m.out_n2), (m.active, m.out_active), (m.qkv, m.kept_qkv),
        (m.probs, m.kept_probs), (m.att_turned, m.kept_turned), (m.middle, m.kept_middle), (m.slope, m.kept_slope),
        (m.mixed, m.out_mixed), (m.proj_delta, m.out_proj), (m.hidden_delta, m.out_hidden),
    )
    n1, att, n2, active, qkv, probs, turned, middle, slope, mixed, proj, hidden = range(len(leaving))

    def puts(i):
        return lambda number: local(leaving[number][0], leaving[number][1].at[i], 6 + number)

    def gets(i):
        return lambda number: local(leaving[number][1].at[i], leaving[number][0], 14 + number)

    def start(copies, *which):
        for number in which:
            copies(number).start()

    def wait(copies, *which):
        for number in which:
            copies(number).wait()

    def settle(i, *which):
        @pl.when(i > 0)
        def _():
            wait(puts(i), *which)

    def text_first(target, source, i):
        value = source[i].astype(jnp.float32)
        pad = jnp.zeros((ROWS - length, value.shape[1]), jnp.float32)
        target[i, :TEXT] = value[PATCHES:].astype(jnp.bfloat16)
        target[i, TEXT:] = jnp.concatenate([value[:PATCHES], pad], axis=0).astype(jnp.bfloat16)

    def mask_targets(i):
        row = lax.broadcasted_iota(jnp.int32, (ROWS, 1), 0)
        position = jnp.where(row < TEXT, row + PATCHES, jnp.where(row < length, row - TEXT, length))
        chosen = jnp.zeros((ROWS, 1), jnp.float32)
        for mask in (m.patch_mask, m.text_mask):
            same = jnp.where(position == mask[i : i + 1, :], 1.0, 0.0)
            chosen = jnp.maximum(chosen, jnp.max(same, 1, keepdims=True))
        target = m.targets[i].astype(jnp.float32) * chosen
        m.targets[i] = target.astype(jnp.bfloat16)
        m.sums[0:1, : target.shape[1]] += jnp.sum(target, 0, keepdims=True)

    def first_front(found, i, carry):
        m.need = needs(found, i)
        text_first(m.tokens, m.in_tokens, i)
        settle(i, n1, att, n2, qkv, probs, turned, middle)
        forward_front(m, m.tokens.at[i], length, False)
        start(puts(i), n1, att, n2, qkv, probs, turned, middle)
        settle(i, active, slope)
        m.need(m.up_w)
        m.need(m.down_w)
        forward_expert(m, 0, TEXT, ROWS)
        m.leaving[i, TEXT:] = m.total[TEXT:].astype(jnp.bfloat16)
        send(i, 1).start()
        m.need(m.up_w, 1)
        m.need(m.down_w, 1)
        forward_expert(m, 1, 0, TEXT)
        m.leaving[i, :TEXT] = m.total[:TEXT].astype(jnp.bfloat16)
        send(i, 0).start()
        start(puts(i), active, slope)
        return carry

    def first_back(i, carry):
        start(gets(i), slope, middle, turned, qkv, probs)

        @pl.when(i > 0)
        def _():
            send(i - 1, 0).wait_send()
            send(i - 1, 1).wait_send()

        settle(i, hidden)
        wait(gets(i), slope)
        gradient = m.landed.at[i]
        send(i, 0).wait_recv()
        back_expert(m, gradient, 1, 0, TEXT)
        send(i, 1).wait_recv()
        branch_copy(m.landed, i).start()
        back_expert(m, gradient, 0, TEXT, ROWS)
        start(puts(i), hidden)
        wait(gets(i), middle, turned, qkv, probs)
        settle(i, mixed, proj)

        def keep(value):
            m.low[i] = value[:, :half]
            m.high[i] = value[:, half:].astype(jnp.bfloat16)

        back_tail(m, m.tokens.at[i], gradient, m.total[...], keep, False)
        for copy in side_copies(i):
            copy.start()
        start(puts(i), mixed, proj)
        branch_copy(m.landed, i).wait()
        return carry

    def second_both(found, i, carry):
        m.need = needs(found, i)
        branch_copy(m.targets, i).start()
        send(i, 0).wait_recv()
        send(i, 1).wait_recv()
        settle(i, n1, att, n2)
        arrived = m.landed.at[i]
        gradient = m.targets.at[i]
        m.need(m.down_w)
        forward_front(m, arrived, length, True, early_delta(m, gradient, m.att.shape[1] // 128))
        start(puts(i), n1, att, n2)
        settle(i, active, hidden)
        m.need(m.up_w)
        both_expert(m)
        start(puts(i), active, hidden)
        settle(i, mixed, proj)

        def keep(value):
            m.leaving[i] = value.astype(jnp.bfloat16)

        back_tail(m, arrived, gradient, m.total[...], keep, True)
        send(i, 0).start()
        send(i, 1).start()
        start(puts(i), mixed, proj)
        branch_copy(m.targets, i).wait()
        return carry

    m.sums[...] = jnp.zeros(m.sums.shape, jnp.float32)
    barrier = pltpu.get_barrier_semaphore()
    pl.semaphore_signal(barrier, inc=1, device_id=across, device_id_type=MESH)

    @pl.when(section == 0)
    def _():
        found = weights((0, 1))
        start_weights(found)
        pl.semaphore_wait(barrier, 1)
        lax.fori_loop(0, items, functools.partial(first_front, found), 0)
        wait(puts(0), n1, att, n2, active, qkv, probs, turned, middle, slope)
        lax.fori_loop(0, items, first_back, 0)
        wait(puts(0), mixed, proj, hidden)
        send(items - 1, 0).wait_send()
        send(items - 1, 1).wait_send()
        for i in range(items):
            for copy in side_copies(i):
                copy.wait()

    @pl.when(section == 1)
    def _():
        found = weights((2,))
        start_weights(found)
        for i in range(items):
            text_first(m.targets, m.cotangent, i)
            mask_targets(i)
        pl.semaphore_wait(barrier, 1)
        lax.fori_loop(0, items, functools.partial(second_both, found), 0)
        wait(puts(0), n1, att, n2, active, mixed, proj, hidden)
        for i in range(items):
            send(i, 0).wait_send()
            send(i, 1).wait_send()


def both_layers(
    tokens, cotangent, patch_mask, text_mask, qkv_weight, out_weight, up_table, down_table, qv, proj, gain, shift, up_b, down_b
):
    items, length, width = tokens.shape
    rows = ROWS
    ff = up_b.shape[1]
    heads = width // HEAD_DIM
    bf16, f32 = jnp.bfloat16, jnp.float32
    dma = pltpu.SemaphoreType.DMA
    vmem, anywhere = pl.BlockSpec(memory_space=pltpu.VMEM), pl.BlockSpec(memory_space=pl.ANY)
    ins = dict(
        in_tokens=(tokens, vmem), cotangent=(cotangent, vmem), patch_mask=(patch_mask, vmem), text_mask=(text_mask, vmem), in_qkv=(qkv_weight, anywhere), in_out=(out_weight, anywhere),
        in_up=(up_table, anywhere), in_down=(down_table, anywhere), qv=(qv, vmem), proj=(proj, vmem), gain=(gain, vmem),
        shift=(shift, vmem), up_b=(up_b, vmem), down_b=(down_b, vmem),
    )

    def made(*shape, kind=bf16, spec=anywhere):
        return jax.ShapeDtypeStruct((items,) + shape, kind), spec

    outs = dict(
        out_n1=made(rows, width), out_att=made(rows, width), out_n2=made(rows, width), out_active=made(rows, ff),
        out_mixed=made(rows, 3 * width), out_proj=made(rows, width), out_hidden=made(rows, ff), branch=made(rows, width),
        kept_qkv=made(rows, 3 * width), kept_probs=made(heads, rows, rows), kept_turned=made(width, rows),
        kept_middle=made(rows, width, kind=f32), kept_slope=made(rows, ff),
        out_low=made(rows, width // 2, kind=f32), out_high=made(rows, width // 2),
        sums=(jax.ShapeDtypeStruct((16, CHUNK), f32), vmem),
    )
    low_row, wide_row = ((rows, width), bf16), ((rows, ff), bf16)
    buffers = dict(
        qkv_w=((width, 3 * width), bf16), out_w=((width, width), bf16), up_w=((2, width, ff), bf16),
        down_w=((2, ff, width), bf16), n1=low_row, att=low_row, n2=low_row, active=wide_row,
        qkv=((rows, 3 * width), bf16), probs=((heads, rows, rows), bf16), att_turned=((width, rows), bf16),
        middle=((rows, width), f32), slope=wide_row, total=((rows, width), f32), mixed=((rows, 3 * width), bf16),
        standard=((rows, width), f32), inverse=((2, rows, 1), f32), proj_delta=low_row, scores=((2, 2, rows, rows), f32),
        score_delta=((2, 2, rows, rows), bf16), inner=((2, 2, 1, rows), f32), hidden=((2, rows, PIECE), f32),
        active_delta=((rows, ff), f32), hidden_delta=wide_row, att_delta=low_row, middle_delta=((rows, width), f32),
        leaving=((items, rows, width), bf16), landed=((items, rows, width), bf16),
        low=((items, rows, width // 2), f32), high=((items, rows, width // 2), bf16),
        tokens=((items, rows, width), bf16), targets=((items, rows, width), bf16),
    )
    semaphores = dict(
        copy_sem=dma((23,)), branch_sem=dma((items,)), side_sem=dma((2, items)), send_sem=dma((items, 2)), recv_sem=dma((items, 2)),
    )
    names = list(ins) + list(outs) + list(buffers) + list(semaphores)
    results = pl.pallas_call(
        functools.partial(layers_kernel, names),
        out_shape=[shape for shape, spec in outs.values()],
        in_specs=[spec for value, spec in ins.values()],
        out_specs=[spec for shape, spec in outs.values()],
        scratch_shapes=[pltpu.VMEM(*kind) for kind in buffers.values()] + list(semaphores.values()),
        compiler_params=pltpu.CompilerParams(
            collective_id=1, has_side_effects=True, vmem_limit_bytes=60 * 1024 * 1024
        ),
        cost_estimate=pl.CostEstimate(flops=40_000_000_000, bytes_accessed=100_000_000, transcendentals=0),
    )(*[value for value, spec in ins.values()])
    m = Refs()
    for name, result in zip(outs, results):
        setattr(m, name, result)
    return m


def small_outs(own, other, is_first, width):
    first = jnp.where(is_first, own, other)
    second = jnp.where(is_first, other, own)
    me = lax.axis_index("dp")

    def columns(rows):
        wide = rows.shape[-1] // lax.axis_size("dp")
        return lax.dynamic_slice_in_dim(rows, me * wide, wide, rows.ndim - 1)

    down = columns(jnp.concatenate([first[:2], second[:1]])[:, :width])
    up = columns(jnp.concatenate([first[9:15].reshape(2, -1), second[9:12].reshape(1, -1)]))
    own = columns(own[2:9, :width])
    return own[0:2], own[2:3], own[3:5], own[5:7], up, down


def flat(value):
    return value.reshape((-1, value.shape[-1]))


def left_parts(m, is_first):
    n1, att, n2, branch_delta = (flat(part) for part in (m.out_n1, m.out_att, m.out_n2, m.branch))
    text = (jnp.arange(n1.shape[0]) % ROWS < TEXT)[:, None]
    vision = jnp.logical_not(text & is_first).astype(jnp.bfloat16)
    text = text.astype(jnp.bfloat16)
    return [
        piece.T for piece in (n2 * vision, branch_delta * vision, n2 * text, branch_delta * text, n1, att)
    ]


def all_grads(m, length):
    up, down, qkv, out, input_grad, *small = finished(
        length,
        *summed_grads(m.out_n1, m.out_att, m.out_n2, m.branch, m.out_hidden, m.out_active, m.out_mixed, m.out_proj, m.out_high, m.sums),
        m.out_low,
    )
    return qkv.T, out.T, up.transpose(0, 2, 1), down, small, input_grad


def large_grads_plain(m, is_first):
    lefts = left_parts(m, is_first)
    hidden_delta, active = flat(m.out_hidden), flat(m.out_active)

    def total_of(left, right):
        product = jnp.dot(left, right, preferred_element_type=jnp.float32).astype(jnp.bfloat16)
        return lax.psum_scatter(product, "dp", scatter_dimension=1, tiled=True)

    def table(vision_part, text_part):
        def swapped(part):
            return lax.psum(part, "section").astype(jnp.float32)

        return jnp.stack(
            [
                swapped(jnp.where(is_first, vision_part, 0)),
                swapped(jnp.where(is_first, text_part, 0)),
                swapped(jnp.where(is_first, 0, vision_part)),
            ]
        )

    up = table(total_of(lefts[0], hidden_delta), total_of(lefts[2], hidden_delta))
    down = table(total_of(lefts[1], active), total_of(lefts[3], active))
    small = lax.psum(m.sums, "dp")
    mixed, proj = flat(m.out_mixed), flat(m.out_proj)
    return (
        total_of(lefts[4], mixed).astype(jnp.float32),
        total_of(lefts[5], proj).astype(jnp.float32),
        up,
        down.transpose(0, 2, 1),
        small,
        lax.ppermute(small, "section", [(0, 1), (1, 0)]),
    )


def shards(
    tokens, cotangent, patch_mask, text_mask, qkv_weight, qv_bias, out_weight, out_bias, norm_gain, norm_bias,
    up_table, up_bias, down_table, down_bias,
):
    is_first = lax.axis_index("section") == 0
    m = both_layers(
        tokens, cotangent, patch_mask, text_mask, qkv_weight, out_weight, up_table, down_table, qv_bias[0], out_bias,
        norm_gain[0], norm_bias[0], up_bias, down_bias,
    )
    if lax.axis_size("dp") == 16:
        qkv, out, up, down, small, input_grad = all_grads(m, tokens.shape[1])
    else:
        qkv, out, up, down, own, other = large_grads_plain(m, is_first)
        small = small_outs(own, other, is_first, tokens.shape[2])
        high = lax.ppermute(m.out_high, "section", [(0, 1)])
        value = jnp.where(is_first, m.out_low, high.astype(jnp.float32))
        input_grad = jnp.concatenate([value[:, TEXT : tokens.shape[1]], value[:, :TEXT]], axis=1)
    qv_part, proj_part, gain_part, shift_part, up_part, down_part = small
    return (
        input_grad, qkv[None], qv_part[None], out[None], proj_part, gain_part[None], shift_part[None],
        up, up_part, down, down_part,
    )


def solution(mesh):
    items, layers = P("dp"), P("section")
    return jax.shard_map(
        shards,
        mesh=mesh,
        in_specs=(items,) * 4 + (layers,) * 6 + (P(),) * 4,
        out_specs=(
            P("dp", None, "section"), P("section", None, "dp"), P("section", None, "dp"), P("section", None, "dp"),
            P("section", "dp"), P("section", None, "dp"), P("section", None, "dp"),
            P(None, None, "dp"), P(None, "dp"), P(None, "dp", None), P(None, "dp"),
        ),
        check_vma=False,
    )
```

```python
import functools

import jax
import jax.numpy as jnp
from jax import lax
from jax.experimental import pallas as pl
from jax.experimental.pallas import tpu as pltpu
from jax.sharding import PartitionSpec as P

HEAD_DIM = 64
PATCHES = 197
EPSILON = 1e-05
BLOCK = 384
WINDOW = 640
RING = 3
TEXT = 64
ROWS = 272
MESH = pl.DeviceIdType.MESH


UNITS = (
    (
        (2, 2, 0), (3, 2, 0), (2, 3, 0), (3, 0, 0), (0, 1, 0), (3, 3, 0), (0, 2, 0), (3, 1, 0), (2,
        0, 0), (4, 3, 1), (1, 0, 0), (0, 3, 0), (0, 0, 1), (2, 1, 0), (1, 3, 0), (1, 1, 0), (4, 0,
        0), (4, 1, 0), (1, 2, 0), (4, 2, 0),
    ),
    (
        (0, 2, 0), (1, 0, 0), (1, 2, 0), (1, 1, 0), (0, 1, 0), (0, 3, 1), (4, 1, 1), (4, 2, 0), (1,
        3, 0), (0, 0, 0), (3, 0, 0), (4, 0, 0), (3, 2, 0), (3, 3, 0), (4, 3, 0), (3, 1, 0), (2, 1,
        0),
    ),
)
WAIT = 4
HOP = 3
MEET = WAIT + 3 * HOP + 1
MEET_LATE = MEET + 2
LEFT_OF = ((0,), (1,), (0,), (1,), (2, 3))
MOVED = [unit[:2] for unit in UNITS[1] if unit[0] in (2, 3)]
MOVED_BITS = sum(1 << (4 * kind + plane) for kind, plane in MOVED)
FIRST_MOVED = min(u for u, unit in enumerate(UNITS[1]) if unit[:2] in MOVED)


def packed(units, handed_on):
    counts = [0, 0]
    codes = []
    for kind, plane, z_first in units:
        slot = 0
        if not (handed_on and (kind, plane) in MOVED):
            slot = counts[z_first]
            counts[z_first] += 1
        codes.append(kind | plane << 3 | z_first << 5 | slot << 6)
    codes += [0] * (-len(codes) % 3)
    return [codes[i] | codes[i + 1] << 10 | codes[i + 2] << 20 for i in range(0, len(codes), 3)], counts


PACKED, COUNTS = zip(*(packed(units, side == 0) for side, units in enumerate(UNITS)))
Y_UNITS, Z_UNITS = (max(COUNTS[0][way], COUNTS[1][way], 1) for way in range(2))


def look_up(words, u):
    word = words[0]
    for n in range(1, len(words)):
        word = jnp.where(u // 3 == n, words[n], word)
    return word >> (10 * (u % 3))


class Refs:
    pass


def sum_kernel(names, *refs):
    m = Refs()
    for name, ref in zip(names, refs):
        setattr(m, name, ref)
    section = lax.axis_index("section")
    me = lax.axis_index("dp")
    z, y, core = me // 4, (me // 2) % 2, me % 2
    peer = (section, me + 1 - 2 * core)
    beside = (section, me + 2 - 4 * y)
    right = (section, me + 4)
    left = (section, me - 4)
    aslant = (1 - section, me + 1 - 2 * core)
    across = (1 - section, me)
    on_first = section == 0
    units = jnp.where(on_first, len(UNITS[0]), len(UNITS[1]))
    computed = jnp.where(on_first, len(UNITS[0]), len(UNITS[1]) - len(MOVED))

    arrivals = [u for u, unit in enumerate(UNITS[1]) if unit[:2] in MOVED]

    def is_moved(kind, plane):
        return ((MOVED_BITS >> (4 * kind + plane)) & 1) == 1

    class Unit:
        def __init__(self, u):
            self.u = u
            code = jnp.where(on_first, look_up(PACKED[0], u), look_up(PACKED[1], u))
            self.kind = code & 7
            self.plane = (code >> 3) & 3
            self.z_first = ((code >> 5) & 1) == 1
            self.slot = (code >> 6) & 15
            moved = is_moved(self.kind, self.plane)
            self.handed_on = on_first & moved
            self.handed_in = jnp.logical_not(on_first) & moved
            self.y_first = jnp.logical_not(self.z_first | self.handed_on)
            self.y_slot = self.slot + jnp.where(self.z_first, Y_UNITS, 0)
            self.uses_text = jnp.logical_not(on_first) | (self.kind > 1)
            self.uses_patches = jnp.logical_not(on_first) | (self.kind < 2) | (self.kind == 4)
            self.order = u
            for at in arrivals:
                self.order = self.order - jnp.where((section == 1) & (u > at), 1, 0)

    def following(u):
        u = u + 1
        for at in arrivals:
            u = u + jnp.where((section == 1) & (u == at), 1, 0)
        return u

    def remote(src, dst, send, recv, device):
        return pltpu.make_async_remote_copy(
            src_ref=src, dst_ref=dst, send_sem=send, recv_sem=recv, device_id=device, device_id_type=MESH
        )

    def core_copy(order, b):
        slot = order % RING
        return remote(m.made.at[slot, 1 - core, b], m.xr.at[slot, b], m.core_send.at[order, b], m.core_recv.at[order, b], peer)

    def y_copy(n):
        return remote(m.part.at[n.u, 0], m.yr.at[n.y_slot], m.y_send.at[n.y_slot], m.y_recv.at[n.y_slot], beside)

    def right_copy(n):
        return remote(m.part.at[n.u, 1], m.zr.at[n.slot], m.right_send.at[n.slot], m.right_recv.at[n.slot], right)

    def left_copy(n):
        return remote(m.part.at[n.u, 1], m.zl.at[n.slot], m.left_send.at[n.slot], m.left_recv.at[n.slot], left)

    def right_pair(n):
        g = n.slot
        return remote(m.part.at[n.u], m.wr.at[g], m.right_send.at[Y_UNITS + g], m.right_recv.at[Y_UNITS + g], right)

    def left_pair(n):
        g = n.slot
        return remote(m.part.at[n.u], m.wl.at[g], m.left_send.at[Y_UNITS + g], m.left_recv.at[Y_UNITS + g], left)

    def over_copy(n, source, target):
        number = 4 * (n.kind - 2) + n.plane
        return remote(m.part.at[source], m.part.at[target], m.over_send.at[number], m.over_recv.at[number], across)

    def over_target(n):
        target = 0
        for at in arrivals:
            kind, plane, unused = UNITS[1][at]
            target = target + jnp.where((n.kind == kind) & (n.plane == plane), at, 0)
        return target

    def half_copy():
        return remote(m.half, m.half_out, m.half_send.at[0], m.half_recv.at[0], across)

    def own_half():
        return pl.ds(pl.multiple_of(core * BLOCK, 128), BLOCK)

    def mine(size):
        return pl.ds(pl.multiple_of(core * size, 16), size)

    def theirs(size):
        return pl.ds(pl.multiple_of((1 - core) * size, 16), size)

    def table_of(k, by_second):
        return jnp.where((k < 2) & by_second, 2, k // 2) + jnp.where(k % 2 == 1, 3, 0)

    def table_rows(k, by_second):
        return m.tables_out.at[table_of(k, by_second), :, own_half()]

    def peer_copy(k):
        return remote(m.turned.at[k, theirs(192)], table_rows(k, section == 1), m.peer_send.at[k], m.peer_recv.at[k], peer)

    def cross_copy(k, by_second, other_core):
        source = theirs(192) if other_core else mine(192)
        device = aslant if other_core else across
        number = 1 if other_core else 0
        return remote(
            m.turned.at[k, source], table_rows(k, by_second), m.cross_send.at[number, k], m.cross_recv.at[number, k], device
        )

    def attention_copies():
        rows = pl.ds(pl.multiple_of(288 + (1 - core) * 48, 16), 48)
        return (
            remote(m.turned.at[4, theirs(144)], m.qkv_out.at[:, own_half()], m.peer_send.at[4], m.peer_recv.at[4], peer),
            remote(m.turned.at[4, rows], m.out_out.at[:, own_half()], m.peer_send.at[5], m.peer_recv.at[5], peer),
        )

    def start_cross(k):
        cross_copy(k, section == 1, False).start()
        cross_copy(k, section == 1, True).start()

    def mixed_start(plane):
        return pl.multiple_of((9 * plane // 2) * 128, 128)

    def proj_start(plane):
        return pl.multiple_of((3 * plane // 2) * 128, 128)

    def tile_copies(n):
        k = n.kind
        slot = n.order % 2
        wide = pl.ds(pl.multiple_of(n.plane * 2 * BLOCK, 128), 2 * BLOCK)
        cases = []
        for ref, number, here, source, target in (
            (m.hidden, 0, (k == 0) | (k == 2), wide, slice(0, 2 * BLOCK)),
            (m.active, 0, (k == 1) | (k == 3), wide, slice(0, 2 * BLOCK)),
            (m.mixed, 0, k == 4, pl.ds(mixed_start(n.plane), WINDOW), slice(0, WINDOW)),
            (m.proj, 1, k == 4, pl.ds(proj_start(n.plane), 256), slice(WINDOW, WINDOW + 256)),
        ):
            copy = pltpu.make_async_copy(
                ref.at[:, :TEXT, source], m.text_tile.at[slot, :, :, target], m.text_sem.at[slot, number]
            )
            cases.append((here & n.uses_text, copy))
            copy = pltpu.make_async_copy(
                ref.at[:, TEXT:, source], m.patch_tile.at[slot, :, :, target], m.patch_sem.at[slot, number]
            )
            cases.append((here & n.uses_patches, copy))
        return cases

    def join_columns(slot, begin):
        for tile, joint in ((m.text_tile, m.text_joint), (m.patch_tile, m.patch_joint)):
            for side in range(2):
                at, mixed, proj = side * BLOCK, begin + side * 288, WINDOW + begin + side * 96
                joint[:, :, at : at + 288] = tile[slot, :, :, mixed : mixed + 288]
                joint[:, :, at + 288 : at + BLOCK] = tile[slot, :, :, proj : proj + 96]

    def start_tile(n):
        for here, copy in tile_copies(n):
            pl.when(here)(copy.start)

    def wait_tile(n):
        for here, copy in tile_copies(n):
            pl.when(here)(copy.wait)

    def add_into(target, source):
        target[...] = target[...] + source[...]

    def rows_dot(left, tile, *columns):
        tile = jnp.concatenate([tile[:, :, at] for at in columns], axis=2)
        return matmul(left, tile.reshape(-1, tile.shape[2]))

    def text_dot(index, slot, *columns):
        return rows_dot(m.text_left[index], m.text_tile.at[slot], *columns)

    def patch_dot(index, slot, *columns):
        return rows_dot(m.patch_left[index], m.patch_tile.at[slot], *columns)

    def joint_dot(index, *columns):
        text = rows_dot(m.text_left[index], m.text_joint, *columns)
        return rows_dot(m.patch_left[index], m.patch_joint, *columns) + text

    def compute(n):
        k = n.kind
        slot = n.order % RING

        @pl.when(n.order >= RING)
        def _():
            core_copy(n.order - RING, 0).wait_send()
            core_copy(n.order - RING, 1).wait_send()
            pl.semaphore_wait(m.credit, 1)

        @pl.when(n.order + 1 < computed)
        def _():
            start_tile(Unit(following(n.u)))

        wait_tile(n)
        tile = n.order % 2
        everything = slice(0, 2 * BLOCK)

        def put(value, columns, begin):
            for half in range(2):
                for side in range(2):
                    piece = value[half * BLOCK : (half + 1) * BLOCK, columns[side]]
                    at = slice(begin, begin + piece.shape[1])
                    m.made[slot, half, jnp.where(y == side, 1, 0), :, at] = piece.astype(jnp.bfloat16)

        sides = (slice(0, BLOCK), slice(BLOCK, 2 * BLOCK))

        @pl.when((k < 4) & jnp.logical_not(n.uses_text))
        def _():
            put(patch_dot(k % 2, tile, everything), sides, 0)

        @pl.when((k < 4) & jnp.logical_not(n.uses_patches))
        def _():
            put(text_dot(k % 2, tile, everything), sides, 0)

        @pl.when((k < 4) & n.uses_text & n.uses_patches)
        def _():
            put(patch_dot(k % 2, tile, everything) + text_dot(k % 2, tile, everything), sides, 0)

        @pl.when(k == 4)
        def _():
            ends = (slice(256, BLOCK), slice(BLOCK + 256, 2 * BLOCK))
            for odd in range(2):
                pl.when(n.plane % 2 == odd)(functools.partial(join_columns, tile, 64 * odd))
            mixed = joint_dot(2, everything)
            proj = joint_dot(3, *ends)
            put(mixed, (slice(0, 256), slice(BLOCK, BLOCK + 256)), 0)
            lanes = lax.broadcasted_iota(jnp.int32, (1, 128), 1)
            last = [jnp.where(lanes < 32, mixed[:, ends[side]], proj[:, 128 * side : 128 * side + 128]) for side in range(2)]
            put(jnp.concatenate(last, axis=1), (slice(0, 128), slice(128, 256)), 256)

        core_copy(n.order, 0).start()
        core_copy(n.order, 1).start()

    def join_core(n):
        slot = n.order % RING

        @pl.when(n.handed_in)
        def _():
            over_copy(n, 0, n.u).wait_recv()

        @pl.when(jnp.logical_not(n.handed_in))
        def _():
            core_copy(n.order, 0).wait_recv()
            m.part[n.u, 0] = m.made[slot, core, 0] + m.xr[slot, 0]

        pl.when(n.y_first)(lambda: y_copy(n).start())

        @pl.when(jnp.logical_not(n.handed_in))
        def _():
            core_copy(n.order, 1).wait_recv()
            m.part[n.u, 1] = m.made[slot, core, 1] + m.xr[slot, 1]

            @pl.when(n.order + RING < computed)
            def _():
                pl.semaphore_signal(m.credit, inc=1, device_id=peer, device_id_type=MESH)

        pl.when(n.handed_on)(lambda: over_copy(n, n.u, over_target(n)).start())

    def join_y(n):
        y_copy(n).wait_recv()
        add_into(m.part.at[n.u, 1], m.yr.at[n.y_slot])

    def take(n, one, pair, single_from, pair_from):
        @pl.when(n.y_first)
        def _():
            one(n).wait_recv()
            add_into(m.part.at[n.u, 1], single_from.at[n.slot])

        @pl.when(n.z_first)
        def _():
            pair(n).wait_recv()
            add_into(m.part.at[n.u], pair_from.at[n.slot])

    def take_right(n):
        take(n, right_copy, right_pair, m.zr, m.wr)

    def take_left(n):
        take(n, left_copy, left_pair, m.zl, m.wl)

    def pass_right(n):
        pl.when(z > 0)(lambda: take_right(n))
        pl.when(n.y_first)(lambda: right_copy(n).start())
        pl.when(n.z_first)(lambda: right_pair(n).start())

    def pass_left(n):
        pl.when(z < 3)(lambda: take_left(n))
        pl.when(n.y_first)(lambda: left_copy(n).start())
        pl.when(n.z_first)(lambda: left_pair(n).start())

    def give(n, i):
        k = n.kind
        m.turned[k] = m.part[n.u, 1].T

        @pl.when(k < 4)
        def _():
            m.tables_out[table_of(k, section == 1), :, own_half()] = m.turned[k, mine(192), :]
            peer_copy(k).start()
            pl.when(on_first | (i > FIRST_MOVED))(lambda: start_cross(k))

        @pl.when(k == 4)
        def _():
            m.qkv_out[:, own_half()] = m.turned[4, mine(144), :]
            m.out_out[:, own_half()] = m.turned[4, pl.ds(pl.multiple_of(288 + core * 48, 16), 48), :]
            for copy in attention_copies():
                copy.start()

    def greet_first(u, carry):
        n = Unit(u)
        ended = jnp.where(n.z_first, MEET_LATE, MEET) + u <= FIRST_MOVED
        pl.when(ended & (n.kind < 4) & (n.plane == z))(lambda: start_cross(n.kind))
        return carry

    def meet(n, i):
        pl.when(z > 0)(lambda: take_right(n))
        pl.when(z < 3)(lambda: take_left(n))
        pl.when(n.z_first)(lambda: y_copy(n).start())
        pl.when(n.y_first)(lambda: give(n, i))

    def meet_late(n, i):
        join_y(n)
        give(n, i)

    flips = (peer, beside, (section, me + 4 - 8 * (z % 2)), (section, me + 8 - 16 * (z // 2)), across)

    def small_copy(j):
        return remote(m.small_sum.at[j], m.small_in.at[j], m.small_send.at[j], m.small_recv.at[j], flips[j])

    def small_step(j):
        if j == 0:
            m.small_sum[0] = m.small[...]
        else:
            small_copy(j - 1).wait_recv()
            if j == 5:
                m.small_out[0] = m.small_sum[4]
                m.small_out[1] = m.small_in[4]
            else:
                m.small_sum[j] = m.small_sum[j - 1] + m.small_in[j - 1]
        if j < 5:
            small_copy(j).start()

    lefts = (m.n2, m.branch, m.n1, m.att)
    turns = [[], []]
    for side in range(2):
        for kind, plane, z_first in UNITS[side]:
            for index in () if side == 1 and (kind, plane) in MOVED else LEFT_OF[kind]:
                if index not in turns[side]:
                    turns[side].append(index)

    def stage_copy(index):
        return pltpu.make_async_copy(lefts[index], m.stage, m.stage_sem.at[0])

    def start_stage(turn):
        for side in range(2):
            pl.when(section == side)(stage_copy(turns[side][turn]).start)

    def prepare(turn):
        stage_copy(0).wait()
        number = jnp.where(on_first, turns[0][turn], turns[1][turn])

        def part(c, carry):
            at = pl.ds(pl.multiple_of(c * 128, 128), 128)
            m.text_left[number, at, :] = m.stage[:, :TEXT, at].reshape(-1, 128).T
            m.patch_left[number, at, :] = m.stage[:, TEXT:, at].reshape(-1, 128).T
            return carry

        lax.fori_loop(0, m.stage.shape[2] // 128, part, 0)
        if turn < 3:
            start_stage(turn + 1)

    barrier = pltpu.get_barrier_semaphore()
    for device in (peer, beside, flips[3]):
        pl.semaphore_signal(barrier, inc=1, device_id=device, device_id_type=MESH)

    @pl.when(section == 1)
    def _():
        for device in (across, aslant):
            pl.semaphore_signal(barrier, inc=1, device_id=device, device_id_type=MESH)

    @pl.when(z < 3)
    def _():
        pl.semaphore_signal(barrier, inc=1, device_id=right, device_id_type=MESH)

    @pl.when(z > 0)
    def _():
        pl.semaphore_signal(barrier, inc=1, device_id=left, device_id_type=MESH)

    start_stage(0)
    start_tile(Unit(jnp.int32(0)))
    prepare(0)
    pl.semaphore_wait(barrier, 3 + jnp.where(on_first, 2, 0) + jnp.where(z < 3, 1, 0) + jnp.where(z > 0, 1, 0))

    @pl.when(on_first)
    def _():
        for device in (across, aslant):
            pl.semaphore_signal(m.ready, inc=1, device_id=device, device_id_type=MESH)
        half_copy().start()


    def at_unit(u, condition, action, *more):
        n = Unit(jnp.maximum(u, 0))

        @pl.when((u >= 0) & (u < units) & condition(n))
        def _():
            action(n, *more)

    def in_flow(n):
        return jnp.logical_not(n.handed_on)

    def step(i, carry):
        @pl.when((i == FIRST_MOVED + 1) & (section == 1))
        def _():
            pl.semaphore_wait(m.ready, 2)
            lax.fori_loop(0, units, greet_first, 0)

        at_unit(i, lambda n: jnp.logical_not(n.handed_in), compute)
        for number in range(3):
            pl.when(i == number)(functools.partial(prepare, number + 1))
        at_unit(i - 1, lambda n: n.kind >= 0, join_core)
        at_unit(i - WAIT, lambda n: n.y_first, join_y)
        at_unit(i - WAIT - HOP * z, lambda n: in_flow(n) & (n.plane > z), pass_right)
        at_unit(i - WAIT - HOP * (3 - z), lambda n: in_flow(n) & (n.plane < z), pass_left)
        at_unit(i - MEET, lambda n: in_flow(n) & (n.plane == z), meet, i)
        at_unit(i - MEET_LATE, lambda n: n.z_first & (n.plane == z), meet_late, i)
        for j in range(4):
            pl.when(i == 3 + j)(functools.partial(small_step, j))
        return carry

    lax.fori_loop(0, units + MEET_LATE, step, 0)
    small_step(4)

    def ours(k):
        return True if k in (0, 1, 4) else is_moved(k, z) == (section == 1)

    def when_ours(k, wanted, action):
        pl.when(jnp.logical_not(ours(k) ^ wanted) if k in (2, 3) else True)(action)

    small_step(5)

    def settle(u, carry):
        n = Unit(u)

        @pl.when(jnp.logical_not(n.handed_in) & (n.order >= computed - RING))
        def _():
            core_copy(n.order, 0).wait_send()
            core_copy(n.order, 1).wait_send()

        pl.when(n.handed_on)(lambda: over_copy(n, n.u, over_target(n)).wait_send())
        pl.when(n.y_first | (n.z_first & (n.plane == z)))(lambda: y_copy(n).wait_send())
        pl.when(n.y_first & (n.plane > z))(lambda: right_copy(n).wait_send())
        pl.when(n.z_first & (n.plane > z))(lambda: right_pair(n).wait_send())
        pl.when(n.y_first & (n.plane < z))(lambda: left_copy(n).wait_send())
        pl.when(n.z_first & (n.plane < z))(lambda: left_pair(n).wait_send())
        return carry

    lax.fori_loop(0, units, settle, 0)
    for j in range(5):
        small_copy(j).wait_send()
    for k in range(4):

        def arrived(k=k):
            for other_core in (False, True):
                cross_copy(k, section == 0, other_core).wait_recv()

        def sent(k=k):
            peer_copy(k).wait()
            for other_core in (False, True):
                cross_copy(k, section == 1, other_core).wait_send()

        when_ours(k, True, sent)
        when_ours(k, False, arrived)
    for copy in attention_copies():
        copy.wait()

    @pl.when(on_first)
    def _():
        half_copy().wait_send()

    @pl.when(section == 1)
    def _():
        half_copy().wait_recv()

def summed_grads(n1, att, n2, branch, hidden, active, mixed, proj, half, small):
    dma = pltpu.SemaphoreType.DMA
    items, depth, width = n1.shape
    bf16, f32 = jnp.bfloat16, jnp.float32
    tile = (BLOCK, BLOCK)
    vmem, anywhere = pl.BlockSpec(memory_space=pltpu.VMEM), pl.BlockSpec(memory_space=pl.ANY)
    ins = dict(n1=n1, att=att, n2=n2, branch=branch, hidden=hidden, active=active, mixed=mixed, proj=proj, half=half,
        small=small)
    outs = dict(
        tables_out=((6, 192, width), bf16), qkv_out=((144, width), bf16),
        out_out=((48, width), bf16), small_out=((2,) + small.shape, f32), half_out=(half.shape, bf16),
    )
    buffers = dict(
        text_tile=((2, items, TEXT, WINDOW + 256), bf16),
        patch_tile=((2, items, depth - TEXT, WINDOW + 256), bf16), text_joint=((items, TEXT, 2 * BLOCK), bf16),
        patch_joint=((items, depth - TEXT, 2 * BLOCK), bf16), part=((20, 2) + tile, bf16), made=((RING, 2, 2) + tile, bf16),
        xr=((RING, 2) + tile, bf16), yr=((Y_UNITS + Z_UNITS,) + tile, bf16), zr=((Y_UNITS,) + tile, bf16), zl=((Y_UNITS,) + tile, bf16),
        wr=((Z_UNITS, 2) + tile, bf16), wl=((Z_UNITS, 2) + tile, bf16), turned=((5,) + tile, bf16),
        text_left=((4, width, items * TEXT), bf16), patch_left=((4, width, items * (depth - TEXT)), bf16), stage=((items, depth, width), bf16), small_sum=((5,) + small.shape, f32),
        small_in=((5,) + small.shape, f32),
    )
    semaphores = dict(
        small_send=dma((5,)), small_recv=dma((5,)), text_sem=dma((2, 2)), patch_sem=dma((2, 2)), stage_sem=dma((1,)), core_send=dma((20, 2)),
        core_recv=dma((20, 2)), y_send=dma((Y_UNITS + Z_UNITS,)), y_recv=dma((Y_UNITS + Z_UNITS,)), right_send=dma((Y_UNITS + Z_UNITS,)), right_recv=dma((Y_UNITS + Z_UNITS,)),
        left_send=dma((Y_UNITS + Z_UNITS,)), left_recv=dma((Y_UNITS + Z_UNITS,)), over_send=dma((8,)), over_recv=dma((8,)), half_send=dma((1,)), half_recv=dma((1,)), peer_send=dma((6,)),
        peer_recv=dma((6,)), cross_send=dma((2, 4)), cross_recv=dma((2, 4)),
        credit=pltpu.SemaphoreType.REGULAR, ready=pltpu.SemaphoreType.REGULAR,
    )
    names = list(ins) + list(outs) + list(buffers) + list(semaphores)
    return pl.pallas_call(
        functools.partial(sum_kernel, names),
        out_shape=[jax.ShapeDtypeStruct(*kind) for kind in outs.values()],
        in_specs=[anywhere] * 9 + [vmem],
        out_specs=[vmem] * (len(outs) - 1) + [anywhere],
        scratch_shapes=[pltpu.VMEM(*kind) for kind in buffers.values()] + list(semaphores.values()),
        compiler_params=pltpu.CompilerParams(
            collective_id=0, has_side_effects=True, vmem_limit_bytes=60 * 1024 * 1024
        ),
        cost_estimate=pl.CostEstimate(flops=48 * 2 * 768 * 384 * items * depth, bytes_accessed=40_000_000, transcendentals=0),
    )(*ins.values())


def finish_kernel(count, *refs):
    sources, targets = refs[:count], refs[count : count + 11]
    held, made, (load_sem, store_sem) = refs[count + 11 : -7], refs[-7:-2], refs[-2:]
    loads = [pltpu.make_async_copy(*pair, load_sem.at[n]) for n, pair in enumerate(zip(sources, held))]
    stores = [pltpu.make_async_copy(*pair, store_sem.at[n]) for n, pair in enumerate(zip(made, targets[:5]))]
    for load in loads:
        load.start()
    tables, qkv, out, small, half, grad = held
    small_outs = targets[5:]
    loads[0].wait()
    for number, source in enumerate((tables.at[:3], tables.at[3:], qkv, out)):
        if number > 1:
            loads[number - 1].wait()
        made[number][...] = source[...].astype(jnp.float32)
        stores[number].start()
    for load in loads[3:]:
        load.wait()
    section, me = lax.axis_index("section"), lax.axis_index("dp")
    width, wide = tables.shape[2], tables.shape[2] // 16
    ff = width * 4

    def columns(row, size):
        return pltpu.roll(row, (row.shape[1] - size * me) % row.shape[1], 1)[:, :size]

    def up_bias(side, slot):
        rows = [small[side, 9 + 4 * slot + j : 10 + 4 * slot + j] for j in range(4)]
        return columns(jnp.concatenate(rows, axis=1), ff // 16)

    own = columns(small[0, :9], wide)
    other = columns(small[1, :9], wide)
    qv_out, proj_out, gain_out, shift_out, up_bias_out, down_bias_out = small_outs
    qv_out[...] = own[2:4]
    proj_out[...] = own[4:5]
    gain_out[...] = own[5:7]
    shift_out[...] = own[7:9]
    for side in range(2):
        mine, theirs = (own, other) if side == 0 else (other, own)

        @pl.when(section == side)
        def _():
            for i in range(grad.shape[0]):
                place(made[4], i, grad[i] if side == 0 else half[i].astype(jnp.float32))
            stores[4].start()
            down_bias_out[0:2] = mine[0:2]
            down_bias_out[2:3] = theirs[0:1]
            up_bias_out[0:1] = up_bias(side, 0)
            up_bias_out[1:2] = up_bias(side, 1)
            up_bias_out[2:3] = up_bias(1 - side, 0)

    for store in stores:
        store.wait()


def place(target, i, value):
    target[i, :PATCHES] = value[TEXT : target.shape[1]]
    target[i, PATCHES:] = value[:TEXT]


def finished(length, *sources):
    tables, qkv, out, small, half, grad = sources
    width = tables.shape[2]
    shapes = [(3,) + tables.shape[1:]] * 2 + [qkv.shape, out.shape, (grad.shape[0], length, grad.shape[2])]
    shapes += [(rows, width // 16) for rows in (2, 1, 2, 2)] + [(3, width // 4), (3, width // 16)]
    return pl.pallas_call(
        functools.partial(finish_kernel, len(sources)),
        out_shape=[jax.ShapeDtypeStruct(shape, jnp.float32) for shape in shapes],
        in_specs=[pl.BlockSpec(memory_space=pltpu.HBM)] * len(sources),
        out_specs=[pl.BlockSpec(memory_space=pl.ANY)] * 5 + [pl.BlockSpec(memory_space=pltpu.VMEM)] * 6,
        scratch_shapes=[pltpu.VMEM(value.shape, value.dtype) for value in sources]
        + [pltpu.VMEM(shape, jnp.float32) for shape in shapes[:5]]
        + [pltpu.SemaphoreType.DMA((len(sources),)), pltpu.SemaphoreType.DMA((5,))],
        compiler_params=pltpu.CompilerParams(vmem_limit_bytes=60 * 1024 * 1024),
    )(*sources)


PIECE = 768
KEY_SPLIT = 256
TAIL = (0.319381530, -0.356563782, 1.781477937, -1.821255978, 1.330274429)
LOG2_E = 1.4426950408889634
LOG2_PEAK = -1.3257480647361593


def normal_parts(z):
    size = jnp.abs(z)
    scale = 1.0 + 0.2316419 * size
    t = pl.reciprocal(scale, approx=True)
    t = t * (2.0 - scale * t)
    bell = jnp.exp2(z * z * (-0.5 * LOG2_E) + LOG2_PEAK)
    series = TAIL[4]
    for factor in TAIL[3::-1]:
        series = series * t + factor
    upper = bell * (series * t)
    return jnp.where(z >= 0, 1.0 - upper, upper), bell


def matmul(left, right):
    return jnp.dot(left, right, preferred_element_type=jnp.float32)


def matmul_turned(left, right):
    return lax.dot_general(left, right, (((1,), (1,)), ((), ())), preferred_element_type=jnp.float32)


def standardized(values):
    centre = values - jnp.mean(values, -1, keepdims=True)
    inverse = lax.rsqrt(jnp.mean(centre * centre, -1, keepdims=True) + EPSILON)
    return centre * inverse, inverse


def norm_step_back(delta, standard, inverse, gain_row):
    scaled = delta * gain_row
    moved = inverse * (
        scaled - jnp.mean(scaled, -1, keepdims=True) - standard * jnp.mean(scaled * standard, -1, keepdims=True)
    )
    return moved, jnp.sum(delta * standard, 0, keepdims=True), jnp.sum(delta, 0, keepdims=True)


def half_mask(half):
    lanes = lax.broadcasted_iota(jnp.int32, (1, 128), 1)
    return (lanes < 64) if half == 0 else (lanes >= 64)


def pair_columns(p, part, width):
    return slice(part * width + p * 128, part * width + p * 128 + 128)


def both_halves(pair):
    return jnp.concatenate([jnp.where(half_mask(half), pair, jnp.zeros_like(pair)) for half in range(2)], axis=0)


def in_turn(count, *stages):
    for turn in range(count + len(stages) - 1):
        for number, stage in enumerate(stages):
            if 0 <= turn - number < count:
                stage(turn - number)


def attention_forward(m, length, beside):
    rows, width = m.att.shape

    def scores(p):
        q2 = m.qkv[:, pair_columns(p, 0, width)]
        k2 = m.qkv[:, pair_columns(p, 1, width)]
        m.scores[p % 2] = matmul_turned(both_halves(k2), q2).reshape(2, rows, rows)

    def soften(p):
        for half in range(2):
            top = m.scores[p % 2, half, :KEY_SPLIT]
            low = m.scores[p % 2, half, KEY_SPLIT:]
            key_row = KEY_SPLIT + lax.broadcasted_iota(jnp.int32, low.shape, 0)
            low = jnp.where(key_row < length, low, -1e30)
            peak = jnp.maximum(jnp.max(top, 0, keepdims=True), jnp.max(low, 0, keepdims=True))
            top = jnp.exp(top - peak)
            low = jnp.exp(low - peak)
            over = 1.0 / (jnp.sum(top, 0, keepdims=True) + jnp.sum(low, 0, keepdims=True))
            m.probs[2 * p + half, :KEY_SPLIT] = (top * over).astype(jnp.bfloat16)
            m.probs[2 * p + half, KEY_SPLIT:] = (low * over).astype(jnp.bfloat16)

    def blend(p):
        v_turned = m.qkv[:, pair_columns(p, 2, width)].T
        parts = [matmul(v_turned[64 * half : 64 * half + 64], m.probs[2 * p + half]) for half in range(2)]
        turned = jnp.concatenate(parts, axis=0)
        m.att_turned[p * 128 : p * 128 + 128, :] = turned.astype(jnp.bfloat16)
        m.att[:, p * 128 : p * 128 + 128] = turned.T.astype(jnp.bfloat16)

    in_turn(width // 128, scores, soften, blend, *beside)


def attention_back(m):
    rows, width = m.att.shape

    def probs_back(p):
        v2 = m.qkv[:, pair_columns(p, 2, width)]
        d_turned = m.att_delta[:, pair_columns(p, 0, width)].T
        m.scores[p % 2] = matmul(both_halves(v2), d_turned).reshape(2, rows, rows)
        product = d_turned.astype(jnp.float32) * m.att_turned[p * 128 : p * 128 + 128, :].astype(jnp.float32)
        for half in range(2):
            m.inner[p % 2, half] = jnp.sum(product[64 * half : 64 * half + 64], 0, keepdims=True)

    def scores_back(p):
        for half in range(2):
            probs = m.probs[2 * p + half].astype(jnp.float32)
            m.score_delta[p % 2, half] = (probs * (m.scores[p % 2, half] - m.inner[p % 2, half])).astype(jnp.bfloat16)

    def heads_back(p):
        q_at, k_at, v_at = (pair_columns(p, part, width) for part in range(3))
        score = m.score_delta[p % 2]
        probs = m.probs[2 * p : 2 * p + 2].reshape(2 * rows, rows)
        k_turned = m.qkv[:, k_at].T
        value = matmul(probs, m.att_delta[:, q_at])
        key = matmul(score.reshape(2 * rows, rows), m.qkv[:, q_at])
        query = jnp.concatenate(
            [matmul(k_turned[64 * half : 64 * half + 64], score[half]) for half in range(2)], axis=0
        )
        dq = (query.T * HEAD_DIM ** (-0.5)).astype(jnp.bfloat16)
        dk = jnp.where(half_mask(0), key[:rows], key[rows:]).astype(jnp.bfloat16)
        dv = jnp.where(half_mask(0), value[:rows], value[rows:]).astype(jnp.bfloat16)
        m.mixed[:, q_at] = dq
        m.mixed[:, k_at] = dk
        m.mixed[:, v_at] = dv
        m.sums[2:3, q_at] += jnp.sum(dq.astype(jnp.float32), 0, keepdims=True)
        m.sums[3:4, q_at] += jnp.sum(dv.astype(jnp.float32), 0, keepdims=True)

    in_turn(width // 128, probs_back, scores_back, heads_back)


def forward_front(m, x_ref, length, hold, *beside):
    x = x_ref[...].astype(jnp.float32)
    standard, inverse = standardized(x)
    if hold:
        m.standard[...] = standard
        m.inverse[0] = inverse
    m.n1[...] = (standard * m.gain[0:1] + m.shift[0:1]).astype(jnp.bfloat16)
    width = x.shape[1]
    m.need(m.qkv_w)

    def part_columns(part):
        return slice(part * width, (part + 1) * width)

    def mix(part):
        m.hidden[part % 2] = matmul(m.n1[...], m.qkv_w[:, part_columns(part)])

    def split(part):
        value = m.hidden[part % 2]
        if part == 0:
            value = (value + m.qv[0:1]).astype(jnp.bfloat16) * jnp.bfloat16(HEAD_DIM ** (-0.5))
        elif part == 2:
            value = value + m.qv[1:2]
        m.qkv[:, part_columns(part)] = value.astype(jnp.bfloat16)

    in_turn(3, mix, split)
    attention_forward(m, length, beside)
    m.need(m.out_w)
    middle = x_ref[...].astype(jnp.float32) + matmul(m.att[...], m.out_w[...]) + m.proj[0:1]
    standard, inverse = standardized(middle)
    m.middle[...] = standard if hold else middle
    if hold:
        m.inverse[1] = inverse
    m.n2[...] = (standard * m.gain[1:2] + m.shift[1:2]).astype(jnp.bfloat16)


def back_tail(m, x_ref, g_ref, n2_delta, keep, held):
    standard, inverse = (m.middle[...], m.inverse[1]) if held else standardized(m.middle[...])
    middle_part, gain, shift = norm_step_back(n2_delta, standard, inverse, m.gain[1:2])
    m.sums[6:7, :gain.shape[1]] += gain
    m.sums[8:9, :gain.shape[1]] += shift
    middle_delta = g_ref[...].astype(jnp.float32) + middle_part
    proj_delta = middle_delta.astype(jnp.bfloat16)
    m.sums[4:5, :gain.shape[1]] += jnp.sum(proj_delta.astype(jnp.float32), 0, keepdims=True)
    m.proj_delta[...] = proj_delta
    m.middle_delta[...] = middle_delta
    m.att_delta[...] = matmul_turned(proj_delta, m.out_w[...]).astype(jnp.bfloat16)
    attention_back(m)
    total = matmul_turned(m.mixed[...], m.qkv_w[...])
    standard, inverse = (m.standard[...], m.inverse[0]) if held else standardized(x_ref[...].astype(jnp.float32))
    input_part, gain, shift = norm_step_back(total, standard, inverse, m.gain[0:1])
    m.sums[5:6, :gain.shape[1]] += gain
    m.sums[7:8, :gain.shape[1]] += shift
    keep(m.middle_delta[...] + input_part)


def forward_expert(m, slot, begin, end):
    def columns(j):
        return slice(j * PIECE, (j + 1) * PIECE)

    def widen(j):
        hidden = matmul(m.n2[begin:end], m.up_w[slot, :, columns(j)])
        m.hidden[j % 2, begin:end] = hidden + m.up_b[slot : slot + 1, columns(j)]

    def bend(j):
        hidden = m.hidden[j % 2, begin:end]
        below, bell = normal_parts(hidden)
        m.active[begin:end, columns(j)] = (hidden * below).astype(jnp.bfloat16)
        m.slope[begin:end, columns(j)] = (below + hidden * bell).astype(jnp.bfloat16)

    def narrow(j):
        piece = matmul(m.active[begin:end, columns(j)], m.down_w[slot, columns(j), :])
        m.total[begin:end] = piece + (m.middle[begin:end] + m.down_b[slot : slot + 1] if j == 0 else m.total[begin:end])

    in_turn(m.up_w.shape[2] // PIECE, widen, bend, narrow)


def keep_hidden_delta(m, slot, begin, end, j, value):
    low = value.astype(jnp.bfloat16)
    m.hidden_delta[begin:end, j * PIECE : (j + 1) * PIECE] = low
    row = 9 + 4 * slot + j
    m.sums[row : row + 1] += jnp.sum(low.astype(jnp.float32), 0, keepdims=True)


def back_expert(m, g_ref, slot, begin, end):
    m.sums[slot : slot + 1, : g_ref.shape[1]] += jnp.sum(g_ref[begin:end].astype(jnp.float32), 0, keepdims=True)

    def columns(j):
        return slice(j * PIECE, (j + 1) * PIECE)

    def widen(j):
        m.hidden[j % 2, begin:end] = matmul_turned(g_ref[begin:end], m.down_w[slot, columns(j), :])

    def bend(j):
        slope = m.slope[begin:end, columns(j)].astype(jnp.float32)
        keep_hidden_delta(m, slot, begin, end, j, m.hidden[j % 2, begin:end] * slope)

    def narrow(j):
        piece = matmul_turned(m.hidden_delta[begin:end, columns(j)], m.up_w[slot, :, columns(j)])
        m.total[begin:end] = piece if j == 0 else m.total[begin:end] + piece

    in_turn(m.up_w.shape[2] // PIECE, widen, bend, narrow)


def early_delta(m, g_ref, pieces):
    size = m.active_delta.shape[1] // pieces

    def stage(p):
        columns = slice(p * size, (p + 1) * size)
        m.active_delta[:, columns] = matmul_turned(g_ref[...], m.down_w[0, columns, :])

    return stage


def both_expert(m):
    def columns(j):
        return slice(j * PIECE, (j + 1) * PIECE)

    def widen(j):
        m.hidden[j % 2] = matmul(m.n2[...], m.up_w[0, :, columns(j)]) + m.up_b[2:3, columns(j)]

    def bend(j):
        hidden = m.hidden[j % 2]
        below, bell = normal_parts(hidden)
        m.active[:, columns(j)] = (hidden * below).astype(jnp.bfloat16)
        slope = below + hidden * bell
        keep_hidden_delta(m, 0, 0, ROWS, j, m.active_delta[:, columns(j)] * slope)

    def narrow(j):
        piece = matmul_turned(m.hidden_delta[:, columns(j)], m.up_w[0, :, columns(j)])
        m.total[...] = piece if j == 0 else m.total[...] + piece

    in_turn(m.up_w.shape[2] // PIECE, widen, bend, narrow)


def layers_kernel(names, *refs):
    m = Refs()
    for name, ref in zip(names, refs):
        setattr(m, name, ref)
    items, length = m.in_tokens.shape[:2]
    half = m.total.shape[1] // 2
    section = lax.axis_index("section")
    across = (1 - section, lax.axis_index("dp"))

    def send(i, part):
        rows = (slice(0, TEXT), slice(TEXT, ROWS))[part]
        return pltpu.make_async_remote_copy(
            src_ref=m.leaving.at[i, rows], dst_ref=m.landed.at[i, rows], send_sem=m.send_sem.at[i, part],
            recv_sem=m.recv_sem.at[i, part], device_id=across, device_id_type=MESH,
        )

    def side_copies(i):
        return (
            pltpu.make_async_copy(m.low.at[i], m.out_low.at[i], m.side_sem.at[0, i]),
            pltpu.make_async_copy(m.high.at[i], m.out_high.at[i], m.side_sem.at[1, i]),
        )

    def local(source, target, number):
        return pltpu.make_async_copy(source, target, m.copy_sem.at[number])

    def branch_copy(source, i):
        return pltpu.make_async_copy(source.at[i], m.branch.at[i], m.branch_sem.at[i])

    def weights(experts):
        found = [
            (m.qkv_w, [local(m.in_qkv.at[0], m.qkv_w, 0)]),
            (m.out_w, [local(m.in_out.at[0], m.out_w, 1)]),
            (m.up_w, []),
            (m.down_w, []),
        ]
        for slot, expert in enumerate(experts):
            found[2][1].append(local(m.in_up.at[expert], m.up_w.at[slot], 2 + slot))
            found[3][1].append(local(m.in_down.at[expert], m.down_w.at[slot], 4 + slot))
        return found

    def start_weights(found):
        copies = found[0][1] + found[1][1]
        for pair in zip(found[2][1], found[3][1]):
            copies += pair
        for copy in copies:
            copy.start()

    def needs(found, i):
        def need(ref, slot=0):
            for here, copies in found:
                if here is ref:
                    pl.when(i == 0)(copies[slot].wait)

        return need

    leaving = (
        (m.n1, m.out_n1), (m.att, m.out_att), (m.n2, m.out_n2), (m.active, m.out_active), (m.qkv, m.kept_qkv),
        (m.probs, m.kept_probs), (m.att_turned, m.kept_turned), (m.middle, m.kept_middle), (m.slope, m.kept_slope),
        (m.mixed, m.out_mixed), (m.proj_delta, m.out_proj), (m.hidden_delta, m.out_hidden),
    )
    n1, att, n2, active, qkv, probs, turned, middle, slope, mixed, proj, hidden = range(len(leaving))

    def puts(i):
        return lambda number: local(leaving[number][0], leaving[number][1].at[i], 6 + number)

    def gets(i):
        return lambda number: local(leaving[number][1].at[i], leaving[number][0], 14 + number)

    def start(copies, *which):
        for number in which:
            copies(number).start()

    def wait(copies, *which):
        for number in which:
            copies(number).wait()

    def settle(i, *which):
        @pl.when(i > 0)
        def _():
            wait(puts(i), *which)

    def text_first(target, source, i):
        value = source[i].astype(jnp.float32)
        pad = jnp.zeros((ROWS - length, value.shape[1]), jnp.float32)
        target[i, :TEXT] = value[PATCHES:].astype(jnp.bfloat16)
        target[i, TEXT:] = jnp.concatenate([value[:PATCHES], pad], axis=0).astype(jnp.bfloat16)

    def mask_targets(i):
        row = lax.broadcasted_iota(jnp.int32, (ROWS, 1), 0)
        position = jnp.where(row < TEXT, row + PATCHES, jnp.where(row < length, row - TEXT, length))
        chosen = jnp.zeros((ROWS, 1), jnp.float32)
        for mask in (m.patch_mask, m.text_mask):
            same = jnp.where(position == mask[i : i + 1, :], 1.0, 0.0)
            chosen = jnp.maximum(chosen, jnp.max(same, 1, keepdims=True))
        target = m.targets[i].astype(jnp.float32) * chosen
        m.targets[i] = target.astype(jnp.bfloat16)
        m.sums[0:1, : target.shape[1]] += jnp.sum(target, 0, keepdims=True)

    def greet(i):
        @pl.when(i == 0)
        def _():
            pl.semaphore_wait(pltpu.get_barrier_semaphore(), 1)

    def first_front(found, i, carry):
        m.need = needs(found, i)
        text_first(m.tokens, m.in_tokens, i)
        settle(i, n1, att, n2, qkv, probs, turned, middle)
        forward_front(m, m.tokens.at[i], length, False)
        start(puts(i), n1, att, n2, qkv, probs, turned, middle)
        settle(i, active, slope)
        m.need(m.up_w)
        m.need(m.down_w)
        forward_expert(m, 0, TEXT, ROWS)
        m.leaving[i, TEXT:] = m.total[TEXT:].astype(jnp.bfloat16)
        greet(i)
        send(i, 1).start()
        m.need(m.up_w, 1)
        m.need(m.down_w, 1)
        forward_expert(m, 1, 0, TEXT)
        m.leaving[i, :TEXT] = m.total[:TEXT].astype(jnp.bfloat16)
        send(i, 0).start()
        start(puts(i), active, slope)
        return carry

    def first_back(i, carry):
        start(gets(i), slope, middle, turned, qkv, probs)

        @pl.when(i > 0)
        def _():
            send(i - 1, 0).wait_send()
            send(i - 1, 1).wait_send()

        settle(i, hidden)
        wait(gets(i), slope)
        gradient = m.landed.at[i]
        send(i, 0).wait_recv()
        back_expert(m, gradient, 1, 0, TEXT)
        send(i, 1).wait_recv()
        branch_copy(m.landed, i).start()
        back_expert(m, gradient, 0, TEXT, ROWS)
        start(puts(i), hidden)
        wait(gets(i), middle, turned, qkv, probs)
        settle(i, mixed, proj)

        def keep(value):
            m.low[i] = value[:, :half]
            m.high[i] = value[:, half:].astype(jnp.bfloat16)

        back_tail(m, m.tokens.at[i], gradient, m.total[...], keep, False)
        for copy in side_copies(i):
            copy.start()
        start(puts(i), mixed, proj)
        branch_copy(m.landed, i).wait()
        return carry

    def second_both(found, i, carry):
        m.need = needs(found, i)
        branch_copy(m.targets, i).start()
        send(i, 0).wait_recv()
        send(i, 1).wait_recv()
        settle(i, n1, att, n2)
        arrived = m.landed.at[i]
        gradient = m.targets.at[i]
        m.need(m.down_w)
        forward_front(m, arrived, length, True, early_delta(m, gradient, m.att.shape[1] // 128))
        start(puts(i), n1, att, n2)
        settle(i, active, hidden)
        m.need(m.up_w)
        both_expert(m)
        start(puts(i), active, hidden)
        settle(i, mixed, proj)

        def keep(value):
            m.leaving[i] = value.astype(jnp.bfloat16)

        back_tail(m, arrived, gradient, m.total[...], keep, True)
        greet(i)
        send(i, 0).start()
        send(i, 1).start()
        start(puts(i), mixed, proj)
        branch_copy(m.targets, i).wait()
        return carry

    m.sums[...] = jnp.zeros(m.sums.shape, jnp.float32)
    barrier = pltpu.get_barrier_semaphore()
    pl.semaphore_signal(barrier, inc=1, device_id=across, device_id_type=MESH)

    @pl.when(section == 0)
    def _():
        found = weights((0, 1))
        start_weights(found)
        lax.fori_loop(0, items, functools.partial(first_front, found), 0)
        wait(puts(0), n1, att, n2, active, qkv, probs, turned, middle, slope)
        lax.fori_loop(0, items, first_back, 0)
        wait(puts(0), mixed, proj, hidden)
        send(items - 1, 0).wait_send()
        send(items - 1, 1).wait_send()
        for i in range(items):
            for copy in side_copies(i):
                copy.wait()

    @pl.when(section == 1)
    def _():
        found = weights((2,))
        start_weights(found)
        for i in range(items):
            text_first(m.targets, m.cotangent, i)
            mask_targets(i)
        lax.fori_loop(0, items, functools.partial(second_both, found), 0)
        wait(puts(0), n1, att, n2, active, mixed, proj, hidden)
        for i in range(items):
            send(i, 0).wait_send()
            send(i, 1).wait_send()


def both_layers(
    tokens, cotangent, patch_mask, text_mask, qkv_weight, out_weight, up_table, down_table, qv, proj, gain, shift, up_b, down_b
):
    items, length, width = tokens.shape
    rows = ROWS
    ff = up_b.shape[1]
    heads = width // HEAD_DIM
    bf16, f32 = jnp.bfloat16, jnp.float32
    dma = pltpu.SemaphoreType.DMA
    vmem, anywhere = pl.BlockSpec(memory_space=pltpu.VMEM), pl.BlockSpec(memory_space=pl.ANY)
    ins = dict(
        in_tokens=(tokens, vmem), cotangent=(cotangent, vmem), patch_mask=(patch_mask, vmem), text_mask=(text_mask, vmem), in_qkv=(qkv_weight, anywhere), in_out=(out_weight, anywhere),
        in_up=(up_table, anywhere), in_down=(down_table, anywhere), qv=(qv, vmem), proj=(proj, vmem), gain=(gain, vmem),
        shift=(shift, vmem), up_b=(up_b, vmem), down_b=(down_b, vmem),
    )

    def made(*shape, kind=bf16, spec=anywhere):
        return jax.ShapeDtypeStruct((items,) + shape, kind), spec

    outs = dict(
        out_n1=made(rows, width), out_att=made(rows, width), out_n2=made(rows, width), out_active=made(rows, ff),
        out_mixed=made(rows, 3 * width), out_proj=made(rows, width), out_hidden=made(rows, ff), branch=made(rows, width),
        kept_qkv=made(rows, 3 * width), kept_probs=made(heads, rows, rows), kept_turned=made(width, rows),
        kept_middle=made(rows, width, kind=f32), kept_slope=made(rows, ff),
        out_low=made(rows, width // 2, kind=f32), out_high=made(rows, width // 2),
        sums=(jax.ShapeDtypeStruct((24, PIECE), f32), vmem),
    )
    low_row, wide_row = ((rows, width), bf16), ((rows, ff), bf16)
    buffers = dict(
        qkv_w=((width, 3 * width), bf16), out_w=((width, width), bf16), up_w=((2, width, ff), bf16),
        down_w=((2, ff, width), bf16), n1=low_row, att=low_row, n2=low_row, active=wide_row,
        qkv=((rows, 3 * width), bf16), probs=((heads, rows, rows), bf16), att_turned=((width, rows), bf16),
        middle=((rows, width), f32), slope=wide_row, total=((rows, width), f32), mixed=((rows, 3 * width), bf16),
        standard=((rows, width), f32), inverse=((2, rows, 1), f32), proj_delta=low_row, scores=((2, 2, rows, rows), f32),
        score_delta=((2, 2, rows, rows), bf16), inner=((2, 2, 1, rows), f32), hidden=((2, rows, PIECE), f32),
        active_delta=((rows, ff), f32), hidden_delta=wide_row, att_delta=low_row, middle_delta=((rows, width), f32),
        leaving=((items, rows, width), bf16), landed=((items, rows, width), bf16),
        low=((items, rows, width // 2), f32), high=((items, rows, width // 2), bf16),
        tokens=((items, rows, width), bf16), targets=((items, rows, width), bf16),
    )
    semaphores = dict(
        copy_sem=dma((23,)), branch_sem=dma((items,)), side_sem=dma((2, items)), send_sem=dma((items, 2)), recv_sem=dma((items, 2)),
    )
    names = list(ins) + list(outs) + list(buffers) + list(semaphores)
    results = pl.pallas_call(
        functools.partial(layers_kernel, names),
        out_shape=[shape for shape, spec in outs.values()],
        in_specs=[spec for value, spec in ins.values()],
        out_specs=[spec for shape, spec in outs.values()],
        scratch_shapes=[pltpu.VMEM(*kind) for kind in buffers.values()] + list(semaphores.values()),
        compiler_params=pltpu.CompilerParams(
            collective_id=1, has_side_effects=True, vmem_limit_bytes=60 * 1024 * 1024
        ),
        cost_estimate=pl.CostEstimate(flops=40_000_000_000, bytes_accessed=100_000_000, transcendentals=0),
    )(*[value for value, spec in ins.values()])
    m = Refs()
    for name, result in zip(outs, results):
        setattr(m, name, result)
    return m


def small_outs(own, other, is_first, width):
    first = jnp.where(is_first, own, other)
    second = jnp.where(is_first, other, own)
    me = lax.axis_index("dp")

    def columns(rows):
        wide = rows.shape[-1] // lax.axis_size("dp")
        return lax.dynamic_slice_in_dim(rows, me * wide, wide, rows.ndim - 1)

    down = columns(jnp.concatenate([first[:2], second[:1]])[:, :width])
    up = columns(jnp.concatenate([first[9:17].reshape(2, -1), second[9:13].reshape(1, -1)]))
    own = columns(own[2:9, :width])
    return own[0:2], own[2:3], own[3:5], own[5:7], up, down


def flat(value):
    return value.reshape((-1, value.shape[-1]))


def left_parts(m, is_first):
    n1, att, n2, branch_delta = (flat(part) for part in (m.out_n1, m.out_att, m.out_n2, m.branch))
    text = (jnp.arange(n1.shape[0]) % ROWS < TEXT)[:, None]
    vision = jnp.logical_not(text & is_first).astype(jnp.bfloat16)
    text = text.astype(jnp.bfloat16)
    return [
        piece.T for piece in (n2 * vision, branch_delta * vision, n2 * text, branch_delta * text, n1, att)
    ]


def all_grads(m, length):
    up, down, qkv, out, input_grad, *small = finished(
        length,
        *summed_grads(m.out_n1, m.out_att, m.out_n2, m.branch, m.out_hidden, m.out_active, m.out_mixed, m.out_proj, m.out_high, m.sums),
        m.out_low,
    )
    return qkv.T, out.T, up.transpose(0, 2, 1), down, small, input_grad


def large_grads_plain(m, is_first):
    lefts = left_parts(m, is_first)
    hidden_delta, active = flat(m.out_hidden), flat(m.out_active)

    def total_of(left, right):
        product = jnp.dot(left, right, preferred_element_type=jnp.float32).astype(jnp.bfloat16)
        return lax.psum_scatter(product, "dp", scatter_dimension=1, tiled=True)

    def table(vision_part, text_part):
        def swapped(part):
            return lax.psum(part, "section").astype(jnp.float32)

        return jnp.stack(
            [
                swapped(jnp.where(is_first, vision_part, 0)),
                swapped(jnp.where(is_first, text_part, 0)),
                swapped(jnp.where(is_first, 0, vision_part)),
            ]
        )

    up = table(total_of(lefts[0], hidden_delta), total_of(lefts[2], hidden_delta))
    down = table(total_of(lefts[1], active), total_of(lefts[3], active))
    small = lax.psum(m.sums, "dp")
    mixed, proj = flat(m.out_mixed), flat(m.out_proj)
    return (
        total_of(lefts[4], mixed).astype(jnp.float32),
        total_of(lefts[5], proj).astype(jnp.float32),
        up,
        down.transpose(0, 2, 1),
        small,
        lax.ppermute(small, "section", [(0, 1), (1, 0)]),
    )


def shards(
    tokens, cotangent, patch_mask, text_mask, qkv_weight, qv_bias, out_weight, out_bias, norm_gain, norm_bias,
    up_table, up_bias, down_table, down_bias,
):
    is_first = lax.axis_index("section") == 0
    m = both_layers(
        tokens, cotangent, patch_mask, text_mask, qkv_weight, out_weight, up_table, down_table, qv_bias[0], out_bias,
        norm_gain[0], norm_bias[0], up_bias, down_bias,
    )
    if lax.axis_size("dp") == 16:
        qkv, out, up, down, small, input_grad = all_grads(m, tokens.shape[1])
    else:
        qkv, out, up, down, own, other = large_grads_plain(m, is_first)
        small = small_outs(own, other, is_first, tokens.shape[2])
        high = lax.ppermute(m.out_high, "section", [(0, 1)])
        value = jnp.where(is_first, m.out_low, high.astype(jnp.float32))
        input_grad = jnp.concatenate([value[:, TEXT : tokens.shape[1]], value[:, :TEXT]], axis=1)
    qv_part, proj_part, gain_part, shift_part, up_part, down_part = small
    return (
        input_grad, qkv[None], qv_part[None], out[None], proj_part, gain_part[None], shift_part[None],
        up, up_part, down, down_part,
    )


def solution(mesh):
    items, layers = P("dp"), P("section")
    return jax.shard_map(
        shards,
        mesh=mesh,
        in_specs=(items,) * 4 + (layers,) * 6 + (P(),) * 4,
        out_specs=(
            P("dp", None, "section"), P("section", None, "dp"), P("section", None, "dp"), P("section", None, "dp"),
            P("section", "dp"), P("section", None, "dp"), P("section", None, "dp"),
            P(None, None, "dp"), P(None, "dp"), P(None, "dp", None), P(None, "dp"),
        ),
        check_vma=False,
    )
```

```python
import functools

import jax
import jax.numpy as jnp
from jax import lax
from jax.experimental import pallas as pl
from jax.experimental.pallas import tpu as pltpu
from jax.sharding import PartitionSpec as P

HEAD_DIM = 64
PATCHES = 197
EPSILON = 1e-05
BLOCK = 384
WINDOW = 640
RING = 3
TEXT = 64
ROWS = 272
MESH = pl.DeviceIdType.MESH


UNITS = (
    (
        (2, 2, 0), (3, 2, 0), (2, 3, 0), (3, 0, 0), (0, 1, 0), (3, 3, 0), (0, 2, 0), (3, 1, 0), (2,
        0, 0), (4, 3, 1), (1, 0, 0), (0, 3, 0), (0, 0, 1), (2, 1, 0), (1, 3, 0), (1, 1, 0), (4, 0,
        0), (4, 1, 0), (1, 2, 0), (4, 2, 0),
    ),
    (
        (0, 2, 0), (1, 0, 0), (1, 2, 0), (1, 1, 0), (0, 1, 0), (0, 3, 1), (4, 1, 1), (4, 2, 0), (1,
        3, 0), (0, 0, 0), (3, 0, 0), (4, 0, 0), (3, 2, 0), (3, 3, 0), (4, 3, 0), (3, 1, 0), (2, 1,
        0),
    ),
)
WAIT = 4
HOP = 3
MEET = WAIT + 3 * HOP + 1
MEET_LATE = MEET + 2
LEFT_OF = ((0,), (1,), (0,), (1,), (2, 3))
MOVED = [unit[:2] for unit in UNITS[1] if unit[0] in (2, 3)]
MOVED_BITS = sum(1 << (4 * kind + plane) for kind, plane in MOVED)
FIRST_MOVED = min(u for u, unit in enumerate(UNITS[1]) if unit[:2] in MOVED)


def packed(units, handed_on):
    counts = [0, 0]
    codes = []
    for kind, plane, z_first in units:
        slot = 0
        if not (handed_on and (kind, plane) in MOVED):
            slot = counts[z_first]
            counts[z_first] += 1
        codes.append(kind | plane << 3 | z_first << 5 | slot << 6)
    codes += [0] * (-len(codes) % 3)
    return [codes[i] | codes[i + 1] << 10 | codes[i + 2] << 20 for i in range(0, len(codes), 3)], counts


PACKED, COUNTS = zip(*(packed(units, side == 0) for side, units in enumerate(UNITS)))
Y_UNITS, Z_UNITS = (max(COUNTS[0][way], COUNTS[1][way], 1) for way in range(2))


def look_up(words, u):
    word = words[0]
    for n in range(1, len(words)):
        word = jnp.where(u // 3 == n, words[n], word)
    return word >> (10 * (u % 3))


class Refs:
    pass


def sum_kernel(names, *refs):
    m = Refs()
    for name, ref in zip(names, refs):
        setattr(m, name, ref)
    section = lax.axis_index("section")
    me = lax.axis_index("dp")
    z, y, core = me // 4, (me // 2) % 2, me % 2
    peer = (section, me + 1 - 2 * core)
    beside = (section, me + 2 - 4 * y)
    right = (section, me + 4)
    left = (section, me - 4)
    aslant = (1 - section, me + 1 - 2 * core)
    across = (1 - section, me)
    on_first = section == 0
    units = jnp.where(on_first, len(UNITS[0]), len(UNITS[1]))
    computed = jnp.where(on_first, len(UNITS[0]), len(UNITS[1]) - len(MOVED))

    arrivals = [u for u, unit in enumerate(UNITS[1]) if unit[:2] in MOVED]

    def is_moved(kind, plane):
        return ((MOVED_BITS >> (4 * kind + plane)) & 1) == 1

    longest = max(map(len, PACKED))
    tables = [table + [0] * (longest - len(table)) for table in PACKED]
    words = [jnp.where(on_first, *pair) for pair in zip(*tables)]

    class Unit:
        def __init__(self, u):
            self.u = u
            code = look_up(words, u)
            self.kind = code & 7
            self.plane = (code >> 3) & 3
            self.z_first = ((code >> 5) & 1) == 1
            self.slot = (code >> 6) & 15
            moved = is_moved(self.kind, self.plane)
            self.handed_on = on_first & moved
            self.handed_in = jnp.logical_not(on_first) & moved
            self.y_first = jnp.logical_not(self.z_first | self.handed_on)
            self.y_slot = self.slot + jnp.where(self.z_first, Y_UNITS, 0)
            self.uses_text = jnp.logical_not(on_first) | (self.kind > 1)
            self.uses_patches = jnp.logical_not(on_first) | (self.kind < 2) | (self.kind == 4)
            self.order = u
            for at in arrivals:
                self.order = self.order - jnp.where((section == 1) & (u > at), 1, 0)

    def following(u):
        u = u + 1
        for at in arrivals:
            u = u + jnp.where((section == 1) & (u == at), 1, 0)
        return u

    def remote(src, dst, send, recv, device):
        return pltpu.make_async_remote_copy(
            src_ref=src, dst_ref=dst, send_sem=send, recv_sem=recv, device_id=device, device_id_type=MESH
        )

    def core_copy(order, b):
        slot = order % RING
        return remote(m.made.at[slot, 1 - core, b], m.xr.at[slot, b], m.core_send.at[order, b], m.core_recv.at[order, b], peer)

    def y_copy(n):
        return remote(m.part.at[n.u, 0], m.yr.at[n.y_slot], m.y_send.at[n.y_slot], m.y_recv.at[n.y_slot], beside)

    def right_copy(n):
        return remote(m.part.at[n.u, 1], m.zr.at[n.slot], m.right_send.at[n.slot], m.right_recv.at[n.slot], right)

    def left_copy(n):
        return remote(m.part.at[n.u, 1], m.zl.at[n.slot], m.left_send.at[n.slot], m.left_recv.at[n.slot], left)

    def right_pair(n):
        g = n.slot
        return remote(m.part.at[n.u], m.wr.at[g], m.right_send.at[Y_UNITS + g], m.right_recv.at[Y_UNITS + g], right)

    def left_pair(n):
        g = n.slot
        return remote(m.part.at[n.u], m.wl.at[g], m.left_send.at[Y_UNITS + g], m.left_recv.at[Y_UNITS + g], left)

    def over_copy(n, source, target):
        number = 4 * (n.kind - 2) + n.plane
        return remote(m.part.at[source], m.part.at[target], m.over_send.at[number], m.over_recv.at[number], across)

    def over_target(n):
        target = 0
        for at in arrivals:
            kind, plane, unused = UNITS[1][at]
            target = target + jnp.where((n.kind == kind) & (n.plane == plane), at, 0)
        return target

    def half_copy():
        return remote(m.half, m.half_out, m.half_send.at[0], m.half_recv.at[0], across)

    def own_half():
        return pl.ds(pl.multiple_of(core * BLOCK, 128), BLOCK)

    def mine(size):
        return pl.ds(pl.multiple_of(core * size, 16), size)

    def theirs(size):
        return pl.ds(pl.multiple_of((1 - core) * size, 16), size)

    def table_of(k, by_second):
        return jnp.where((k < 2) & by_second, 2, k // 2) + jnp.where(k % 2 == 1, 3, 0)

    def table_rows(k, by_second):
        return m.tables_out.at[table_of(k, by_second), :, own_half()]

    def peer_copy(k):
        return remote(m.turned.at[k, theirs(192)], table_rows(k, section == 1), m.peer_send.at[k], m.peer_recv.at[k], peer)

    def cross_copy(k, by_second, other_core):
        source = theirs(192) if other_core else mine(192)
        device = aslant if other_core else across
        number = 1 if other_core else 0
        return remote(
            m.turned.at[k, source], table_rows(k, by_second), m.cross_send.at[number, k], m.cross_recv.at[number, k], device
        )

    def attention_copies():
        rows = pl.ds(pl.multiple_of(288 + (1 - core) * 48, 16), 48)
        return (
            remote(m.turned.at[4, theirs(144)], m.qkv_out.at[:, own_half()], m.peer_send.at[4], m.peer_recv.at[4], peer),
            remote(m.turned.at[4, rows], m.out_out.at[:, own_half()], m.peer_send.at[5], m.peer_recv.at[5], peer),
        )

    def start_cross(k):
        cross_copy(k, section == 1, False).start()
        cross_copy(k, section == 1, True).start()

    def mixed_start(plane):
        return pl.multiple_of((9 * plane // 2) * 128, 128)

    def proj_start(plane):
        return pl.multiple_of((3 * plane // 2) * 128, 128)

    def tile_copies(n):
        k = n.kind
        slot = n.order % 2
        wide = pl.ds(pl.multiple_of(n.plane * 2 * BLOCK, 128), 2 * BLOCK)
        cases = []
        for ref, number, here, source, target in (
            (m.hidden, 0, (k == 0) | (k == 2), wide, slice(0, 2 * BLOCK)),
            (m.active, 0, (k == 1) | (k == 3), wide, slice(0, 2 * BLOCK)),
            (m.mixed, 0, k == 4, pl.ds(mixed_start(n.plane), WINDOW), slice(0, WINDOW)),
            (m.proj, 1, k == 4, pl.ds(proj_start(n.plane), 256), slice(WINDOW, WINDOW + 256)),
        ):
            copy = pltpu.make_async_copy(
                ref.at[:, :TEXT, source], m.text_tile.at[slot, :, :, target], m.text_sem.at[slot, number]
            )
            cases.append((here & n.uses_text, copy))
            copy = pltpu.make_async_copy(
                ref.at[:, TEXT:, source], m.patch_tile.at[slot, :, :, target], m.patch_sem.at[slot, number]
            )
            cases.append((here & n.uses_patches, copy))
        return cases

    def join_columns(slot, begin):
        for tile, joint in ((m.text_tile, m.text_joint), (m.patch_tile, m.patch_joint)):
            for side in range(2):
                at, mixed, proj = side * BLOCK, begin + side * 288, WINDOW + begin + side * 96
                joint[:, :, at : at + 288] = tile[slot, :, :, mixed : mixed + 288]
                joint[:, :, at + 288 : at + BLOCK] = tile[slot, :, :, proj : proj + 96]

    def start_tile(n):
        for here, copy in tile_copies(n):
            pl.when(here)(copy.start)

    def wait_tile(n):
        for here, copy in tile_copies(n):
            pl.when(here)(copy.wait)

    def add_into(target, source):
        target[...] = target[...] + source[...]

    def rows_dot(left, tile, *columns):
        tile = jnp.concatenate([tile[:, :, at] for at in columns], axis=2)
        return matmul(left, tile.reshape(-1, tile.shape[2]))

    def text_dot(index, slot, *columns):
        return rows_dot(m.text_left[index], m.text_tile.at[slot], *columns)

    def patch_dot(index, slot, *columns):
        return rows_dot(m.patch_left[index], m.patch_tile.at[slot], *columns)

    def joint_dot(index, *columns):
        text = rows_dot(m.text_left[index], m.text_joint, *columns)
        return rows_dot(m.patch_left[index], m.patch_joint, *columns) + text

    def compute(n):
        k = n.kind
        slot = n.order % RING

        @pl.when(n.order >= RING)
        def _():
            core_copy(n.order - RING, 0).wait_send()
            core_copy(n.order - RING, 1).wait_send()
            pl.semaphore_wait(m.credit, 1)

        @pl.when(n.order + 1 < computed)
        def _():
            start_tile(Unit(following(n.u)))

        wait_tile(n)
        tile = n.order % 2
        everything = slice(0, 2 * BLOCK)

        def put(value, columns, begin):
            for half in range(2):
                for side in range(2):
                    piece = value[half * BLOCK : (half + 1) * BLOCK, columns[side]]
                    at = slice(begin, begin + piece.shape[1])
                    m.made[slot, half, jnp.where(y == side, 1, 0), :, at] = piece.astype(jnp.bfloat16)

        sides = (slice(0, BLOCK), slice(BLOCK, 2 * BLOCK))

        @pl.when((k < 4) & jnp.logical_not(n.uses_text))
        def _():
            put(patch_dot(k % 2, tile, everything), sides, 0)

        @pl.when((k < 4) & jnp.logical_not(n.uses_patches))
        def _():
            put(text_dot(k % 2, tile, everything), sides, 0)

        @pl.when((k < 4) & n.uses_text & n.uses_patches)
        def _():
            put(patch_dot(k % 2, tile, everything) + text_dot(k % 2, tile, everything), sides, 0)

        @pl.when(k == 4)
        def _():
            ends = (slice(256, BLOCK), slice(BLOCK + 256, 2 * BLOCK))
            for odd in range(2):
                pl.when(n.plane % 2 == odd)(functools.partial(join_columns, tile, 64 * odd))
            mixed = joint_dot(2, everything)
            proj = joint_dot(3, *ends)
            put(mixed, (slice(0, 256), slice(BLOCK, BLOCK + 256)), 0)
            lanes = lax.broadcasted_iota(jnp.int32, (1, 128), 1)
            last = [jnp.where(lanes < 32, mixed[:, ends[side]], proj[:, 128 * side : 128 * side + 128]) for side in range(2)]
            put(jnp.concatenate(last, axis=1), (slice(0, 128), slice(128, 256)), 256)

        core_copy(n.order, 0).start()
        core_copy(n.order, 1).start()

    def join_core(n):
        slot = n.order % RING

        @pl.when(n.handed_in)
        def _():
            over_copy(n, 0, n.u).wait_recv()

        @pl.when(jnp.logical_not(n.handed_in))
        def _():
            core_copy(n.order, 0).wait_recv()
            m.part[n.u, 0] = m.made[slot, core, 0] + m.xr[slot, 0]

        pl.when(n.y_first)(lambda: y_copy(n).start())

        @pl.when(jnp.logical_not(n.handed_in))
        def _():
            core_copy(n.order, 1).wait_recv()
            m.part[n.u, 1] = m.made[slot, core, 1] + m.xr[slot, 1]

            @pl.when(n.order + RING < computed)
            def _():
                pl.semaphore_signal(m.credit, inc=1, device_id=peer, device_id_type=MESH)

        pl.when(n.handed_on)(lambda: over_copy(n, n.u, over_target(n)).start())

    def join_y(n):
        y_copy(n).wait_recv()
        add_into(m.part.at[n.u, 1], m.yr.at[n.y_slot])

    def take(n, one, pair, single_from, pair_from):
        @pl.when(n.y_first)
        def _():
            one(n).wait_recv()
            add_into(m.part.at[n.u, 1], single_from.at[n.slot])

        @pl.when(n.z_first)
        def _():
            pair(n).wait_recv()
            add_into(m.part.at[n.u], pair_from.at[n.slot])

    def take_right(n):
        take(n, right_copy, right_pair, m.zr, m.wr)

    def take_left(n):
        take(n, left_copy, left_pair, m.zl, m.wl)

    def pass_right(n):
        pl.when(z > 0)(lambda: take_right(n))
        pl.when(n.y_first)(lambda: right_copy(n).start())
        pl.when(n.z_first)(lambda: right_pair(n).start())

    def pass_left(n):
        pl.when(z < 3)(lambda: take_left(n))
        pl.when(n.y_first)(lambda: left_copy(n).start())
        pl.when(n.z_first)(lambda: left_pair(n).start())

    def give(n, i):
        k = n.kind
        m.turned[k] = m.part[n.u, 1].T

        @pl.when(k < 4)
        def _():
            m.tables_out[table_of(k, section == 1), :, own_half()] = m.turned[k, mine(192), :]
            peer_copy(k).start()
            pl.when(on_first | (i > FIRST_MOVED))(lambda: start_cross(k))

        @pl.when(k == 4)
        def _():
            m.qkv_out[:, own_half()] = m.turned[4, mine(144), :]
            m.out_out[:, own_half()] = m.turned[4, pl.ds(pl.multiple_of(288 + core * 48, 16), 48), :]
            for copy in attention_copies():
                copy.start()

    def greet_first(u, carry):
        n = Unit(u)
        ended = jnp.where(n.z_first, MEET_LATE, MEET) + u <= FIRST_MOVED
        pl.when(ended & (n.kind < 4) & (n.plane == z))(lambda: start_cross(n.kind))
        return carry

    def meet(n, i):
        pl.when(z > 0)(lambda: take_right(n))
        pl.when(z < 3)(lambda: take_left(n))
        pl.when(n.z_first)(lambda: y_copy(n).start())
        pl.when(n.y_first)(lambda: give(n, i))

    def meet_late(n, i):
        join_y(n)
        give(n, i)

    flips = (peer, beside, (section, me + 4 - 8 * (z % 2)), (section, me + 8 - 16 * (z // 2)), across)

    def small_copy(j):
        return remote(m.small_sum.at[j], m.small_in.at[j], m.small_send.at[j], m.small_recv.at[j], flips[j])

    def small_step(j):
        if j == 0:
            m.small_sum[0] = m.small[...]
        else:
            small_copy(j - 1).wait_recv()
            if j == 5:
                m.small_out[0] = m.small_sum[4]
                m.small_out[1] = m.small_in[4]
            else:
                m.small_sum[j] = m.small_sum[j - 1] + m.small_in[j - 1]
        if j < 5:
            small_copy(j).start()

    lefts = (m.n2, m.branch, m.n1, m.att)
    turns = [[], []]
    for side in range(2):
        for kind, plane, z_first in UNITS[side]:
            for index in () if side == 1 and (kind, plane) in MOVED else LEFT_OF[kind]:
                if index not in turns[side]:
                    turns[side].append(index)

    def stage_copy(index):
        return pltpu.make_async_copy(lefts[index], m.stage, m.stage_sem.at[0])

    def start_stage(turn):
        for side in range(2):
            pl.when(section == side)(stage_copy(turns[side][turn]).start)

    def prepare(turn):
        stage_copy(0).wait()
        number = jnp.where(on_first, turns[0][turn], turns[1][turn])

        def part(c, carry):
            at = pl.ds(pl.multiple_of(c * 128, 128), 128)
            m.text_left[number, at, :] = m.stage[:, :TEXT, at].reshape(-1, 128).T
            m.patch_left[number, at, :] = m.stage[:, TEXT:, at].reshape(-1, 128).T
            return carry

        lax.fori_loop(0, m.stage.shape[2] // 128, part, 0)
        if turn < 3:
            start_stage(turn + 1)

    barrier = pltpu.get_barrier_semaphore()
    for device in (peer, beside, flips[3]):
        pl.semaphore_signal(barrier, inc=1, device_id=device, device_id_type=MESH)

    @pl.when(section == 1)
    def _():
        for device in (across, aslant):
            pl.semaphore_signal(barrier, inc=1, device_id=device, device_id_type=MESH)

    @pl.when(z < 3)
    def _():
        pl.semaphore_signal(barrier, inc=1, device_id=right, device_id_type=MESH)

    @pl.when(z > 0)
    def _():
        pl.semaphore_signal(barrier, inc=1, device_id=left, device_id_type=MESH)

    start_stage(0)
    start_tile(Unit(jnp.int32(0)))
    prepare(0)
    pl.semaphore_wait(barrier, 3 + jnp.where(on_first, 2, 0) + jnp.where(z < 3, 1, 0) + jnp.where(z > 0, 1, 0))

    @pl.when(on_first)
    def _():
        for device in (across, aslant):
            pl.semaphore_signal(m.ready, inc=1, device_id=device, device_id_type=MESH)
        half_copy().start()


    def at_unit(u, condition, action, *more):
        @pl.when((u >= 0) & (u < units))
        def _():
            n = Unit(u)
            pl.when(condition(n))(lambda: action(n, *more))

    def in_flow(n):
        return jnp.logical_not(n.handed_on)

    def step(i, carry):
        @pl.when((i == FIRST_MOVED + 1) & (section == 1))
        def _():
            pl.semaphore_wait(m.ready, 2)
            lax.fori_loop(0, units, greet_first, 0)

        at_unit(i, lambda n: jnp.logical_not(n.handed_in), compute)
        for number in range(3):
            pl.when(i == number)(functools.partial(prepare, number + 1))
        at_unit(i - 1, lambda n: n.kind >= 0, join_core)
        at_unit(i - WAIT, lambda n: n.y_first, join_y)
        at_unit(i - WAIT - HOP * z, lambda n: in_flow(n) & (n.plane > z), pass_right)
        at_unit(i - WAIT - HOP * (3 - z), lambda n: in_flow(n) & (n.plane < z), pass_left)
        at_unit(i - MEET, lambda n: in_flow(n) & (n.plane == z), meet, i)
        at_unit(i - MEET_LATE, lambda n: n.z_first & (n.plane == z), meet_late, i)
        for j in range(4):
            pl.when(i == 3 + j)(functools.partial(small_step, j))
        return carry

    lax.fori_loop(0, units + MEET_LATE, step, 0)
    small_step(4)

    def ours(k):
        return True if k in (0, 1, 4) else is_moved(k, z) == (section == 1)

    def when_ours(k, wanted, action):
        pl.when(jnp.logical_not(ours(k) ^ wanted) if k in (2, 3) else True)(action)

    small_step(5)

    def settle(u, carry):
        n = Unit(u)

        @pl.when(jnp.logical_not(n.handed_in) & (n.order >= computed - RING))
        def _():
            core_copy(n.order, 0).wait_send()
            core_copy(n.order, 1).wait_send()

        pl.when(n.handed_on)(lambda: over_copy(n, n.u, over_target(n)).wait_send())
        pl.when(n.y_first | (n.z_first & (n.plane == z)))(lambda: y_copy(n).wait_send())
        pl.when(n.y_first & (n.plane > z))(lambda: right_copy(n).wait_send())
        pl.when(n.z_first & (n.plane > z))(lambda: right_pair(n).wait_send())
        pl.when(n.y_first & (n.plane < z))(lambda: left_copy(n).wait_send())
        pl.when(n.z_first & (n.plane < z))(lambda: left_pair(n).wait_send())
        return carry

    lax.fori_loop(0, units, settle, 0)
    for j in range(5):
        small_copy(j).wait_send()
    for k in range(4):

        def arrived(k=k):
            for other_core in (False, True):
                cross_copy(k, section == 0, other_core).wait_recv()

        def sent(k=k):
            peer_copy(k).wait()
            for other_core in (False, True):
                cross_copy(k, section == 1, other_core).wait_send()

        when_ours(k, True, sent)
        when_ours(k, False, arrived)
    for copy in attention_copies():
        copy.wait()

    @pl.when(on_first)
    def _():
        half_copy().wait_send()

    @pl.when(section == 1)
    def _():
        half_copy().wait_recv()

def summed_grads(n1, att, n2, branch, hidden, active, mixed, proj, half, small):
    dma = pltpu.SemaphoreType.DMA
    items, depth, width = n1.shape
    bf16, f32 = jnp.bfloat16, jnp.float32
    tile = (BLOCK, BLOCK)
    vmem, anywhere = pl.BlockSpec(memory_space=pltpu.VMEM), pl.BlockSpec(memory_space=pl.ANY)
    ins = dict(n1=n1, att=att, n2=n2, branch=branch, hidden=hidden, active=active, mixed=mixed, proj=proj, half=half,
        small=small)
    outs = dict(
        tables_out=((6, 192, width), bf16), qkv_out=((144, width), bf16),
        out_out=((48, width), bf16), small_out=((2,) + small.shape, f32), half_out=(half.shape, bf16),
    )
    buffers = dict(
        text_tile=((2, items, TEXT, WINDOW + 256), bf16),
        patch_tile=((2, items, depth - TEXT, WINDOW + 256), bf16), text_joint=((items, TEXT, 2 * BLOCK), bf16),
        patch_joint=((items, depth - TEXT, 2 * BLOCK), bf16), part=((20, 2) + tile, bf16), made=((RING, 2, 2) + tile, bf16),
        xr=((RING, 2) + tile, bf16), yr=((Y_UNITS + Z_UNITS,) + tile, bf16), zr=((Y_UNITS,) + tile, bf16), zl=((Y_UNITS,) + tile, bf16),
        wr=((Z_UNITS, 2) + tile, bf16), wl=((Z_UNITS, 2) + tile, bf16), turned=((5,) + tile, bf16),
        text_left=((4, width, items * TEXT), bf16), patch_left=((4, width, items * (depth - TEXT)), bf16), stage=((items, depth, width), bf16), small_sum=((5,) + small.shape, f32),
        small_in=((5,) + small.shape, f32),
    )
    semaphores = dict(
        small_send=dma((5,)), small_recv=dma((5,)), text_sem=dma((2, 2)), patch_sem=dma((2, 2)), stage_sem=dma((1,)), core_send=dma((20, 2)),
        core_recv=dma((20, 2)), y_send=dma((Y_UNITS + Z_UNITS,)), y_recv=dma((Y_UNITS + Z_UNITS,)), right_send=dma((Y_UNITS + Z_UNITS,)), right_recv=dma((Y_UNITS + Z_UNITS,)),
        left_send=dma((Y_UNITS + Z_UNITS,)), left_recv=dma((Y_UNITS + Z_UNITS,)), over_send=dma((8,)), over_recv=dma((8,)), half_send=dma((1,)), half_recv=dma((1,)), peer_send=dma((6,)),
        peer_recv=dma((6,)), cross_send=dma((2, 4)), cross_recv=dma((2, 4)),
        credit=pltpu.SemaphoreType.REGULAR, ready=pltpu.SemaphoreType.REGULAR,
    )
    names = list(ins) + list(outs) + list(buffers) + list(semaphores)
    return pl.pallas_call(
        functools.partial(sum_kernel, names),
        out_shape=[jax.ShapeDtypeStruct(*kind) for kind in outs.values()],
        in_specs=[anywhere] * 9 + [vmem],
        out_specs=[vmem] * (len(outs) - 1) + [anywhere],
        scratch_shapes=[pltpu.VMEM(*kind) for kind in buffers.values()] + list(semaphores.values()),
        compiler_params=pltpu.CompilerParams(
            collective_id=0, has_side_effects=True, vmem_limit_bytes=60 * 1024 * 1024
        ),
        cost_estimate=pl.CostEstimate(flops=48 * 2 * 768 * 384 * items * depth, bytes_accessed=40_000_000, transcendentals=0),
    )(*ins.values())


def finish_kernel(count, *refs):
    sources, targets = refs[:count], refs[count : count + 11]
    held, made, (load_sem, store_sem) = refs[count + 11 : -7], refs[-7:-2], refs[-2:]
    loads = [pltpu.make_async_copy(*pair, load_sem.at[n]) for n, pair in enumerate(zip(sources, held))]
    stores = [pltpu.make_async_copy(*pair, store_sem.at[n]) for n, pair in enumerate(zip(made, targets[:5]))]
    for load in loads:
        load.start()
    tables, qkv, out, small, half, grad = held
    small_outs = targets[5:]
    loads[0].wait()
    for number, source in enumerate((tables.at[:3], tables.at[3:], qkv, out)):
        if number > 1:
            loads[number - 1].wait()
        made[number][...] = source[...].astype(jnp.float32)
        stores[number].start()
    for load in loads[3:]:
        load.wait()
    section, me = lax.axis_index("section"), lax.axis_index("dp")
    width, wide = tables.shape[2], tables.shape[2] // 16
    ff = width * 4

    def columns(row, size):
        return pltpu.roll(row, (row.shape[1] - size * me) % row.shape[1], 1)[:, :size]

    def up_bias(side, slot):
        rows = [small[side, 9 + 4 * slot + j : 10 + 4 * slot + j] for j in range(4)]
        return columns(jnp.concatenate(rows, axis=1), ff // 16)

    own = columns(small[0, :9], wide)
    other = columns(small[1, :9], wide)
    qv_out, proj_out, gain_out, shift_out, up_bias_out, down_bias_out = small_outs
    qv_out[...] = own[2:4]
    proj_out[...] = own[4:5]
    gain_out[...] = own[5:7]
    shift_out[...] = own[7:9]
    for side in range(2):
        mine, theirs = (own, other) if side == 0 else (other, own)

        @pl.when(section == side)
        def _():
            for i in range(grad.shape[0]):
                place(made[4], i, grad[i] if side == 0 else half[i].astype(jnp.float32))
            stores[4].start()
            down_bias_out[0:2] = mine[0:2]
            down_bias_out[2:3] = theirs[0:1]
            up_bias_out[0:1] = up_bias(side, 0)
            up_bias_out[1:2] = up_bias(side, 1)
            up_bias_out[2:3] = up_bias(1 - side, 0)

    for store in stores:
        store.wait()


def place(target, i, value):
    target[i, :PATCHES] = value[TEXT : target.shape[1]]
    target[i, PATCHES:] = value[:TEXT]


def finished(length, *sources):
    tables, qkv, out, small, half, grad = sources
    width = tables.shape[2]
    shapes = [(3,) + tables.shape[1:]] * 2 + [qkv.shape, out.shape, (grad.shape[0], length, grad.shape[2])]
    shapes += [(rows, width // 16) for rows in (2, 1, 2, 2)] + [(3, width // 4), (3, width // 16)]
    return pl.pallas_call(
        functools.partial(finish_kernel, len(sources)),
        out_shape=[jax.ShapeDtypeStruct(shape, jnp.float32) for shape in shapes],
        in_specs=[pl.BlockSpec(memory_space=pltpu.HBM)] * len(sources),
        out_specs=[pl.BlockSpec(memory_space=pl.ANY)] * 5 + [pl.BlockSpec(memory_space=pltpu.VMEM)] * 6,
        scratch_shapes=[pltpu.VMEM(value.shape, value.dtype) for value in sources]
        + [pltpu.VMEM(shape, jnp.float32) for shape in shapes[:5]]
        + [pltpu.SemaphoreType.DMA((len(sources),)), pltpu.SemaphoreType.DMA((5,))],
        compiler_params=pltpu.CompilerParams(vmem_limit_bytes=60 * 1024 * 1024),
    )(*sources)


PIECE = 768
KEY_SPLIT = 256
TAIL = (0.319381530, -0.356563782, 1.781477937, -1.821255978, 1.330274429)
LOG2_E = 1.4426950408889634
LOG2_PEAK = -1.3257480647361593


def normal_parts(z):
    size = jnp.abs(z)
    scale = 1.0 + 0.2316419 * size
    t = pl.reciprocal(scale, approx=True)
    t = t * (2.0 - scale * t)
    bell = jnp.exp2(z * z * (-0.5 * LOG2_E) + LOG2_PEAK)
    series = TAIL[4]
    for factor in TAIL[3::-1]:
        series = series * t + factor
    upper = bell * (series * t)
    return jnp.where(z >= 0, 1.0 - upper, upper), bell


def matmul(left, right):
    return jnp.dot(left, right, preferred_element_type=jnp.float32)


def matmul_turned(left, right):
    return lax.dot_general(left, right, (((1,), (1,)), ((), ())), preferred_element_type=jnp.float32)


def standardized(values):
    centre = values - jnp.mean(values, -1, keepdims=True)
    inverse = lax.rsqrt(jnp.mean(centre * centre, -1, keepdims=True) + EPSILON)
    return centre * inverse, inverse


def norm_step_back(delta, standard, inverse, gain_row):
    scaled = delta * gain_row
    moved = inverse * (
        scaled - jnp.mean(scaled, -1, keepdims=True) - standard * jnp.mean(scaled * standard, -1, keepdims=True)
    )
    return moved, jnp.sum(delta * standard, 0, keepdims=True), jnp.sum(delta, 0, keepdims=True)


def half_mask(half):
    lanes = lax.broadcasted_iota(jnp.int32, (1, 128), 1)
    return (lanes < 64) if half == 0 else (lanes >= 64)


def pair_columns(p, part, width):
    return slice(part * width + p * 128, part * width + p * 128 + 128)


def both_halves(pair):
    return jnp.concatenate([jnp.where(half_mask(half), pair, jnp.zeros_like(pair)) for half in range(2)], axis=0)


def in_turn(count, *stages):
    for turn in range(count + len(stages) - 1):
        for number, stage in enumerate(stages):
            if 0 <= turn - number < count:
                stage(turn - number)


def attention_forward(m, length, beside):
    rows, width = m.att.shape

    def scores(p):
        q2 = m.qkv[:, pair_columns(p, 0, width)]
        k2 = m.qkv[:, pair_columns(p, 1, width)]
        m.scores[p % 2] = matmul_turned(both_halves(k2), q2).reshape(2, rows, rows)

    def soften(p):
        for half in range(2):
            top = m.scores[p % 2, half, :KEY_SPLIT]
            low = m.scores[p % 2, half, KEY_SPLIT:]
            key_row = KEY_SPLIT + lax.broadcasted_iota(jnp.int32, low.shape, 0)
            low = jnp.where(key_row < length, low, -1e30)
            peak = jnp.maximum(jnp.max(top, 0, keepdims=True), jnp.max(low, 0, keepdims=True))
            top = jnp.exp(top - peak)
            low = jnp.exp(low - peak)
            over = 1.0 / (jnp.sum(top, 0, keepdims=True) + jnp.sum(low, 0, keepdims=True))
            m.probs[2 * p + half, :KEY_SPLIT] = (top * over).astype(jnp.bfloat16)
            m.probs[2 * p + half, KEY_SPLIT:] = (low * over).astype(jnp.bfloat16)

    def blend(p):
        v_turned = m.qkv[:, pair_columns(p, 2, width)].T
        parts = [matmul(v_turned[64 * half : 64 * half + 64], m.probs[2 * p + half]) for half in range(2)]
        turned = jnp.concatenate(parts, axis=0)
        m.att_turned[p * 128 : p * 128 + 128, :] = turned.astype(jnp.bfloat16)
        m.att[:, p * 128 : p * 128 + 128] = turned.T.astype(jnp.bfloat16)

    in_turn(width // 128, scores, soften, blend, *beside)


def attention_back(m):
    rows, width = m.att.shape

    def probs_back(p):
        v2 = m.qkv[:, pair_columns(p, 2, width)]
        d_turned = m.att_delta[:, pair_columns(p, 0, width)].T
        m.scores[p % 2] = matmul(both_halves(v2), d_turned).reshape(2, rows, rows)
        product = d_turned.astype(jnp.float32) * m.att_turned[p * 128 : p * 128 + 128, :].astype(jnp.float32)
        for half in range(2):
            m.inner[p % 2, half] = jnp.sum(product[64 * half : 64 * half + 64], 0, keepdims=True)

    def scores_back(p):
        for half in range(2):
            probs = m.probs[2 * p + half].astype(jnp.float32)
            m.score_delta[p % 2, half] = (probs * (m.scores[p % 2, half] - m.inner[p % 2, half])).astype(jnp.bfloat16)

    def heads_back(p):
        q_at, k_at, v_at = (pair_columns(p, part, width) for part in range(3))
        score = m.score_delta[p % 2]
        probs = m.probs[2 * p : 2 * p + 2].reshape(2 * rows, rows)
        k_turned = m.qkv[:, k_at].T
        value = matmul(probs, m.att_delta[:, q_at])
        key = matmul(score.reshape(2 * rows, rows), m.qkv[:, q_at])
        query = jnp.concatenate(
            [matmul(k_turned[64 * half : 64 * half + 64], score[half]) for half in range(2)], axis=0
        )
        dq = (query.T * HEAD_DIM ** (-0.5)).astype(jnp.bfloat16)
        dk = jnp.where(half_mask(0), key[:rows], key[rows:]).astype(jnp.bfloat16)
        dv = jnp.where(half_mask(0), value[:rows], value[rows:]).astype(jnp.bfloat16)
        m.mixed[:, q_at] = dq
        m.mixed[:, k_at] = dk
        m.mixed[:, v_at] = dv
        m.sums[2:3, q_at] += jnp.sum(dq.astype(jnp.float32), 0, keepdims=True)
        m.sums[3:4, q_at] += jnp.sum(dv.astype(jnp.float32), 0, keepdims=True)

    in_turn(width // 128, probs_back, scores_back, heads_back)


def forward_front(m, x_ref, length, hold, *beside):
    x = x_ref[...].astype(jnp.float32)
    standard, inverse = standardized(x)
    if hold:
        m.standard[...] = standard
        m.inverse[0] = inverse
    m.n1[...] = (standard * m.gain[0:1] + m.shift[0:1]).astype(jnp.bfloat16)
    width = x.shape[1]
    m.need(m.qkv_w)

    def part_columns(part):
        return slice(part * width, (part + 1) * width)

    def mix(part):
        m.hidden[part % 2] = matmul(m.n1[...], m.qkv_w[:, part_columns(part)])

    def split(part):
        value = m.hidden[part % 2]
        if part == 0:
            value = (value + m.qv[0:1]).astype(jnp.bfloat16) * jnp.bfloat16(HEAD_DIM ** (-0.5))
        elif part == 2:
            value = value + m.qv[1:2]
        m.qkv[:, part_columns(part)] = value.astype(jnp.bfloat16)

    in_turn(3, mix, split)
    attention_forward(m, length, beside)
    m.need(m.out_w)
    middle = x_ref[...].astype(jnp.float32) + matmul(m.att[...], m.out_w[...]) + m.proj[0:1]
    standard, inverse = standardized(middle)
    m.middle[...] = standard if hold else middle
    if hold:
        m.inverse[1] = inverse
    m.n2[...] = (standard * m.gain[1:2] + m.shift[1:2]).astype(jnp.bfloat16)


def back_tail(m, x_ref, g_ref, n2_delta, keep, held):
    standard, inverse = (m.middle[...], m.inverse[1]) if held else standardized(m.middle[...])
    middle_part, gain, shift = norm_step_back(n2_delta, standard, inverse, m.gain[1:2])
    m.sums[6:7, :gain.shape[1]] += gain
    m.sums[8:9, :gain.shape[1]] += shift
    middle_delta = g_ref[...].astype(jnp.float32) + middle_part
    proj_delta = middle_delta.astype(jnp.bfloat16)
    m.sums[4:5, :gain.shape[1]] += jnp.sum(proj_delta.astype(jnp.float32), 0, keepdims=True)
    m.proj_delta[...] = proj_delta
    m.middle_delta[...] = middle_delta
    m.att_delta[...] = matmul_turned(proj_delta, m.out_w[...]).astype(jnp.bfloat16)
    attention_back(m)
    total = matmul_turned(m.mixed[...], m.qkv_w[...])
    standard, inverse = (m.standard[...], m.inverse[0]) if held else standardized(x_ref[...].astype(jnp.float32))
    input_part, gain, shift = norm_step_back(total, standard, inverse, m.gain[0:1])
    m.sums[5:6, :gain.shape[1]] += gain
    m.sums[7:8, :gain.shape[1]] += shift
    keep(m.middle_delta[...] + input_part)


def forward_expert(m, slot, begin, end):
    def columns(j):
        return slice(j * PIECE, (j + 1) * PIECE)

    def widen(j):
        hidden = matmul(m.n2[begin:end], m.up_w[slot, :, columns(j)])
        m.hidden[j % 2, begin:end] = hidden + m.up_b[slot : slot + 1, columns(j)]

    def bend(j):
        hidden = m.hidden[j % 2, begin:end]
        below, bell = normal_parts(hidden)
        m.active[begin:end, columns(j)] = (hidden * below).astype(jnp.bfloat16)
        m.slope[begin:end, columns(j)] = (below + hidden * bell).astype(jnp.bfloat16)

    def narrow(j):
        piece = matmul(m.active[begin:end, columns(j)], m.down_w[slot, columns(j), :])
        m.total[begin:end] = piece + (m.middle[begin:end] + m.down_b[slot : slot + 1] if j == 0 else m.total[begin:end])

    in_turn(m.up_w.shape[2] // PIECE, widen, bend, narrow)


def keep_hidden_delta(m, slot, begin, end, j, value):
    low = value.astype(jnp.bfloat16)
    m.hidden_delta[begin:end, j * PIECE : (j + 1) * PIECE] = low
    row = 9 + 4 * slot + j
    m.sums[row : row + 1] += jnp.sum(low.astype(jnp.float32), 0, keepdims=True)


def back_expert(m, g_ref, slot, begin, end):
    m.sums[slot : slot + 1, : g_ref.shape[1]] += jnp.sum(g_ref[begin:end].astype(jnp.float32), 0, keepdims=True)

    def columns(j):
        return slice(j * PIECE, (j + 1) * PIECE)

    def widen(j):
        m.hidden[j % 2, begin:end] = matmul_turned(g_ref[begin:end], m.down_w[slot, columns(j), :])

    def bend(j):
        slope = m.slope[begin:end, columns(j)].astype(jnp.float32)
        keep_hidden_delta(m, slot, begin, end, j, m.hidden[j % 2, begin:end] * slope)

    def narrow(j):
        piece = matmul_turned(m.hidden_delta[begin:end, columns(j)], m.up_w[slot, :, columns(j)])
        m.total[begin:end] = piece if j == 0 else m.total[begin:end] + piece

    in_turn(m.up_w.shape[2] // PIECE, widen, bend, narrow)


def early_delta(m, g_ref, pieces):
    size = m.active_delta.shape[1] // pieces

    def stage(p):
        columns = slice(p * size, (p + 1) * size)
        m.active_delta[:, columns] = matmul_turned(g_ref[...], m.down_w[0, columns, :])

    return stage


def both_expert(m):
    def columns(j):
        return slice(j * PIECE, (j + 1) * PIECE)

    def widen(j):
        m.hidden[j % 2] = matmul(m.n2[...], m.up_w[0, :, columns(j)]) + m.up_b[2:3, columns(j)]

    def bend(j):
        hidden = m.hidden[j % 2]
        below, bell = normal_parts(hidden)
        m.active[:, columns(j)] = (hidden * below).astype(jnp.bfloat16)
        slope = below + hidden * bell
        keep_hidden_delta(m, 0, 0, ROWS, j, m.active_delta[:, columns(j)] * slope)

    def narrow(j):
        piece = matmul_turned(m.hidden_delta[:, columns(j)], m.up_w[0, :, columns(j)])
        m.total[...] = piece if j == 0 else m.total[...] + piece

    in_turn(m.up_w.shape[2] // PIECE, widen, bend, narrow)


def layers_kernel(names, *refs):
    m = Refs()
    for name, ref in zip(names, refs):
        setattr(m, name, ref)
    items, length = m.in_tokens.shape[:2]
    half = m.total.shape[1] // 2
    section = lax.axis_index("section")
    across = (1 - section, lax.axis_index("dp"))

    def send(i, part):
        rows = (slice(0, TEXT), slice(TEXT, ROWS))[part]
        return pltpu.make_async_remote_copy(
            src_ref=m.leaving.at[i, rows], dst_ref=m.landed.at[i, rows], send_sem=m.send_sem.at[i, part],
            recv_sem=m.recv_sem.at[i, part], device_id=across, device_id_type=MESH,
        )

    def side_copies(i):
        return (
            pltpu.make_async_copy(m.low.at[i], m.out_low.at[i], m.side_sem.at[0, i]),
            pltpu.make_async_copy(m.high.at[i], m.out_high.at[i], m.side_sem.at[1, i]),
        )

    def local(source, target, number):
        return pltpu.make_async_copy(source, target, m.copy_sem.at[number])

    def branch_copy(source, i):
        return pltpu.make_async_copy(source.at[i], m.branch.at[i], m.branch_sem.at[i])

    def weights(experts):
        found = [
            (m.qkv_w, [local(m.in_qkv.at[0], m.qkv_w, 0)]),
            (m.out_w, [local(m.in_out.at[0], m.out_w, 1)]),
            (m.up_w, []),
            (m.down_w, []),
        ]
        for slot, expert in enumerate(experts):
            found[2][1].append(local(m.in_up.at[expert], m.up_w.at[slot], 2 + slot))
            found[3][1].append(local(m.in_down.at[expert], m.down_w.at[slot], 4 + slot))
        return found

    def start_weights(found):
        copies = found[0][1] + found[1][1]
        for pair in zip(found[2][1], found[3][1]):
            copies += pair
        for copy in copies:
            copy.start()

    def needs(found, i):
        def need(ref, slot=0):
            for here, copies in found:
                if here is ref:
                    pl.when(i == 0)(copies[slot].wait)

        return need

    leaving = (
        (m.n1, m.out_n1), (m.att, m.out_att), (m.n2, m.out_n2), (m.active, m.out_active), (m.qkv, m.kept_qkv),
        (m.probs, m.kept_probs), (m.att_turned, m.kept_turned), (m.middle, m.kept_middle), (m.slope, m.kept_slope),
        (m.mixed, m.out_mixed), (m.proj_delta, m.out_proj), (m.hidden_delta, m.out_hidden),
    )
    n1, att, n2, active, qkv, probs, turned, middle, slope, mixed, proj, hidden = range(len(leaving))

    def puts(i):
        return lambda number: local(leaving[number][0], leaving[number][1].at[i], 6 + number)

    def gets(i):
        return lambda number: local(leaving[number][1].at[i], leaving[number][0], 14 + number)

    def start(copies, *which):
        for number in which:
            copies(number).start()

    def wait(copies, *which):
        for number in which:
            copies(number).wait()

    def settle(i, *which):
        @pl.when(i > 0)
        def _():
            wait(puts(i), *which)

    def text_first(target, source, i):
        value = source[i].astype(jnp.float32)
        pad = jnp.zeros((ROWS - length, value.shape[1]), jnp.float32)
        target[i, :TEXT] = value[PATCHES:].astype(jnp.bfloat16)
        target[i, TEXT:] = jnp.concatenate([value[:PATCHES], pad], axis=0).astype(jnp.bfloat16)

    def mask_targets(i):
        row = lax.broadcasted_iota(jnp.int32, (ROWS, 1), 0)
        position = jnp.where(row < TEXT, row + PATCHES, jnp.where(row < length, row - TEXT, length))
        chosen = jnp.zeros((ROWS, 1), jnp.float32)
        for mask in (m.patch_mask, m.text_mask):
            same = jnp.where(position == mask[i : i + 1, :], 1.0, 0.0)
            chosen = jnp.maximum(chosen, jnp.max(same, 1, keepdims=True))
        target = m.targets[i].astype(jnp.float32) * chosen
        m.targets[i] = target.astype(jnp.bfloat16)
        m.sums[0:1, : target.shape[1]] += jnp.sum(target, 0, keepdims=True)

    def greet(i):
        @pl.when(i == 0)
        def _():
            pl.semaphore_wait(pltpu.get_barrier_semaphore(), 1)

    def first_front(found, i, carry):
        m.need = needs(found, i)
        text_first(m.tokens, m.in_tokens, i)
        settle(i, n1, att, n2, qkv, probs, turned, middle)
        forward_front(m, m.tokens.at[i], length, False)
        start(puts(i), n1, att, n2, qkv, probs, turned, middle)
        settle(i, active, slope)
        m.need(m.up_w)
        m.need(m.down_w)
        forward_expert(m, 0, TEXT, ROWS)
        m.leaving[i, TEXT:] = m.total[TEXT:].astype(jnp.bfloat16)
        greet(i)
        send(i, 1).start()
        m.need(m.up_w, 1)
        m.need(m.down_w, 1)
        forward_expert(m, 1, 0, TEXT)
        m.leaving[i, :TEXT] = m.total[:TEXT].astype(jnp.bfloat16)
        send(i, 0).start()
        start(puts(i), active, slope)
        return carry

    def first_back(i, carry):
        start(gets(i), slope, middle, turned, qkv, probs)

        @pl.when(i > 0)
        def _():
            send(i - 1, 0).wait_send()
            send(i - 1, 1).wait_send()

        settle(i, hidden)
        wait(gets(i), slope)
        gradient = m.landed.at[i]
        send(i, 0).wait_recv()
        back_expert(m, gradient, 1, 0, TEXT)
        send(i, 1).wait_recv()
        branch_copy(m.landed, i).start()
        back_expert(m, gradient, 0, TEXT, ROWS)
        start(puts(i), hidden)
        wait(gets(i), middle, turned, qkv, probs)
        settle(i, mixed, proj)

        def keep(value):
            m.low[i] = value[:, :half]
            m.high[i] = value[:, half:].astype(jnp.bfloat16)

        back_tail(m, m.tokens.at[i], gradient, m.total[...], keep, False)
        for copy in side_copies(i):
            copy.start()
        start(puts(i), mixed, proj)
        branch_copy(m.landed, i).wait()
        return carry

    def second_both(found, i, carry):
        m.need = needs(found, i)
        branch_copy(m.targets, i).start()
        send(i, 0).wait_recv()
        send(i, 1).wait_recv()
        settle(i, n1, att, n2)
        arrived = m.landed.at[i]
        gradient = m.targets.at[i]
        m.need(m.down_w)
        forward_front(m, arrived, length, True, early_delta(m, gradient, m.att.shape[1] // 128))
        start(puts(i), n1, att, n2)
        settle(i, active, hidden)
        m.need(m.up_w)
        both_expert(m)
        start(puts(i), active, hidden)
        settle(i, mixed, proj)

        def keep(value):
            m.leaving[i] = value.astype(jnp.bfloat16)

        back_tail(m, arrived, gradient, m.total[...], keep, True)
        greet(i)
        send(i, 0).start()
        send(i, 1).start()
        start(puts(i), mixed, proj)
        branch_copy(m.targets, i).wait()
        return carry

    m.sums[...] = jnp.zeros(m.sums.shape, jnp.float32)
    barrier = pltpu.get_barrier_semaphore()
    pl.semaphore_signal(barrier, inc=1, device_id=across, device_id_type=MESH)

    @pl.when(section == 0)
    def _():
        found = weights((0, 1))
        start_weights(found)
        lax.fori_loop(0, items, functools.partial(first_front, found), 0)
        wait(puts(0), n1, att, n2, active, qkv, probs, turned, middle, slope)
        lax.fori_loop(0, items, first_back, 0)
        wait(puts(0), mixed, proj, hidden)
        send(items - 1, 0).wait_send()
        send(items - 1, 1).wait_send()
        for i in range(items):
            for copy in side_copies(i):
                copy.wait()

    @pl.when(section == 1)
    def _():
        found = weights((2,))
        start_weights(found)
        for i in range(items):
            text_first(m.targets, m.cotangent, i)
            mask_targets(i)
        lax.fori_loop(0, items, functools.partial(second_both, found), 0)
        wait(puts(0), n1, att, n2, active, mixed, proj, hidden)
        for i in range(items):
            send(i, 0).wait_send()
            send(i, 1).wait_send()


def both_layers(
    tokens, cotangent, patch_mask, text_mask, qkv_weight, out_weight, up_table, down_table, qv, proj, gain, shift, up_b, down_b
):
    items, length, width = tokens.shape
    rows = ROWS
    ff = up_b.shape[1]
    heads = width // HEAD_DIM
    bf16, f32 = jnp.bfloat16, jnp.float32
    dma = pltpu.SemaphoreType.DMA
    vmem, anywhere = pl.BlockSpec(memory_space=pltpu.VMEM), pl.BlockSpec(memory_space=pl.ANY)
    ins = dict(
        in_tokens=(tokens, vmem), cotangent=(cotangent, vmem), patch_mask=(patch_mask, vmem), text_mask=(text_mask, vmem), in_qkv=(qkv_weight, anywhere), in_out=(out_weight, anywhere),
        in_up=(up_table, anywhere), in_down=(down_table, anywhere), qv=(qv, vmem), proj=(proj, vmem), gain=(gain, vmem),
        shift=(shift, vmem), up_b=(up_b, vmem), down_b=(down_b, vmem),
    )

    def made(*shape, kind=bf16, spec=anywhere):
        return jax.ShapeDtypeStruct((items,) + shape, kind), spec

    outs = dict(
        out_n1=made(rows, width), out_att=made(rows, width), out_n2=made(rows, width), out_active=made(rows, ff),
        out_mixed=made(rows, 3 * width), out_proj=made(rows, width), out_hidden=made(rows, ff), branch=made(rows, width),
        kept_qkv=made(rows, 3 * width), kept_probs=made(heads, rows, rows), kept_turned=made(width, rows),
        kept_middle=made(rows, width, kind=f32), kept_slope=made(rows, ff),
        out_low=made(rows, width // 2, kind=f32), out_high=made(rows, width // 2),
        sums=(jax.ShapeDtypeStruct((24, PIECE), f32), vmem),
    )
    low_row, wide_row = ((rows, width), bf16), ((rows, ff), bf16)
    buffers = dict(
        qkv_w=((width, 3 * width), bf16), out_w=((width, width), bf16), up_w=((2, width, ff), bf16),
        down_w=((2, ff, width), bf16), n1=low_row, att=low_row, n2=low_row, active=wide_row,
        qkv=((rows, 3 * width), bf16), probs=((heads, rows, rows), bf16), att_turned=((width, rows), bf16),
        middle=((rows, width), f32), slope=wide_row, total=((rows, width), f32), mixed=((rows, 3 * width), bf16),
        standard=((rows, width), f32), inverse=((2, rows, 1), f32), proj_delta=low_row, scores=((2, 2, rows, rows), f32),
        score_delta=((2, 2, rows, rows), bf16), inner=((2, 2, 1, rows), f32), hidden=((2, rows, PIECE), f32),
        active_delta=((rows, ff), f32), hidden_delta=wide_row, att_delta=low_row, middle_delta=((rows, width), f32),
        leaving=((items, rows, width), bf16), landed=((items, rows, width), bf16),
        low=((items, rows, width // 2), f32), high=((items, rows, width // 2), bf16),
        tokens=((items, rows, width), bf16), targets=((items, rows, width), bf16),
    )
    semaphores = dict(
        copy_sem=dma((23,)), branch_sem=dma((items,)), side_sem=dma((2, items)), send_sem=dma((items, 2)), recv_sem=dma((items, 2)),
    )
    names = list(ins) + list(outs) + list(buffers) + list(semaphores)
    results = pl.pallas_call(
        functools.partial(layers_kernel, names),
        out_shape=[shape for shape, spec in outs.values()],
        in_specs=[spec for value, spec in ins.values()],
        out_specs=[spec for shape, spec in outs.values()],
        scratch_shapes=[pltpu.VMEM(*kind) for kind in buffers.values()] + list(semaphores.values()),
        compiler_params=pltpu.CompilerParams(
            collective_id=1, has_side_effects=True, vmem_limit_bytes=60 * 1024 * 1024
        ),
        cost_estimate=pl.CostEstimate(flops=40_000_000_000, bytes_accessed=100_000_000, transcendentals=0),
    )(*[value for value, spec in ins.values()])
    m = Refs()
    for name, result in zip(outs, results):
        setattr(m, name, result)
    return m


def small_outs(own, other, is_first, width):
    first = jnp.where(is_first, own, other)
    second = jnp.where(is_first, other, own)
    me = lax.axis_index("dp")

    def columns(rows):
        wide = rows.shape[-1] // lax.axis_size("dp")
        return lax.dynamic_slice_in_dim(rows, me * wide, wide, rows.ndim - 1)

    down = columns(jnp.concatenate([first[:2], second[:1]])[:, :width])
    up = columns(jnp.concatenate([first[9:17].reshape(2, -1), second[9:13].reshape(1, -1)]))
    own = columns(own[2:9, :width])
    return own[0:2], own[2:3], own[3:5], own[5:7], up, down


def flat(value):
    return value.reshape((-1, value.shape[-1]))


def left_parts(m, is_first):
    n1, att, n2, branch_delta = (flat(part) for part in (m.out_n1, m.out_att, m.out_n2, m.branch))
    text = (jnp.arange(n1.shape[0]) % ROWS < TEXT)[:, None]
    vision = jnp.logical_not(text & is_first).astype(jnp.bfloat16)
    text = text.astype(jnp.bfloat16)
    return [
        piece.T for piece in (n2 * vision, branch_delta * vision, n2 * text, branch_delta * text, n1, att)
    ]


def all_grads(m, length):
    up, down, qkv, out, input_grad, *small = finished(
        length,
        *summed_grads(m.out_n1, m.out_att, m.out_n2, m.branch, m.out_hidden, m.out_active, m.out_mixed, m.out_proj, m.out_high, m.sums),
        m.out_low,
    )
    return qkv.T, out.T, up.transpose(0, 2, 1), down, small, input_grad


def large_grads_plain(m, is_first):
    lefts = left_parts(m, is_first)
    hidden_delta, active = flat(m.out_hidden), flat(m.out_active)

    def total_of(left, right):
        product = jnp.dot(left, right, preferred_element_type=jnp.float32).astype(jnp.bfloat16)
        return lax.psum_scatter(product, "dp", scatter_dimension=1, tiled=True)

    def table(vision_part, text_part):
        def swapped(part):
            return lax.psum(part, "section").astype(jnp.float32)

        return jnp.stack(
            [
                swapped(jnp.where(is_first, vision_part, 0)),
                swapped(jnp.where(is_first, text_part, 0)),
                swapped(jnp.where(is_first, 0, vision_part)),
            ]
        )

    up = table(total_of(lefts[0], hidden_delta), total_of(lefts[2], hidden_delta))
    down = table(total_of(lefts[1], active), total_of(lefts[3], active))
    small = lax.psum(m.sums, "dp")
    mixed, proj = flat(m.out_mixed), flat(m.out_proj)
    return (
        total_of(lefts[4], mixed).astype(jnp.float32),
        total_of(lefts[5], proj).astype(jnp.float32),
        up,
        down.transpose(0, 2, 1),
        small,
        lax.ppermute(small, "section", [(0, 1), (1, 0)]),
    )


def shards(
    tokens, cotangent, patch_mask, text_mask, qkv_weight, qv_bias, out_weight, out_bias, norm_gain, norm_bias,
    up_table, up_bias, down_table, down_bias,
):
    is_first = lax.axis_index("section") == 0
    m = both_layers(
        tokens, cotangent, patch_mask, text_mask, qkv_weight, out_weight, up_table, down_table, qv_bias[0], out_bias,
        norm_gain[0], norm_bias[0], up_bias, down_bias,
    )
    if lax.axis_size("dp") == 16:
        qkv, out, up, down, small, input_grad = all_grads(m, tokens.shape[1])
    else:
        qkv, out, up, down, own, other = large_grads_plain(m, is_first)
        small = small_outs(own, other, is_first, tokens.shape[2])
        high = lax.ppermute(m.out_high, "section", [(0, 1)])
        value = jnp.where(is_first, m.out_low, high.astype(jnp.float32))
        input_grad = jnp.concatenate([value[:, TEXT : tokens.shape[1]], value[:, :TEXT]], axis=1)
    qv_part, proj_part, gain_part, shift_part, up_part, down_part = small
    return (
        input_grad, qkv[None], qv_part[None], out[None], proj_part, gain_part[None], shift_part[None],
        up, up_part, down, down_part,
    )


def solution(mesh):
    items, layers = P("dp"), P("section")
    return jax.shard_map(
        shards,
        mesh=mesh,
        in_specs=(items,) * 4 + (layers,) * 6 + (P(),) * 4,
        out_specs=(
            P("dp", None, "section"), P("section", None, "dp"), P("section", None, "dp"), P("section", None, "dp"),
            P("section", "dp"), P("section", None, "dp"), P("section", None, "dp"),
            P(None, None, "dp"), P(None, "dp"), P(None, "dp", None), P(None, "dp"),
        ),
        check_vma=False,
    )
```
